32 devices in a mesh: grp: 2 (over x), row: 16 (over z, y, core).
Axes of the slice: x: 2, y: 2, z: 4, core: 2. Of those that a mesh axis runs over, the one named last changes fastest.
Arguments:
- cell_coeffs: float32 [6, 32, 384], P(None, 'row'), may hold values from 0.5 to 2
- z_factor: float32 [4, 64, 384, 128], P(None, ('grp', 'row')), parts along dimension 1, may hold values from -0.022552745 to 0.022552745
- noise_cols: float32 [4, 64, 384, 128], P(None, ('grp', 'row')), parts along dimension 1, may hold values from -0.022552745 to 0.022552745
- q_bar: float32 [4, 64, 384, 256], P(None, ('grp', 'row')), parts along dimension 1, may hold values from -10 to 10
- r_bar: float32 [512, 256], P('grp'), parts along dimension 0, may hold values from -11.085125 to 11.085125
Outputs:
- z_grad: float32 [4, 64, 384, 128], P(None, ('grp', 'row')), parts along dimension 1
- noise_grad: float32 [4, 64, 384, 128], P(None, ('grp', 'row')), parts along dimension 1
The draws below stay inside these ranges and needn't reach their ends.
There are 2 independent parts, one for each index of `grp`. The reference program is written for one: setup_inputs(seed, part) draws one part's arguments, and reference() takes and returns one part's arrays. A program takes and returns all parts, laid end to end along the dimension named above; an argument that names none is the same for every part. Nothing has to cross between parts.
All inputs are finite; a program needn't handle non-finite values.
Results may differ from the reference program's by a relative error of at most 0.000061.
Values sent between devices are 32-bit elements; how exact they have to be, the bound alone decides.
No kernel may reach another device: no remote copies, remote signals or barrier semaphores. Data moves between devices by JAX's collectives and lax.ppermute only.
A program may use at most 64 MiB of HBM per device.

```python
import math
import jax
import jax.numpy as jnp
from jax import lax

LX = 384
K = 128
KN = 128
NR = 32
ROWS = 49152


def draw_piece(key, shape):
    return jnp.clip(jax.random.normal(key, shape, jnp.float32), -5.0, 5.0)


def draw_shared(key):
    spread = float(ROWS) ** (-0.5)
    base_z = draw_piece(jax.random.fold_in(key, 11), (4, NR, LX, K))
    base_n = draw_piece(jax.random.fold_in(key, 12), (4, NR, LX, KN))
    loose = draw_piece(jax.random.fold_in(key, 13), (4, NR, LX, K + KN))
    bar_q = jnp.concatenate([base_z, base_n], axis=3) + loose
    bar_r = jnp.clip(jax.random.normal(jax.random.fold_in(key, 14), (K + KN, K + KN), jnp.float32), -5.0, 5.0) * (0.01 * float(ROWS) ** 0.5)
    return (base_z * spread, base_n * spread, bar_q, bar_r)


def draw_z_factor(key, part):
    return draw_shared(key)[0]


def draw_noise_cols(key, part):
    return draw_shared(key)[1]


def draw_q_bar(key, part):
    return draw_shared(key)[2]


def draw_r_bar(key, part):
    return draw_shared(key)[3]


def levels(key, shape, split, least, high):
    loudness = 1.0
    for position, blocks in split:
        draws = jax.random.uniform(jax.random.fold_in(jax.random.fold_in(key, 6), position), (blocks,), jnp.float32, least / len(split), high / len(split))
        loudness = loudness * jnp.repeat(jnp.exp(draws), shape[position] // blocks).reshape((-1,) + (1,) * (len(shape) - 1 - position))
    return loudness


def setup_inputs(seed: int = 0, part: int = 0) -> dict:
    key_of = jax.random.split(jax.random.key(seed), 6)
    part_splits = jax.random.split(jax.random.fold_in(key_of[5], part), 6)
    return {
        "cell_coeffs": jnp.clip(jnp.exp(math.log(2.0) - 1.3862944 * jax.random.uniform(key_of[0], (6, NR, LX), jnp.float32) ** levels(key_of[0], (6, NR, LX), ((1, 16),), -0.2, 0.2)), 0.5, 2.0),
        "z_factor": draw_z_factor(jax.random.fold_in(jax.random.fold_in(key_of[5], part), 71), part),
        "noise_cols": draw_noise_cols(jax.random.fold_in(jax.random.fold_in(key_of[5], part), 71), part),
        "q_bar": draw_q_bar(jax.random.fold_in(jax.random.fold_in(key_of[5], part), 71), part),
        "r_bar": draw_r_bar(jax.random.fold_in(jax.random.fold_in(key_of[5], part), 71), part),
    }


rate_scales = (0.4, 0.4, 0.1, 0.2, 0.1, 0.1)
exact = lax.Precision.HIGHEST

def local_part(values, scaled, transposed):
    detuning = scaled[0][..., None]
    mech_freq = scaled[1][..., None]
    coupling = scaled[2][..., None]
    cavity_loss = scaled[3][..., None]
    phonon_loss = scaled[4][..., None]
    light_x, light_p, motion_x, motion_p = (values[0], values[1], values[2], values[3])
    if transposed:
        return jnp.stack([-0.5 * cavity_loss * light_x + detuning * light_p - 2.0 * coupling * motion_p, -detuning * light_x - 0.5 * cavity_loss * light_p, -2.0 * coupling * light_p - mech_freq * motion_p, mech_freq * motion_x - 0.5 * phonon_loss * motion_p])
    return jnp.stack([-0.5 * cavity_loss * light_x - detuning * light_p, detuning * light_x - 0.5 * cavity_loss * light_p - 2.0 * coupling * motion_x, mech_freq * motion_p, -mech_freq * motion_x - 0.5 * phonon_loss * motion_p - 2.0 * coupling * light_x])

def hop_sources(values, scaled, transposed):
    hopping = scaled[5][..., None]
    if transposed:
        return jnp.stack([hopping * values[0], hopping * values[1]])
    return jnp.stack([values[1], values[0]])

def neighbours(source):
    middle = source[:, 1:-1]
    sideways = jnp.pad(middle, ((0, 0), (0, 0), (1, 1), (0, 0)))
    return source[:, :-2] + source[:, 2:] + sideways[:, :, :-2] + sideways[:, :, 2:]

def hop_add(local_term, hop_sums, scaled, transposed):
    hopping = scaled[5][..., None]
    if transposed:
        return jnp.stack([local_term[0] + hop_sums[1], local_term[1] - hop_sums[0], local_term[2], local_term[3]])
    return jnp.stack([local_term[0] - hopping * hop_sums[0], local_term[1] + hopping * hop_sums[1], local_term[2], local_term[3]])

def apply_full(values, scaled, transposed):
    source = hop_sources(values, scaled, transposed)
    extended = jnp.pad(source, ((0, 0), (1, 1), (0, 0), (0, 0)))
    return hop_add(local_part(values, scaled, transposed), neighbours(extended), scaled, transposed)

def expand(values, scaled, transposed):
    first_term = apply_full(values, scaled, transposed)
    second = apply_full(first_term, scaled, transposed)
    return values + first_term + 0.5 * second

def reference(cell_coeffs, z_factor, noise_cols, q_bar, r_bar):
    scaled = cell_coeffs * jnp.array(rate_scales, jnp.float32)[:, None, None]
    rank_cols = z_factor.shape[3]
    stacked = jnp.concatenate([expand(z_factor, scaled, False), noise_cols], axis=3)
    flat_rows = stacked.reshape(-1, stacked.shape[3])
    bar_rows = q_bar.reshape(-1, q_bar.shape[3])
    gram_matrix = jnp.einsum('ik,il->kl', flat_rows, flat_rows, precision=exact)
    lower_factor = jnp.linalg.cholesky(gram_matrix)
    identity = jnp.eye(gram_matrix.shape[0], dtype=jnp.float32)
    r_inv = lax.linalg.triangular_solve(lower_factor, identity, left_side=True, lower=True).T
    upper_factor = lower_factor.T
    q_fact = jnp.dot(flat_rows, r_inv, precision=exact)
    cross = jnp.einsum('ik,il->kl', bar_rows, q_fact, precision=exact)
    middle = jnp.dot(upper_factor, jnp.triu(r_bar).T, precision=exact) - cross
    symmetric = jnp.tril(middle) + jnp.tril(middle, -1).T
    grad_rows = jnp.dot(bar_rows + jnp.dot(q_fact, symmetric, precision=exact), r_inv.T, precision=exact)
    grad_x = grad_rows.reshape(q_bar.shape)
    z_grad = expand(grad_x[..., :rank_cols], scaled, True)
    return (z_grad, grad_x[..., rank_cols:])
```

```python
import jax
import jax.numpy as jnp
from jax import lax
from jax.experimental import pallas as pl
from jax.experimental.pallas import tpu as pltpu
from jax.sharding import PartitionSpec as P

rate_scales = (0.4, 0.4, 0.1, 0.2, 0.1, 0.1)
exact = lax.Precision.HIGHEST
f32 = jnp.float32
bf16 = jnp.bfloat16
VMEM = pl.BlockSpec(memory_space=pltpu.VMEM)
LIMIT = 56 * 1024 * 1024
PANEL = 16


def call(kernel, outs, flops, moved, scratch=()):
    return pl.pallas_call(
        kernel,
        out_shape=outs,
        scratch_shapes=list(scratch),
        compiler_params=pltpu.CompilerParams(vmem_limit_bytes=LIMIT),
        cost_estimate=pl.CostEstimate(flops=flops, bytes_accessed=moved, transcendentals=0),
    )


def split2(value):
    high = value.astype(bf16)
    low = (value - high.astype(f32)).astype(bf16)
    return high, low


def split3(value):
    high = value.astype(bf16)
    rest = value - high.astype(f32)
    mid = rest.astype(bf16)
    low = (rest - mid.astype(f32)).astype(bf16)
    return high, mid, low


def dot(a, b, contract):
    return lax.dot_general(a, b, ((contract[0], contract[1]), ((), ())), preferred_element_type=f32)


def coefficients(coeff_ref):
    table = coeff_ref[...]
    cols = jnp.transpose(table)
    out = []
    for r in range(2):
        out.append([cols[:, 2 * k + r : 2 * k + r + 1] * rate_scales[k] for k in range(6)])
    return out


def side(v):
    n = v.shape[0]
    place = lax.broadcasted_iota(jnp.int32, v.shape, 0)
    left = jnp.where(place == 0, 0.0, pltpu.roll(v, 1, 0))
    right = jnp.where(place == n - 1, 0.0, pltpu.roll(v, n - 1, 0))
    return left + right


def forward_light(c, xa, pa, xb, hop_x, hop_p):
    d, w, g, l, m, j = c
    return (
        -0.5 * l * xa - d * pa - j * hop_p,
        d * xa - 0.5 * l * pa - 2.0 * g * xb + j * hop_x,
    )


def forward_heavy(c, xa, xb, pb):
    d, w, g, l, m, j = c
    return w * pb, -w * xb - 0.5 * m * pb - 2.0 * g * xa


def backward_light(c, xa, pa, pb, hop_x, hop_p):
    d, w, g, l, m, j = c
    return (
        -0.5 * l * xa + d * pa - 2.0 * g * pb + hop_p,
        -d * xa - 0.5 * l * pa - hop_x,
    )


def backward_heavy(c, pa, xb, pb):
    d, w, g, l, m, j = c
    return -2.0 * g * pa - w * pb, w * xb - 0.5 * m * pb


def forward_rim(coeff_ref, z_ref, down_ref, up_ref):
    c = coefficients(coeff_ref)
    n = z_ref.shape[2]
    for r, out in ((0, down_ref), (1, up_ref)):
        xa, pa, xb = z_ref[0, r], z_ref[1, r], z_ref[2, r]
        hop_x = z_ref[0, 1 - r] + side(xa)
        hop_p = z_ref[1, 1 - r] + side(pa)
        bx, bp = forward_light(c[r], xa, pa, xb, hop_x, hop_p)
        out[0:n] = xa
        out[n : 2 * n] = pa
        out[2 * n : 3 * n] = bx
        out[3 * n : 4 * n] = bp
        hopping = coeff_ref[10 + r : 11 + r, :] * rate_scales[5]
        pieces = [hopping[:, k * 128 : (k + 1) * 128] for k in range(n // 128)]
        pieces.append(jnp.zeros((8 - n // 128, 128), f32))
        out[4 * n :] = jnp.concatenate(pieces, axis=0)


def far_hopping(recv_ref, n):
    tail = jnp.transpose(recv_ref[4 * n : 4 * n + 8])
    return jnp.concatenate([tail[:, k : k + 1] for k in range(n // 128)], axis=0)


def noise_products(noise_ref, q_ref, gram_ref, cross_ref, nh_ref, nl_ref, qh_ref, ql_ref):
    nh, nl = split2(noise_ref[...])
    qh, ql = split2(q_ref[...])
    nh_ref[...] = nh
    nl_ref[...] = nl
    qh_ref[...] = qh
    ql_ref[...] = ql
    down = ((0,), (0,))
    mixed = dot(nh, nl, down)
    gram_ref[...] = dot(nh, nh, down) + mixed + jnp.transpose(mixed)
    cross_ref[...] = dot(qh, nh, down) + dot(qh, nl, down) + dot(ql, nh, down)


def expand_products(
    coeff_ref, z_ref, low_ref, high_ref, nh_ref, nl_ref, qh_ref, ql_ref,
    gzz_ref, gzn_ref, cross_ref, xh_ref, xl_ref, first_ref,
):
    c = coefficients(coeff_ref)
    n = z_ref.shape[2]
    jlow = far_hopping(low_ref, n)
    jhigh = far_hopping(high_ref, n)
    low = [low_ref[k * n : (k + 1) * n] for k in range(4)]
    high = [high_ref[k * n : (k + 1) * n] for k in range(4)]
    far = ((low, jlow), (high, jhigh))
    for r in range(2):
        xa, pa, xb, pb = (z_ref[k, r] for k in range(4))
        hop_x = z_ref[0, 1 - r] + far[r][0][0] + side(xa)
        hop_p = z_ref[1, 1 - r] + far[r][0][1] + side(pa)
        first_ref[0, r], first_ref[1, r] = forward_light(c[r], xa, pa, xb, hop_x, hop_p)
        first_ref[2, r], first_ref[3, r] = forward_heavy(c[r], xa, xb, pb)
    for r in range(2):
        xa, pa, xb, pb = (first_ref[k, r] for k in range(4))
        beyond, jfar = far[r]
        far_x = beyond[2] - jfar * z_ref[1, r]
        far_p = beyond[3] + jfar * z_ref[0, r]
        hop_x = first_ref[0, 1 - r] + far_x + side(xa)
        hop_p = first_ref[1, 1 - r] + far_p + side(pa)
        second = forward_light(c[r], xa, pa, xb, hop_x, hop_p) + forward_heavy(c[r], xa, xb, pb)
        for k, (f, s) in enumerate(zip((xa, pa, xb, pb), second)):
            start = (2 * k + r) * n
            h, l = split2(z_ref[k, r] + f + 0.5 * s)
            xh_ref[start : start + n] = h
            xl_ref[start : start + n] = l
    down = ((0,), (0,))
    xh, xl = xh_ref[...], xl_ref[...]
    mixed = dot(xh, xl, down)
    gzz_ref[...] = dot(xh, xh, down) + mixed + jnp.transpose(mixed)
    gzn_ref[...] = dot(xh, nh_ref[...], down) + dot(xh, nl_ref[...], down) + dot(xl, nh_ref[...], down)
    cross_ref[...] = dot(qh_ref[...], xh, down) + dot(qh_ref[...], xl, down) + dot(ql_ref[...], xh, down)


def factor(sums_ref, r_bar_ref, nh_ref, nl_ref, sh_ref, sl_ref, a_ref, u_ref, inv_ref):
    size = 256
    tile = 128
    a_ref[0:tile, 0:tile] = sums_ref[0:tile]
    a_ref[0:tile, tile:size] = sums_ref[tile : 2 * tile]
    a_ref[tile:size, tile:size] = sums_ref[2 * tile : 3 * tile]
    row = lax.broadcasted_iota(jnp.int32, (size, size), 0)
    col = lax.broadcasted_iota(jnp.int32, (size, size), 1)
    a_ref[:, size : 2 * size] = jnp.where(row == col, 1.0, 0.0)
    u_ref[...] = jnp.zeros((size, size), f32)
    inv_ref[...] = jnp.zeros((size, size), f32)
    place = lax.broadcasted_iota(jnp.int32, (8, 3 * tile), 0)
    for start in range(0, size, PANEL):
        base = (start // tile) * tile
        lanes = slice(base, base + 3 * tile)
        offset = start - base
        rows = [jnp.broadcast_to(a_ref[start + i : start + i + 1, lanes], (8, 3 * tile)) for i in range(PANEL)]
        s = {}
        for i in range(PANEL):
            for m in range(i, PANEL):
                s[i, m] = jnp.broadcast_to(rows[i][:, offset + m : offset + m + 1], (8, tile))
        done = []
        for i in range(PANEL):
            inverse = pl.reciprocal(s[i, i])
            root = lax.rsqrt(s[i, i])
            root = root * (1.5 - 0.5 * s[i, i] * root * root)
            for k in range(i + 1, PANEL):
                factor_k = s[i, k] * inverse
                for m in range(k, PANEL):
                    s[k, m] = s[k, m] - factor_k * s[i, m]
                rows[k] = rows[k] - jnp.concatenate([factor_k] * 3, axis=1) * rows[i]
            done.append(rows[i] * jnp.concatenate([root] * 3, axis=1))
        groups = []
        for first in range(0, PANEL, 8):
            group = done[first]
            for i in range(1, 8):
                group = jnp.where(place == i, done[first + i], group)
            groups.append(group)
        panel = jnp.concatenate(groups, axis=0)
        stop = start + PANEL
        if base == 0:
            u_ref[start:stop, :] = panel[:, : 2 * tile]
            inv_ref[start:stop, :tile] = panel[:, 2 * tile :]
        else:
            u_ref[start:stop, tile:] = panel[:, :tile]
            inv_ref[start:stop, :] = panel[:, tile:]
        if stop < size:
            h, m, l = split3(panel)
            width = size - base
            left = jnp.concatenate([h, h, m, m, h, l], axis=0)[:, :width]
            right = jnp.concatenate([h, m, h, m, l, h], axis=0)
            change = dot(left, right, ((0,), (0,)))
            a_ref[stop:, lanes] = a_ref[stop:, lanes] - change[stop - base :]
    upper = jnp.where(row <= col, u_ref[...], 0.0)
    inv = jnp.where(row >= col, inv_ref[...], 0.0)
    bar = jnp.where(row <= col, r_bar_ref[...], 0.0)
    cross = jnp.concatenate([sums_ref[3 * tile : 5 * tile], sums_ref[5 * tile : 7 * tile]], axis=1)

    def product(a, b, contract):
        return lax.dot_general(a, b, ((contract[0], contract[1]), ((), ())), precision=exact, preferred_element_type=f32)

    across = ((1,), (1,))
    middle = product(upper, bar, across) - product(cross, inv, across)
    symmetric = jnp.where(row >= col, middle, 0.0) + jnp.transpose(jnp.where(row > col, middle, 0.0))
    spread = product(inv, product(symmetric, inv, ((1,), (0,))), ((0,), (0,)))
    nh_ref[...], nl_ref[...] = split2(inv)
    sh_ref[...], sl_ref[...] = split2(spread)


def gradient(
    coeff_ref, qh_ref, ql_ref, xh_ref, xl_ref, nh_ref, nl_ref, ih_ref, il_ref, sh_ref, sl_ref,
    w_ref, noise_ref, down_ref, up_ref,
):
    n = w_ref.shape[2]
    plain = ((1,), (0,))
    for k in range(4):
        for r in range(2):
            start = (2 * k + r) * n
            here = slice(start, start + n)
            qh, ql = qh_ref[here], ql_ref[here]
            xh = jnp.concatenate([xh_ref[here], nh_ref[here]], axis=1)
            xl = jnp.concatenate([xl_ref[here], nl_ref[here]], axis=1)
            grad = (
                dot(qh, ih_ref[...], plain) + dot(ql, ih_ref[...], plain) + dot(qh, il_ref[...], plain)
                + dot(xh, sh_ref[...], plain) + dot(xl, sh_ref[...], plain) + dot(xh, sl_ref[...], plain)
            )
            w_ref[k, r] = grad[:, :128]
            noise_ref[k, r] = grad[:, 128:]
    c = coefficients(coeff_ref)
    for r, out in ((0, down_ref), (1, up_ref)):
        xa, pa, pb = w_ref[0, r], w_ref[1, r], w_ref[3, r]
        j = c[r][5]
        jother = c[1 - r][5]
        jx, jp = j * xa, j * pa
        hop_x = jother * w_ref[0, 1 - r] + side(jx)
        hop_p = jother * w_ref[1, 1 - r] + side(jp)
        bx, bp = backward_light(c[r], xa, pa, pb, hop_x, hop_p)
        out[0:n] = jx
        out[n : 2 * n] = jp
        out[2 * n : 3 * n] = j * bx
        out[3 * n : 4 * n] = j * bp


def contract_back(coeff_ref, w_ref, low_ref, high_ref, flow_ref, fhigh_ref, out_ref, first_ref):
    c = coefficients(coeff_ref)
    n = w_ref.shape[2]
    far = ((low_ref, far_hopping(flow_ref, n)), (high_ref, far_hopping(fhigh_ref, n)))
    for r in range(2):
        xa, pa, xb, pb = (w_ref[k, r] for k in range(4))
        j, jother = c[r][5], c[1 - r][5]
        beyond = far[r][0]
        hop_x = jother * w_ref[0, 1 - r] + beyond[0:n] + side(j * xa)
        hop_p = jother * w_ref[1, 1 - r] + beyond[n : 2 * n] + side(j * pa)
        first_ref[0, r], first_ref[1, r] = backward_light(c[r], xa, pa, pb, hop_x, hop_p)
        first_ref[2, r], first_ref[3, r] = backward_heavy(c[r], pa, xb, pb)
    for r in range(2):
        xa, pa, xb, pb = (first_ref[k, r] for k in range(4))
        j, jother = c[r][5], c[1 - r][5]
        beyond, jfar = far[r]
        far_x = beyond[2 * n : 3 * n] + jfar * (j * w_ref[1, r])
        far_p = beyond[3 * n : 4 * n] - jfar * (j * w_ref[0, r])
        hop_x = jother * first_ref[0, 1 - r] + far_x + side(j * xa)
        hop_p = jother * first_ref[1, 1 - r] + far_p + side(j * pa)
        second = backward_light(c[r], xa, pa, pb, hop_x, hop_p) + backward_heavy(c[r], pa, xb, pb)
        for k, (f, s) in enumerate(zip((xa, pa, xb, pb), second)):
            out_ref[k, r] = w_ref[k, r] + f + 0.5 * s


def exchange(up, down):
    count = lax.axis_size("row")
    forward = [(i, i + 1) for i in range(count - 1)]
    backward = [(i + 1, i) for i in range(count - 1)]
    low = lax.ppermute(up, "row", forward)
    high = lax.ppermute(down, "row", backward)
    return low, high


def sum_over_rows(x):
    count = lax.axis_size("row")
    parts = lax.all_to_all(x.reshape((count, -1) + x.shape[1:]), "row", 0, 0)
    mine = parts.sum(0)
    whole = lax.all_to_all(jnp.broadcast_to(mine[None], parts.shape), "row", 0, 0)
    return whole.reshape(x.shape)


def on_device(cell_coeffs, z_factor, noise_cols, q_bar, r_bar):
    quads, lattice, n, rank = z_factor.shape
    flat = quads * lattice * n
    coeffs = cell_coeffs.reshape(12, n)
    noise = noise_cols.reshape(flat, -1)
    bar = q_bar.reshape(flat, -1)
    shape = jax.ShapeDtypeStruct
    rim = shape((4 * n + 8, rank), f32)
    up_down = call(forward_rim, (rim, rim), 10**6, 2 * 10**6)(coeffs, z_factor)
    low, high = exchange(up_down[1], up_down[0])
    half = shape((flat, 128), bf16)
    full = shape((flat, 256), bf16)
    block = shape((128, 128), f32)
    tall = shape((256, 128), f32)
    gnn, cross_n, nh, nl, qh, ql = call(
        noise_products, (block, tall, half, half, full, full), 2 * flat * 128 * 128 * 11, 9 * 10**6
    )(noise, bar)
    gzz, gzn, cross_z, xh, xl = call(
        expand_products, (block, block, tall, half, half), 2 * flat * 128 * 128 * 11, 9 * 10**6,
        [pltpu.VMEM(z_factor.shape, f32)],
    )(coeffs, z_factor, low, high, nh, nl, qh, ql)
    sums = sum_over_rows(jnp.concatenate([gzz, gzn, gnn, cross_z, cross_n], axis=0))
    square = shape((256, 256), bf16)
    ih, il, sh, sl = call(
        factor, (square,) * 4, 10**9, 10**6,
        [pltpu.VMEM((256, 512), f32), pltpu.VMEM((256, 256), f32), pltpu.VMEM((256, 256), f32)],
    )(sums, r_bar)
    rim = shape((4 * n, rank), f32)
    w, noise_grad, down, up = call(
        gradient, (shape(z_factor.shape, f32), shape(noise_cols.shape, f32), rim, rim),
        2 * flat * 256 * 256 * 6, 12 * 10**6,
    )(coeffs, qh, ql, xh, xl, nh, nl, ih, il, sh, sl)
    back_low, back_high = exchange(up, down)
    z_grad = call(
        contract_back, shape(z_factor.shape, f32), 10**7, 6 * 10**6, [pltpu.VMEM(z_factor.shape, f32)]
    )(coeffs, w, back_low, back_high, low, high)
    return z_grad, noise_grad


def solution(mesh):
    return jax.shard_map(
        on_device,
        mesh=mesh,
        in_specs=(
            P(None, "row", None),
            P(None, ("grp", "row"), None, None),
            P(None, ("grp", "row"), None, None),
            P(None, ("grp", "row"), None, None),
            P("grp", None),
        ),
        out_specs=(P(None, ("grp", "row"), None, None), P(None, ("grp", "row"), None, None)),
        check_vma=False,
    )
```

```python
import jax
import jax.numpy as jnp
from jax import lax
from jax.experimental import pallas as pl
from jax.experimental.pallas import tpu as pltpu
from jax.sharding import PartitionSpec as P

rate_scales = (0.4, 0.4, 0.1, 0.2, 0.1, 0.1)
exact = lax.Precision.HIGHEST
f32 = jnp.float32
bf16 = jnp.bfloat16
VMEM = pl.BlockSpec(memory_space=pltpu.VMEM)
LIMIT = 24 * 1024 * 1024
PANEL = 16


def call(kernel, outs, flops, moved, scratch=(), scalar=False):
    def run(*args):
        specs = [pl.BlockSpec() for _ in args]
        if scalar:
            specs[0] = pl.BlockSpec(memory_space=pltpu.SMEM)
        return pl.pallas_call(
            kernel,
            out_shape=outs,
            in_specs=specs,
            scratch_shapes=list(scratch),
            compiler_params=pltpu.CompilerParams(vmem_limit_bytes=LIMIT),
            cost_estimate=pl.CostEstimate(flops=flops, bytes_accessed=moved, transcendentals=0),
        )(*args)

    return run


def split2(value):
    high = value.astype(bf16)
    low = (value - high.astype(f32)).astype(bf16)
    return high, low


def split3(value):
    high = value.astype(bf16)
    rest = value - high.astype(f32)
    mid = rest.astype(bf16)
    low = (rest - mid.astype(f32)).astype(bf16)
    return high, mid, low


def dot(a, b, contract):
    return lax.dot_general(a, b, ((contract[0], contract[1]), ((), ())), preferred_element_type=f32)


def coefficients(coeff_ref):
    cols = jnp.transpose(jnp.concatenate([coeff_ref[k] for k in range(6)], axis=0))
    out = []
    for r in range(2):
        out.append([cols[:, 2 * k + r : 2 * k + r + 1] * rate_scales[k] for k in range(6)])
    return out


def side(v):
    n = v.shape[0]
    place = lax.broadcasted_iota(jnp.int32, v.shape, 0)
    left = jnp.where(place == 0, 0.0, pltpu.roll(v, 1, 0))
    right = jnp.where(place == n - 1, 0.0, pltpu.roll(v, n - 1, 0))
    return left + right


def forward_light(c, xa, pa, xb, hop_x, hop_p):
    d, w, g, l, m, j = c
    return (
        -0.5 * l * xa - d * pa - j * hop_p,
        d * xa - 0.5 * l * pa - 2.0 * g * xb + j * hop_x,
    )


def forward_heavy(c, xa, xb, pb):
    d, w, g, l, m, j = c
    return w * pb, -w * xb - 0.5 * m * pb - 2.0 * g * xa


def backward_light(c, xa, pa, pb, hop_x, hop_p):
    d, w, g, l, m, j = c
    return (
        -0.5 * l * xa + d * pa - 2.0 * g * pb + hop_p,
        -d * xa - 0.5 * l * pa - hop_x,
    )


def backward_heavy(c, pa, xb, pb):
    d, w, g, l, m, j = c
    return -2.0 * g * pa - w * pb, w * xb - 0.5 * m * pb


def forward_rim(coeff_ref, z_ref, down_ref, up_ref):
    c = coefficients(coeff_ref)
    n = z_ref.shape[2]
    for r, out in ((0, down_ref), (1, up_ref)):
        xa, pa, xb = z_ref[0, r], z_ref[1, r], z_ref[2, r]
        hop_x = z_ref[0, 1 - r] + side(xa)
        hop_p = z_ref[1, 1 - r] + side(pa)
        bx, bp = forward_light(c[r], xa, pa, xb, hop_x, hop_p)
        out[0:n] = xa
        out[n : 2 * n] = pa
        out[2 * n : 3 * n] = bx
        out[3 * n : 4 * n] = bp
        hopping = coeff_ref[5, r : r + 1, :] * rate_scales[5]
        pieces = [hopping[:, k * 128 : (k + 1) * 128] for k in range(n // 128)]
        pieces.append(jnp.zeros((8 - n // 128, 128), f32))
        out[4 * n :] = jnp.concatenate(pieces, axis=0)


def far_hopping(recv_ref, n):
    tail = jnp.transpose(recv_ref[4 * n : 4 * n + 8])
    return jnp.concatenate([tail[:, k : k + 1] for k in range(n // 128)], axis=0)


def packed(gram, cross):
    row = lax.broadcasted_iota(jnp.int32, gram.shape, 0)
    col = lax.broadcasted_iota(jnp.int32, gram.shape, 1)
    diagonal = jnp.sum(jnp.where(row == col, cross, 0.0), axis=0, keepdims=True)
    return jnp.where(row <= col, gram, cross), jnp.broadcast_to(diagonal, (8, gram.shape[1]))


def noise_products(noise_ref, q_ref, pack_ref, nh_ref, nl_ref, qh_ref, ql_ref):
    nh, nl = split2(noise_ref[...])
    qh, ql = split2(q_ref[...])
    nh_ref[...] = nh
    nl_ref[...] = nl
    qh_ref[...] = qh
    ql_ref[...] = ql
    down = ((0,), (0,))
    mixed = dot(nh, nl, down)
    gram = dot(nh, nh, down) + mixed + jnp.transpose(mixed)
    qh, ql = qh[:, 128:], ql[:, 128:]
    cross = dot(qh, nh, down) + dot(qh, nl, down) + dot(ql, nh, down)
    pack_ref[0:128], pack_ref[128:] = packed(gram, cross)


def expand_products(
    core_ref, coeff_ref, z_ref, low_ref, high_ref, pack_ref, nh_ref, nl_ref, qh_ref, ql_ref,
    mine_ref, other_ref, xh_ref, xl_ref, first_ref, sums_ref,
):
    c = coefficients(coeff_ref)
    n = z_ref.shape[2]
    jlow = far_hopping(low_ref, n)
    jhigh = far_hopping(high_ref, n)
    low = [low_ref[k * n : (k + 1) * n] for k in range(4)]
    high = [high_ref[k * n : (k + 1) * n] for k in range(4)]
    far = ((low, jlow), (high, jhigh))
    for r in range(2):
        xa, pa, xb, pb = (z_ref[k, r] for k in range(4))
        hop_x = z_ref[0, 1 - r] + far[r][0][0] + side(xa)
        hop_p = z_ref[1, 1 - r] + far[r][0][1] + side(pa)
        first_ref[0, r], first_ref[1, r] = forward_light(c[r], xa, pa, xb, hop_x, hop_p)
        first_ref[2, r], first_ref[3, r] = forward_heavy(c[r], xa, xb, pb)
    for r in range(2):
        xa, pa, xb, pb = (first_ref[k, r] for k in range(4))
        beyond, jfar = far[r]
        far_x = beyond[2] - jfar * z_ref[1, r]
        far_p = beyond[3] + jfar * z_ref[0, r]
        hop_x = first_ref[0, 1 - r] + far_x + side(xa)
        hop_p = first_ref[1, 1 - r] + far_p + side(pa)
        second = forward_light(c[r], xa, pa, xb, hop_x, hop_p) + forward_heavy(c[r], xa, xb, pb)
        for k, (f, s) in enumerate(zip((xa, pa, xb, pb), second)):
            start = (2 * k + r) * n
            h, l = split2(z_ref[k, r] + f + 0.5 * s)
            xh_ref[start : start + n] = h
            xl_ref[start : start + n] = l
    down = ((0,), (0,))
    xh, xl = xh_ref[...], xl_ref[...]
    mixed = dot(xh, xl, down)
    gram = dot(xh, xh, down) + mixed + jnp.transpose(mixed)
    cross = dot(qh_ref[...], xh, down) + dot(qh_ref[...], xl, down) + dot(ql_ref[...], xh, down)
    sums_ref[0:128], sums_ref[512:520] = packed(gram, cross[:128])
    sums_ref[128:256] = dot(xh, nh_ref[...], down) + dot(xh, nl_ref[...], down) + dot(xl, nh_ref[...], down)
    sums_ref[256:384] = cross[128:]
    sums_ref[384:512] = pack_ref[0:128]
    sums_ref[520:528] = pack_ref[128:136]
    core = core_ref[0]
    mine_ref[...] = sums_ref[pl.ds(pl.multiple_of(core * 264, 8), 264)]
    other_ref[...] = sums_ref[pl.ds(pl.multiple_of((1 - core) * 264, 8), 264)]


def factor(
    core_ref, mine_ref, other_ref, r_bar_ref, nh_ref, nl_ref, sh_ref, sl_ref, sums_ref, a_ref, u_ref, inv_ref
):
    size = 256
    tile = 128
    core = core_ref[0]
    sums_ref[pl.ds(pl.multiple_of(core * 264, 8), 264)] = mine_ref[...]
    sums_ref[pl.ds(pl.multiple_of((1 - core) * 264, 8), 264)] = other_ref[...]
    a_ref[0:tile, 0:tile] = sums_ref[0:tile]
    a_ref[0:tile, tile:size] = sums_ref[tile : 2 * tile]
    a_ref[tile:size, tile:size] = sums_ref[3 * tile : 4 * tile]
    row = lax.broadcasted_iota(jnp.int32, (size, size), 0)
    col = lax.broadcasted_iota(jnp.int32, (size, size), 1)
    a_ref[:, size : 2 * size] = jnp.where(row == col, 1.0, 0.0)
    u_ref[...] = jnp.zeros((size, size), f32)
    inv_ref[...] = jnp.zeros((size, size), f32)
    place = lax.broadcasted_iota(jnp.int32, (8, 3 * tile), 0)
    for start in range(0, size, PANEL):
        base = (start // tile) * tile
        lanes = slice(base, base + 3 * tile)
        offset = start - base
        rows = [jnp.broadcast_to(a_ref[start + i : start + i + 1, lanes], (8, 3 * tile)) for i in range(PANEL)]
        s = {}
        for i in range(PANEL):
            for m in range(i, PANEL):
                s[i, m] = jnp.broadcast_to(rows[i][:, offset + m : offset + m + 1], (8, tile))
        done = []
        for i in range(PANEL):
            inverse = pl.reciprocal(s[i, i])
            root = lax.rsqrt(s[i, i])
            root = root * (1.5 - 0.5 * s[i, i] * root * root)
            for k in range(i + 1, PANEL):
                factor_k = s[i, k] * inverse
                for m in range(k, PANEL):
                    s[k, m] = s[k, m] - factor_k * s[i, m]
                rows[k] = rows[k] - jnp.concatenate([factor_k] * 3, axis=1) * rows[i]
            done.append(rows[i] * jnp.concatenate([root] * 3, axis=1))
        groups = []
        for first in range(0, PANEL, 8):
            group = done[first]
            for i in range(1, 8):
                group = jnp.where(place == i, done[first + i], group)
            groups.append(group)
        panel = jnp.concatenate(groups, axis=0)
        stop = start + PANEL
        if base == 0:
            u_ref[start:stop, :] = panel[:, : 2 * tile]
            inv_ref[start:stop, :tile] = panel[:, 2 * tile :]
        else:
            u_ref[start:stop, tile:] = panel[:, :tile]
            inv_ref[start:stop, :] = panel[:, tile:]
        if stop < size:
            h, m, l = split3(panel)
            width = size - base
            left = jnp.concatenate([h, h, m, m, h, l], axis=0)[:, :width]
            right = jnp.concatenate([h, m, h, m, l, h], axis=0)
            change = dot(left, right, ((0,), (0,)))
            a_ref[stop:, lanes] = a_ref[stop:, lanes] - change[stop - base :]
    upper = jnp.where(row <= col, u_ref[...], 0.0)
    inv = jnp.where(row >= col, inv_ref[...], 0.0)
    bar = jnp.where(row <= col, r_bar_ref[...], 0.0)
    corner = jnp.zeros((tile, tile), f32)
    top = jnp.concatenate([sums_ref[0:tile], corner], axis=1)
    bottom = jnp.concatenate([sums_ref[2 * tile : 3 * tile], sums_ref[3 * tile : 4 * tile]], axis=1)
    cross = jnp.concatenate([top, bottom], axis=0)
    diagonal = jnp.concatenate([sums_ref[512:513], sums_ref[520:521]], axis=1)
    cross = jnp.where(row > col, cross, jnp.where(row == col, diagonal, 0.0))

    def product(a, b, contract):
        return lax.dot_general(a, b, ((contract[0], contract[1]), ((), ())), precision=exact, preferred_element_type=f32)

    across = ((1,), (1,))
    middle = product(upper, bar, across) - product(cross, inv, across)
    symmetric = jnp.where(row >= col, middle, 0.0) + jnp.transpose(jnp.where(row > col, middle, 0.0))
    spread = product(inv, product(symmetric, inv, ((1,), (0,))), ((0,), (0,)))
    nh_ref[...], nl_ref[...] = split2(inv)
    sh_ref[...], sl_ref[...] = split2(spread)


def gradient(
    coeff_ref, qh_ref, ql_ref, xh_ref, xl_ref, nh_ref, nl_ref, ih_ref, il_ref, sh_ref, sl_ref,
    w_ref, noise_ref, down_ref, up_ref,
):
    n = w_ref.shape[2]
    plain = ((1,), (0,))
    for k in range(4):
        for r in range(2):
            start = (2 * k + r) * n
            here = slice(start, start + n)
            qh, ql = qh_ref[here], ql_ref[here]
            xh = jnp.concatenate([xh_ref[here], nh_ref[here]], axis=1)
            xl = jnp.concatenate([xl_ref[here], nl_ref[here]], axis=1)
            grad = (
                dot(qh, ih_ref[...], plain) + dot(ql, ih_ref[...], plain) + dot(qh, il_ref[...], plain)
                + dot(xh, sh_ref[...], plain) + dot(xl, sh_ref[...], plain) + dot(xh, sl_ref[...], plain)
            )
            w_ref[k, r] = grad[:, :128]
            noise_ref[k, r] = grad[:, 128:]
    c = coefficients(coeff_ref)
    for r, out in ((0, down_ref), (1, up_ref)):
        xa, pa, pb = w_ref[0, r], w_ref[1, r], w_ref[3, r]
        j = c[r][5]
        jother = c[1 - r][5]
        jx, jp = j * xa, j * pa
        hop_x = jother * w_ref[0, 1 - r] + side(jx)
        hop_p = jother * w_ref[1, 1 - r] + side(jp)
        bx, bp = backward_light(c[r], xa, pa, pb, hop_x, hop_p)
        out[0:n] = jx
        out[n : 2 * n] = jp
        out[2 * n : 3 * n] = j * bx
        out[3 * n : 4 * n] = j * bp


def contract_back(coeff_ref, w_ref, low_ref, high_ref, flow_ref, fhigh_ref, out_ref, first_ref):
    c = coefficients(coeff_ref)
    n = w_ref.shape[2]
    far = ((low_ref, far_hopping(flow_ref, n)), (high_ref, far_hopping(fhigh_ref, n)))
    for r in range(2):
        xa, pa, xb, pb = (w_ref[k, r] for k in range(4))
        j, jother = c[r][5], c[1 - r][5]
        beyond = far[r][0]
        hop_x = jother * w_ref[0, 1 - r] + beyond[0:n] + side(j * xa)
        hop_p = jother * w_ref[1, 1 - r] + beyond[n : 2 * n] + side(j * pa)
        first_ref[0, r], first_ref[1, r] = backward_light(c[r], xa, pa, pb, hop_x, hop_p)
        first_ref[2, r], first_ref[3, r] = backward_heavy(c[r], pa, xb, pb)
    for r in range(2):
        xa, pa, xb, pb = (first_ref[k, r] for k in range(4))
        j, jother = c[r][5], c[1 - r][5]
        beyond, jfar = far[r]
        far_x = beyond[2 * n : 3 * n] + jfar * (j * w_ref[1, r])
        far_p = beyond[3 * n : 4 * n] - jfar * (j * w_ref[0, r])
        hop_x = jother * first_ref[0, 1 - r] + far_x + side(j * xa)
        hop_p = jother * first_ref[1, 1 - r] + far_p + side(j * pa)
        second = backward_light(c[r], xa, pa, pb, hop_x, hop_p) + backward_heavy(c[r], pa, xb, pb)
        for k, (f, s) in enumerate(zip((xa, pa, xb, pb), second)):
            out_ref[k, r] = w_ref[k, r] + f + 0.5 * s


def exchange(up, down):
    count = lax.axis_size("row")
    forward = [(i, i + 1) for i in range(count - 1)]
    backward = [(i + 1, i) for i in range(count - 1)]
    low = lax.ppermute(up, "row", forward)
    high = lax.ppermute(down, "row", backward)
    return low, high


def sum_over_rows(mine, other):
    count = lax.axis_size("row")
    bits = count.bit_length() - 1
    swap = [(i, i ^ 1) for i in range(count)]
    mine = mine + lax.ppermute(other, "row", swap)
    for step in range(bits - 1):
        turn = [1 + step, 1 + (step + 1) % (bits - 1)]
        mine = mine + lax.ppermute(mine, "row", [(i, i ^ (1 << turn[i & 1])) for i in range(count)])
    return mine, lax.ppermute(mine, "row", swap)


def on_device(cell_coeffs, z_factor, noise_cols, q_bar, r_bar):
    quads, lattice, n, rank = z_factor.shape
    flat = quads * lattice * n
    coeffs = cell_coeffs
    core = (lax.axis_index("row") & 1).reshape(1)
    noise = noise_cols.reshape(flat, -1)
    bar = q_bar.reshape(flat, -1)
    shape = jax.ShapeDtypeStruct
    rim = shape((4 * n + 8, rank), f32)
    up_down = call(forward_rim, (rim, rim), 10**6, 2 * 10**6)(coeffs, z_factor)
    low, high = exchange(up_down[1], up_down[0])
    half = shape((flat, 128), bf16)
    full = shape((flat, 256), bf16)
    pack, nh, nl, qh, ql = call(
        noise_products, (shape((136, 128), f32), half, half, full, full), 2 * flat * 128 * 128 * 11, 9 * 10**6
    )(noise, bar)
    part = shape((264, 128), f32)
    mine, other, xh, xl = call(
        expand_products, (part, part, half, half), 2 * flat * 128 * 128 * 11, 9 * 10**6,
        [pltpu.VMEM(z_factor.shape, f32), pltpu.VMEM((528, 128), f32)], scalar=True,
    )(core, coeffs, z_factor, low, high, pack, nh, nl, qh, ql)
    mine, other = sum_over_rows(mine, other)
    square = shape((256, 256), bf16)
    ih, il, sh, sl = call(
        factor, (square,) * 4, 10**9, 10**6,
        [pltpu.VMEM((528, 128), f32), pltpu.VMEM((256, 512), f32), pltpu.VMEM((256, 256), f32), pltpu.VMEM((256, 256), f32)],
        scalar=True,
    )(core, mine, other, r_bar)
    rim = shape((4 * n, rank), f32)
    w, noise_grad, down, up = call(
        gradient, (shape(z_factor.shape, f32), shape(noise_cols.shape, f32), rim, rim),
        2 * flat * 256 * 256 * 6, 12 * 10**6,
    )(coeffs, qh, ql, xh, xl, nh, nl, ih, il, sh, sl)
    back_low, back_high = exchange(up, down)
    z_grad = call(
        contract_back, shape(z_factor.shape, f32), 10**7, 6 * 10**6, [pltpu.VMEM(z_factor.shape, f32)]
    )(coeffs, w, back_low, back_high, low, high)
    return z_grad, noise_grad


def solution(mesh):
    return jax.shard_map(
        on_device,
        mesh=mesh,
        in_specs=(
            P(None, "row", None),
            P(None, ("grp", "row"), None, None),
            P(None, ("grp", "row"), None, None),
            P(None, ("grp", "row"), None, None),
            P("grp", None),
        ),
        out_specs=(P(None, ("grp", "row"), None, None), P(None, ("grp", "row"), None, None)),
        check_vma=False,
    )
```

```python
import jax
import jax.numpy as jnp
from jax import lax
from jax.experimental import pallas as pl
from jax.experimental.pallas import tpu as pltpu
from jax.sharding import PartitionSpec as P

rate_scales = (0.4, 0.4, 0.1, 0.2, 0.1, 0.1)
exact = lax.Precision.HIGHEST
f32 = jnp.float32
bf16 = jnp.bfloat16
VMEM = pl.BlockSpec(memory_space=pltpu.VMEM)
LIMIT = 24 * 1024 * 1024
FAR_LIMIT = 63 * 1024 * 1024
PANEL = 16


def call(kernel, outs, flops, moved, scratch=(), scalar=False, far=False):
    def run(*args):
        specs = [pl.BlockSpec(memory_space=pltpu.HBM) if far else pl.BlockSpec() for _ in args]
        if scalar:
            specs[0] = pl.BlockSpec(memory_space=pltpu.SMEM)
        return pl.pallas_call(
            kernel,
            out_shape=outs,
            in_specs=specs,
            **({"out_specs": (pl.BlockSpec(memory_space=pltpu.HBM),) * len(outs)} if far else {}),
            scratch_shapes=list(scratch),
            compiler_params=pltpu.CompilerParams(vmem_limit_bytes=FAR_LIMIT if far else LIMIT),
            cost_estimate=pl.CostEstimate(flops=flops, bytes_accessed=moved, transcendentals=0),
        )(*args)

    return run


def split2(value):
    high = value.astype(bf16)
    low = (value - high.astype(f32)).astype(bf16)
    return high, low


def split3(value):
    high = value.astype(bf16)
    rest = value - high.astype(f32)
    mid = rest.astype(bf16)
    low = (rest - mid.astype(f32)).astype(bf16)
    return high, mid, low


def dot(a, b, contract):
    return lax.dot_general(a, b, ((contract[0], contract[1]), ((), ())), preferred_element_type=f32)


def coefficients(coeff_ref):
    cols = jnp.transpose(jnp.concatenate([coeff_ref[k] for k in range(6)], axis=0))
    out = []
    for r in range(2):
        out.append([cols[:, 2 * k + r : 2 * k + r + 1] * rate_scales[k] for k in range(6)])
    return out


def side(v):
    n = v.shape[0]
    place = lax.broadcasted_iota(jnp.int32, v.shape, 0)
    left = jnp.where(place == 0, 0.0, pltpu.roll(v, 1, 0))
    right = jnp.where(place == n - 1, 0.0, pltpu.roll(v, n - 1, 0))
    return left + right


def forward_light(c, xa, pa, xb, hop_x, hop_p):
    d, w, g, l, m, j = c
    return (
        -0.5 * l * xa - d * pa - j * hop_p,
        d * xa - 0.5 * l * pa - 2.0 * g * xb + j * hop_x,
    )


def forward_heavy(c, xa, xb, pb):
    d, w, g, l, m, j = c
    return w * pb, -w * xb - 0.5 * m * pb - 2.0 * g * xa


def backward_light(c, xa, pa, pb, hop_x, hop_p):
    d, w, g, l, m, j = c
    return (
        -0.5 * l * xa + d * pa - 2.0 * g * pb + hop_p,
        -d * xa - 0.5 * l * pa - hop_x,
    )


def backward_heavy(c, pa, xb, pb):
    d, w, g, l, m, j = c
    return -2.0 * g * pa - w * pb, w * xb - 0.5 * m * pb


def light_rows(z_ref, down_ref, up_ref, sems):
    copies = [
        pltpu.make_async_copy(z_ref.at[0:2, r], out, sems.at[r]) for r, out in ((0, down_ref), (1, up_ref))
    ]
    for copy in copies:
        copy.start()
    for copy in copies:
        copy.wait()


def forward_rim(coeff_ref, z_ref, down_ref, up_ref):
    c = coefficients(coeff_ref)
    n = z_ref.shape[2]
    for r, out in ((0, down_ref), (1, up_ref)):
        xa, pa, xb = z_ref[0, r], z_ref[1, r], z_ref[2, r]
        hop_x = z_ref[0, 1 - r] + side(xa)
        hop_p = z_ref[1, 1 - r] + side(pa)
        out[0:n], out[n : 2 * n] = forward_light(c[r], xa, pa, xb, hop_x, hop_p)
        hopping = coeff_ref[5, r : r + 1, :] * rate_scales[5]
        pieces = [hopping[:, k * 128 : (k + 1) * 128] for k in range(n // 128)]
        pieces.append(jnp.zeros((8 - n // 128, 128), f32))
        out[2 * n :] = jnp.concatenate(pieces, axis=0)


def far_hopping(recv_ref, n):
    tail = jnp.transpose(recv_ref[2 * n : 2 * n + 8])
    return jnp.concatenate([tail[:, k : k + 1] for k in range(n // 128)], axis=0)


def packed(gram, cross):
    row = lax.broadcasted_iota(jnp.int32, gram.shape, 0)
    col = lax.broadcasted_iota(jnp.int32, gram.shape, 1)
    diagonal = jnp.sum(jnp.where(row == col, cross, 0.0), axis=0, keepdims=True)
    return jnp.where(row <= col, gram, cross), jnp.broadcast_to(diagonal, (8, gram.shape[1]))


def noise_products(noise_ref, q_ref, pack_ref, nh_ref, nl_ref, qh_ref, ql_ref, nht_ref, nlt_ref, qht_ref, qlt_ref):
    nh, nl = split2(noise_ref[...])
    qh, ql = split2(q_ref[...])
    nh_ref[...] = nh
    nl_ref[...] = nl
    qh_ref[...] = qh
    ql_ref[...] = ql
    for value, out in ((nh, nht_ref), (nl, nlt_ref), (qh, qht_ref), (ql, qlt_ref)):
        out[...] = jnp.transpose(value)
    plain = ((1,), (0,))
    high = dot(jnp.concatenate([nht_ref[...], qht_ref[128:]], axis=0), jnp.concatenate([nh, nl], axis=1), plain)
    low = dot(qlt_ref[128:], nh, plain)
    mixed = high[:128, 128:]
    gram = high[:128, :128] + mixed + jnp.transpose(mixed)
    cross = high[128:, :128] + high[128:, 128:] + low
    pack_ref[0:128], pack_ref[128:] = packed(gram, cross)


def row_products(xh, xl, nht, nlt, qht, qlt):
    plain = ((1,), (0,))
    left = jnp.concatenate([jnp.transpose(xh), nht, qht], axis=0)
    high = dot(left, jnp.concatenate([xh, xl], axis=1), plain)
    low = dot(jnp.concatenate([nlt, qlt], axis=0), xh, plain)
    mixed = high[:128, 128:]
    return (
        high[:128, :128] + mixed + jnp.transpose(mixed),
        high[128:, :128] + high[128:, 128:] + low,
    )


def expand_first(
    coeff_ref, z_ref, low_ref, high_ref, nht_ref, nlt_ref, qht_ref, qlt_ref,
    light_ref, xh_ref, xl_ref, gram_ref, rest_ref, first_ref,
):
    c = coefficients(coeff_ref)
    n = z_ref.shape[2]
    far = (low_ref, high_ref)
    for r in range(2):
        xa, pa, xb, pb = (z_ref[k, r] for k in range(4))
        hop_x = z_ref[0, 1 - r] + far[r][0] + side(xa)
        hop_p = z_ref[1, 1 - r] + far[r][1] + side(pa)
        first_ref[0, r], first_ref[1, r] = forward_light(c[r], xa, pa, xb, hop_x, hop_p)
        first_ref[2, r], first_ref[3, r] = forward_heavy(c[r], xa, xb, pb)
    for r in range(2):
        xa, pa, xb, pb = (first_ref[k, r] for k in range(4))
        for k, (f, s) in enumerate(zip((xb, pb), forward_heavy(c[r], xa, xb, pb))):
            start = (2 * k + r) * n
            h, l = split2(z_ref[2 + k, r] + f + 0.5 * s)
            xh_ref[start : start + n] = h
            xl_ref[start : start + n] = l
    half = 4 * n
    gram_ref[...], rest_ref[...] = row_products(
        xh_ref[...], xl_ref[...], nht_ref[:, half:], nlt_ref[:, half:], qht_ref[:, half:], qlt_ref[:, half:]
    )
    for r in range(2):
        xa, pa, xb, pb = (first_ref[k, r] for k in range(4))
        hop_x = first_ref[0, 1 - r] + side(xa)
        hop_p = first_ref[1, 1 - r] + side(pa)
        second = forward_light(c[r], xa, pa, xb, hop_x, hop_p)
        for k, (f, s) in enumerate(zip((xa, pa), second)):
            light_ref[k, r] = z_ref[k, r] + f + 0.5 * s


def expand_last(
    core_ref, coeff_ref, z_ref, low_ref, high_ref, light_ref, gram_ref, rest_ref, pack_ref,
    nht_ref, nlt_ref, qht_ref, qlt_ref, mine_ref, other_ref, xh_ref, xl_ref, sums_ref,
):
    c = coefficients(coeff_ref)
    n = z_ref.shape[2]
    for r, far in enumerate((low_ref, high_ref)):
        jfar = far_hopping(far, n)
        far_x = far[0:n] - jfar * z_ref[1, r]
        far_p = far[n : 2 * n] + jfar * z_ref[0, r]
        j = 0.5 * c[r][5]
        for k, value in enumerate((light_ref[0, r] - j * far_p, light_ref[1, r] + j * far_x)):
            start = (2 * k + r) * n
            h, l = split2(value)
            xh_ref[start : start + n] = h
            xl_ref[start : start + n] = l
    half = 4 * n
    gram, rest = row_products(
        xh_ref[...], xl_ref[...], nht_ref[:, :half], nlt_ref[:, :half], qht_ref[:, :half], qlt_ref[:, :half]
    )
    gram = gram + gram_ref[...]
    rest = rest + rest_ref[...]
    sums_ref[0:128], sums_ref[512:520] = packed(gram, rest[128:256])
    sums_ref[128:256] = jnp.transpose(rest[:128])
    sums_ref[256:384] = rest[256:]
    sums_ref[384:512] = pack_ref[0:128]
    sums_ref[520:528] = pack_ref[128:136]
    core = core_ref[0]
    mine_ref[...] = sums_ref[pl.ds(pl.multiple_of(core * 264, 8), 264)]
    other_ref[...] = sums_ref[pl.ds(pl.multiple_of((1 - core) * 264, 8), 264)]


def factor(
    core_ref, mine_ref, other_ref, r_bar_ref, nh_ref, nl_ref, sh_ref, sl_ref, sums_ref, a_ref, u_ref, inv_ref
):
    size = 256
    tile = 128
    core = core_ref[0]
    sums_ref[pl.ds(pl.multiple_of(core * 264, 8), 264)] = mine_ref[...]
    sums_ref[pl.ds(pl.multiple_of((1 - core) * 264, 8), 264)] = other_ref[...]
    a_ref[0:tile, 0:tile] = sums_ref[0:tile]
    a_ref[0:tile, tile:size] = sums_ref[tile : 2 * tile]
    a_ref[tile:size, tile:size] = sums_ref[3 * tile : 4 * tile]
    row = lax.broadcasted_iota(jnp.int32, (size, size), 0)
    col = lax.broadcasted_iota(jnp.int32, (size, size), 1)
    a_ref[:, size : 2 * size] = jnp.where(row == col, 1.0, 0.0)
    u_ref[...] = jnp.zeros((size, size), f32)
    inv_ref[...] = jnp.zeros((size, size), f32)
    place = lax.broadcasted_iota(jnp.int32, (8, 3 * tile), 0)
    for start in range(0, size, PANEL):
        base = (start // tile) * tile
        lanes = slice(base, base + 3 * tile)
        offset = start - base
        rows = [jnp.broadcast_to(a_ref[start + i : start + i + 1, lanes], (8, 3 * tile)) for i in range(PANEL)]
        s = {}
        for i in range(PANEL):
            for m in range(i, PANEL):
                s[i, m] = jnp.broadcast_to(rows[i][:, offset + m : offset + m + 1], (8, tile))
        done = []
        for i in range(PANEL):
            inverse = pl.reciprocal(s[i, i])
            root = lax.rsqrt(s[i, i])
            root = root * (1.5 - 0.5 * s[i, i] * root * root)
            for k in range(i + 1, PANEL):
                factor_k = s[i, k] * inverse
                for m in range(k, PANEL):
                    s[k, m] = s[k, m] - factor_k * s[i, m]
                rows[k] = rows[k] - jnp.concatenate([factor_k] * 3, axis=1) * rows[i]
            done.append(rows[i] * jnp.concatenate([root] * 3, axis=1))
        groups = []
        for first in range(0, PANEL, 8):
            group = done[first]
            for i in range(1, 8):
                group = jnp.where(place == i, done[first + i], group)
            groups.append(group)
        panel = jnp.concatenate(groups, axis=0)
        stop = start + PANEL
        if base == 0:
            u_ref[start:stop, :] = panel[:, : 2 * tile]
            inv_ref[start:stop, :tile] = panel[:, 2 * tile :]
        else:
            u_ref[start:stop, tile:] = panel[:, :tile]
            inv_ref[start:stop, :] = panel[:, tile:]
        if stop < size:
            h, m, l = split3(panel)
            width = size - base
            left = jnp.concatenate([h, h, m, m, h, l], axis=0)[:, :width]
            right = jnp.concatenate([h, m, h, m, l, h], axis=0)
            change = dot(left, right, ((0,), (0,)))
            a_ref[stop:, lanes] = a_ref[stop:, lanes] - change[stop - base :]
    upper = jnp.where(row <= col, u_ref[...], 0.0)
    inv = jnp.where(row >= col, inv_ref[...], 0.0)
    bar = jnp.where(row <= col, r_bar_ref[...], 0.0)
    corner = jnp.zeros((tile, tile), f32)
    top = jnp.concatenate([sums_ref[0:tile], corner], axis=1)
    bottom = jnp.concatenate([sums_ref[2 * tile : 3 * tile], sums_ref[3 * tile : 4 * tile]], axis=1)
    cross = jnp.concatenate([top, bottom], axis=0)
    diagonal = jnp.concatenate([sums_ref[512:513], sums_ref[520:521]], axis=1)
    cross = jnp.where(row > col, cross, jnp.where(row == col, diagonal, 0.0))

    def product(a, b, contract):
        return lax.dot_general(a, b, ((contract[0], contract[1]), ((), ())), precision=exact, preferred_element_type=f32)

    across = ((1,), (1,))
    middle = product(upper, bar, across) - product(cross, inv, across)
    symmetric = jnp.where(row >= col, middle, 0.0) + jnp.transpose(jnp.where(row > col, middle, 0.0))
    spread = product(inv, product(symmetric, inv, ((1,), (0,))), ((0,), (0,)))
    nh_ref[...], nl_ref[...] = split2(inv)
    sh_ref[...], sl_ref[...] = split2(spread)


def columns(qh, ql, nh, nl, xh, xl, ih, il, sh, sl):
    plain = ((1,), (0,))
    xh = jnp.concatenate([xh, nh], axis=1)
    xl = jnp.concatenate([xl, nl], axis=1)
    high = dot(qh, jnp.concatenate([ih, il], axis=1), plain) + dot(xh, jnp.concatenate([sh, sl], axis=1), plain)
    return high[:, :128] + high[:, 128:] + dot(ql, ih, plain) + dot(xl, sh, plain)


def gradient_light(
    coeff_ref, qh_ref, ql_ref, nh_ref, nl_ref, xh_ref, xl_ref, ih_ref, il_ref, sh_ref, sl_ref,
    w_ref, down_ref, up_ref,
):
    c = coefficients(coeff_ref)
    n = w_ref.shape[2]
    weights = [ref[:, :128] for ref in (ih_ref, il_ref, sh_ref, sl_ref)]
    for k in range(2):
        for r, out in ((0, down_ref), (1, up_ref)):
            here = slice((2 * k + r) * n, (2 * k + r + 1) * n)
            parts = [ref[here] for ref in (qh_ref, ql_ref, nh_ref, nl_ref, xh_ref, xl_ref)]
            w = columns(*parts, *weights)
            w_ref[k, r] = w
            out[k] = c[r][5] * w


def gradient_heavy(
    coeff_ref, light_ref, jdown_ref, jup_ref, qh_ref, ql_ref, nh_ref, nl_ref, xh_ref, xl_ref,
    ih_ref, il_ref, sh_ref, sl_ref, w_ref, down_ref, up_ref,
):
    c = coefficients(coeff_ref)
    n = w_ref.shape[2]
    weights = [ref[:, :128] for ref in (ih_ref, il_ref, sh_ref, sl_ref)]
    half = 4 * n
    for k in (1, 0):
        for r in range(2):
            here = slice((2 * k + r) * n, (2 * k + r + 1) * n)
            there = slice(half + here.start, half + here.stop)
            parts = [ref[there] for ref in (qh_ref, ql_ref, nh_ref, nl_ref)] + [xh_ref[here], xl_ref[here]]
            w_ref[k, r] = columns(*parts, *weights)
    hops = (jdown_ref, jup_ref)
    for r, out in ((0, down_ref), (1, up_ref)):
        j = c[r][5]
        hop_x = hops[1 - r][0] + side(hops[r][0])
        hop_p = hops[1 - r][1] + side(hops[r][1])
        bx, bp = backward_light(c[r], light_ref[0, r], light_ref[1, r], w_ref[1, r], hop_x, hop_p)
        out[0] = j * bx
        out[1] = j * bp


def gradient_noise(
    qh_ref, ql_ref, nh_ref, nl_ref, xlight_h, xlight_l, xheavy_h, xheavy_l, ih_ref, il_ref, sh_ref, sl_ref, out_ref
):
    n = out_ref.shape[2]
    weights = [ref[:, 128:] for ref in (ih_ref, il_ref, sh_ref, sl_ref)]
    for k in range(4):
        xh_ref, xl_ref = (xlight_h, xlight_l) if k < 2 else (xheavy_h, xheavy_l)
        for r in range(2):
            here = slice((2 * k + r) * n, (2 * k + r + 1) * n)
            there = slice((2 * (k % 2) + r) * n, (2 * (k % 2) + r + 1) * n)
            parts = [ref[here] for ref in (qh_ref, ql_ref, nh_ref, nl_ref)] + [xh_ref[there], xl_ref[there]]
            out_ref[k, r] = columns(*parts, *weights)


def contract_first(
    coeff_ref, light_ref, heavy_ref, jdown_ref, jup_ref, low_ref, high_ref, flow_ref, fhigh_ref,
    out_light_ref, out_heavy_ref, first_ref,
):
    c = coefficients(coeff_ref)
    n = light_ref.shape[2]
    hops = (jdown_ref, jup_ref)
    far = (low_ref, high_ref)
    for r in range(2):
        xa, pa, xb, pb = light_ref[0, r], light_ref[1, r], heavy_ref[0, r], heavy_ref[1, r]
        hop_x = hops[1 - r][0] + far[r][0] + side(hops[r][0])
        hop_p = hops[1 - r][1] + far[r][1] + side(hops[r][1])
        first_ref[0, r], first_ref[1, r] = backward_light(c[r], xa, pa, pb, hop_x, hop_p)
        first_ref[2, r], first_ref[3, r] = backward_heavy(c[r], pa, xb, pb)
    for r, fref in enumerate((flow_ref, fhigh_ref)):
        xa, pa, xb, pb = (first_ref[k, r] for k in range(4))
        jfar = far_hopping(fref, n)
        j, jother = c[r][5], c[1 - r][5]
        hop_x = jother * first_ref[0, 1 - r] + jfar * hops[r][1] + side(j * xa)
        hop_p = jother * first_ref[1, 1 - r] - jfar * hops[r][0] + side(j * pa)
        light = backward_light(c[r], xa, pa, pb, hop_x, hop_p)
        heavy = backward_heavy(c[r], pa, xb, pb)
        for k in range(2):
            out_light_ref[k, r] = light_ref[k, r] + first_ref[k, r] + 0.5 * light[k]
            out_heavy_ref[k, r] = heavy_ref[k, r] + first_ref[2 + k, r] + 0.5 * heavy[k]


def contract_last(light_ref, heavy_ref, low_ref, high_ref, out_ref):
    for r, far in enumerate((low_ref, high_ref)):
        out_ref[0, r] = light_ref[0, r] + 0.5 * far[1]
        out_ref[1, r] = light_ref[1, r] - 0.5 * far[0]
        out_ref[2, r] = heavy_ref[0, r]
        out_ref[3, r] = heavy_ref[1, r]


def exchange(up, down):
    count = lax.axis_size("row")
    forward = [(i, i + 1) for i in range(count - 1)]
    backward = [(i + 1, i) for i in range(count - 1)]
    low = lax.ppermute(up, "row", forward)
    high = lax.ppermute(down, "row", backward)
    return low, high


def sum_over_rows(mine, other):
    count = lax.axis_size("row")
    bits = count.bit_length() - 1
    swap = [(i, i ^ 1) for i in range(count)]
    mine = mine + lax.ppermute(other, "row", swap)
    for step in range(bits - 1):
        turn = [1 + step, 1 + (step + 1) % (bits - 1)]
        mine = mine + lax.ppermute(mine, "row", [(i, i ^ (1 << turn[i & 1])) for i in range(count)])
    return mine, lax.ppermute(mine, "row", swap)


def on_device(cell_coeffs, z_factor, noise_cols, q_bar, r_bar):
    quads, lattice, n, rank = z_factor.shape
    flat = quads * lattice * n
    coeffs = cell_coeffs
    core = (lax.axis_index("row") & 1).reshape(1)
    noise = noise_cols.reshape(flat, -1)
    bar = q_bar.reshape(flat, -1)
    shape = jax.ShapeDtypeStruct
    hops = shape((2, n, rank), f32)
    down, up = call(
        light_rows, (hops, hops), 0, 2 * 10**6, [pltpu.SemaphoreType.DMA((2,))], far=True
    )(z_factor)
    low, high = exchange(up, down)
    rim = shape((2 * n + 8, rank), f32)
    down, up = call(forward_rim, (rim, rim), 10**6, 2 * 10**6)(coeffs, z_factor)
    far_low, far_high = exchange(up, down)
    wide, tall = shape((flat, 256), bf16), shape((flat, 128), bf16)
    wide_t, tall_t = shape((256, flat), bf16), shape((128, flat), bf16)
    work = 2 * flat * 128 * 128
    pack, nh, nl, qh, ql, nht, nlt, qht, qlt = call(
        noise_products, (shape((136, 128), f32), tall, tall, wide, wide, tall_t, tall_t, wide_t, wide_t),
        work * 5, 9 * 10**6,
    )(noise, bar)
    transposed = (nht, nlt, qht, qlt)
    half = shape((flat // 2, 128), bf16)
    pair = shape((2, lattice, n, rank), f32)
    light, xh_heavy, xl_heavy, gram, rest = call(
        expand_first, (pair, half, half, shape((128, 128), f32), shape((384, 128), f32)), work * 6, 9 * 10**6,
        [pltpu.VMEM(z_factor.shape, f32)],
    )(coeffs, z_factor, low, high, *transposed)
    part = shape((264, 128), f32)
    mine, other, xh_light, xl_light = call(
        expand_last, (part, part, half, half), work * 6, 9 * 10**6, [pltpu.VMEM((528, 128), f32)], scalar=True
    )(core, coeffs, z_factor, far_low, far_high, light, gram, rest, pack, *transposed)
    mine, other = sum_over_rows(mine, other)
    square = shape((256, 256), bf16)
    weights = call(
        factor, (square,) * 4, 10**9, 10**6,
        [
            pltpu.VMEM((528, 128), f32),
            pltpu.VMEM((256, 512), f32),
            pltpu.VMEM((256, 256), f32),
            pltpu.VMEM((256, 256), f32),
        ],
        scalar=True,
    )(core, mine, other, r_bar)
    left = (qh, ql, nh, nl)
    w_light, jdown, jup = call(gradient_light, (pair, hops, hops), work * 6, 6 * 10**6)(
        coeffs, *left, xh_light, xl_light, *weights
    )
    low, high = exchange(jup, jdown)
    w_heavy, down, up = call(gradient_heavy, (pair, hops, hops), work * 6, 6 * 10**6)(
        coeffs, w_light, jdown, jup, *left, xh_heavy, xl_heavy, *weights
    )
    last_low, last_high = exchange(up, down)
    noise_grad = call(gradient_noise, shape(noise_cols.shape, f32), work * 12, 9 * 10**6)(
        *left, xh_light, xl_light, xh_heavy, xl_heavy, *weights
    )
    out_light, out_heavy = call(contract_first, (pair, pair), 10**7, 6 * 10**6, [pltpu.VMEM(z_factor.shape, f32)])(
        coeffs, w_light, w_heavy, jdown, jup, low, high, far_low, far_high
    )
    z_grad = call(contract_last, shape(z_factor.shape, f32), 10**6, 6 * 10**6)(
        out_light, out_heavy, last_low, last_high
    )
    return z_grad, noise_grad


def solution(mesh):
    return jax.shard_map(
        on_device,
        mesh=mesh,
        in_specs=(
            P(None, "row", None),
            P(None, ("grp", "row"), None, None),
            P(None, ("grp", "row"), None, None),
            P(None, ("grp", "row"), None, None),
            P("grp", None),
        ),
        out_specs=(P(None, ("grp", "row"), None, None), P(None, ("grp", "row"), None, None)),
        check_vma=False,
    )
```

```python
import jax
import jax.numpy as jnp
from jax import lax
from jax.experimental import pallas as pl
from jax.experimental.pallas import tpu as pltpu
from jax.sharding import PartitionSpec as P

rate_scales = (0.4, 0.4, 0.1, 0.2, 0.1, 0.1)
exact = lax.Precision.HIGHEST
f32 = jnp.float32
bf16 = jnp.bfloat16
VMEM = pl.BlockSpec(memory_space=pltpu.VMEM)
LIMIT = 24 * 1024 * 1024
FAR_LIMIT = 63 * 1024 * 1024
PANEL = 16


def call(kernel, outs, flops, moved, scratch=(), scalar=False, far=False):
    def run(*args):
        specs = [pl.BlockSpec(memory_space=pltpu.HBM) if far else pl.BlockSpec() for _ in args]
        if scalar:
            specs[0] = pl.BlockSpec(memory_space=pltpu.SMEM)
        return pl.pallas_call(
            kernel,
            out_shape=outs,
            in_specs=specs,
            scratch_shapes=list(scratch),
            compiler_params=pltpu.CompilerParams(vmem_limit_bytes=FAR_LIMIT if far else LIMIT),
            cost_estimate=pl.CostEstimate(flops=flops, bytes_accessed=moved, transcendentals=0),
        )(*args)

    return run


def split2(value):
    high = value.astype(bf16)
    low = (value - high.astype(f32)).astype(bf16)
    return high, low


def split3(value):
    high = value.astype(bf16)
    rest = value - high.astype(f32)
    mid = rest.astype(bf16)
    low = (rest - mid.astype(f32)).astype(bf16)
    return high, mid, low


def dot(a, b, contract):
    return lax.dot_general(a, b, ((contract[0], contract[1]), ((), ())), preferred_element_type=f32)


def coefficients(coeff_ref):
    cols = jnp.transpose(jnp.concatenate([coeff_ref[k] for k in range(6)], axis=0))
    out = []
    for r in range(2):
        out.append([cols[:, 2 * k + r : 2 * k + r + 1] * rate_scales[k] for k in range(6)])
    return out


def side(v):
    n = v.shape[0]
    place = lax.broadcasted_iota(jnp.int32, v.shape, 0)
    left = jnp.where(place == 0, 0.0, pltpu.roll(v, 1, 0))
    right = jnp.where(place == n - 1, 0.0, pltpu.roll(v, n - 1, 0))
    return left + right


def forward_light(c, xa, pa, xb, hop_x, hop_p):
    d, w, g, l, m, j = c
    return (
        -0.5 * l * xa - d * pa - j * hop_p,
        d * xa - 0.5 * l * pa - 2.0 * g * xb + j * hop_x,
    )


def forward_heavy(c, xa, xb, pb):
    d, w, g, l, m, j = c
    return w * pb, -w * xb - 0.5 * m * pb - 2.0 * g * xa


def backward_light(c, xa, pa, pb, hop_x, hop_p):
    d, w, g, l, m, j = c
    return (
        -0.5 * l * xa + d * pa - 2.0 * g * pb + hop_p,
        -d * xa - 0.5 * l * pa - hop_x,
    )


def backward_heavy(c, pa, xb, pb):
    d, w, g, l, m, j = c
    return -2.0 * g * pa - w * pb, w * xb - 0.5 * m * pb


def light_rows(z_ref, down_ref, up_ref, sems):
    copies = [
        pltpu.make_async_copy(z_ref.at[0:2, r], out, sems.at[r]) for r, out in ((0, down_ref), (1, up_ref))
    ]
    for copy in copies:
        copy.start()
    for copy in copies:
        copy.wait()


def forward_rim(coeff_ref, z_ref, down_ref, up_ref):
    c = coefficients(coeff_ref)
    n = z_ref.shape[2]
    for r, out in ((0, down_ref), (1, up_ref)):
        xa, pa, xb = z_ref[0, r], z_ref[1, r], z_ref[2, r]
        hop_x = z_ref[0, 1 - r] + side(xa)
        hop_p = z_ref[1, 1 - r] + side(pa)
        out[0:n], out[n : 2 * n] = forward_light(c[r], xa, pa, xb, hop_x, hop_p)
        hopping = coeff_ref[5, r : r + 1, :] * rate_scales[5]
        pieces = [hopping[:, k * 128 : (k + 1) * 128] for k in range(n // 128)]
        pieces.append(jnp.zeros((8 - n // 128, 128), f32))
        out[2 * n :] = jnp.concatenate(pieces, axis=0)


def far_hopping(recv_ref, n):
    tail = jnp.transpose(recv_ref[2 * n : 2 * n + 8])
    return jnp.concatenate([tail[:, k : k + 1] for k in range(n // 128)], axis=0)


def packed(gram, cross):
    row = lax.broadcasted_iota(jnp.int32, gram.shape, 0)
    col = lax.broadcasted_iota(jnp.int32, gram.shape, 1)
    diagonal = jnp.sum(jnp.where(row == col, cross, 0.0), axis=0, keepdims=True)
    return jnp.where(row <= col, gram, cross), jnp.broadcast_to(diagonal, (8, gram.shape[1]))


def noise_products(noise_ref, q_ref, pack_ref, nh_ref, nl_ref, qh_ref, ql_ref, nht_ref, nlt_ref, qht_ref, qlt_ref):
    nh, nl = split2(noise_ref[...])
    qh, ql = split2(q_ref[...])
    nh_ref[...] = nh
    nl_ref[...] = nl
    qh_ref[...] = qh
    ql_ref[...] = ql
    for value, out in ((nh, nht_ref), (nl, nlt_ref), (qh, qht_ref), (ql, qlt_ref)):
        out[...] = jnp.transpose(value)
    plain = ((1,), (0,))
    high = dot(jnp.concatenate([nht_ref[...], qht_ref[128:]], axis=0), jnp.concatenate([nh, nl], axis=1), plain)
    low = dot(qlt_ref[128:], nh, plain)
    mixed = high[:128, 128:]
    gram = high[:128, :128] + mixed + jnp.transpose(mixed)
    cross = high[128:, :128] + high[128:, 128:] + low
    pack_ref[0:128], pack_ref[128:] = packed(gram, cross)


def row_products(xh, xl, nht, nlt, qht, qlt):
    plain = ((1,), (0,))
    left = jnp.concatenate([jnp.transpose(xh), nht, qht], axis=0)
    high = dot(left, jnp.concatenate([xh, xl], axis=1), plain)
    low = dot(jnp.concatenate([nlt, qlt], axis=0), xh, plain)
    mixed = high[:128, 128:]
    return (
        high[:128, :128] + mixed + jnp.transpose(mixed),
        high[128:, :128] + high[128:, 128:] + low,
    )


def expand_first(
    coeff_ref, z_ref, low_ref, high_ref, nht_ref, nlt_ref, qht_ref, qlt_ref,
    light_ref, xh_ref, xl_ref, gram_ref, rest_ref, first_ref,
):
    c = coefficients(coeff_ref)
    n = z_ref.shape[2]
    far = (low_ref, high_ref)
    for r in range(2):
        xa, pa, xb, pb = (z_ref[k, r] for k in range(4))
        hop_x = z_ref[0, 1 - r] + far[r][0] + side(xa)
        hop_p = z_ref[1, 1 - r] + far[r][1] + side(pa)
        first_ref[0, r], first_ref[1, r] = forward_light(c[r], xa, pa, xb, hop_x, hop_p)
        first_ref[2, r], first_ref[3, r] = forward_heavy(c[r], xa, xb, pb)
    for r in range(2):
        xa, pa, xb, pb = (first_ref[k, r] for k in range(4))
        for k, (f, s) in enumerate(zip((xb, pb), forward_heavy(c[r], xa, xb, pb))):
            start = (2 * k + r) * n
            h, l = split2(z_ref[2 + k, r] + f + 0.5 * s)
            xh_ref[start : start + n] = h
            xl_ref[start : start + n] = l
    half = 4 * n
    gram_ref[...], rest_ref[...] = row_products(
        xh_ref[...], xl_ref[...], nht_ref[:, half:], nlt_ref[:, half:], qht_ref[:, half:], qlt_ref[:, half:]
    )
    for r in range(2):
        xa, pa, xb, pb = (first_ref[k, r] for k in range(4))
        hop_x = first_ref[0, 1 - r] + side(xa)
        hop_p = first_ref[1, 1 - r] + side(pa)
        second = forward_light(c[r], xa, pa, xb, hop_x, hop_p)
        for k, (f, s) in enumerate(zip((xa, pa), second)):
            light_ref[k, r] = z_ref[k, r] + f + 0.5 * s


def expand_last(
    core_ref, coeff_ref, z_ref, low_ref, high_ref, light_ref, gram_ref, rest_ref, pack_ref,
    nht_ref, nlt_ref, qht_ref, qlt_ref, mine_ref, other_ref, xh_ref, xl_ref, sums_ref,
):
    c = coefficients(coeff_ref)
    n = z_ref.shape[2]
    for r, far in enumerate((low_ref, high_ref)):
        jfar = far_hopping(far, n)
        far_x = far[0:n] - jfar * z_ref[1, r]
        far_p = far[n : 2 * n] + jfar * z_ref[0, r]
        j = 0.5 * c[r][5]
        for k, value in enumerate((light_ref[0, r] - j * far_p, light_ref[1, r] + j * far_x)):
            start = (2 * k + r) * n
            h, l = split2(value)
            xh_ref[start : start + n] = h
            xl_ref[start : start + n] = l
    half = 4 * n
    gram, rest = row_products(
        xh_ref[...], xl_ref[...], nht_ref[:, :half], nlt_ref[:, :half], qht_ref[:, :half], qlt_ref[:, :half]
    )
    gram = gram + gram_ref[...]
    rest = rest + rest_ref[...]
    sums_ref[0:128], sums_ref[512:520] = packed(gram, rest[128:256])
    sums_ref[128:256] = jnp.transpose(rest[:128])
    sums_ref[256:384] = rest[256:]
    sums_ref[384:512] = pack_ref[0:128]
    sums_ref[520:528] = pack_ref[128:136]
    core = core_ref[0]
    mine_ref[...] = sums_ref[pl.ds(pl.multiple_of(core * 264, 8), 264)]
    other_ref[...] = sums_ref[pl.ds(pl.multiple_of((1 - core) * 264, 8), 264)]


def factor(
    core_ref, mine_ref, other_ref, r_bar_ref, nh_ref, nl_ref, sh_ref, sl_ref, sums_ref, a_ref, u_ref, inv_ref
):
    size = 256
    tile = 128
    core = core_ref[0]
    sums_ref[pl.ds(pl.multiple_of(core * 264, 8), 264)] = mine_ref[...]
    sums_ref[pl.ds(pl.multiple_of((1 - core) * 264, 8), 264)] = other_ref[...]
    a_ref[0:tile, 0:tile] = sums_ref[0:tile]
    a_ref[0:tile, tile:size] = sums_ref[tile : 2 * tile]
    a_ref[tile:size, tile:size] = sums_ref[3 * tile : 4 * tile]
    row = lax.broadcasted_iota(jnp.int32, (size, size), 0)
    col = lax.broadcasted_iota(jnp.int32, (size, size), 1)
    a_ref[:, size : 2 * size] = jnp.where(row == col, 1.0, 0.0)
    u_ref[...] = jnp.zeros((size, size), f32)
    inv_ref[...] = jnp.zeros((size, size), f32)
    place = lax.broadcasted_iota(jnp.int32, (8, 3 * tile), 0)
    for start in range(0, size, PANEL):
        base = (start // tile) * tile
        lanes = slice(base, base + 3 * tile)
        offset = start - base
        rows = [jnp.broadcast_to(a_ref[start + i : start + i + 1, lanes], (8, 3 * tile)) for i in range(PANEL)]
        s = {}
        for i in range(PANEL):
            for m in range(i, PANEL):
                s[i, m] = jnp.broadcast_to(rows[i][:, offset + m : offset + m + 1], (8, tile))
        done = []
        for i in range(PANEL):
            inverse = pl.reciprocal(s[i, i])
            root = lax.rsqrt(s[i, i])
            root = root * (1.5 - 0.5 * s[i, i] * root * root)
            for k in range(i + 1, PANEL):
                factor_k = s[i, k] * inverse
                for m in range(k, PANEL):
                    s[k, m] = s[k, m] - factor_k * s[i, m]
                rows[k] = rows[k] - jnp.concatenate([factor_k] * 3, axis=1) * rows[i]
            done.append(rows[i] * jnp.concatenate([root] * 3, axis=1))
        groups = []
        for first in range(0, PANEL, 8):
            group = done[first]
            for i in range(1, 8):
                group = jnp.where(place == i, done[first + i], group)
            groups.append(group)
        panel = jnp.concatenate(groups, axis=0)
        stop = start + PANEL
        if base == 0:
            u_ref[start:stop, :] = panel[:, : 2 * tile]
            inv_ref[start:stop, :tile] = panel[:, 2 * tile :]
        else:
            u_ref[start:stop, tile:] = panel[:, :tile]
            inv_ref[start:stop, :] = panel[:, tile:]
        if stop < size:
            h, m, l = split3(panel)
            width = size - base
            left = jnp.concatenate([h, h, m, m, h, l], axis=0)[:, :width]
            right = jnp.concatenate([h, m, h, m, l, h], axis=0)
            change = dot(left, right, ((0,), (0,)))
            a_ref[stop:, lanes] = a_ref[stop:, lanes] - change[stop - base :]
    upper = jnp.where(row <= col, u_ref[...], 0.0)
    inv = jnp.where(row >= col, inv_ref[...], 0.0)
    bar = jnp.where(row <= col, r_bar_ref[...], 0.0)
    corner = jnp.zeros((tile, tile), f32)
    top = jnp.concatenate([sums_ref[0:tile], corner], axis=1)
    bottom = jnp.concatenate([sums_ref[2 * tile : 3 * tile], sums_ref[3 * tile : 4 * tile]], axis=1)
    cross = jnp.concatenate([top, bottom], axis=0)
    diagonal = jnp.concatenate([sums_ref[512:513], sums_ref[520:521]], axis=1)
    cross = jnp.where(row > col, cross, jnp.where(row == col, diagonal, 0.0))

    def product(a, b, contract):
        return lax.dot_general(a, b, ((contract[0], contract[1]), ((), ())), precision=exact, preferred_element_type=f32)

    across = ((1,), (1,))
    middle = product(upper, bar, across) - product(cross, inv, across)
    symmetric = jnp.where(row >= col, middle, 0.0) + jnp.transpose(jnp.where(row > col, middle, 0.0))
    spread = product(inv, product(symmetric, inv, ((1,), (0,))), ((0,), (0,)))
    nh_ref[...], nl_ref[...] = split2(inv)
    sh_ref[...], sl_ref[...] = split2(spread)


def columns(qh, ql, nh, nl, xh, xl, ih, il, sh, sl):
    plain = ((1,), (0,))
    xh = jnp.concatenate([xh, nh], axis=1)
    xl = jnp.concatenate([xl, nl], axis=1)
    high = dot(qh, jnp.concatenate([ih, il], axis=1), plain) + dot(xh, jnp.concatenate([sh, sl], axis=1), plain)
    return high[:, :128] + high[:, 128:] + dot(ql, ih, plain) + dot(xl, sh, plain)


def gradient_light(
    coeff_ref, qh_ref, ql_ref, nh_ref, nl_ref, xh_ref, xl_ref, ih_ref, il_ref, sh_ref, sl_ref,
    w_ref, down_ref, up_ref,
):
    c = coefficients(coeff_ref)
    n = w_ref.shape[2]
    weights = [ref[:, :128] for ref in (ih_ref, il_ref, sh_ref, sl_ref)]
    for k in range(2):
        for r, out in ((0, down_ref), (1, up_ref)):
            here = slice((2 * k + r) * n, (2 * k + r + 1) * n)
            parts = [ref[here] for ref in (qh_ref, ql_ref, nh_ref, nl_ref, xh_ref, xl_ref)]
            w = columns(*parts, *weights)
            w_ref[k, r] = w
            out[k] = c[r][5] * w


def gradient_heavy(
    coeff_ref, light_ref, jdown_ref, jup_ref, qh_ref, ql_ref, nh_ref, nl_ref, xh_ref, xl_ref,
    ih_ref, il_ref, sh_ref, sl_ref, w_ref, down_ref, up_ref,
):
    c = coefficients(coeff_ref)
    n = w_ref.shape[2]
    weights = [ref[:, :128] for ref in (ih_ref, il_ref, sh_ref, sl_ref)]
    half = 4 * n
    for k in (1, 0):
        for r in range(2):
            here = slice((2 * k + r) * n, (2 * k + r + 1) * n)
            there = slice(half + here.start, half + here.stop)
            parts = [ref[there] for ref in (qh_ref, ql_ref, nh_ref, nl_ref)] + [xh_ref[here], xl_ref[here]]
            w_ref[k, r] = columns(*parts, *weights)
    hops = (jdown_ref, jup_ref)
    for r, out in ((0, down_ref), (1, up_ref)):
        j = c[r][5]
        hop_x = hops[1 - r][0] + side(hops[r][0])
        hop_p = hops[1 - r][1] + side(hops[r][1])
        bx, bp = backward_light(c[r], light_ref[0, r], light_ref[1, r], w_ref[1, r], hop_x, hop_p)
        out[0] = j * bx
        out[1] = j * bp


def gradient_noise(
    qh_ref, ql_ref, nh_ref, nl_ref, xlight_h, xlight_l, xheavy_h, xheavy_l, ih_ref, il_ref, sh_ref, sl_ref, out_ref
):
    n = out_ref.shape[2]
    weights = [ref[:, 128:] for ref in (ih_ref, il_ref, sh_ref, sl_ref)]
    for k in range(4):
        xh_ref, xl_ref = (xlight_h, xlight_l) if k < 2 else (xheavy_h, xheavy_l)
        for r in range(2):
            here = slice((2 * k + r) * n, (2 * k + r + 1) * n)
            there = slice((2 * (k % 2) + r) * n, (2 * (k % 2) + r + 1) * n)
            parts = [ref[here] for ref in (qh_ref, ql_ref, nh_ref, nl_ref)] + [xh_ref[there], xl_ref[there]]
            out_ref[k, r] = columns(*parts, *weights)


def contract_first(
    coeff_ref, light_ref, heavy_ref, jdown_ref, jup_ref, low_ref, high_ref, flow_ref, fhigh_ref,
    out_light_ref, out_heavy_ref, first_ref,
):
    c = coefficients(coeff_ref)
    n = light_ref.shape[2]
    hops = (jdown_ref, jup_ref)
    far = (low_ref, high_ref)
    for r in range(2):
        xa, pa, xb, pb = light_ref[0, r], light_ref[1, r], heavy_ref[0, r], heavy_ref[1, r]
        hop_x = hops[1 - r][0] + far[r][0] + side(hops[r][0])
        hop_p = hops[1 - r][1] + far[r][1] + side(hops[r][1])
        first_ref[0, r], first_ref[1, r] = backward_light(c[r], xa, pa, pb, hop_x, hop_p)
        first_ref[2, r], first_ref[3, r] = backward_heavy(c[r], pa, xb, pb)
    for r, fref in enumerate((flow_ref, fhigh_ref)):
        xa, pa, xb, pb = (first_ref[k, r] for k in range(4))
        jfar = far_hopping(fref, n)
        j, jother = c[r][5], c[1 - r][5]
        hop_x = jother * first_ref[0, 1 - r] + jfar * hops[r][1] + side(j * xa)
        hop_p = jother * first_ref[1, 1 - r] - jfar * hops[r][0] + side(j * pa)
        light = backward_light(c[r], xa, pa, pb, hop_x, hop_p)
        heavy = backward_heavy(c[r], pa, xb, pb)
        for k in range(2):
            out_light_ref[k, r] = light_ref[k, r] + first_ref[k, r] + 0.5 * light[k]
            out_heavy_ref[k, r] = heavy_ref[k, r] + first_ref[2 + k, r] + 0.5 * heavy[k]


def contract_last(light_ref, heavy_ref, low_ref, high_ref, out_ref):
    for r, far in enumerate((low_ref, high_ref)):
        out_ref[0, r] = light_ref[0, r] + 0.5 * far[1]
        out_ref[1, r] = light_ref[1, r] - 0.5 * far[0]
        out_ref[2, r] = heavy_ref[0, r]
        out_ref[3, r] = heavy_ref[1, r]


def exchange(up, down):
    count = lax.axis_size("row")
    forward = [(i, i + 1) for i in range(count - 1)]
    backward = [(i + 1, i) for i in range(count - 1)]
    low = lax.ppermute(up, "row", forward)
    high = lax.ppermute(down, "row", backward)
    return low, high


def sum_over_rows(mine, other):
    count = lax.axis_size("row")
    bits = count.bit_length() - 1
    swap = [(i, i ^ 1) for i in range(count)]
    mine = mine + lax.ppermute(other, "row", swap)
    for step in range(bits - 1):
        turn = [1 + step, 1 + (step + 1) % (bits - 1)]
        mine = mine + lax.ppermute(mine, "row", [(i, i ^ (1 << turn[i & 1])) for i in range(count)])
    return mine, lax.ppermute(mine, "row", swap)


def on_device(cell_coeffs, z_factor, noise_cols, q_bar, r_bar):
    quads, lattice, n, rank = z_factor.shape
    flat = quads * lattice * n
    coeffs = cell_coeffs
    core = (lax.axis_index("row") & 1).reshape(1)
    noise = noise_cols.reshape(flat, -1)
    bar = q_bar.reshape(flat, -1)
    shape = jax.ShapeDtypeStruct
    hops = shape((2, n, rank), f32)
    down, up = call(
        light_rows, (hops, hops), 0, 2 * 10**6, [pltpu.SemaphoreType.DMA((2,))], far=True
    )(z_factor)
    low, high = exchange(up, down)
    rim = shape((2 * n + 8, rank), f32)
    down, up = call(forward_rim, (rim, rim), 10**6, 2 * 10**6)(coeffs, z_factor)
    far_low, far_high = exchange(up, down)
    wide, tall = shape((flat, 256), bf16), shape((flat, 128), bf16)
    wide_t, tall_t = shape((256, flat), bf16), shape((128, flat), bf16)
    work = 2 * flat * 128 * 128
    pack, nh, nl, qh, ql, nht, nlt, qht, qlt = call(
        noise_products, (shape((136, 128), f32), tall, tall, wide, wide, tall_t, tall_t, wide_t, wide_t),
        work * 5, 9 * 10**6,
    )(noise, bar)
    transposed = (nht, nlt, qht, qlt)
    half = shape((flat // 2, 128), bf16)
    pair = shape((2, lattice, n, rank), f32)
    light, xh_heavy, xl_heavy, gram, rest = call(
        expand_first, (pair, half, half, shape((128, 128), f32), shape((384, 128), f32)), work * 6, 9 * 10**6,
        [pltpu.VMEM(z_factor.shape, f32)],
    )(coeffs, z_factor, low, high, *transposed)
    part = shape((264, 128), f32)
    mine, other, xh_light, xl_light = call(
        expand_last, (part, part, half, half), work * 6, 9 * 10**6, [pltpu.VMEM((528, 128), f32)], scalar=True
    )(core, coeffs, z_factor, far_low, far_high, light, gram, rest, pack, *transposed)
    mine, other = sum_over_rows(mine, other)
    square = shape((256, 256), bf16)
    weights = call(
        factor, (square,) * 4, 10**9, 10**6,
        [
            pltpu.VMEM((528, 128), f32),
            pltpu.VMEM((256, 512), f32),
            pltpu.VMEM((256, 256), f32),
            pltpu.VMEM((256, 256), f32),
        ],
        scalar=True,
    )(core, mine, other, r_bar)
    left = (qh, ql, nh, nl)
    w_light, jdown, jup = call(gradient_light, (pair, hops, hops), work * 6, 6 * 10**6)(
        coeffs, *left, xh_light, xl_light, *weights
    )
    low, high = exchange(jup, jdown)
    w_heavy, down, up = call(gradient_heavy, (pair, hops, hops), work * 6, 6 * 10**6)(
        coeffs, w_light, jdown, jup, *left, xh_heavy, xl_heavy, *weights
    )
    last_low, last_high = exchange(up, down)
    noise_grad = call(gradient_noise, shape(noise_cols.shape, f32), work * 12, 9 * 10**6)(
        *left, xh_light, xl_light, xh_heavy, xl_heavy, *weights
    )
    out_light, out_heavy = call(contract_first, (pair, pair), 10**7, 6 * 10**6, [pltpu.VMEM(z_factor.shape, f32)])(
        coeffs, w_light, w_heavy, jdown, jup, low, high, far_low, far_high
    )
    z_grad = call(contract_last, shape(z_factor.shape, f32), 10**6, 6 * 10**6)(
        out_light, out_heavy, last_low, last_high
    )
    return z_grad, noise_grad


def solution(mesh):
    return jax.shard_map(
        on_device,
        mesh=mesh,
        in_specs=(
            P(None, "row", None),
            P(None, ("grp", "row"), None, None),
            P(None, ("grp", "row"), None, None),
            P(None, ("grp", "row"), None, None),
            P("grp", None),
        ),
        out_specs=(P(None, ("grp", "row"), None, None), P(None, ("grp", "row"), None, None)),
        check_vma=False,
    )
```

```python
import jax
import jax.numpy as jnp
from jax import lax
from jax.experimental import pallas as pl
from jax.experimental.pallas import tpu as pltpu
from jax.sharding import PartitionSpec as P

rate_scales = (0.4, 0.4, 0.1, 0.2, 0.1, 0.1)
exact = lax.Precision.HIGHEST
f32 = jnp.float32
bf16 = jnp.bfloat16
VMEM = pl.BlockSpec(memory_space=pltpu.VMEM)
LIMIT = 24 * 1024 * 1024
FAR_LIMIT = 63 * 1024 * 1024
PANEL = 16


def call(kernel, outs, flops, moved, scratch=(), scalar=False, far=False):
    def run(*args):
        specs = [pl.BlockSpec(memory_space=pltpu.HBM) if far else pl.BlockSpec() for _ in args]
        if scalar:
            specs[0] = pl.BlockSpec(memory_space=pltpu.SMEM)
        return pl.pallas_call(
            kernel,
            out_shape=outs,
            in_specs=specs,
            scratch_shapes=list(scratch),
            compiler_params=pltpu.CompilerParams(vmem_limit_bytes=FAR_LIMIT if far else LIMIT),
            cost_estimate=pl.CostEstimate(flops=flops, bytes_accessed=moved, transcendentals=0),
        )(*args)

    return run


def split2(value):
    high = value.astype(bf16)
    low = (value - high.astype(f32)).astype(bf16)
    return high, low


def split3(value):
    high = value.astype(bf16)
    rest = value - high.astype(f32)
    mid = rest.astype(bf16)
    low = (rest - mid.astype(f32)).astype(bf16)
    return high, mid, low


def dot(a, b, contract):
    return lax.dot_general(a, b, ((contract[0], contract[1]), ((), ())), preferred_element_type=f32)


def coefficients(coeff_ref):
    cols = jnp.transpose(jnp.concatenate([coeff_ref[k] for k in range(6)], axis=0))
    out = []
    for r in range(2):
        out.append([cols[:, 2 * k + r : 2 * k + r + 1] * rate_scales[k] for k in range(6)])
    return out


def side(v):
    n = v.shape[0]
    place = lax.broadcasted_iota(jnp.int32, v.shape, 0)
    left = jnp.where(place == 0, 0.0, pltpu.roll(v, 1, 0))
    right = jnp.where(place == n - 1, 0.0, pltpu.roll(v, n - 1, 0))
    return left + right


def forward_light(c, xa, pa, xb, hop_x, hop_p):
    d, w, g, l, m, j = c
    return (
        -0.5 * l * xa - d * pa - j * hop_p,
        d * xa - 0.5 * l * pa - 2.0 * g * xb + j * hop_x,
    )


def forward_heavy(c, xa, xb, pb):
    d, w, g, l, m, j = c
    return w * pb, -w * xb - 0.5 * m * pb - 2.0 * g * xa


def backward_light(c, xa, pa, pb, hop_x, hop_p):
    d, w, g, l, m, j = c
    return (
        -0.5 * l * xa + d * pa - 2.0 * g * pb + hop_p,
        -d * xa - 0.5 * l * pa - hop_x,
    )


def backward_heavy(c, pa, xb, pb):
    d, w, g, l, m, j = c
    return -2.0 * g * pa - w * pb, w * xb - 0.5 * m * pb


def forward_rim(coeff_hbm, z_hbm, down1_ref, up1_ref, down2_ref, up2_ref, coeff_ref, xb_ref, sems):
    copies = [
        pltpu.make_async_copy(z_hbm.at[0:2, 0], down1_ref, sems.at[0]),
        pltpu.make_async_copy(z_hbm.at[0:2, 1], up1_ref, sems.at[1]),
        pltpu.make_async_copy(coeff_hbm, coeff_ref, sems.at[2]),
        pltpu.make_async_copy(z_hbm.at[2], xb_ref, sems.at[3]),
    ]
    for copy in copies:
        copy.start()
    for copy in copies:
        copy.wait()
    c = coefficients(coeff_ref)
    n = xb_ref.shape[1]
    rows = (down1_ref, up1_ref)
    for r, out in ((0, down2_ref), (1, up2_ref)):
        xa, pa, xb = rows[r][0], rows[r][1], xb_ref[r]
        hop_x = rows[1 - r][0] + side(xa)
        hop_p = rows[1 - r][1] + side(pa)
        out[0:n], out[n : 2 * n] = forward_light(c[r], xa, pa, xb, hop_x, hop_p)
        hopping = coeff_ref[5, r : r + 1, :] * rate_scales[5]
        pieces = [hopping[:, k * 128 : (k + 1) * 128] for k in range(n // 128)]
        pieces.append(jnp.zeros((8 - n // 128, 128), f32))
        out[2 * n :] = jnp.concatenate(pieces, axis=0)


def far_hopping(recv_ref, n):
    tail = jnp.transpose(recv_ref[2 * n : 2 * n + 8])
    return jnp.concatenate([tail[:, k : k + 1] for k in range(n // 128)], axis=0)


def packed(gram, cross):
    row = lax.broadcasted_iota(jnp.int32, gram.shape, 0)
    col = lax.broadcasted_iota(jnp.int32, gram.shape, 1)
    diagonal = jnp.sum(jnp.where(row == col, cross, 0.0), axis=0, keepdims=True)
    return jnp.where(row <= col, gram, cross), jnp.broadcast_to(diagonal, (8, gram.shape[1]))


def noise_products(noise_ref, q_ref, pack_ref, nh_ref, nl_ref, qh_ref, ql_ref, nht_ref, nlt_ref, qht_ref, qlt_ref):
    nh, nl = split2(noise_ref[...])
    qh, ql = split2(q_ref[...])
    nh_ref[...] = nh
    nl_ref[...] = nl
    qh_ref[...] = qh
    ql_ref[...] = ql
    for value, out in ((nh, nht_ref), (nl, nlt_ref), (qh, qht_ref), (ql, qlt_ref)):
        out[...] = jnp.transpose(value)
    plain = ((1,), (0,))
    high = dot(jnp.concatenate([nht_ref[...], qht_ref[128:]], axis=0), jnp.concatenate([nh, nl], axis=1), plain)
    low = dot(qlt_ref[128:], nh, plain)
    mixed = high[:128, 128:]
    gram = high[:128, :128] + mixed + jnp.transpose(mixed)
    cross = high[128:, :128] + high[128:, 128:] + low
    pack_ref[0:128], pack_ref[128:] = packed(gram, cross)


def row_products(xh, xl, nht, nlt, qht, qlt):
    plain = ((1,), (0,))
    left = jnp.concatenate([jnp.transpose(xh), nht, qht], axis=0)
    high = dot(left, jnp.concatenate([xh, xl], axis=1), plain)
    low = dot(jnp.concatenate([nlt, qlt], axis=0), xh, plain)
    mixed = high[:128, 128:]
    return (
        high[:128, :128] + mixed + jnp.transpose(mixed),
        high[128:, :128] + high[128:, 128:] + low,
    )


def expand_first(
    coeff_ref, z_ref, low_ref, high_ref, nht_ref, nlt_ref, qht_ref, qlt_ref,
    light_ref, xh_ref, xl_ref, gram_ref, rest_ref, first_ref,
):
    c = coefficients(coeff_ref)
    n = z_ref.shape[2]
    far = (low_ref, high_ref)
    for r in range(2):
        xa, pa, xb, pb = (z_ref[k, r] for k in range(4))
        hop_x = z_ref[0, 1 - r] + far[r][0] + side(xa)
        hop_p = z_ref[1, 1 - r] + far[r][1] + side(pa)
        first_ref[0, r], first_ref[1, r] = forward_light(c[r], xa, pa, xb, hop_x, hop_p)
        first_ref[2, r], first_ref[3, r] = forward_heavy(c[r], xa, xb, pb)
    for r in range(2):
        xa, pa, xb, pb = (first_ref[k, r] for k in range(4))
        for k, (f, s) in enumerate(zip((xb, pb), forward_heavy(c[r], xa, xb, pb))):
            start = (2 * k + r) * n
            h, l = split2(z_ref[2 + k, r] + f + 0.5 * s)
            xh_ref[start : start + n] = h
            xl_ref[start : start + n] = l
    half = 4 * n
    gram_ref[...], rest_ref[...] = row_products(
        xh_ref[...], xl_ref[...], nht_ref[:, half:], nlt_ref[:, half:], qht_ref[:, half:], qlt_ref[:, half:]
    )
    for r in range(2):
        xa, pa, xb, pb = (first_ref[k, r] for k in range(4))
        hop_x = first_ref[0, 1 - r] + side(xa)
        hop_p = first_ref[1, 1 - r] + side(pa)
        second = forward_light(c[r], xa, pa, xb, hop_x, hop_p)
        for k, (f, s) in enumerate(zip((xa, pa), second)):
            light_ref[k, r] = z_ref[k, r] + f + 0.5 * s


def expand_last(
    core_ref, coeff_ref, z_ref, low_ref, high_ref, light_ref, gram_ref, rest_ref, pack_ref,
    nht_ref, nlt_ref, qht_ref, qlt_ref, mine_ref, other_ref, xh_ref, xl_ref, sums_ref,
):
    c = coefficients(coeff_ref)
    n = z_ref.shape[2]
    for r, far in enumerate((low_ref, high_ref)):
        jfar = far_hopping(far, n)
        far_x = far[0:n] - jfar * z_ref[1, r]
        far_p = far[n : 2 * n] + jfar * z_ref[0, r]
        j = 0.5 * c[r][5]
        for k, value in enumerate((light_ref[0, r] - j * far_p, light_ref[1, r] + j * far_x)):
            start = (2 * k + r) * n
            h, l = split2(value)
            xh_ref[start : start + n] = h
            xl_ref[start : start + n] = l
    half = 4 * n
    gram, rest = row_products(
        xh_ref[...], xl_ref[...], nht_ref[:, :half], nlt_ref[:, :half], qht_ref[:, :half], qlt_ref[:, :half]
    )
    gram = gram + gram_ref[...]
    rest = rest + rest_ref[...]
    sums_ref[0:128], sums_ref[512:520] = packed(gram, rest[128:256])
    sums_ref[128:256] = jnp.transpose(rest[:128])
    sums_ref[256:384] = rest[256:]
    sums_ref[384:512] = pack_ref[0:128]
    sums_ref[520:528] = pack_ref[128:136]
    core = core_ref[0]
    mine_ref[...] = sums_ref[pl.ds(pl.multiple_of(core * 264, 8), 264)]
    other_ref[...] = sums_ref[pl.ds(pl.multiple_of((1 - core) * 264, 8), 264)]


def factor(
    core_ref, mine_ref, other_ref, r_bar_ref, nh_ref, nl_ref, sh_ref, sl_ref, sums_ref, a_ref, u_ref, inv_ref
):
    size = 256
    tile = 128
    core = core_ref[0]
    sums_ref[pl.ds(pl.multiple_of(core * 264, 8), 264)] = mine_ref[...]
    sums_ref[pl.ds(pl.multiple_of((1 - core) * 264, 8), 264)] = other_ref[...]
    a_ref[0:tile, 0:tile] = sums_ref[0:tile]
    a_ref[0:tile, tile:size] = sums_ref[tile : 2 * tile]
    a_ref[tile:size, tile:size] = sums_ref[3 * tile : 4 * tile]
    row = lax.broadcasted_iota(jnp.int32, (size, size), 0)
    col = lax.broadcasted_iota(jnp.int32, (size, size), 1)
    a_ref[:, size : 2 * size] = jnp.where(row == col, 1.0, 0.0)
    u_ref[...] = jnp.zeros((size, size), f32)
    inv_ref[...] = jnp.zeros((size, size), f32)
    place = lax.broadcasted_iota(jnp.int32, (8, 3 * tile), 0)
    for start in range(0, size, PANEL):
        base = (start // tile) * tile
        lanes = slice(base, base + 3 * tile)
        offset = start - base
        rows = [jnp.broadcast_to(a_ref[start + i : start + i + 1, lanes], (8, 3 * tile)) for i in range(PANEL)]
        s = {}
        for i in range(PANEL):
            for m in range(i, PANEL):
                s[i, m] = jnp.broadcast_to(rows[i][:, offset + m : offset + m + 1], (8, tile))
        done = []
        for i in range(PANEL):
            inverse = pl.reciprocal(s[i, i])
            root = lax.rsqrt(s[i, i])
            root = root * (1.5 - 0.5 * s[i, i] * root * root)
            for k in range(i + 1, PANEL):
                factor_k = s[i, k] * inverse
                for m in range(k, PANEL):
                    s[k, m] = s[k, m] - factor_k * s[i, m]
                rows[k] = rows[k] - jnp.concatenate([factor_k] * 3, axis=1) * rows[i]
            done.append(rows[i] * jnp.concatenate([root] * 3, axis=1))
        groups = []
        for first in range(0, PANEL, 8):
            group = done[first]
            for i in range(1, 8):
                group = jnp.where(place == i, done[first + i], group)
            groups.append(group)
        panel = jnp.concatenate(groups, axis=0)
        stop = start + PANEL
        if base == 0:
            u_ref[start:stop, :] = panel[:, : 2 * tile]
            inv_ref[start:stop, :tile] = panel[:, 2 * tile :]
        else:
            u_ref[start:stop, tile:] = panel[:, :tile]
            inv_ref[start:stop, :] = panel[:, tile:]
        if stop < size:
            h, m, l = split3(panel)
            width = size - base
            left = jnp.concatenate([h, h, m, m, h, l], axis=0)[:, :width]
            right = jnp.concatenate([h, m, h, m, l, h], axis=0)
            change = dot(left, right, ((0,), (0,)))
            a_ref[stop:, lanes] = a_ref[stop:, lanes] - change[stop - base :]
    upper = jnp.where(row <= col, u_ref[...], 0.0)
    inv = jnp.where(row >= col, inv_ref[...], 0.0)
    bar = jnp.where(row <= col, r_bar_ref[...], 0.0)
    corner = jnp.zeros((tile, tile), f32)
    top = jnp.concatenate([sums_ref[0:tile], corner], axis=1)
    bottom = jnp.concatenate([sums_ref[2 * tile : 3 * tile], sums_ref[3 * tile : 4 * tile]], axis=1)
    cross = jnp.concatenate([top, bottom], axis=0)
    diagonal = jnp.concatenate([sums_ref[512:513], sums_ref[520:521]], axis=1)
    cross = jnp.where(row > col, cross, jnp.where(row == col, diagonal, 0.0))

    def product(a, b, contract):
        return lax.dot_general(a, b, ((contract[0], contract[1]), ((), ())), precision=exact, preferred_element_type=f32)

    across = ((1,), (1,))
    middle = product(upper, bar, across) - product(cross, inv, across)
    symmetric = jnp.where(row >= col, middle, 0.0) + jnp.transpose(jnp.where(row > col, middle, 0.0))
    spread = product(inv, product(symmetric, inv, ((1,), (0,))), ((0,), (0,)))
    nh_ref[...], nl_ref[...] = split2(inv)
    sh_ref[...], sl_ref[...] = split2(spread)


def columns(qh, ql, nh, nl, xh, xl, ih, il, sh, sl):
    plain = ((1,), (0,))
    xh = jnp.concatenate([xh, nh], axis=1)
    xl = jnp.concatenate([xl, nl], axis=1)
    high = dot(qh, jnp.concatenate([ih, il], axis=1), plain) + dot(xh, jnp.concatenate([sh, sl], axis=1), plain)
    return high[:, :128] + high[:, 128:] + dot(ql, ih, plain) + dot(xl, sh, plain)


def gradient_light(
    coeff_ref, qh_ref, ql_ref, nh_ref, nl_ref, xh_ref, xl_ref, ih_ref, il_ref, sh_ref, sl_ref,
    w_ref, down_ref, up_ref,
):
    c = coefficients(coeff_ref)
    n = w_ref.shape[2]
    weights = [ref[:, :128] for ref in (ih_ref, il_ref, sh_ref, sl_ref)]
    for k in range(2):
        for r, out in ((0, down_ref), (1, up_ref)):
            here = slice((2 * k + r) * n, (2 * k + r + 1) * n)
            parts = [ref[here] for ref in (qh_ref, ql_ref, nh_ref, nl_ref, xh_ref, xl_ref)]
            w = columns(*parts, *weights)
            w_ref[k, r] = w
            out[k] = c[r][5] * w


def gradient_heavy(
    coeff_ref, light_ref, jdown_ref, jup_ref, qh_ref, ql_ref, nh_ref, nl_ref, xh_ref, xl_ref,
    ih_ref, il_ref, sh_ref, sl_ref, w_ref, down_ref, up_ref,
):
    c = coefficients(coeff_ref)
    n = w_ref.shape[2]
    weights = [ref[:, :128] for ref in (ih_ref, il_ref, sh_ref, sl_ref)]
    half = 4 * n
    for k in (1, 0):
        for r in range(2):
            here = slice((2 * k + r) * n, (2 * k + r + 1) * n)
            there = slice(half + here.start, half + here.stop)
            parts = [ref[there] for ref in (qh_ref, ql_ref, nh_ref, nl_ref)] + [xh_ref[here], xl_ref[here]]
            w_ref[k, r] = columns(*parts, *weights)
    hops = (jdown_ref, jup_ref)
    for r, out in ((0, down_ref), (1, up_ref)):
        j = c[r][5]
        hop_x = hops[1 - r][0] + side(hops[r][0])
        hop_p = hops[1 - r][1] + side(hops[r][1])
        bx, bp = backward_light(c[r], light_ref[0, r], light_ref[1, r], w_ref[1, r], hop_x, hop_p)
        out[0] = j * bx
        out[1] = j * bp


def gradient_noise(
    qh_ref, ql_ref, nh_ref, nl_ref, xlight_h, xlight_l, xheavy_h, xheavy_l, ih_ref, il_ref, sh_ref, sl_ref, out_ref
):
    n = out_ref.shape[2]
    weights = [ref[:, 128:] for ref in (ih_ref, il_ref, sh_ref, sl_ref)]
    for k in range(4):
        xh_ref, xl_ref = (xlight_h, xlight_l) if k < 2 else (xheavy_h, xheavy_l)
        for r in range(2):
            here = slice((2 * k + r) * n, (2 * k + r + 1) * n)
            there = slice((2 * (k % 2) + r) * n, (2 * (k % 2) + r + 1) * n)
            parts = [ref[here] for ref in (qh_ref, ql_ref, nh_ref, nl_ref)] + [xh_ref[there], xl_ref[there]]
            out_ref[k, r] = columns(*parts, *weights)


def contract_first(
    coeff_ref, light_ref, heavy_ref, jdown_ref, jup_ref, low_ref, high_ref, flow_ref, fhigh_ref,
    out_light_ref, out_heavy_ref, first_ref,
):
    c = coefficients(coeff_ref)
    n = light_ref.shape[2]
    hops = (jdown_ref, jup_ref)
    far = (low_ref, high_ref)
    for r in range(2):
        xa, pa, xb, pb = light_ref[0, r], light_ref[1, r], heavy_ref[0, r], heavy_ref[1, r]
        hop_x = hops[1 - r][0] + far[r][0] + side(hops[r][0])
        hop_p = hops[1 - r][1] + far[r][1] + side(hops[r][1])
        first_ref[0, r], first_ref[1, r] = backward_light(c[r], xa, pa, pb, hop_x, hop_p)
        first_ref[2, r], first_ref[3, r] = backward_heavy(c[r], pa, xb, pb)
    for r, fref in enumerate((flow_ref, fhigh_ref)):
        xa, pa, xb, pb = (first_ref[k, r] for k in range(4))
        jfar = far_hopping(fref, n)
        j, jother = c[r][5], c[1 - r][5]
        hop_x = jother * first_ref[0, 1 - r] + jfar * hops[r][1] + side(j * xa)
        hop_p = jother * first_ref[1, 1 - r] - jfar * hops[r][0] + side(j * pa)
        light = backward_light(c[r], xa, pa, pb, hop_x, hop_p)
        heavy = backward_heavy(c[r], pa, xb, pb)
        for k in range(2):
            out_light_ref[k, r] = light_ref[k, r] + first_ref[k, r] + 0.5 * light[k]
            out_heavy_ref[k, r] = heavy_ref[k, r] + first_ref[2 + k, r] + 0.5 * heavy[k]


def contract_last(light_ref, heavy_ref, low_ref, high_ref, out_ref):
    for r, far in enumerate((low_ref, high_ref)):
        out_ref[0, r] = light_ref[0, r] + 0.5 * far[1]
        out_ref[1, r] = light_ref[1, r] - 0.5 * far[0]
        out_ref[2, r] = heavy_ref[0, r]
        out_ref[3, r] = heavy_ref[1, r]


def exchange(up, down):
    count = lax.axis_size("row")
    forward = [(i, i + 1) for i in range(count - 1)]
    backward = [(i + 1, i) for i in range(count - 1)]
    low = lax.ppermute(up, "row", forward)
    high = lax.ppermute(down, "row", backward)
    return low, high


def sum_over_rows(mine, other):
    count = lax.axis_size("row")
    bits = count.bit_length() - 1
    swap = [(i, i ^ 1) for i in range(count)]
    mine = mine + lax.ppermute(other, "row", swap)
    for step in range(bits - 1):
        turn = [1 + step, 1 + (step + 1) % (bits - 1)]
        mine = mine + lax.ppermute(mine, "row", [(i, i ^ (1 << turn[i & 1])) for i in range(count)])
    return mine, lax.ppermute(mine, "row", swap)


def on_device(cell_coeffs, z_factor, noise_cols, q_bar, r_bar):
    quads, lattice, n, rank = z_factor.shape
    flat = quads * lattice * n
    coeffs = cell_coeffs
    core = (lax.axis_index("row") & 1).reshape(1)
    noise = noise_cols.reshape(flat, -1)
    bar = q_bar.reshape(flat, -1)
    shape = jax.ShapeDtypeStruct
    hops = shape((2, n, rank), f32)
    rim = shape((2 * n + 8, rank), f32)
    down, up, far_down, far_up = call(
        forward_rim, (hops, hops, rim, rim), 10**6, 3 * 10**6,
        [
            pltpu.VMEM(cell_coeffs.shape, f32),
            pltpu.VMEM(z_factor.shape[1:], f32),
            pltpu.SemaphoreType.DMA((4,)),
        ],
        far=True,
    )(coeffs, z_factor)
    low, high = exchange(up, down)
    far_low, far_high = exchange(far_up, far_down)
    wide, tall = shape((flat, 256), bf16), shape((flat, 128), bf16)
    wide_t, tall_t = shape((256, flat), bf16), shape((128, flat), bf16)
    work = 2 * flat * 128 * 128
    pack, nh, nl, qh, ql, nht, nlt, qht, qlt = call(
        noise_products, (shape((136, 128), f32), tall, tall, wide, wide, tall_t, tall_t, wide_t, wide_t),
        work * 5, 9 * 10**6,
    )(noise, bar)
    transposed = (nht, nlt, qht, qlt)
    half = shape((flat // 2, 128), bf16)
    pair = shape((2, lattice, n, rank), f32)
    light, xh_heavy, xl_heavy, gram, rest = call(
        expand_first, (pair, half, half, shape((128, 128), f32), shape((384, 128), f32)), work * 6, 9 * 10**6,
        [pltpu.VMEM(z_factor.shape, f32)],
    )(coeffs, z_factor, low, high, *transposed)
    part = shape((264, 128), f32)
    mine, other, xh_light, xl_light = call(
        expand_last, (part, part, half, half), work * 6, 9 * 10**6, [pltpu.VMEM((528, 128), f32)], scalar=True
    )(core, coeffs, z_factor, far_low, far_high, light, gram, rest, pack, *transposed)
    mine, other = sum_over_rows(mine, other)
    square = shape((256, 256), bf16)
    weights = call(
        factor, (square,) * 4, 10**9, 10**6,
        [
            pltpu.VMEM((528, 128), f32),
            pltpu.VMEM((256, 512), f32),
            pltpu.VMEM((256, 256), f32),
            pltpu.VMEM((256, 256), f32),
        ],
        scalar=True,
    )(core, mine, other, r_bar)
    left = (qh, ql, nh, nl)
    w_light, jdown, jup = call(gradient_light, (pair, hops, hops), work * 6, 6 * 10**6)(
        coeffs, *left, xh_light, xl_light, *weights
    )
    low, high = exchange(jup, jdown)
    w_heavy, down, up = call(gradient_heavy, (pair, hops, hops), work * 6, 6 * 10**6)(
        coeffs, w_light, jdown, jup, *left, xh_heavy, xl_heavy, *weights
    )
    last_low, last_high = exchange(up, down)
    noise_grad = call(gradient_noise, shape(noise_cols.shape, f32), work * 12, 9 * 10**6)(
        *left, xh_light, xl_light, xh_heavy, xl_heavy, *weights
    )
    out_light, out_heavy = call(contract_first, (pair, pair), 10**7, 6 * 10**6, [pltpu.VMEM(z_factor.shape, f32)])(
        coeffs, w_light, w_heavy, jdown, jup, low, high, far_low, far_high
    )
    z_grad = call(contract_last, shape(z_factor.shape, f32), 10**6, 6 * 10**6)(
        out_light, out_heavy, last_low, last_high
    )
    return z_grad, noise_grad


def solution(mesh):
    return jax.shard_map(
        on_device,
        mesh=mesh,
        in_specs=(
            P(None, "row", None),
            P(None, ("grp", "row"), None, None),
            P(None, ("grp", "row"), None, None),
            P(None, ("grp", "row"), None, None),
            P("grp", None),
        ),
        out_specs=(P(None, ("grp", "row"), None, None), P(None, ("grp", "row"), None, None)),
        check_vma=False,
    )
```

```python
import jax
import jax.numpy as jnp
from jax import lax
from jax.experimental import pallas as pl
from jax.experimental.pallas import tpu as pltpu
from jax.sharding import PartitionSpec as P

rate_scales = (0.4, 0.4, 0.1, 0.2, 0.1, 0.1)
exact = lax.Precision.HIGHEST
f32 = jnp.float32
bf16 = jnp.bfloat16
VMEM = pl.BlockSpec(memory_space=pltpu.VMEM)
LIMIT = 24 * 1024 * 1024
FAR_LIMIT = 63 * 1024 * 1024
PANEL = 16


def call(kernel, outs, flops, moved, scratch=(), scalar=False, far=False):
    def run(*args):
        specs = [pl.BlockSpec(memory_space=pltpu.HBM) if far else pl.BlockSpec() for _ in args]
        if scalar:
            specs[0] = pl.BlockSpec(memory_space=pltpu.SMEM)
        return pl.pallas_call(
            kernel,
            out_shape=outs,
            in_specs=specs,
            scratch_shapes=list(scratch),
            compiler_params=pltpu.CompilerParams(vmem_limit_bytes=FAR_LIMIT if far else LIMIT),
            cost_estimate=pl.CostEstimate(flops=flops, bytes_accessed=moved, transcendentals=0),
        )(*args)

    return run


def split2(value):
    high = value.astype(bf16)
    low = (value - high.astype(f32)).astype(bf16)
    return high, low


def split3(value):
    high = value.astype(bf16)
    rest = value - high.astype(f32)
    mid = rest.astype(bf16)
    low = (rest - mid.astype(f32)).astype(bf16)
    return high, mid, low


def dot(a, b, contract):
    return lax.dot_general(a, b, ((contract[0], contract[1]), ((), ())), preferred_element_type=f32)


def coefficients(table_ref):
    return [[table_ref[:, 6 * s + k : 6 * s + k + 1] for k in range(6)] for s in range(2)]


def side(v):
    n = v.shape[0]
    place = lax.broadcasted_iota(jnp.int32, v.shape, 0)
    left = jnp.where(place == 0, 0.0, pltpu.roll(v, 1, 0))
    right = jnp.where(place == n - 1, 0.0, pltpu.roll(v, n - 1, 0))
    return left + right


def forward_light(c, xa, pa, xb, hop_x, hop_p):
    d, w, g, l, m, j = c
    return (
        -0.5 * l * xa - d * pa - j * hop_p,
        d * xa - 0.5 * l * pa - 2.0 * g * xb + j * hop_x,
    )


def forward_heavy(c, xa, xb, pb):
    d, w, g, l, m, j = c
    return w * pb, -w * xb - 0.5 * m * pb - 2.0 * g * xa


def backward_light(c, xa, pa, pb, hop_x, hop_p):
    d, w, g, l, m, j = c
    return (
        -0.5 * l * xa + d * pa - 2.0 * g * pb + hop_p,
        -d * xa - 0.5 * l * pa - hop_x,
    )


def backward_heavy(c, pa, xb, pb):
    d, w, g, l, m, j = c
    return -2.0 * g * pa - w * pb, w * xb - 0.5 * m * pb


def forward_rim(core_ref, coeff_hbm, z_hbm, outer1_ref, outer2_ref, inner_ref, table_ref, coeff_ref, z_ref, sems):
    n = z_ref.shape[2]
    core = core_ref[0]
    copies = [
        pltpu.make_async_copy(z_hbm.at[0:3, core], z_ref.at[0], sems.at[0]),
        pltpu.make_async_copy(z_hbm.at[0:3, 1 - core], z_ref.at[1], sems.at[1]),
        pltpu.make_async_copy(coeff_hbm, coeff_ref, sems.at[2]),
    ]
    for copy in copies:
        copy.start()
    for copy in copies:
        copy.wait()
    cols = jnp.transpose(jnp.concatenate([coeff_ref[k] for k in range(6)], axis=0))
    swapped = core == 1
    both = []
    for s in range(2):
        for k in range(6):
            column = jnp.where(swapped, cols[:, 2 * k + 1 - s : 2 * k + 2 - s], cols[:, 2 * k + s : 2 * k + s + 1])
            both.append(column * rate_scales[k])
    for place, column in enumerate(both):
        table_ref[:, place : place + 1] = column
    far = []
    for s in range(2):
        xa, pa, xb = z_ref[s, 0], z_ref[s, 1], z_ref[s, 2]
        hop_x = z_ref[1 - s, 0] + side(xa)
        hop_p = z_ref[1 - s, 1] + side(pa)
        far.append(forward_light(both[6 * s : 6 * s + 6], xa, pa, xb, hop_x, hop_p))
    outer1_ref[0:n] = z_ref[0, 0]
    outer1_ref[n : 2 * n] = z_ref[0, 1]
    inner_ref[0:n] = z_ref[1, 0]
    inner_ref[n : 2 * n] = z_ref[1, 1]
    for s, out, base in ((0, outer2_ref, 0), (1, inner_ref, 2 * n)):
        out[base : base + n], out[base + n : base + 2 * n] = far[s]
        hopping = jnp.where(swapped, coeff_ref[5, 1 - s : 2 - s, :], coeff_ref[5, s : s + 1, :]) * rate_scales[5]
        pieces = [hopping[:, k * 128 : (k + 1) * 128] for k in range(n // 128)]
        pieces.append(jnp.zeros((8 - n // 128, 128), f32))
        out[base + 2 * n :] = jnp.concatenate(pieces, axis=0)


def far_hopping(recv_ref, n):
    size = recv_ref.shape[0]
    tail = jnp.transpose(recv_ref[size - 8 : size])
    return jnp.concatenate([tail[:, k : k + 1] for k in range(n // 128)], axis=0)


def cells(row, k, n):
    return pl.ds(pl.multiple_of((2 * k + row) * n, 128), n)


def packed(gram, cross):
    row = lax.broadcasted_iota(jnp.int32, gram.shape, 0)
    col = lax.broadcasted_iota(jnp.int32, gram.shape, 1)
    diagonal = jnp.sum(jnp.where(row == col, cross, 0.0), axis=0, keepdims=True)
    return jnp.where(row <= col, gram, cross), jnp.broadcast_to(diagonal, (8, gram.shape[1]))


def noise_products(noise_ref, q_ref, pack_ref, nh_ref, nl_ref, qh_ref, ql_ref, nht_ref, nlt_ref, qht_ref, qlt_ref):
    nh, nl = split2(noise_ref[...])
    qh, ql = split2(q_ref[...])
    nh_ref[...] = nh
    nl_ref[...] = nl
    qh_ref[...] = qh
    ql_ref[...] = ql
    for value, out in ((nh, nht_ref), (nl, nlt_ref), (qh, qht_ref), (ql, qlt_ref)):
        out[...] = jnp.transpose(value)
    plain = ((1,), (0,))
    high = dot(jnp.concatenate([nht_ref[...], qht_ref[128:]], axis=0), jnp.concatenate([nh, nl], axis=1), plain)
    low = dot(qlt_ref[128:], nh, plain)
    mixed = high[:128, 128:]
    gram = high[:128, :128] + mixed + jnp.transpose(mixed)
    cross = high[128:, :128] + high[128:, 128:] + low
    pack_ref[0:128], pack_ref[128:] = packed(gram, cross)


def row_products(xh, xl, nht, nlt, qht, qlt):
    plain = ((1,), (0,))
    left = jnp.concatenate([jnp.transpose(xh), nht, qht], axis=0)
    high = dot(left, jnp.concatenate([xh, xl], axis=1), plain)
    low = dot(jnp.concatenate([nlt, qlt], axis=0), xh, plain)
    mixed = high[:128, 128:]
    return (
        high[:128, :128] + mixed + jnp.transpose(mixed),
        high[128:, :128] + high[128:, 128:] + low,
    )


def expand_first(
    core_ref, table_ref, z_ref, inner_ref, outer1_ref, nht_ref, nlt_ref, qht_ref, qlt_ref,
    light_ref, hh_ref, hl_ref, ih_ref, il_ref, gram_ref, rest_ref, first_ref,
):
    c = coefficients(table_ref)
    n = z_ref.shape[2]
    core = core_ref[0]
    rows = (core, 1 - core)
    z = [[z_ref[k, row] for k in range(4)] for row in rows]
    for s, beyond in enumerate((outer1_ref, inner_ref)):
        xa, pa, xb, pb = z[s]
        hop_x = z[1 - s][0] + beyond[0:n] + side(xa)
        hop_p = z[1 - s][1] + beyond[n : 2 * n] + side(pa)
        first_ref[0, s], first_ref[1, s] = forward_light(c[s], xa, pa, xb, hop_x, hop_p)
        first_ref[2, s], first_ref[3, s] = forward_heavy(c[s], xa, xb, pb)
    for s in range(2):
        xa, pa, xb, pb = (first_ref[k, s] for k in range(4))
        for k, (f, second) in enumerate(zip((xb, pb), forward_heavy(c[s], xa, xb, pb))):
            h, l = split2(z[s][2 + k] + f + 0.5 * second)
            hh_ref[cells(rows[s], k, n)] = h
            hl_ref[cells(rows[s], k, n)] = l
    jfar = far_hopping(inner_ref, n)
    for s in range(2):
        xa, pa, xb, pb = (first_ref[k, s] for k in range(4))
        hop_x = first_ref[0, 1 - s] + side(xa)
        hop_p = first_ref[1, 1 - s] + side(pa)
        if s == 1:
            hop_x = hop_x + inner_ref[2 * n : 3 * n] - jfar * z[s][1]
            hop_p = hop_p + inner_ref[3 * n : 4 * n] + jfar * z[s][0]
        second = forward_light(c[s], xa, pa, xb, hop_x, hop_p)
        for k in range(2):
            value = z[s][k] + first_ref[k, s] + 0.5 * second[k]
            if s == 0:
                light_ref[k] = value
            else:
                ih_ref[k * n : (k + 1) * n], il_ref[k * n : (k + 1) * n] = split2(value)
    half = 4 * n
    parts = (nht_ref, nlt_ref, qht_ref, qlt_ref)
    gram, rest = row_products(hh_ref[...], hl_ref[...], *(ref[:, half:] for ref in parts))
    for k in range(2):
        there = cells(1 - core, k, n)
        here = slice(k * n, (k + 1) * n)
        more = row_products(ih_ref[here], il_ref[here], *(ref[:, there] for ref in parts))
        gram = gram + more[0]
        rest = rest + more[1]
    gram_ref[...] = gram
    rest_ref[...] = rest


def expand_last(
    core_ref, table_ref, z_ref, outer2_ref, light_ref, gram_ref, rest_ref, pack_ref,
    nht_ref, nlt_ref, qht_ref, qlt_ref, mine_ref, other_ref, oh_ref, ol_ref, sums_ref,
):
    n = z_ref.shape[2]
    core = core_ref[0]
    jfar = far_hopping(outer2_ref, n)
    far_x = outer2_ref[0:n] - jfar * z_ref[1, core]
    far_p = outer2_ref[n : 2 * n] + jfar * z_ref[0, core]
    j = 0.5 * table_ref[:, 5:6]
    gram, rest = gram_ref[...], rest_ref[...]
    for k, value in enumerate((light_ref[0] - j * far_p, light_ref[1] + j * far_x)):
        h, l = split2(value)
        oh_ref[k * n : (k + 1) * n] = h
        ol_ref[k * n : (k + 1) * n] = l
        there = cells(core, k, n)
        more = row_products(h, l, *(ref[:, there] for ref in (nht_ref, nlt_ref, qht_ref, qlt_ref)))
        gram = gram + more[0]
        rest = rest + more[1]
    sums_ref[0:128], sums_ref[512:520] = packed(gram, rest[128:256])
    sums_ref[128:256] = jnp.transpose(rest[:128])
    sums_ref[256:384] = rest[256:]
    sums_ref[384:512] = pack_ref[0:128]
    sums_ref[520:528] = pack_ref[128:136]
    mine_ref[...] = sums_ref[pl.ds(pl.multiple_of(core * 264, 8), 264)]
    other_ref[...] = sums_ref[pl.ds(pl.multiple_of((1 - core) * 264, 8), 264)]


def factor(
    core_ref, mine_ref, other_ref, r_bar_ref, nh_ref, nl_ref, sh_ref, sl_ref, sums_ref, a_ref, u_ref, inv_ref
):
    size = 256
    tile = 128
    core = core_ref[0]
    sums_ref[pl.ds(pl.multiple_of(core * 264, 8), 264)] = mine_ref[...]
    sums_ref[pl.ds(pl.multiple_of((1 - core) * 264, 8), 264)] = other_ref[...]
    a_ref[0:tile, 0:tile] = sums_ref[0:tile]
    a_ref[0:tile, tile:size] = sums_ref[tile : 2 * tile]
    a_ref[tile:size, tile:size] = sums_ref[3 * tile : 4 * tile]
    row = lax.broadcasted_iota(jnp.int32, (size, size), 0)
    col = lax.broadcasted_iota(jnp.int32, (size, size), 1)
    a_ref[:, size : 2 * size] = jnp.where(row == col, 1.0, 0.0)
    u_ref[...] = jnp.zeros((size, size), f32)
    inv_ref[...] = jnp.zeros((size, size), f32)
    place = lax.broadcasted_iota(jnp.int32, (8, 3 * tile), 0)
    for start in range(0, size, PANEL):
        base = (start // tile) * tile
        lanes = slice(base, base + 3 * tile)
        offset = start - base
        rows = [jnp.broadcast_to(a_ref[start + i : start + i + 1, lanes], (8, 3 * tile)) for i in range(PANEL)]
        s = {}
        for i in range(PANEL):
            for m in range(i, PANEL):
                s[i, m] = jnp.broadcast_to(rows[i][:, offset + m : offset + m + 1], (8, tile))
        done = []
        for i in range(PANEL):
            inverse = pl.reciprocal(s[i, i])
            root = lax.rsqrt(s[i, i])
            root = root * (1.5 - 0.5 * s[i, i] * root * root)
            for k in range(i + 1, PANEL):
                factor_k = s[i, k] * inverse
                for m in range(k, PANEL):
                    s[k, m] = s[k, m] - factor_k * s[i, m]
                rows[k] = rows[k] - jnp.concatenate([factor_k] * 3, axis=1) * rows[i]
            done.append(rows[i] * jnp.concatenate([root] * 3, axis=1))
        groups = []
        for first in range(0, PANEL, 8):
            group = done[first]
            for i in range(1, 8):
                group = jnp.where(place == i, done[first + i], group)
            groups.append(group)
        panel = jnp.concatenate(groups, axis=0)
        stop = start + PANEL
        if base == 0:
            u_ref[start:stop, :] = panel[:, : 2 * tile]
            inv_ref[start:stop, :tile] = panel[:, 2 * tile :]
        else:
            u_ref[start:stop, tile:] = panel[:, :tile]
            inv_ref[start:stop, :] = panel[:, tile:]
        if stop < size:
            h, m, l = split3(panel)
            width = size - base
            left = jnp.concatenate([h, h, m, m, h, l], axis=0)[:, :width]
            right = jnp.concatenate([h, m, h, m, l, h], axis=0)
            change = dot(left, right, ((0,), (0,)))
            a_ref[stop:, lanes] = a_ref[stop:, lanes] - change[stop - base :]
    upper = jnp.where(row <= col, u_ref[...], 0.0)
    inv = jnp.where(row >= col, inv_ref[...], 0.0)
    bar = jnp.where(row <= col, r_bar_ref[...], 0.0)
    corner = jnp.zeros((tile, tile), f32)
    top = jnp.concatenate([sums_ref[0:tile], corner], axis=1)
    bottom = jnp.concatenate([sums_ref[2 * tile : 3 * tile], sums_ref[3 * tile : 4 * tile]], axis=1)
    cross = jnp.concatenate([top, bottom], axis=0)
    diagonal = jnp.concatenate([sums_ref[512:513], sums_ref[520:521]], axis=1)
    cross = jnp.where(row > col, cross, jnp.where(row == col, diagonal, 0.0))

    def product(a, b, contract):
        return lax.dot_general(a, b, ((contract[0], contract[1]), ((), ())), precision=exact, preferred_element_type=f32)

    across = ((1,), (1,))
    middle = product(upper, bar, across) - product(cross, inv, across)
    symmetric = jnp.where(row >= col, middle, 0.0) + jnp.transpose(jnp.where(row > col, middle, 0.0))
    spread = product(inv, product(symmetric, inv, ((1,), (0,))), ((0,), (0,)))
    nh_ref[...], nl_ref[...] = split2(inv)
    sh_ref[...], sl_ref[...] = split2(spread)


def columns(qh, ql, nh, nl, xh, xl, ih, il, sh, sl):
    plain = ((1,), (0,))
    xh = jnp.concatenate([xh, nh], axis=1)
    xl = jnp.concatenate([xl, nl], axis=1)
    high = dot(qh, jnp.concatenate([ih, il], axis=1), plain) + dot(xh, jnp.concatenate([sh, sl], axis=1), plain)
    return high[:, :128] + high[:, 128:] + dot(ql, ih, plain) + dot(xl, sh, plain)


def gradient_outer(
    core_ref, table_ref, qh_ref, ql_ref, nh_ref, nl_ref, oh_ref, ol_ref, ih_ref, il_ref, sh_ref, sl_ref,
    w_ref, outer1_ref,
):
    n = w_ref.shape[1]
    j = table_ref[:, 5:6]
    weights = [ref[:, :128] for ref in (ih_ref, il_ref, sh_ref, sl_ref)]
    for k in range(2):
        there = cells(core_ref[0], k, n)
        here = slice(k * n, (k + 1) * n)
        parts = [ref[there] for ref in (qh_ref, ql_ref, nh_ref, nl_ref)] + [oh_ref[here], ol_ref[here]]
        w = columns(*parts, *weights)
        w_ref[k] = w
        outer1_ref[here] = j * w


def gradient_rest(
    core_ref, table_ref, outer_ref, outer1_ref, qh_ref, ql_ref, nh_ref, nl_ref, lh_ref, ll_ref, hh_ref, hl_ref,
    ih_ref, il_ref, sh_ref, sl_ref, light_ref, heavy_ref, outer2_ref, inner_ref,
):
    c = coefficients(table_ref)
    n = outer_ref.shape[1]
    core = core_ref[0]
    weights = [ref[:, :128] for ref in (ih_ref, il_ref, sh_ref, sl_ref)]
    left = (qh_ref, ql_ref, nh_ref, nl_ref)
    for k in range(2):
        there = cells(1 - core, k, n)
        here = slice(k * n, (k + 1) * n)
        w = columns(*[ref[there] for ref in left], lh_ref[here], ll_ref[here], *weights)
        light_ref[k] = w
        inner_ref[here] = c[1][5] * w
    for k in (1, 0):
        for s, row in enumerate((core, 1 - core)):
            there = cells(row, 2 + k, n)
            here = cells(row, k, n)
            heavy_ref[k, s] = columns(*[ref[there] for ref in left], hh_ref[here], hl_ref[here], *weights)
    own = (outer1_ref, inner_ref)
    for s, w, out, base in ((0, outer_ref, outer2_ref, 0), (1, light_ref, inner_ref, 2 * n)):
        hop_x = own[1 - s][0:n] + side(own[s][0:n])
        hop_p = own[1 - s][n : 2 * n] + side(own[s][n : 2 * n])
        bx, bp = backward_light(c[s], w[0], w[1], heavy_ref[1, s], hop_x, hop_p)
        out[base : base + n] = c[s][5] * bx
        out[base + n : base + 2 * n] = c[s][5] * bp


def gradient_noise(
    core_ref, qh_ref, ql_ref, nh_ref, nl_ref, oh_ref, ol_ref, lh_ref, ll_ref, hh_ref, hl_ref,
    ih_ref, il_ref, sh_ref, sl_ref, out_ref,
):
    n = out_ref.shape[2]
    core = core_ref[0]
    weights = [ref[:, 128:] for ref in (ih_ref, il_ref, sh_ref, sl_ref)]
    for k in range(4):
        for s, row in enumerate((core, 1 - core)):
            there = cells(row, k, n)
            if k < 2:
                here = slice(k * n, (k + 1) * n)
                x = (oh_ref[here], ol_ref[here]) if s == 0 else (lh_ref[here], ll_ref[here])
            else:
                here = cells(row, k - 2, n)
                x = (hh_ref[here], hl_ref[here])
            out_ref[k, row] = columns(*[ref[there] for ref in (qh_ref, ql_ref, nh_ref, nl_ref)], *x, *weights)


def contract_first(
    table_ref, outer_ref, light_ref, heavy_ref, own1_ref, own_ref, outer1_ref, inner_ref, fouter2_ref, finner_ref,
    out_light_ref, out_heavy_ref, first_ref,
):
    c = coefficients(table_ref)
    n = outer_ref.shape[1]
    w = [
        (outer_ref[0], outer_ref[1], heavy_ref[0, 0], heavy_ref[1, 0]),
        (light_ref[0], light_ref[1], heavy_ref[0, 1], heavy_ref[1, 1]),
    ]
    own = [(ref[0:n], ref[n : 2 * n]) for ref in (own1_ref, own_ref)]
    for s, far in enumerate((outer1_ref, inner_ref)):
        xa, pa, xb, pb = w[s]
        hop_x = own[1 - s][0] + far[0:n] + side(own[s][0])
        hop_p = own[1 - s][1] + far[n : 2 * n] + side(own[s][1])
        first_ref[0, s], first_ref[1, s] = backward_light(c[s], xa, pa, pb, hop_x, hop_p)
        first_ref[2, s], first_ref[3, s] = backward_heavy(c[s], pa, xb, pb)
    for s, fref in enumerate((fouter2_ref, finner_ref)):
        xa, pa, xb, pb = (first_ref[k, s] for k in range(4))
        jfar = far_hopping(fref, n)
        j, jother = c[s][5], c[1 - s][5]
        hop_x = jother * first_ref[0, 1 - s] + jfar * own[s][1] + side(j * xa)
        hop_p = jother * first_ref[1, 1 - s] - jfar * own[s][0] + side(j * pa)
        if s == 1:
            hop_x = hop_x + inner_ref[2 * n : 3 * n]
            hop_p = hop_p + inner_ref[3 * n : 4 * n]
        light = backward_light(c[s], xa, pa, pb, hop_x, hop_p)
        heavy = backward_heavy(c[s], pa, xb, pb)
        for k in range(2):
            out_light_ref[k, s] = w[s][k] + first_ref[k, s] + 0.5 * light[k]
            out_heavy_ref[k, s] = w[s][2 + k] + first_ref[2 + k, s] + 0.5 * heavy[k]


def contract_last(core_ref, light_ref, heavy_ref, outer2_ref, out_ref):
    n = out_ref.shape[2]
    core = core_ref[0]
    out_ref[0, core] = light_ref[0, 0] + 0.5 * outer2_ref[n : 2 * n]
    out_ref[1, core] = light_ref[1, 0] - 0.5 * outer2_ref[0:n]
    for k in range(2):
        out_ref[k, 1 - core] = light_ref[k, 1]
        out_ref[2 + k, core] = heavy_ref[k, 0]
        out_ref[2 + k, 1 - core] = heavy_ref[k, 1]


def swap_inner(message):
    count = lax.axis_size("row")
    return lax.ppermute(message, "row", [(i, i ^ 1) for i in range(count)])


def swap_outer(message):
    count = lax.axis_size("row")
    pairs = [(i, i + 1) for i in range(1, count - 1, 2)]
    return lax.ppermute(message, "row", pairs + [(j, i) for i, j in pairs])


def sum_over_rows(mine, other):
    count = lax.axis_size("row")
    bits = count.bit_length() - 1
    swap = [(i, i ^ 1) for i in range(count)]
    mine = mine + lax.ppermute(other, "row", swap)
    for step in range(bits - 1):
        turn = [1 + step, 1 + (step + 1) % (bits - 1)]
        mine = mine + lax.ppermute(mine, "row", [(i, i ^ (1 << turn[i & 1])) for i in range(count)])
    return mine, lax.ppermute(mine, "row", swap)


def on_device(cell_coeffs, z_factor, noise_cols, q_bar, r_bar):
    quads, lattice, n, rank = z_factor.shape
    flat = quads * lattice * n
    coeffs = cell_coeffs
    core = (lax.axis_index("row") & 1).reshape(1)
    noise = noise_cols.reshape(flat, -1)
    bar = q_bar.reshape(flat, -1)
    shape = jax.ShapeDtypeStruct
    hops = shape((2 * n, rank), f32)
    rim = shape((2 * n + 8, rank), f32)
    table = shape((n, 16), f32)
    outer1, outer2, inner, table = call(
        forward_rim, (hops, rim, shape((4 * n + 8, rank), f32), table), 10**6, 3 * 10**6,
        [
            pltpu.VMEM(cell_coeffs.shape, f32),
            pltpu.VMEM((2, 3, n, rank), f32),
            pltpu.SemaphoreType.DMA((3,)),
        ],
        scalar=True, far=True,
    )(core, coeffs, z_factor)
    outer1, outer2, inner = swap_outer(outer1), swap_outer(outer2), swap_inner(inner)
    wide, tall = shape((flat, 256), bf16), shape((flat, 128), bf16)
    wide_t, tall_t = shape((256, flat), bf16), shape((128, flat), bf16)
    work = 2 * flat * 128 * 128
    pack, nh, nl, qh, ql, nht, nlt, qht, qlt = call(
        noise_products, (shape((136, 128), f32), tall, tall, wide, wide, tall_t, tall_t, wide_t, wide_t),
        work * 5, 9 * 10**6,
    )(noise, bar)
    transposed = (nht, nlt, qht, qlt)
    half, quarter = shape((flat // 2, 128), bf16), shape((flat // 4, 128), bf16)
    single, pair = shape((2, n, rank), f32), shape((2, lattice, n, rank), f32)
    light, hh, hl, lh, ll, gram, rest = call(
        expand_first,
        (single, half, half, quarter, quarter, shape((128, 128), f32), shape((384, 128), f32)),
        work * 8, 9 * 10**6, [pltpu.VMEM(z_factor.shape, f32)], scalar=True,
    )(core, table, z_factor, inner, outer1, *transposed)
    part = shape((264, 128), f32)
    mine, other, oh, ol = call(
        expand_last, (part, part, quarter, quarter), work * 3, 5 * 10**6, [pltpu.VMEM((528, 128), f32)], scalar=True
    )(core, table, z_factor, outer2, light, gram, rest, pack, *transposed)
    mine, other = sum_over_rows(mine, other)
    square = shape((256, 256), bf16)
    weights = call(
        factor, (square,) * 4, 10**9, 10**6,
        [
            pltpu.VMEM((528, 128), f32),
            pltpu.VMEM((256, 512), f32),
            pltpu.VMEM((256, 256), f32),
            pltpu.VMEM((256, 256), f32),
        ],
        scalar=True,
    )(core, mine, other, r_bar)
    left = (qh, ql, nh, nl)
    w_outer, own1 = call(gradient_outer, (single, hops), work * 3, 3 * 10**6, scalar=True)(
        core, table, *left, oh, ol, *weights
    )
    back1 = swap_outer(own1)
    w_inner, w_heavy, own2, own = call(
        gradient_rest, (single, pair, hops, shape((4 * n, rank), f32)), 10**10, 6 * 10**6, scalar=True
    )(core, table, w_outer, own1, *left, lh, ll, hh, hl, *weights)
    back2, back = swap_outer(own2), swap_inner(own)
    noise_grad = call(gradient_noise, shape(noise_cols.shape, f32), 0, 0, scalar=True)(
        core, *left, oh, ol, lh, ll, hh, hl, *weights
    )
    out_light, out_heavy = call(contract_first, (pair, pair), 10**7, 6 * 10**6, [pltpu.VMEM(z_factor.shape, f32)])(
        table, w_outer, w_inner, w_heavy, own1, own, back1, back, outer2, inner
    )
    z_grad = call(contract_last, shape(z_factor.shape, f32), 10**6, 6 * 10**6, scalar=True)(
        core, out_light, out_heavy, back2
    )
    return z_grad, noise_grad


def solution(mesh):
    return jax.shard_map(
        on_device,
        mesh=mesh,
        in_specs=(
            P(None, "row", None),
            P(None, ("grp", "row"), None, None),
            P(None, ("grp", "row"), None, None),
            P(None, ("grp", "row"), None, None),
            P("grp", None),
        ),
        out_specs=(P(None, ("grp", "row"), None, None), P(None, ("grp", "row"), None, None)),
        check_vma=False,
    )
```

```python
import jax
import jax.numpy as jnp
from jax import lax
from jax.experimental import pallas as pl
from jax.experimental.pallas import tpu as pltpu
from jax.sharding import PartitionSpec as P

rate_scales = (0.4, 0.4, 0.1, 0.2, 0.1, 0.1)
exact = lax.Precision.HIGHEST
f32 = jnp.float32
bf16 = jnp.bfloat16
VMEM = pl.BlockSpec(memory_space=pltpu.VMEM)
LIMIT = 24 * 1024 * 1024
FAR_LIMIT = 63 * 1024 * 1024
PANEL = 16


def call(kernel, outs, flops, moved, scratch=(), scalar=False, far=False):
    def run(*args):
        specs = [pl.BlockSpec(memory_space=pltpu.HBM) if far else pl.BlockSpec() for _ in args]
        if scalar:
            specs[0] = pl.BlockSpec(memory_space=pltpu.SMEM)
        return pl.pallas_call(
            kernel,
            out_shape=outs,
            in_specs=specs,
            scratch_shapes=list(scratch),
            compiler_params=pltpu.CompilerParams(vmem_limit_bytes=FAR_LIMIT if far else LIMIT),
            cost_estimate=pl.CostEstimate(flops=flops, bytes_accessed=moved, transcendentals=0),
        )(*args)

    return run


def split2(value):
    high = value.astype(bf16)
    low = (value - high.astype(f32)).astype(bf16)
    return high, low


def split3(value):
    high = value.astype(bf16)
    rest = value - high.astype(f32)
    mid = rest.astype(bf16)
    low = (rest - mid.astype(f32)).astype(bf16)
    return high, mid, low


def dot(a, b, contract):
    return lax.dot_general(a, b, ((contract[0], contract[1]), ((), ())), preferred_element_type=f32)


def coefficients(table_ref):
    return [[table_ref[:, 6 * s + k : 6 * s + k + 1] for k in range(6)] for s in range(2)]


def side(v):
    n = v.shape[0]
    place = lax.broadcasted_iota(jnp.int32, v.shape, 0)
    left = jnp.where(place == 0, 0.0, pltpu.roll(v, 1, 0))
    right = jnp.where(place == n - 1, 0.0, pltpu.roll(v, n - 1, 0))
    return left + right


def forward_light(c, xa, pa, xb, hop_x, hop_p):
    d, w, g, l, m, j = c
    return (
        -0.5 * l * xa - d * pa - j * hop_p,
        d * xa - 0.5 * l * pa - 2.0 * g * xb + j * hop_x,
    )


def forward_heavy(c, xa, xb, pb):
    d, w, g, l, m, j = c
    return w * pb, -w * xb - 0.5 * m * pb - 2.0 * g * xa


def backward_light(c, xa, pa, pb, hop_x, hop_p):
    d, w, g, l, m, j = c
    return (
        -0.5 * l * xa + d * pa - 2.0 * g * pb + hop_p,
        -d * xa - 0.5 * l * pa - hop_x,
    )


def backward_heavy(c, pa, xb, pb):
    d, w, g, l, m, j = c
    return -2.0 * g * pa - w * pb, w * xb - 0.5 * m * pb


def forward_rim(core_ref, coeff_hbm, z_hbm, outer1_ref, outer2_ref, inner_ref, table_ref, coeff_ref, z_ref, sems):
    n = z_ref.shape[2]
    core = core_ref[0]
    copies = [
        pltpu.make_async_copy(z_hbm.at[0:3, core], z_ref.at[0], sems.at[0]),
        pltpu.make_async_copy(z_hbm.at[0:3, 1 - core], z_ref.at[1], sems.at[1]),
        pltpu.make_async_copy(coeff_hbm, coeff_ref, sems.at[2]),
    ]
    for copy in copies:
        copy.start()
    for copy in copies:
        copy.wait()
    cols = jnp.transpose(jnp.concatenate([coeff_ref[k] for k in range(6)], axis=0))
    swapped = core == 1
    both = []
    for s in range(2):
        for k in range(6):
            column = jnp.where(swapped, cols[:, 2 * k + 1 - s : 2 * k + 2 - s], cols[:, 2 * k + s : 2 * k + s + 1])
            both.append(column * rate_scales[k])
    for place, column in enumerate(both):
        table_ref[:, place : place + 1] = column
    far = []
    for s in range(2):
        xa, pa, xb = z_ref[s, 0], z_ref[s, 1], z_ref[s, 2]
        hop_x = z_ref[1 - s, 0] + side(xa)
        hop_p = z_ref[1 - s, 1] + side(pa)
        far.append(forward_light(both[6 * s : 6 * s + 6], xa, pa, xb, hop_x, hop_p))
    outer1_ref[0:n] = z_ref[0, 0]
    outer1_ref[n : 2 * n] = z_ref[0, 1]
    inner_ref[0:n] = z_ref[1, 0]
    inner_ref[n : 2 * n] = z_ref[1, 1]
    for s, out, base in ((0, outer2_ref, 0), (1, inner_ref, 2 * n)):
        out[base : base + n], out[base + n : base + 2 * n] = far[s]
        hopping = jnp.where(swapped, coeff_ref[5, 1 - s : 2 - s, :], coeff_ref[5, s : s + 1, :]) * rate_scales[5]
        pieces = [hopping[:, k * 128 : (k + 1) * 128] for k in range(n // 128)]
        pieces.append(jnp.zeros((8 - n // 128, 128), f32))
        out[base + 2 * n :] = jnp.concatenate(pieces, axis=0)


def far_hopping(recv_ref, n):
    size = recv_ref.shape[0]
    tail = jnp.transpose(recv_ref[size - 8 : size])
    return jnp.concatenate([tail[:, k : k + 1] for k in range(n // 128)], axis=0)


def cells(row, k, n):
    return pl.ds(pl.multiple_of((2 * k + row) * n, 128), n)


def packed(gram, cross):
    row = lax.broadcasted_iota(jnp.int32, gram.shape, 0)
    col = lax.broadcasted_iota(jnp.int32, gram.shape, 1)
    diagonal = jnp.sum(jnp.where(row == col, cross, 0.0), axis=0, keepdims=True)
    return jnp.where(row <= col, gram, cross), jnp.broadcast_to(diagonal, (8, gram.shape[1]))


def noise_products(noise_ref, q_ref, pack_ref, nh_ref, nl_ref, qh_ref, ql_ref, nht_ref, nlt_ref, qht_ref, qlt_ref):
    nh, nl = split2(noise_ref[...])
    qh, ql = split2(q_ref[...])
    nh_ref[...] = nh
    nl_ref[...] = nl
    qh_ref[...] = qh
    ql_ref[...] = ql
    for value, out in ((nh, nht_ref), (nl, nlt_ref), (qh, qht_ref), (ql, qlt_ref)):
        out[...] = jnp.transpose(value)
    plain = ((1,), (0,))
    high = dot(jnp.concatenate([nht_ref[...], qht_ref[128:]], axis=0), jnp.concatenate([nh, nl], axis=1), plain)
    low = dot(qlt_ref[128:], nh, plain)
    mixed = high[:128, 128:]
    gram = high[:128, :128] + mixed + jnp.transpose(mixed)
    cross = high[128:, :128] + high[128:, 128:] + low
    pack_ref[0:128], pack_ref[128:] = packed(gram, cross)


def row_products(xh, xl, nht, nlt, qht, qlt):
    plain = ((1,), (0,))
    left = jnp.concatenate([jnp.transpose(xh), nht, qht], axis=0)
    high = dot(left, jnp.concatenate([xh, xl], axis=1), plain)
    low = dot(jnp.concatenate([nlt, qlt], axis=0), xh, plain)
    mixed = high[:128, 128:]
    return (
        high[:128, :128] + mixed + jnp.transpose(mixed),
        high[128:, :128] + high[128:, 128:] + low,
    )


def expand_first(
    core_ref, table_ref, z_ref, inner_ref, outer1_ref, nht_ref, nlt_ref, qht_ref, qlt_ref,
    light_ref, hh_ref, hl_ref, ih_ref, il_ref, gram_ref, rest_ref, first_ref,
):
    c = coefficients(table_ref)
    n = z_ref.shape[2]
    core = core_ref[0]
    rows = (core, 1 - core)
    z = [[z_ref[k, row] for k in range(4)] for row in rows]
    for s, beyond in enumerate((outer1_ref, inner_ref)):
        xa, pa, xb, pb = z[s]
        hop_x = z[1 - s][0] + beyond[0:n] + side(xa)
        hop_p = z[1 - s][1] + beyond[n : 2 * n] + side(pa)
        first_ref[0, s], first_ref[1, s] = forward_light(c[s], xa, pa, xb, hop_x, hop_p)
        first_ref[2, s], first_ref[3, s] = forward_heavy(c[s], xa, xb, pb)
    for s in range(2):
        xa, pa, xb, pb = (first_ref[k, s] for k in range(4))
        for k, (f, second) in enumerate(zip((xb, pb), forward_heavy(c[s], xa, xb, pb))):
            h, l = split2(z[s][2 + k] + f + 0.5 * second)
            hh_ref[cells(rows[s], k, n)] = h
            hl_ref[cells(rows[s], k, n)] = l
    jfar = far_hopping(inner_ref, n)
    for s in range(2):
        xa, pa, xb, pb = (first_ref[k, s] for k in range(4))
        hop_x = first_ref[0, 1 - s] + side(xa)
        hop_p = first_ref[1, 1 - s] + side(pa)
        if s == 1:
            hop_x = hop_x + inner_ref[2 * n : 3 * n] - jfar * z[s][1]
            hop_p = hop_p + inner_ref[3 * n : 4 * n] + jfar * z[s][0]
        second = forward_light(c[s], xa, pa, xb, hop_x, hop_p)
        for k in range(2):
            value = z[s][k] + first_ref[k, s] + 0.5 * second[k]
            if s == 0:
                light_ref[k] = value
            else:
                ih_ref[k * n : (k + 1) * n], il_ref[k * n : (k + 1) * n] = split2(value)
    half = 4 * n
    parts = (nht_ref, nlt_ref, qht_ref, qlt_ref)
    gram, rest = row_products(hh_ref[...], hl_ref[...], *(ref[:, half:] for ref in parts))
    for k in range(2):
        there = cells(1 - core, k, n)
        here = slice(k * n, (k + 1) * n)
        more = row_products(ih_ref[here], il_ref[here], *(ref[:, there] for ref in parts))
        gram = gram + more[0]
        rest = rest + more[1]
    gram_ref[...] = gram
    rest_ref[...] = rest


def expand_last(
    core_ref, table_ref, z_ref, outer2_ref, light_ref, gram_ref, rest_ref, pack_ref,
    nht_ref, nlt_ref, qht_ref, qlt_ref, mine_ref, other_ref, oh_ref, ol_ref, sums_ref,
):
    n = z_ref.shape[2]
    core = core_ref[0]
    jfar = far_hopping(outer2_ref, n)
    far_x = outer2_ref[0:n] - jfar * z_ref[1, core]
    far_p = outer2_ref[n : 2 * n] + jfar * z_ref[0, core]
    j = 0.5 * table_ref[:, 5:6]
    gram, rest = gram_ref[...], rest_ref[...]
    for k, value in enumerate((light_ref[0] - j * far_p, light_ref[1] + j * far_x)):
        h, l = split2(value)
        oh_ref[k * n : (k + 1) * n] = h
        ol_ref[k * n : (k + 1) * n] = l
        there = cells(core, k, n)
        more = row_products(h, l, *(ref[:, there] for ref in (nht_ref, nlt_ref, qht_ref, qlt_ref)))
        gram = gram + more[0]
        rest = rest + more[1]
    sums_ref[0:128], sums_ref[512:520] = packed(gram, rest[128:256])
    sums_ref[128:256] = jnp.transpose(rest[:128])
    sums_ref[256:384] = rest[256:]
    sums_ref[384:512] = pack_ref[0:128]
    sums_ref[520:528] = pack_ref[128:136]
    mine_ref[...] = sums_ref[pl.ds(pl.multiple_of(core * 264, 8), 264)]
    other_ref[...] = sums_ref[pl.ds(pl.multiple_of((1 - core) * 264, 8), 264)]


def factor(
    core_ref, mine_ref, other_ref, r_bar_ref, nh_ref, nl_ref, sh_ref, sl_ref, sums_ref, a_ref, u_ref, inv_ref
):
    size = 256
    tile = 128
    core = core_ref[0]
    sums_ref[pl.ds(pl.multiple_of(core * 264, 8), 264)] = mine_ref[...]
    sums_ref[pl.ds(pl.multiple_of((1 - core) * 264, 8), 264)] = other_ref[...]
    a_ref[0:tile, 0:tile] = sums_ref[0:tile]
    a_ref[0:tile, tile:size] = sums_ref[tile : 2 * tile]
    a_ref[tile:size, tile:size] = sums_ref[3 * tile : 4 * tile]
    row = lax.broadcasted_iota(jnp.int32, (size, size), 0)
    col = lax.broadcasted_iota(jnp.int32, (size, size), 1)
    a_ref[:, size : 2 * size] = jnp.where(row == col, 1.0, 0.0)
    u_ref[...] = jnp.zeros((size, size), f32)
    inv_ref[...] = jnp.zeros((size, size), f32)
    place = lax.broadcasted_iota(jnp.int32, (8, 3 * tile), 0)
    for start in range(0, size, PANEL):
        base = (start // tile) * tile
        lanes = slice(base, base + 3 * tile)
        offset = start - base
        rows = [jnp.broadcast_to(a_ref[start + i : start + i + 1, lanes], (8, 3 * tile)) for i in range(PANEL)]
        s = {}
        for i in range(PANEL):
            for m in range(i, PANEL):
                s[i, m] = jnp.broadcast_to(rows[i][:, offset + m : offset + m + 1], (8, tile))
        done = []
        for i in range(PANEL):
            inverse = pl.reciprocal(s[i, i])
            root = lax.rsqrt(s[i, i])
            root = root * (1.5 - 0.5 * s[i, i] * root * root)
            for k in range(i + 1, PANEL):
                factor_k = s[i, k] * inverse
                for m in range(k, PANEL):
                    s[k, m] = s[k, m] - factor_k * s[i, m]
                rows[k] = rows[k] - jnp.concatenate([factor_k] * 3, axis=1) * rows[i]
            done.append(rows[i] * jnp.concatenate([root] * 3, axis=1))
        groups = []
        for first in range(0, PANEL, 8):
            group = done[first]
            for i in range(1, 8):
                group = jnp.where(place == i, done[first + i], group)
            groups.append(group)
        panel = jnp.concatenate(groups, axis=0)
        stop = start + PANEL
        if base == 0:
            u_ref[start:stop, :] = panel[:, : 2 * tile]
            inv_ref[start:stop, :tile] = panel[:, 2 * tile :]
        else:
            u_ref[start:stop, tile:] = panel[:, :tile]
            inv_ref[start:stop, :] = panel[:, tile:]
        if stop < size:
            h, m, l = split3(panel)
            width = size - base
            left = jnp.concatenate([h, h, m, m, h, l], axis=0)[:, :width]
            right = jnp.concatenate([h, m, h, m, l, h], axis=0)
            change = dot(left, right, ((0,), (0,)))
            a_ref[stop:, lanes] = a_ref[stop:, lanes] - change[stop - base :]
    upper = jnp.where(row <= col, u_ref[...], 0.0)
    inv = jnp.where(row >= col, inv_ref[...], 0.0)
    bar = jnp.where(row <= col, r_bar_ref[...], 0.0)
    corner = jnp.zeros((tile, tile), f32)
    top = jnp.concatenate([sums_ref[0:tile], corner], axis=1)
    bottom = jnp.concatenate([sums_ref[2 * tile : 3 * tile], sums_ref[3 * tile : 4 * tile]], axis=1)
    cross = jnp.concatenate([top, bottom], axis=0)
    diagonal = jnp.concatenate([sums_ref[512:513], sums_ref[520:521]], axis=1)
    cross = jnp.where(row > col, cross, jnp.where(row == col, diagonal, 0.0))

    def product(a, b, contract):
        return lax.dot_general(a, b, ((contract[0], contract[1]), ((), ())), precision=exact, preferred_element_type=f32)

    across = ((1,), (1,))
    middle = product(upper, bar, across) - product(cross, inv, across)
    symmetric = jnp.where(row >= col, middle, 0.0) + jnp.transpose(jnp.where(row > col, middle, 0.0))
    spread = product(inv, product(symmetric, inv, ((1,), (0,))), ((0,), (0,)))
    nh_ref[...], nl_ref[...] = split2(inv)
    sh_ref[...], sl_ref[...] = split2(spread)


def columns(qh, ql, nh, nl, xh, xl, ih, il, sh, sl):
    plain = ((1,), (0,))
    xh = jnp.concatenate([xh, nh], axis=1)
    xl = jnp.concatenate([xl, nl], axis=1)
    high = dot(qh, jnp.concatenate([ih, il], axis=1), plain) + dot(xh, jnp.concatenate([sh, sl], axis=1), plain)
    return high[:, :128] + high[:, 128:] + dot(ql, ih, plain) + dot(xl, sh, plain)


def gradient_outer(
    core_ref, table_ref, qh_ref, ql_ref, nh_ref, nl_ref, oh_ref, ol_ref, ih_ref, il_ref, sh_ref, sl_ref,
    w_ref, outer1_ref,
):
    n = w_ref.shape[1]
    j = table_ref[:, 5:6]
    weights = [ref[:, :128] for ref in (ih_ref, il_ref, sh_ref, sl_ref)]
    for k in range(2):
        there = cells(core_ref[0], k, n)
        here = slice(k * n, (k + 1) * n)
        parts = [ref[there] for ref in (qh_ref, ql_ref, nh_ref, nl_ref)] + [oh_ref[here], ol_ref[here]]
        w = columns(*parts, *weights)
        w_ref[k] = w
        outer1_ref[here] = j * w


def gradient_rest(
    core_ref, table_ref, outer_ref, outer1_ref, qh_ref, ql_ref, nh_ref, nl_ref, lh_ref, ll_ref, hh_ref, hl_ref,
    ih_ref, il_ref, sh_ref, sl_ref, light_ref, heavy_ref, outer2_ref, inner_ref,
):
    c = coefficients(table_ref)
    n = outer_ref.shape[1]
    core = core_ref[0]
    weights = [ref[:, :128] for ref in (ih_ref, il_ref, sh_ref, sl_ref)]
    left = (qh_ref, ql_ref, nh_ref, nl_ref)
    for k in range(2):
        there = cells(1 - core, k, n)
        here = slice(k * n, (k + 1) * n)
        w = columns(*[ref[there] for ref in left], lh_ref[here], ll_ref[here], *weights)
        light_ref[k] = w
        inner_ref[here] = c[1][5] * w
    for k in (1, 0):
        for s, row in enumerate((core, 1 - core)):
            there = cells(row, 2 + k, n)
            here = cells(row, k, n)
            heavy_ref[k, s] = columns(*[ref[there] for ref in left], hh_ref[here], hl_ref[here], *weights)
    own = (outer1_ref, inner_ref)
    for s, w, out, base in ((0, outer_ref, outer2_ref, 0), (1, light_ref, inner_ref, 2 * n)):
        hop_x = own[1 - s][0:n] + side(own[s][0:n])
        hop_p = own[1 - s][n : 2 * n] + side(own[s][n : 2 * n])
        bx, bp = backward_light(c[s], w[0], w[1], heavy_ref[1, s], hop_x, hop_p)
        out[base : base + n] = c[s][5] * bx
        out[base + n : base + 2 * n] = c[s][5] * bp


def gradient_noise(
    core_ref, qh_ref, ql_ref, nh_ref, nl_ref, oh_ref, ol_ref, lh_ref, ll_ref, hh_ref, hl_ref,
    ih_ref, il_ref, sh_ref, sl_ref, out_ref,
):
    n = out_ref.shape[2]
    core = core_ref[0]
    weights = [ref[:, 128:] for ref in (ih_ref, il_ref, sh_ref, sl_ref)]
    for k in range(4):
        for s, row in enumerate((core, 1 - core)):
            there = cells(row, k, n)
            if k < 2:
                here = slice(k * n, (k + 1) * n)
                x = (oh_ref[here], ol_ref[here]) if s == 0 else (lh_ref[here], ll_ref[here])
            else:
                here = cells(row, k - 2, n)
                x = (hh_ref[here], hl_ref[here])
            out_ref[k, row] = columns(*[ref[there] for ref in (qh_ref, ql_ref, nh_ref, nl_ref)], *x, *weights)


def contract_first(
    table_ref, outer_ref, light_ref, heavy_ref, own1_ref, own_ref, outer1_ref, inner_ref, fouter2_ref, finner_ref,
    out_light_ref, out_heavy_ref, first_ref,
):
    c = coefficients(table_ref)
    n = outer_ref.shape[1]
    w = [
        (outer_ref[0], outer_ref[1], heavy_ref[0, 0], heavy_ref[1, 0]),
        (light_ref[0], light_ref[1], heavy_ref[0, 1], heavy_ref[1, 1]),
    ]
    own = [(ref[0:n], ref[n : 2 * n]) for ref in (own1_ref, own_ref)]
    for s, far in enumerate((outer1_ref, inner_ref)):
        xa, pa, xb, pb = w[s]
        hop_x = own[1 - s][0] + far[0:n] + side(own[s][0])
        hop_p = own[1 - s][1] + far[n : 2 * n] + side(own[s][1])
        first_ref[0, s], first_ref[1, s] = backward_light(c[s], xa, pa, pb, hop_x, hop_p)
        first_ref[2, s], first_ref[3, s] = backward_heavy(c[s], pa, xb, pb)
    for s, fref in enumerate((fouter2_ref, finner_ref)):
        xa, pa, xb, pb = (first_ref[k, s] for k in range(4))
        jfar = far_hopping(fref, n)
        j, jother = c[s][5], c[1 - s][5]
        hop_x = jother * first_ref[0, 1 - s] + jfar * own[s][1] + side(j * xa)
        hop_p = jother * first_ref[1, 1 - s] - jfar * own[s][0] + side(j * pa)
        if s == 1:
            hop_x = hop_x + inner_ref[2 * n : 3 * n]
            hop_p = hop_p + inner_ref[3 * n : 4 * n]
        light = backward_light(c[s], xa, pa, pb, hop_x, hop_p)
        heavy = backward_heavy(c[s], pa, xb, pb)
        for k in range(2):
            out_light_ref[k, s] = w[s][k] + first_ref[k, s] + 0.5 * light[k]
            out_heavy_ref[k, s] = w[s][2 + k] + first_ref[2 + k, s] + 0.5 * heavy[k]


def contract_last(core_ref, light_ref, heavy_ref, outer2_ref, out_ref):
    n = out_ref.shape[2]
    core = core_ref[0]
    out_ref[0, core] = light_ref[0, 0] + 0.5 * outer2_ref[n : 2 * n]
    out_ref[1, core] = light_ref[1, 0] - 0.5 * outer2_ref[0:n]
    for k in range(2):
        out_ref[k, 1 - core] = light_ref[k, 1]
        out_ref[2 + k, core] = heavy_ref[k, 0]
        out_ref[2 + k, 1 - core] = heavy_ref[k, 1]


def swap_inner(message):
    count = lax.axis_size("row")
    return lax.ppermute(message, "row", [(i, i ^ 1) for i in range(count)])


def swap_outer(message):
    count = lax.axis_size("row")
    pairs = [(i, i + 2) for i in range(1, count - 2, 2)] + [(i, i - 2) for i in range(2, count, 2)]
    return swap_inner(lax.ppermute(message, "row", pairs))


def sum_over_rows(mine, other):
    count = lax.axis_size("row")
    bits = count.bit_length() - 1
    swap = [(i, i ^ 1) for i in range(count)]
    mine = mine + lax.ppermute(other, "row", swap)
    for step in range(bits - 1):
        turn = [1 + step, 1 + (step + 1) % (bits - 1)]
        mine = mine + lax.ppermute(mine, "row", [(i, i ^ (1 << turn[i & 1])) for i in range(count)])
    return mine, lax.ppermute(mine, "row", swap)


def on_device(cell_coeffs, z_factor, noise_cols, q_bar, r_bar):
    quads, lattice, n, rank = z_factor.shape
    flat = quads * lattice * n
    coeffs = cell_coeffs
    core = (lax.axis_index("row") & 1).reshape(1)
    noise = noise_cols.reshape(flat, -1)
    bar = q_bar.reshape(flat, -1)
    shape = jax.ShapeDtypeStruct
    hops = shape((2 * n, rank), f32)
    rim = shape((2 * n + 8, rank), f32)
    table = shape((n, 16), f32)
    outer1, outer2, inner, table = call(
        forward_rim, (hops, rim, shape((4 * n + 8, rank), f32), table), 10**6, 3 * 10**6,
        [
            pltpu.VMEM(cell_coeffs.shape, f32),
            pltpu.VMEM((2, 3, n, rank), f32),
            pltpu.SemaphoreType.DMA((3,)),
        ],
        scalar=True, far=True,
    )(core, coeffs, z_factor)
    outer1, outer2, inner = swap_outer(outer1), swap_outer(outer2), swap_inner(inner)
    wide, tall = shape((flat, 256), bf16), shape((flat, 128), bf16)
    wide_t, tall_t = shape((256, flat), bf16), shape((128, flat), bf16)
    work = 2 * flat * 128 * 128
    pack, nh, nl, qh, ql, nht, nlt, qht, qlt = call(
        noise_products, (shape((136, 128), f32), tall, tall, wide, wide, tall_t, tall_t, wide_t, wide_t),
        work * 5, 9 * 10**6,
    )(noise, bar)
    transposed = (nht, nlt, qht, qlt)
    half, quarter = shape((flat // 2, 128), bf16), shape((flat // 4, 128), bf16)
    single, pair = shape((2, n, rank), f32), shape((2, lattice, n, rank), f32)
    light, hh, hl, lh, ll, gram, rest = call(
        expand_first,
        (single, half, half, quarter, quarter, shape((128, 128), f32), shape((384, 128), f32)),
        work * 8, 9 * 10**6, [pltpu.VMEM(z_factor.shape, f32)], scalar=True,
    )(core, table, z_factor, inner, outer1, *transposed)
    part = shape((264, 128), f32)
    mine, other, oh, ol = call(
        expand_last, (part, part, quarter, quarter), work * 3, 5 * 10**6, [pltpu.VMEM((528, 128), f32)], scalar=True
    )(core, table, z_factor, outer2, light, gram, rest, pack, *transposed)
    mine, other = sum_over_rows(mine, other)
    square = shape((256, 256), bf16)
    weights = call(
        factor, (square,) * 4, 10**9, 10**6,
        [
            pltpu.VMEM((528, 128), f32),
            pltpu.VMEM((256, 512), f32),
            pltpu.VMEM((256, 256), f32),
            pltpu.VMEM((256, 256), f32),
        ],
        scalar=True,
    )(core, mine, other, r_bar)
    left = (qh, ql, nh, nl)
    w_outer, own1 = call(gradient_outer, (single, hops), work * 3, 3 * 10**6, scalar=True)(
        core, table, *left, oh, ol, *weights
    )
    back1 = swap_outer(own1)
    w_inner, w_heavy, own2, own = call(
        gradient_rest, (single, pair, hops, shape((4 * n, rank), f32)), 10**10, 6 * 10**6, scalar=True
    )(core, table, w_outer, own1, *left, lh, ll, hh, hl, *weights)
    back2, back = swap_outer(own2), swap_inner(own)
    noise_grad = call(gradient_noise, shape(noise_cols.shape, f32), 0, 0, scalar=True)(
        core, *left, oh, ol, lh, ll, hh, hl, *weights
    )
    out_light, out_heavy = call(contract_first, (pair, pair), 10**7, 6 * 10**6, [pltpu.VMEM(z_factor.shape, f32)])(
        table, w_outer, w_inner, w_heavy, own1, own, back1, back, outer2, inner
    )
    z_grad = call(contract_last, shape(z_factor.shape, f32), 10**6, 6 * 10**6, scalar=True)(
        core, out_light, out_heavy, back2
    )
    return z_grad, noise_grad


def solution(mesh):
    return jax.shard_map(
        on_device,
        mesh=mesh,
        in_specs=(
            P(None, "row", None),
            P(None, ("grp", "row"), None, None),
            P(None, ("grp", "row"), None, None),
            P(None, ("grp", "row"), None, None),
            P("grp", None),
        ),
        out_specs=(P(None, ("grp", "row"), None, None), P(None, ("grp", "row"), None, None)),
        check_vma=False,
    )
```

```python
import jax
import jax.numpy as jnp
from jax import lax
from jax.experimental import pallas as pl
from jax.experimental.pallas import tpu as pltpu
from jax.sharding import PartitionSpec as P

rate_scales = (0.4, 0.4, 0.1, 0.2, 0.1, 0.1)
exact = lax.Precision.HIGHEST
f32 = jnp.float32
bf16 = jnp.bfloat16
VMEM = pl.BlockSpec(memory_space=pltpu.VMEM)
LIMIT = 24 * 1024 * 1024
FAR_LIMIT = 63 * 1024 * 1024


def call(kernel, outs, flops, moved, scratch=(), scalar=False, far=False):
    def run(*args):
        specs = [pl.BlockSpec(memory_space=pltpu.HBM) if far else pl.BlockSpec() for _ in args]
        if scalar:
            specs[0] = pl.BlockSpec(memory_space=pltpu.SMEM)
        return pl.pallas_call(
            kernel,
            out_shape=outs,
            in_specs=specs,
            scratch_shapes=list(scratch),
            compiler_params=pltpu.CompilerParams(vmem_limit_bytes=FAR_LIMIT if far else LIMIT),
            cost_estimate=pl.CostEstimate(flops=flops, bytes_accessed=moved, transcendentals=0),
        )(*args)

    return run


def split2(value):
    high = value.astype(bf16)
    low = (value - high.astype(f32)).astype(bf16)
    return high, low


def split3(value):
    high = value.astype(bf16)
    rest = value - high.astype(f32)
    mid = rest.astype(bf16)
    low = (rest - mid.astype(f32)).astype(bf16)
    return high, mid, low


def dot(a, b, contract):
    return lax.dot_general(a, b, ((contract[0], contract[1]), ((), ())), preferred_element_type=f32)


def coefficients(table_ref):
    return [[table_ref[:, 6 * s + k : 6 * s + k + 1] for k in range(6)] for s in range(2)]


def side(v):
    n = v.shape[0]
    place = lax.broadcasted_iota(jnp.int32, v.shape, 0)
    left = jnp.where(place == 0, 0.0, pltpu.roll(v, 1, 0))
    right = jnp.where(place == n - 1, 0.0, pltpu.roll(v, n - 1, 0))
    return left + right


def forward_light(c, xa, pa, xb, hop_x, hop_p):
    d, w, g, l, m, j = c
    return (
        -0.5 * l * xa - d * pa - j * hop_p,
        d * xa - 0.5 * l * pa - 2.0 * g * xb + j * hop_x,
    )


def forward_heavy(c, xa, xb, pb):
    d, w, g, l, m, j = c
    return w * pb, -w * xb - 0.5 * m * pb - 2.0 * g * xa


def backward_light(c, xa, pa, pb, hop_x, hop_p):
    d, w, g, l, m, j = c
    return (
        -0.5 * l * xa + d * pa - 2.0 * g * pb + hop_p,
        -d * xa - 0.5 * l * pa - hop_x,
    )


def backward_heavy(c, pa, xb, pb):
    d, w, g, l, m, j = c
    return -2.0 * g * pa - w * pb, w * xb - 0.5 * m * pb


def forward_rim(core_ref, coeff_hbm, z_hbm, outer1_ref, outer2_ref, inner_ref, table_ref, coeff_ref, z_ref, sems):
    n = z_ref.shape[2]
    core = core_ref[0]
    copies = [
        pltpu.make_async_copy(z_hbm.at[0:3, core], z_ref.at[0], sems.at[0]),
        pltpu.make_async_copy(z_hbm.at[0:3, 1 - core], z_ref.at[1], sems.at[1]),
        pltpu.make_async_copy(coeff_hbm, coeff_ref, sems.at[2]),
    ]
    for copy in copies:
        copy.start()
    for copy in copies:
        copy.wait()
    cols = jnp.transpose(jnp.concatenate([coeff_ref[k] for k in range(6)], axis=0))
    swapped = core == 1
    both = []
    for s in range(2):
        for k in range(6):
            column = jnp.where(swapped, cols[:, 2 * k + 1 - s : 2 * k + 2 - s], cols[:, 2 * k + s : 2 * k + s + 1])
            both.append(column * rate_scales[k])
    for place, column in enumerate(both):
        table_ref[:, place : place + 1] = column
    far = []
    for s in range(2):
        xa, pa, xb = z_ref[s, 0], z_ref[s, 1], z_ref[s, 2]
        hop_x = z_ref[1 - s, 0] + side(xa)
        hop_p = z_ref[1 - s, 1] + side(pa)
        far.append(forward_light(both[6 * s : 6 * s + 6], xa, pa, xb, hop_x, hop_p))
    outer1_ref[0:n] = z_ref[0, 0]
    outer1_ref[n : 2 * n] = z_ref[0, 1]
    inner_ref[0:n] = z_ref[1, 0]
    inner_ref[n : 2 * n] = z_ref[1, 1]
    for s, out, base in ((0, outer2_ref, 0), (1, inner_ref, 2 * n)):
        out[base : base + n], out[base + n : base + 2 * n] = far[s]
        hopping = jnp.where(swapped, coeff_ref[5, 1 - s : 2 - s, :], coeff_ref[5, s : s + 1, :]) * rate_scales[5]
        pieces = [hopping[:, k * 128 : (k + 1) * 128] for k in range(n // 128)]
        pieces.append(jnp.zeros((8 - n // 128, 128), f32))
        out[base + 2 * n :] = jnp.concatenate(pieces, axis=0)


def far_hopping(recv_ref, n):
    size = recv_ref.shape[0]
    tail = jnp.transpose(recv_ref[size - 8 : size])
    return jnp.concatenate([tail[:, k : k + 1] for k in range(n // 128)], axis=0)


def cells(row, k, n):
    return pl.ds(pl.multiple_of((2 * k + row) * n, 128), n)


def packed(gram, cross):
    row = lax.broadcasted_iota(jnp.int32, gram.shape, 0)
    col = lax.broadcasted_iota(jnp.int32, gram.shape, 1)
    diagonal = jnp.sum(jnp.where(row == col, cross, 0.0), axis=0, keepdims=True)
    return jnp.where(row <= col, gram, cross), jnp.broadcast_to(diagonal, (8, gram.shape[1]))


def noise_products(noise_ref, q_ref, pack_ref, nh_ref, nl_ref, qh_ref, ql_ref, nht_ref, nlt_ref, qht_ref, qlt_ref):
    nh, nl = split2(noise_ref[...])
    qh, ql = split2(q_ref[...])
    nh_ref[...] = nh
    nl_ref[...] = nl
    qh_ref[...] = qh
    ql_ref[...] = ql
    for value, out in ((nh, nht_ref), (nl, nlt_ref), (qh, qht_ref), (ql, qlt_ref)):
        out[...] = jnp.transpose(value)
    plain = ((1,), (0,))
    high = dot(jnp.concatenate([nht_ref[...], qht_ref[128:]], axis=0), jnp.concatenate([nh, nl], axis=1), plain)
    low = dot(qlt_ref[128:], nh, plain)
    mixed = high[:128, 128:]
    gram = high[:128, :128] + mixed + jnp.transpose(mixed)
    cross = high[128:, :128] + high[128:, 128:] + low
    pack_ref[0:128], pack_ref[128:] = packed(gram, cross)


def row_products(xh, xl, nht, nlt, qht, qlt):
    plain = ((1,), (0,))
    left = jnp.concatenate([jnp.transpose(xh), nht, qht], axis=0)
    high = dot(left, jnp.concatenate([xh, xl], axis=1), plain)
    low = dot(jnp.concatenate([nlt, qlt], axis=0), xh, plain)
    mixed = high[:128, 128:]
    return (
        high[:128, :128] + mixed + jnp.transpose(mixed),
        high[128:, :128] + high[128:, 128:] + low,
    )


def expand_first(
    core_ref, table_ref, z_ref, inner_ref, outer1_ref, nht_ref, nlt_ref, qht_ref, qlt_ref,
    light_ref, hh_ref, hl_ref, ih_ref, il_ref, gram_ref, rest_ref, first_ref,
):
    c = coefficients(table_ref)
    n = z_ref.shape[2]
    core = core_ref[0]
    rows = (core, 1 - core)
    z = [[z_ref[k, row] for k in range(4)] for row in rows]
    for s, beyond in enumerate((outer1_ref, inner_ref)):
        xa, pa, xb, pb = z[s]
        hop_x = z[1 - s][0] + beyond[0:n] + side(xa)
        hop_p = z[1 - s][1] + beyond[n : 2 * n] + side(pa)
        first_ref[0, s], first_ref[1, s] = forward_light(c[s], xa, pa, xb, hop_x, hop_p)
        first_ref[2, s], first_ref[3, s] = forward_heavy(c[s], xa, xb, pb)
    for s in range(2):
        xa, pa, xb, pb = (first_ref[k, s] for k in range(4))
        for k, (f, second) in enumerate(zip((xb, pb), forward_heavy(c[s], xa, xb, pb))):
            h, l = split2(z[s][2 + k] + f + 0.5 * second)
            hh_ref[cells(rows[s], k, n)] = h
            hl_ref[cells(rows[s], k, n)] = l
    jfar = far_hopping(inner_ref, n)
    for s in range(2):
        xa, pa, xb, pb = (first_ref[k, s] for k in range(4))
        hop_x = first_ref[0, 1 - s] + side(xa)
        hop_p = first_ref[1, 1 - s] + side(pa)
        if s == 1:
            hop_x = hop_x + inner_ref[2 * n : 3 * n] - jfar * z[s][1]
            hop_p = hop_p + inner_ref[3 * n : 4 * n] + jfar * z[s][0]
        second = forward_light(c[s], xa, pa, xb, hop_x, hop_p)
        for k in range(2):
            value = z[s][k] + first_ref[k, s] + 0.5 * second[k]
            if s == 0:
                light_ref[k] = value
            else:
                ih_ref[k * n : (k + 1) * n], il_ref[k * n : (k + 1) * n] = split2(value)
    half = 4 * n
    parts = (nht_ref, nlt_ref, qht_ref, qlt_ref)
    gram, rest = row_products(hh_ref[...], hl_ref[...], *(ref[:, half:] for ref in parts))
    for k in range(2):
        there = cells(1 - core, k, n)
        here = slice(k * n, (k + 1) * n)
        more = row_products(ih_ref[here], il_ref[here], *(ref[:, there] for ref in parts))
        gram = gram + more[0]
        rest = rest + more[1]
    gram_ref[...] = gram
    rest_ref[...] = rest


def expand_last(
    core_ref, table_ref, z_ref, outer2_ref, light_ref, gram_ref, rest_ref, pack_ref,
    nht_ref, nlt_ref, qht_ref, qlt_ref, mine_ref, other_ref, oh_ref, ol_ref, sums_ref,
):
    n = z_ref.shape[2]
    core = core_ref[0]
    jfar = far_hopping(outer2_ref, n)
    far_x = outer2_ref[0:n] - jfar * z_ref[1, core]
    far_p = outer2_ref[n : 2 * n] + jfar * z_ref[0, core]
    j = 0.5 * table_ref[:, 5:6]
    gram, rest = gram_ref[...], rest_ref[...]
    for k, value in enumerate((light_ref[0] - j * far_p, light_ref[1] + j * far_x)):
        h, l = split2(value)
        oh_ref[k * n : (k + 1) * n] = h
        ol_ref[k * n : (k + 1) * n] = l
        there = cells(core, k, n)
        more = row_products(h, l, *(ref[:, there] for ref in (nht_ref, nlt_ref, qht_ref, qlt_ref)))
        gram = gram + more[0]
        rest = rest + more[1]
    sums_ref[0:128], sums_ref[512:520] = packed(gram, rest[128:256])
    sums_ref[128:256] = jnp.transpose(rest[:128])
    sums_ref[256:384] = rest[256:]
    sums_ref[384:512] = pack_ref[0:128]
    sums_ref[520:528] = pack_ref[128:136]
    mine_ref[...] = sums_ref[pl.ds(pl.multiple_of(core * 264, 8), 264)]
    other_ref[...] = sums_ref[pl.ds(pl.multiple_of((1 - core) * 264, 8), 264)]


def inverse_factor(w_ref, out_ref):
    size = w_ref.shape[0]
    step = 8
    lane = lax.broadcasted_iota(jnp.int32, (step, size), 1)
    place = lax.broadcasted_iota(jnp.int32, (step, size), 0)

    def load(start):
        return [jnp.broadcast_to(w_ref[start + i : start + i + 1, :], (step, size)) for i in range(step)]

    rows = load(0)
    for start in range(0, size, step):
        last = start + step >= size
        reach = step if last else 2 * step
        s = {
            (i, m): jnp.broadcast_to(rows[i][:, start + m : start + m + 1], (step, size))
            for i in range(step)
            for m in range(i, reach)
        }
        inside = (lane >= start) & (lane < start + step)
        rows = [jnp.where(lane == start + i, 1.0, jnp.where(inside, 0.0, rows[i])) for i in range(step)]
        if not last:
            following = [jnp.where(inside, 0.0, row) for row in load(start + step)]
        done = []
        for i in range(step):
            inverse = pl.reciprocal(s[i, i])
            root = lax.rsqrt(s[i, i])
            for k in range(i + 1, step):
                ratio = s[i, k] * inverse
                for m in range(k, reach):
                    s[k, m] = s[k, m] - ratio * s[i, m]
                rows[k] = rows[k] - ratio * rows[i]
            if not last:
                scaled = rows[i] * inverse
                for k in range(step):
                    following[k] = following[k] - s[i, step + k] * scaled
            done.append(rows[i] * root)
        panel = done[0]
        for i in range(1, step):
            panel = jnp.where(place == i, done[i], panel)
        out_ref[start : start + step, :] = panel
        beyond = start + 2 * step
        if beyond < size:
            high, mid, low = (part.astype(f32) for part in split3(panel))
            left = jnp.concatenate([high, high, mid, mid, high, low], axis=0).astype(bf16)
            right = jnp.concatenate([high, mid, high, mid, low, high], axis=0).astype(bf16)
            change = dot(left, right, ((0,), (0,)))[beyond:]
            old = w_ref[beyond:, :]
            column = lax.broadcasted_iota(jnp.int32, old.shape, 1)
            old = jnp.where((column >= start) & (column < start + step), 0.0, old)
            w_ref[beyond:, :] = old - change
        if not last:
            rows = following
    value = out_ref[...]
    row = lax.broadcasted_iota(jnp.int32, value.shape, 0)
    column = lax.broadcasted_iota(jnp.int32, value.shape, 1)
    out_ref[...] = jnp.where(row >= column, value, 0.0)


def factor(
    core_ref, mine_ref, other_ref, r_bar_ref, nh_ref, nl_ref, sh_ref, sl_ref, sums_ref, w_ref, inv1_ref, inv2_ref
):
    tile = 128
    core = core_ref[0]
    sums_ref[pl.ds(pl.multiple_of(core * 264, 8), 264)] = mine_ref[...]
    sums_ref[pl.ds(pl.multiple_of((1 - core) * 264, 8), 264)] = other_ref[...]

    def product(a, b, contract):
        return lax.dot_general(a, b, ((contract[0], contract[1]), ((), ())), precision=exact, preferred_element_type=f32)

    down, across, plain = ((0,), (0,)), ((1,), (1,)), ((1,), (0,))
    row = lax.broadcasted_iota(jnp.int32, (2 * tile, 2 * tile), 0)
    col = lax.broadcasted_iota(jnp.int32, (2 * tile, 2 * tile), 1)

    def corner(value, keep):
        return jnp.where(keep[:tile, :tile], value, 0.0)

    def whole(value):
        return corner(value, row <= col) + jnp.transpose(corner(value, row < col))

    pack1, g12, pack2 = sums_ref[0:tile], sums_ref[tile : 2 * tile], sums_ref[3 * tile : 4 * tile]
    w_ref[...] = corner(pack1, row <= col)
    inverse_factor(w_ref, inv1_ref)
    inv1 = inv1_ref[...]
    u12 = product(inv1, g12, plain)
    w_ref[...] = corner(pack2, row <= col) - product(u12, u12, down)
    inverse_factor(w_ref, inv2_ref)
    inv2 = inv2_ref[...]
    inv21 = -product(inv2, product(u12, inv1, down), plain)
    zero = jnp.zeros((tile, tile), f32)
    inv = jnp.concatenate(
        [jnp.concatenate([inv1, zero], axis=1), jnp.concatenate([inv21, inv2], axis=1)], axis=0
    )
    gram = jnp.concatenate(
        [
            jnp.concatenate([whole(pack1), g12], axis=1),
            jnp.concatenate([jnp.transpose(g12), whole(pack2)], axis=1),
        ],
        axis=0,
    )
    bar = jnp.where(row <= col, r_bar_ref[...], 0.0)
    top = jnp.concatenate([pack1, zero], axis=1)
    bottom = jnp.concatenate([sums_ref[2 * tile : 3 * tile], pack2], axis=1)
    cross = jnp.concatenate([top, bottom], axis=0)
    diagonal = jnp.concatenate([sums_ref[512:513], sums_ref[520:521]], axis=1)
    cross = jnp.where(row > col, cross, jnp.where(row == col, diagonal, 0.0))
    middle = product(inv, product(gram, bar, across), plain) - product(cross, inv, across)
    symmetric = jnp.where(row >= col, middle, 0.0) + jnp.transpose(jnp.where(row > col, middle, 0.0))
    spread = product(inv, product(symmetric, inv, plain), down)
    nh_ref[...], nl_ref[...] = split2(inv)
    sh_ref[...], sl_ref[...] = split2(spread)


def columns(qh, ql, nh, nl, xh, xl, ih, il, sh, sl):
    plain = ((1,), (0,))
    xh = jnp.concatenate([xh, nh], axis=1)
    xl = jnp.concatenate([xl, nl], axis=1)
    high = dot(qh, jnp.concatenate([ih, il], axis=1), plain) + dot(xh, jnp.concatenate([sh, sl], axis=1), plain)
    return high[:, :128] + high[:, 128:] + dot(ql, ih, plain) + dot(xl, sh, plain)


def gradient_outer(
    core_ref, table_ref, qh_ref, ql_ref, nh_ref, nl_ref, oh_ref, ol_ref, ih_ref, il_ref, sh_ref, sl_ref,
    w_ref, outer1_ref,
):
    n = w_ref.shape[1]
    j = table_ref[:, 5:6]
    weights = [ref[:, :128] for ref in (ih_ref, il_ref, sh_ref, sl_ref)]
    for k in range(2):
        there = cells(core_ref[0], k, n)
        here = slice(k * n, (k + 1) * n)
        parts = [ref[there] for ref in (qh_ref, ql_ref, nh_ref, nl_ref)] + [oh_ref[here], ol_ref[here]]
        w = columns(*parts, *weights)
        w_ref[k] = w
        outer1_ref[here] = j * w


def gradient_rest(
    core_ref, table_ref, outer_ref, outer1_ref, qh_ref, ql_ref, nh_ref, nl_ref, lh_ref, ll_ref, hh_ref, hl_ref,
    ih_ref, il_ref, sh_ref, sl_ref, light_ref, heavy_ref, outer2_ref, inner_ref,
):
    c = coefficients(table_ref)
    n = outer_ref.shape[1]
    core = core_ref[0]
    weights = [ref[:, :128] for ref in (ih_ref, il_ref, sh_ref, sl_ref)]
    left = (qh_ref, ql_ref, nh_ref, nl_ref)
    for k in range(2):
        there = cells(1 - core, k, n)
        here = slice(k * n, (k + 1) * n)
        w = columns(*[ref[there] for ref in left], lh_ref[here], ll_ref[here], *weights)
        light_ref[k] = w
        inner_ref[here] = c[1][5] * w
    for k in (1, 0):
        for s, row in enumerate((core, 1 - core)):
            there = cells(row, 2 + k, n)
            here = cells(row, k, n)
            heavy_ref[k, s] = columns(*[ref[there] for ref in left], hh_ref[here], hl_ref[here], *weights)
    own = (outer1_ref, inner_ref)
    for s, w, out, base in ((0, outer_ref, outer2_ref, 0), (1, light_ref, inner_ref, 2 * n)):
        hop_x = own[1 - s][0:n] + side(own[s][0:n])
        hop_p = own[1 - s][n : 2 * n] + side(own[s][n : 2 * n])
        bx, bp = backward_light(c[s], w[0], w[1], heavy_ref[1, s], hop_x, hop_p)
        out[base : base + n] = c[s][5] * bx
        out[base + n : base + 2 * n] = c[s][5] * bp


def gradient_noise(
    core_ref, qh_ref, ql_ref, nh_ref, nl_ref, oh_ref, ol_ref, lh_ref, ll_ref, hh_ref, hl_ref,
    ih_ref, il_ref, sh_ref, sl_ref, out_ref,
):
    n = out_ref.shape[2]
    core = core_ref[0]
    weights = [ref[:, 128:] for ref in (ih_ref, il_ref, sh_ref, sl_ref)]
    for k in range(4):
        for s, row in enumerate((core, 1 - core)):
            there = cells(row, k, n)
            if k < 2:
                here = slice(k * n, (k + 1) * n)
                x = (oh_ref[here], ol_ref[here]) if s == 0 else (lh_ref[here], ll_ref[here])
            else:
                here = cells(row, k - 2, n)
                x = (hh_ref[here], hl_ref[here])
            out_ref[k, row] = columns(*[ref[there] for ref in (qh_ref, ql_ref, nh_ref, nl_ref)], *x, *weights)


def contract_first(
    table_ref, outer_ref, light_ref, heavy_ref, own1_ref, own_ref, outer1_ref, inner_ref, fouter2_ref, finner_ref,
    out_light_ref, out_heavy_ref, first_ref,
):
    c = coefficients(table_ref)
    n = outer_ref.shape[1]
    w = [
        (outer_ref[0], outer_ref[1], heavy_ref[0, 0], heavy_ref[1, 0]),
        (light_ref[0], light_ref[1], heavy_ref[0, 1], heavy_ref[1, 1]),
    ]
    own = [(ref[0:n], ref[n : 2 * n]) for ref in (own1_ref, own_ref)]
    for s, far in enumerate((outer1_ref, inner_ref)):
        xa, pa, xb, pb = w[s]
        hop_x = own[1 - s][0] + far[0:n] + side(own[s][0])
        hop_p = own[1 - s][1] + far[n : 2 * n] + side(own[s][1])
        first_ref[0, s], first_ref[1, s] = backward_light(c[s], xa, pa, pb, hop_x, hop_p)
        first_ref[2, s], first_ref[3, s] = backward_heavy(c[s], pa, xb, pb)
    for s, fref in enumerate((fouter2_ref, finner_ref)):
        xa, pa, xb, pb = (first_ref[k, s] for k in range(4))
        jfar = far_hopping(fref, n)
        j, jother = c[s][5], c[1 - s][5]
        hop_x = jother * first_ref[0, 1 - s] + jfar * own[s][1] + side(j * xa)
        hop_p = jother * first_ref[1, 1 - s] - jfar * own[s][0] + side(j * pa)
        if s == 1:
            hop_x = hop_x + inner_ref[2 * n : 3 * n]
            hop_p = hop_p + inner_ref[3 * n : 4 * n]
        light = backward_light(c[s], xa, pa, pb, hop_x, hop_p)
        heavy = backward_heavy(c[s], pa, xb, pb)
        for k in range(2):
            out_light_ref[k, s] = w[s][k] + first_ref[k, s] + 0.5 * light[k]
            out_heavy_ref[k, s] = w[s][2 + k] + first_ref[2 + k, s] + 0.5 * heavy[k]


def contract_last(core_ref, light_ref, heavy_ref, outer2_ref, out_ref):
    n = out_ref.shape[2]
    core = core_ref[0]
    out_ref[0, core] = light_ref[0, 0] + 0.5 * outer2_ref[n : 2 * n]
    out_ref[1, core] = light_ref[1, 0] - 0.5 * outer2_ref[0:n]
    for k in range(2):
        out_ref[k, 1 - core] = light_ref[k, 1]
        out_ref[2 + k, core] = heavy_ref[k, 0]
        out_ref[2 + k, 1 - core] = heavy_ref[k, 1]


def swap_inner(message):
    count = lax.axis_size("row")
    return lax.ppermute(message, "row", [(i, i ^ 1) for i in range(count)])


def swap_outer(message):
    count = lax.axis_size("row")
    pairs = [(i, i + 1) for i in range(1, count - 1, 2)]
    return lax.ppermute(message, "row", pairs + [(j, i) for i, j in pairs])


def sum_over_rows(mine, other):
    count = lax.axis_size("row")
    bits = count.bit_length() - 1
    swap = [(i, i ^ 1) for i in range(count)]
    mine = mine + lax.ppermute(other, "row", swap)
    for step in range(bits - 1):
        turn = [1 + step, 1 + (step + 1) % (bits - 1)]
        mine = mine + lax.ppermute(mine, "row", [(i, i ^ (1 << turn[i & 1])) for i in range(count)])
    return mine, lax.ppermute(mine, "row", swap)


def on_device(cell_coeffs, z_factor, noise_cols, q_bar, r_bar):
    quads, lattice, n, rank = z_factor.shape
    flat = quads * lattice * n
    coeffs = cell_coeffs
    core = (lax.axis_index("row") & 1).reshape(1)
    noise = noise_cols.reshape(flat, -1)
    bar = q_bar.reshape(flat, -1)
    shape = jax.ShapeDtypeStruct
    hops = shape((2 * n, rank), f32)
    rim = shape((2 * n + 8, rank), f32)
    table = shape((n, 16), f32)
    outer1, outer2, inner, table = call(
        forward_rim, (hops, rim, shape((4 * n + 8, rank), f32), table), 10**6, 3 * 10**6,
        [
            pltpu.VMEM(cell_coeffs.shape, f32),
            pltpu.VMEM((2, 3, n, rank), f32),
            pltpu.SemaphoreType.DMA((3,)),
        ],
        scalar=True, far=True,
    )(core, coeffs, z_factor)
    outer1, outer2, inner = swap_outer(outer1), swap_outer(outer2), swap_inner(inner)
    wide, tall = shape((flat, 256), bf16), shape((flat, 128), bf16)
    wide_t, tall_t = shape((256, flat), bf16), shape((128, flat), bf16)
    work = 2 * flat * 128 * 128
    pack, nh, nl, qh, ql, nht, nlt, qht, qlt = call(
        noise_products, (shape((136, 128), f32), tall, tall, wide, wide, tall_t, tall_t, wide_t, wide_t),
        work * 5, 9 * 10**6,
    )(noise, bar)
    transposed = (nht, nlt, qht, qlt)
    half, quarter = shape((flat // 2, 128), bf16), shape((flat // 4, 128), bf16)
    single, pair = shape((2, n, rank), f32), shape((2, lattice, n, rank), f32)
    light, hh, hl, lh, ll, gram, rest = call(
        expand_first,
        (single, half, half, quarter, quarter, shape((128, 128), f32), shape((384, 128), f32)),
        work * 8, 9 * 10**6, [pltpu.VMEM(z_factor.shape, f32)], scalar=True,
    )(core, table, z_factor, inner, outer1, *transposed)
    part = shape((264, 128), f32)
    mine, other, oh, ol = call(
        expand_last, (part, part, quarter, quarter), work * 3, 5 * 10**6, [pltpu.VMEM((528, 128), f32)], scalar=True
    )(core, table, z_factor, outer2, light, gram, rest, pack, *transposed)
    mine, other = sum_over_rows(mine, other)
    square = shape((256, 256), bf16)
    weights = call(
        factor, (square,) * 4, 10**9, 10**6,
        [
            pltpu.VMEM((528, 128), f32),
            pltpu.VMEM((128, 128), f32),
            pltpu.VMEM((128, 128), f32),
            pltpu.VMEM((128, 128), f32),
        ],
        scalar=True,
    )(core, mine, other, r_bar)
    left = (qh, ql, nh, nl)
    w_outer, own1 = call(gradient_outer, (single, hops), work * 3, 3 * 10**6, scalar=True)(
        core, table, *left, oh, ol, *weights
    )
    back1 = swap_outer(own1)
    w_inner, w_heavy, own2, own = call(
        gradient_rest, (single, pair, hops, shape((4 * n, rank), f32)), 10**10, 6 * 10**6, scalar=True
    )(core, table, w_outer, own1, *left, lh, ll, hh, hl, *weights)
    back2, back = swap_outer(own2), swap_inner(own)
    noise_grad = call(gradient_noise, shape(noise_cols.shape, f32), 0, 0, scalar=True)(
        core, *left, oh, ol, lh, ll, hh, hl, *weights
    )
    out_light, out_heavy = call(contract_first, (pair, pair), 10**7, 6 * 10**6, [pltpu.VMEM(z_factor.shape, f32)])(
        table, w_outer, w_inner, w_heavy, own1, own, back1, back, outer2, inner
    )
    z_grad = call(contract_last, shape(z_factor.shape, f32), 10**6, 6 * 10**6, scalar=True)(
        core, out_light, out_heavy, back2
    )
    return z_grad, noise_grad


def solution(mesh):
    return jax.shard_map(
        on_device,
        mesh=mesh,
        in_specs=(
            P(None, "row", None),
            P(None, ("grp", "row"), None, None),
            P(None, ("grp", "row"), None, None),
            P(None, ("grp", "row"), None, None),
            P("grp", None),
        ),
        out_specs=(P(None, ("grp", "row"), None, None), P(None, ("grp", "row"), None, None)),
        check_vma=False,
    )
```

```python
import jax
import jax.numpy as jnp
from jax import lax
from jax.experimental import pallas as pl
from jax.experimental.pallas import tpu as pltpu
from jax.sharding import PartitionSpec as P

rate_scales = (0.4, 0.4, 0.1, 0.2, 0.1, 0.1)
exact = lax.Precision.HIGHEST
f32 = jnp.float32
bf16 = jnp.bfloat16
VMEM = pl.BlockSpec(memory_space=pltpu.VMEM)
LIMIT = 24 * 1024 * 1024
FAR_LIMIT = 63 * 1024 * 1024


def call(kernel, outs, flops, moved, scratch=(), scalar=False, far=False):
    def run(*args):
        specs = [pl.BlockSpec(memory_space=pltpu.HBM) if far else pl.BlockSpec() for _ in args]
        if scalar:
            specs[0] = pl.BlockSpec(memory_space=pltpu.SMEM)
        return pl.pallas_call(
            kernel,
            out_shape=outs,
            in_specs=specs,
            scratch_shapes=list(scratch),
            compiler_params=pltpu.CompilerParams(vmem_limit_bytes=FAR_LIMIT if far else LIMIT),
            cost_estimate=pl.CostEstimate(flops=flops, bytes_accessed=moved, transcendentals=0),
        )(*args)

    return run


def split2(value):
    high = value.astype(bf16)
    low = (value - high.astype(f32)).astype(bf16)
    return high, low


def split3(value):
    high = value.astype(bf16)
    rest = value - high.astype(f32)
    mid = rest.astype(bf16)
    low = (rest - mid.astype(f32)).astype(bf16)
    return high, mid, low


def dot(a, b, contract):
    return lax.dot_general(a, b, ((contract[0], contract[1]), ((), ())), preferred_element_type=f32)


def coefficients(table_ref):
    return [[table_ref[:, 6 * s + k : 6 * s + k + 1] for k in range(6)] for s in range(2)]


def side(v):
    n = v.shape[0]
    place = lax.broadcasted_iota(jnp.int32, v.shape, 0)
    left = jnp.where(place == 0, 0.0, pltpu.roll(v, 1, 0))
    right = jnp.where(place == n - 1, 0.0, pltpu.roll(v, n - 1, 0))
    return left + right


def forward_light(c, xa, pa, xb, hop_x, hop_p):
    d, w, g, l, m, j = c
    return (
        -0.5 * l * xa - d * pa - j * hop_p,
        d * xa - 0.5 * l * pa - 2.0 * g * xb + j * hop_x,
    )


def forward_heavy(c, xa, xb, pb):
    d, w, g, l, m, j = c
    return w * pb, -w * xb - 0.5 * m * pb - 2.0 * g * xa


def backward_light(c, xa, pa, pb, hop_x, hop_p):
    d, w, g, l, m, j = c
    return (
        -0.5 * l * xa + d * pa - 2.0 * g * pb + hop_p,
        -d * xa - 0.5 * l * pa - hop_x,
    )


def backward_heavy(c, pa, xb, pb):
    d, w, g, l, m, j = c
    return -2.0 * g * pa - w * pb, w * xb - 0.5 * m * pb


def forward_rim(core_ref, coeff_hbm, z_hbm, outer1_ref, outer2_ref, inner_ref, table_ref, coeff_ref, z_ref, sems):
    n = z_ref.shape[2]
    core = core_ref[0]
    copies = [
        pltpu.make_async_copy(z_hbm.at[0:3, core], z_ref.at[0], sems.at[0]),
        pltpu.make_async_copy(z_hbm.at[0:3, 1 - core], z_ref.at[1], sems.at[1]),
        pltpu.make_async_copy(coeff_hbm, coeff_ref, sems.at[2]),
    ]
    for copy in copies:
        copy.start()
    for copy in copies:
        copy.wait()
    cols = jnp.transpose(jnp.concatenate([coeff_ref[k] for k in range(6)], axis=0))
    swapped = core == 1
    both = []
    for s in range(2):
        for k in range(6):
            column = jnp.where(swapped, cols[:, 2 * k + 1 - s : 2 * k + 2 - s], cols[:, 2 * k + s : 2 * k + s + 1])
            both.append(column * rate_scales[k])
    for place, column in enumerate(both):
        table_ref[:, place : place + 1] = column
    far = []
    for s in range(2):
        xa, pa, xb = z_ref[s, 0], z_ref[s, 1], z_ref[s, 2]
        hop_x = z_ref[1 - s, 0] + side(xa)
        hop_p = z_ref[1 - s, 1] + side(pa)
        far.append(forward_light(both[6 * s : 6 * s + 6], xa, pa, xb, hop_x, hop_p))
    outer1_ref[0:n] = z_ref[0, 0]
    outer1_ref[n : 2 * n] = z_ref[0, 1]
    inner_ref[0:n] = z_ref[1, 0]
    inner_ref[n : 2 * n] = z_ref[1, 1]
    for s, out, base in ((0, outer2_ref, 0), (1, inner_ref, 2 * n)):
        out[base : base + n], out[base + n : base + 2 * n] = far[s]
        hopping = jnp.where(swapped, coeff_ref[5, 1 - s : 2 - s, :], coeff_ref[5, s : s + 1, :]) * rate_scales[5]
        pieces = [hopping[:, k * 128 : (k + 1) * 128] for k in range(n // 128)]
        pieces.append(jnp.zeros((8 - n // 128, 128), f32))
        out[base + 2 * n :] = jnp.concatenate(pieces, axis=0)


def far_hopping(recv_ref, n):
    size = recv_ref.shape[0]
    tail = jnp.transpose(recv_ref[size - 8 : size])
    return jnp.concatenate([tail[:, k : k + 1] for k in range(n // 128)], axis=0)


def cells(row, k, n):
    return pl.ds(pl.multiple_of((2 * k + row) * n, 128), n)


def packed(gram, cross):
    row = lax.broadcasted_iota(jnp.int32, gram.shape, 0)
    col = lax.broadcasted_iota(jnp.int32, gram.shape, 1)
    diagonal = jnp.sum(jnp.where(row == col, cross, 0.0), axis=0, keepdims=True)
    return jnp.where(row <= col, gram, cross), jnp.broadcast_to(diagonal, (8, gram.shape[1]))


def noise_products(noise_ref, q_ref, pack_ref, nh_ref, nl_ref, qh_ref, ql_ref, nht_ref, nlt_ref, qht_ref, qlt_ref):
    nh, nl = split2(noise_ref[...])
    qh, ql = split2(q_ref[...])
    nh_ref[...] = nh
    nl_ref[...] = nl
    qh_ref[...] = qh
    ql_ref[...] = ql
    for value, out in ((nh, nht_ref), (nl, nlt_ref), (qh, qht_ref), (ql, qlt_ref)):
        out[...] = jnp.transpose(value)
    plain = ((1,), (0,))
    high = dot(jnp.concatenate([nht_ref[...], qht_ref[128:]], axis=0), jnp.concatenate([nh, nl], axis=1), plain)
    low = dot(qlt_ref[128:], nh, plain)
    mixed = high[:128, 128:]
    gram = high[:128, :128] + mixed + jnp.transpose(mixed)
    cross = high[128:, :128] + high[128:, 128:] + low
    pack_ref[0:128], pack_ref[128:] = packed(gram, cross)


def row_products(xh, xl, nht, nlt, qht, qlt):
    plain = ((1,), (0,))
    left = jnp.concatenate([jnp.transpose(xh), nht, qht], axis=0)
    high = dot(left, jnp.concatenate([xh, xl], axis=1), plain)
    low = dot(jnp.concatenate([nlt, qlt], axis=0), xh, plain)
    mixed = high[:128, 128:]
    return (
        high[:128, :128] + mixed + jnp.transpose(mixed),
        high[128:, :128] + high[128:, 128:] + low,
    )


def expand_first(
    core_ref, table_ref, z_ref, inner_ref, outer1_ref, nht_ref, nlt_ref, qht_ref, qlt_ref,
    light_ref, hh_ref, hl_ref, ih_ref, il_ref, gram_ref, rest_ref, first_ref,
):
    c = coefficients(table_ref)
    n = z_ref.shape[2]
    core = core_ref[0]
    rows = (core, 1 - core)
    z = [[z_ref[k, row] for k in range(4)] for row in rows]
    for s, beyond in enumerate((outer1_ref, inner_ref)):
        xa, pa, xb, pb = z[s]
        hop_x = z[1 - s][0] + beyond[0:n] + side(xa)
        hop_p = z[1 - s][1] + beyond[n : 2 * n] + side(pa)
        first_ref[0, s], first_ref[1, s] = forward_light(c[s], xa, pa, xb, hop_x, hop_p)
        first_ref[2, s], first_ref[3, s] = forward_heavy(c[s], xa, xb, pb)
    for s in range(2):
        xa, pa, xb, pb = (first_ref[k, s] for k in range(4))
        for k, (f, second) in enumerate(zip((xb, pb), forward_heavy(c[s], xa, xb, pb))):
            h, l = split2(z[s][2 + k] + f + 0.5 * second)
            hh_ref[cells(rows[s], k, n)] = h
            hl_ref[cells(rows[s], k, n)] = l
    jfar = far_hopping(inner_ref, n)
    for s in range(2):
        xa, pa, xb, pb = (first_ref[k, s] for k in range(4))
        hop_x = first_ref[0, 1 - s] + side(xa)
        hop_p = first_ref[1, 1 - s] + side(pa)
        if s == 1:
            hop_x = hop_x + inner_ref[2 * n : 3 * n] - jfar * z[s][1]
            hop_p = hop_p + inner_ref[3 * n : 4 * n] + jfar * z[s][0]
        second = forward_light(c[s], xa, pa, xb, hop_x, hop_p)
        for k in range(2):
            value = z[s][k] + first_ref[k, s] + 0.5 * second[k]
            if s == 0:
                light_ref[k] = value
            else:
                ih_ref[k * n : (k + 1) * n], il_ref[k * n : (k + 1) * n] = split2(value)
    half = 4 * n
    parts = (nht_ref, nlt_ref, qht_ref, qlt_ref)
    gram, rest = row_products(hh_ref[...], hl_ref[...], *(ref[:, half:] for ref in parts))
    for k in range(2):
        there = cells(1 - core, k, n)
        here = slice(k * n, (k + 1) * n)
        more = row_products(ih_ref[here], il_ref[here], *(ref[:, there] for ref in parts))
        gram = gram + more[0]
        rest = rest + more[1]
    gram_ref[...] = gram
    rest_ref[...] = rest


def quarters(core):
    parts = []
    for owner in (core, 1 - core):
        first = pl.multiple_of(owner * 264, 8)
        parts += [pl.ds(first, 136), pl.ds(pl.multiple_of(first + 136, 8), 128)]
    return parts


def expand_last(
    core_ref, table_ref, z_ref, outer2_ref, light_ref, gram_ref, rest_ref, pack_ref,
    nht_ref, nlt_ref, qht_ref, qlt_ref, mine1_ref, mine2_ref, other1_ref, other2_ref, oh_ref, ol_ref, sums_ref,
):
    n = z_ref.shape[2]
    core = core_ref[0]
    jfar = far_hopping(outer2_ref, n)
    far_x = outer2_ref[0:n] - jfar * z_ref[1, core]
    far_p = outer2_ref[n : 2 * n] + jfar * z_ref[0, core]
    j = 0.5 * table_ref[:, 5:6]
    gram, rest = gram_ref[...], rest_ref[...]
    for k, value in enumerate((light_ref[0] - j * far_p, light_ref[1] + j * far_x)):
        h, l = split2(value)
        oh_ref[k * n : (k + 1) * n] = h
        ol_ref[k * n : (k + 1) * n] = l
        there = cells(core, k, n)
        more = row_products(h, l, *(ref[:, there] for ref in (nht_ref, nlt_ref, qht_ref, qlt_ref)))
        gram = gram + more[0]
        rest = rest + more[1]
    sums_ref[0:128], sums_ref[512:520] = packed(gram, rest[128:256])
    sums_ref[128:256] = jnp.transpose(rest[:128])
    sums_ref[256:384] = rest[256:]
    sums_ref[384:512] = pack_ref[0:128]
    sums_ref[520:528] = pack_ref[128:136]
    for part, out in zip(quarters(core), (mine1_ref, mine2_ref, other1_ref, other2_ref)):
        out[...] = sums_ref[part]


def inverse_factor(w_ref, out_ref):
    size = w_ref.shape[0]
    step = 8
    lane = lax.broadcasted_iota(jnp.int32, (step, size), 1)
    place = lax.broadcasted_iota(jnp.int32, (step, size), 0)

    def load(start):
        return [jnp.broadcast_to(w_ref[start + i : start + i + 1, :], (step, size)) for i in range(step)]

    rows = load(0)
    for start in range(0, size, step):
        last = start + step >= size
        reach = step if last else 2 * step
        s = {
            (i, m): jnp.broadcast_to(rows[i][:, start + m : start + m + 1], (step, size))
            for i in range(step)
            for m in range(i, reach)
        }
        inside = (lane >= start) & (lane < start + step)
        rows = [jnp.where(lane == start + i, 1.0, jnp.where(inside, 0.0, rows[i])) for i in range(step)]
        if not last:
            following = [jnp.where(inside, 0.0, row) for row in load(start + step)]
        done = []
        for i in range(step):
            inverse = pl.reciprocal(s[i, i])
            root = lax.rsqrt(s[i, i])
            for k in range(i + 1, step):
                ratio = s[i, k] * inverse
                for m in range(k, reach):
                    s[k, m] = s[k, m] - ratio * s[i, m]
                rows[k] = rows[k] - ratio * rows[i]
            if not last:
                scaled = rows[i] * inverse
                for k in range(step):
                    following[k] = following[k] - s[i, step + k] * scaled
            done.append(rows[i] * root)
        panel = done[0]
        for i in range(1, step):
            panel = jnp.where(place == i, done[i], panel)
        out_ref[start : start + step, :] = panel
        beyond = start + 2 * step
        if beyond < size:
            high, mid, low = (part.astype(f32) for part in split3(panel))
            left = jnp.concatenate([high, high, mid, mid, high, low], axis=0).astype(bf16)
            right = jnp.concatenate([high, mid, high, mid, low, high], axis=0).astype(bf16)
            change = dot(left, right, ((0,), (0,)))[beyond:]
            old = w_ref[beyond:, :]
            column = lax.broadcasted_iota(jnp.int32, old.shape, 1)
            old = jnp.where((column >= start) & (column < start + step), 0.0, old)
            w_ref[beyond:, :] = old - change
        if not last:
            rows = following
    value = out_ref[...]
    row = lax.broadcasted_iota(jnp.int32, value.shape, 0)
    column = lax.broadcasted_iota(jnp.int32, value.shape, 1)
    out_ref[...] = jnp.where(row >= column, value, 0.0)


def factor(
    core_ref, mine1_ref, mine2_ref, other1_ref, other2_ref, r_bar_ref, nh_ref, nl_ref, sh_ref, sl_ref, sums_ref, w_ref, inv1_ref, inv2_ref
):
    tile = 128
    core = core_ref[0]
    for part, value in zip(quarters(core), (mine1_ref, mine2_ref, other1_ref, other2_ref)):
        sums_ref[part] = value[...]

    def product(a, b, contract):
        return lax.dot_general(a, b, ((contract[0], contract[1]), ((), ())), precision=exact, preferred_element_type=f32)

    down, across, plain = ((0,), (0,)), ((1,), (1,)), ((1,), (0,))
    row = lax.broadcasted_iota(jnp.int32, (2 * tile, 2 * tile), 0)
    col = lax.broadcasted_iota(jnp.int32, (2 * tile, 2 * tile), 1)

    def corner(value, keep):
        return jnp.where(keep[:tile, :tile], value, 0.0)

    def whole(value):
        return corner(value, row <= col) + jnp.transpose(corner(value, row < col))

    pack1, g12, pack2 = sums_ref[0:tile], sums_ref[tile : 2 * tile], sums_ref[3 * tile : 4 * tile]
    w_ref[...] = corner(pack1, row <= col)
    inverse_factor(w_ref, inv1_ref)
    inv1 = inv1_ref[...]
    u12 = product(inv1, g12, plain)
    w_ref[...] = corner(pack2, row <= col) - product(u12, u12, down)
    inverse_factor(w_ref, inv2_ref)
    inv2 = inv2_ref[...]
    inv21 = -product(inv2, product(u12, inv1, down), plain)
    zero = jnp.zeros((tile, tile), f32)
    inv = jnp.concatenate(
        [jnp.concatenate([inv1, zero], axis=1), jnp.concatenate([inv21, inv2], axis=1)], axis=0
    )
    gram = jnp.concatenate(
        [
            jnp.concatenate([whole(pack1), g12], axis=1),
            jnp.concatenate([jnp.transpose(g12), whole(pack2)], axis=1),
        ],
        axis=0,
    )
    bar = jnp.where(row <= col, r_bar_ref[...], 0.0)
    top = jnp.concatenate([pack1, zero], axis=1)
    bottom = jnp.concatenate([sums_ref[2 * tile : 3 * tile], pack2], axis=1)
    cross = jnp.concatenate([top, bottom], axis=0)
    diagonal = jnp.concatenate([sums_ref[512:513], sums_ref[520:521]], axis=1)
    cross = jnp.where(row > col, cross, jnp.where(row == col, diagonal, 0.0))
    middle = product(inv, product(gram, bar, across), plain) - product(cross, inv, across)
    symmetric = jnp.where(row >= col, middle, 0.0) + jnp.transpose(jnp.where(row > col, middle, 0.0))
    spread = product(inv, product(symmetric, inv, plain), down)
    nh_ref[...], nl_ref[...] = split2(inv)
    sh_ref[...], sl_ref[...] = split2(spread)


def columns(qh, ql, nh, nl, xh, xl, ih, il, sh, sl):
    plain = ((1,), (0,))
    xh = jnp.concatenate([xh, nh], axis=1)
    xl = jnp.concatenate([xl, nl], axis=1)
    high = dot(qh, jnp.concatenate([ih, il], axis=1), plain) + dot(xh, jnp.concatenate([sh, sl], axis=1), plain)
    return high[:, :128] + high[:, 128:] + dot(ql, ih, plain) + dot(xl, sh, plain)


def gradient_outer(
    core_ref, table_ref, qh_ref, ql_ref, nh_ref, nl_ref, oh_ref, ol_ref, ih_ref, il_ref, sh_ref, sl_ref,
    w_ref, outer1_ref,
):
    n = w_ref.shape[1]
    j = table_ref[:, 5:6]
    weights = [ref[:, :128] for ref in (ih_ref, il_ref, sh_ref, sl_ref)]
    for k in range(2):
        there = cells(core_ref[0], k, n)
        here = slice(k * n, (k + 1) * n)
        parts = [ref[there] for ref in (qh_ref, ql_ref, nh_ref, nl_ref)] + [oh_ref[here], ol_ref[here]]
        w = columns(*parts, *weights)
        w_ref[k] = w
        outer1_ref[here] = j * w


def gradient_rest(
    core_ref, table_ref, outer_ref, outer1_ref, qh_ref, ql_ref, nh_ref, nl_ref, lh_ref, ll_ref, hh_ref, hl_ref,
    ih_ref, il_ref, sh_ref, sl_ref, light_ref, heavy_ref, outer2_ref, inner_ref,
):
    c = coefficients(table_ref)
    n = outer_ref.shape[1]
    core = core_ref[0]
    weights = [ref[:, :128] for ref in (ih_ref, il_ref, sh_ref, sl_ref)]
    left = (qh_ref, ql_ref, nh_ref, nl_ref)
    for k in range(2):
        there = cells(1 - core, k, n)
        here = slice(k * n, (k + 1) * n)
        w = columns(*[ref[there] for ref in left], lh_ref[here], ll_ref[here], *weights)
        light_ref[k] = w
        inner_ref[here] = c[1][5] * w
    for k in (1, 0):
        for s, row in enumerate((core, 1 - core)):
            there = cells(row, 2 + k, n)
            here = cells(row, k, n)
            heavy_ref[k, s] = columns(*[ref[there] for ref in left], hh_ref[here], hl_ref[here], *weights)
    own = (outer1_ref, inner_ref)
    for s, w, out, base in ((0, outer_ref, outer2_ref, 0), (1, light_ref, inner_ref, 2 * n)):
        hop_x = own[1 - s][0:n] + side(own[s][0:n])
        hop_p = own[1 - s][n : 2 * n] + side(own[s][n : 2 * n])
        bx, bp = backward_light(c[s], w[0], w[1], heavy_ref[1, s], hop_x, hop_p)
        out[base : base + n] = c[s][5] * bx
        out[base + n : base + 2 * n] = c[s][5] * bp


def gradient_noise(
    core_ref, qh_ref, ql_ref, nh_ref, nl_ref, oh_ref, ol_ref, lh_ref, ll_ref, hh_ref, hl_ref,
    ih_ref, il_ref, sh_ref, sl_ref, out_ref,
):
    n = out_ref.shape[2]
    core = core_ref[0]
    weights = [ref[:, 128:] for ref in (ih_ref, il_ref, sh_ref, sl_ref)]
    for k in range(4):
        for s, row in enumerate((core, 1 - core)):
            there = cells(row, k, n)
            if k < 2:
                here = slice(k * n, (k + 1) * n)
                x = (oh_ref[here], ol_ref[here]) if s == 0 else (lh_ref[here], ll_ref[here])
            else:
                here = cells(row, k - 2, n)
                x = (hh_ref[here], hl_ref[here])
            out_ref[k, row] = columns(*[ref[there] for ref in (qh_ref, ql_ref, nh_ref, nl_ref)], *x, *weights)


def contract_first(
    table_ref, outer_ref, light_ref, heavy_ref, own1_ref, own_ref, outer1_ref, inner_ref, fouter2_ref, finner_ref,
    out_light_ref, out_heavy_ref, first_ref,
):
    c = coefficients(table_ref)
    n = outer_ref.shape[1]
    w = [
        (outer_ref[0], outer_ref[1], heavy_ref[0, 0], heavy_ref[1, 0]),
        (light_ref[0], light_ref[1], heavy_ref[0, 1], heavy_ref[1, 1]),
    ]
    own = [(ref[0:n], ref[n : 2 * n]) for ref in (own1_ref, own_ref)]
    for s, far in enumerate((outer1_ref, inner_ref)):
        xa, pa, xb, pb = w[s]
        hop_x = own[1 - s][0] + far[0:n] + side(own[s][0])
        hop_p = own[1 - s][1] + far[n : 2 * n] + side(own[s][1])
        first_ref[0, s], first_ref[1, s] = backward_light(c[s], xa, pa, pb, hop_x, hop_p)
        first_ref[2, s], first_ref[3, s] = backward_heavy(c[s], pa, xb, pb)
    for s, fref in enumerate((fouter2_ref, finner_ref)):
        xa, pa, xb, pb = (first_ref[k, s] for k in range(4))
        jfar = far_hopping(fref, n)
        j, jother = c[s][5], c[1 - s][5]
        hop_x = jother * first_ref[0, 1 - s] + jfar * own[s][1] + side(j * xa)
        hop_p = jother * first_ref[1, 1 - s] - jfar * own[s][0] + side(j * pa)
        if s == 1:
            hop_x = hop_x + inner_ref[2 * n : 3 * n]
            hop_p = hop_p + inner_ref[3 * n : 4 * n]
        light = backward_light(c[s], xa, pa, pb, hop_x, hop_p)
        heavy = backward_heavy(c[s], pa, xb, pb)
        for k in range(2):
            out_light_ref[k, s] = w[s][k] + first_ref[k, s] + 0.5 * light[k]
            out_heavy_ref[k, s] = w[s][2 + k] + first_ref[2 + k, s] + 0.5 * heavy[k]


def contract_last(core_ref, light_ref, heavy_ref, outer2_ref, out_ref):
    n = out_ref.shape[2]
    core = core_ref[0]
    out_ref[0, core] = light_ref[0, 0] + 0.5 * outer2_ref[n : 2 * n]
    out_ref[1, core] = light_ref[1, 0] - 0.5 * outer2_ref[0:n]
    for k in range(2):
        out_ref[k, 1 - core] = light_ref[k, 1]
        out_ref[2 + k, core] = heavy_ref[k, 0]
        out_ref[2 + k, 1 - core] = heavy_ref[k, 1]


def swap_inner(message):
    count = lax.axis_size("row")
    return lax.ppermute(message, "row", [(i, i ^ 1) for i in range(count)])


def swap_outer(message):
    count = lax.axis_size("row")
    pairs = [(i, i + 1) for i in range(1, count - 1, 2)]
    return lax.ppermute(message, "row", pairs + [(j, i) for i, j in pairs])


def sum_over_rows(mine, other):
    count = lax.axis_size("row")
    bits = count.bit_length() - 1
    mine = [m + swap_inner(o) for m, o in zip(mine, other)]
    for step in range(bits - 1):
        for stream in range(2):
            turn = [1 + (step + (core ^ stream)) % (bits - 1) for core in range(2)]
            pairs = [(i, i ^ (1 << turn[i & 1])) for i in range(count)]
            mine[stream] = mine[stream] + lax.ppermute(mine[stream], "row", pairs)
    return mine + [swap_inner(m) for m in mine]


def on_device(cell_coeffs, z_factor, noise_cols, q_bar, r_bar):
    quads, lattice, n, rank = z_factor.shape
    flat = quads * lattice * n
    coeffs = cell_coeffs
    core = (lax.axis_index("row") & 1).reshape(1)
    noise = noise_cols.reshape(flat, -1)
    bar = q_bar.reshape(flat, -1)
    shape = jax.ShapeDtypeStruct
    hops = shape((2 * n, rank), f32)
    rim = shape((2 * n + 8, rank), f32)
    table = shape((n, 16), f32)
    outer1, outer2, inner, table = call(
        forward_rim, (hops, rim, shape((4 * n + 8, rank), f32), table), 10**6, 3 * 10**6,
        [
            pltpu.VMEM(cell_coeffs.shape, f32),
            pltpu.VMEM((2, 3, n, rank), f32),
            pltpu.SemaphoreType.DMA((3,)),
        ],
        scalar=True, far=True,
    )(core, coeffs, z_factor)
    outer1, outer2, inner = swap_outer(outer1), swap_outer(outer2), swap_inner(inner)
    wide, tall = shape((flat, 256), bf16), shape((flat, 128), bf16)
    wide_t, tall_t = shape((256, flat), bf16), shape((128, flat), bf16)
    work = 2 * flat * 128 * 128
    pack, nh, nl, qh, ql, nht, nlt, qht, qlt = call(
        noise_products, (shape((136, 128), f32), tall, tall, wide, wide, tall_t, tall_t, wide_t, wide_t),
        work * 5, 9 * 10**6,
    )(noise, bar)
    transposed = (nht, nlt, qht, qlt)
    half, quarter = shape((flat // 2, 128), bf16), shape((flat // 4, 128), bf16)
    single, pair = shape((2, n, rank), f32), shape((2, lattice, n, rank), f32)
    light, hh, hl, lh, ll, gram, rest = call(
        expand_first,
        (single, half, half, quarter, quarter, shape((128, 128), f32), shape((384, 128), f32)),
        work * 8, 9 * 10**6, [pltpu.VMEM(z_factor.shape, f32)], scalar=True,
    )(core, table, z_factor, inner, outer1, *transposed)
    part1, part2 = shape((136, 128), f32), shape((128, 128), f32)
    *parts, oh, ol = call(
        expand_last, (part1, part2, part1, part2, quarter, quarter), work * 3, 5 * 10**6, [pltpu.VMEM((528, 128), f32)], scalar=True
    )(core, table, z_factor, outer2, light, gram, rest, pack, *transposed)
    parts = sum_over_rows(parts[:2], parts[2:])
    square = shape((256, 256), bf16)
    weights = call(
        factor, (square,) * 4, 10**9, 10**6,
        [
            pltpu.VMEM((528, 128), f32),
            pltpu.VMEM((128, 128), f32),
            pltpu.VMEM((128, 128), f32),
            pltpu.VMEM((128, 128), f32),
        ],
        scalar=True,
    )(core, *parts, r_bar)
    left = (qh, ql, nh, nl)
    w_outer, own1 = call(gradient_outer, (single, hops), work * 3, 3 * 10**6, scalar=True)(
        core, table, *left, oh, ol, *weights
    )
    back1 = swap_outer(own1)
    w_inner, w_heavy, own2, own = call(
        gradient_rest, (single, pair, hops, shape((4 * n, rank), f32)), 10**10, 6 * 10**6, scalar=True
    )(core, table, w_outer, own1, *left, lh, ll, hh, hl, *weights)
    back2, back = swap_outer(own2), swap_inner(own)
    noise_grad = call(gradient_noise, shape(noise_cols.shape, f32), 0, 0, scalar=True)(
        core, *left, oh, ol, lh, ll, hh, hl, *weights
    )
    out_light, out_heavy = call(contract_first, (pair, pair), 10**7, 6 * 10**6, [pltpu.VMEM(z_factor.shape, f32)])(
        table, w_outer, w_inner, w_heavy, own1, own, back1, back, outer2, inner
    )
    z_grad = call(contract_last, shape(z_factor.shape, f32), 10**6, 6 * 10**6, scalar=True)(
        core, out_light, out_heavy, back2
    )
    return z_grad, noise_grad


def solution(mesh):
    return jax.shard_map(
        on_device,
        mesh=mesh,
        in_specs=(
            P(None, "row", None),
            P(None, ("grp", "row"), None, None),
            P(None, ("grp", "row"), None, None),
            P(None, ("grp", "row"), None, None),
            P("grp", None),
        ),
        out_specs=(P(None, ("grp", "row"), None, None), P(None, ("grp", "row"), None, None)),
        check_vma=False,
    )
```

```python
import jax
import jax.numpy as jnp
from jax import lax
from jax.experimental import pallas as pl
from jax.experimental.pallas import tpu as pltpu
from jax.sharding import PartitionSpec as P

rate_scales = (0.4, 0.4, 0.1, 0.2, 0.1, 0.1)
exact = lax.Precision.HIGHEST
f32 = jnp.float32
bf16 = jnp.bfloat16
VMEM = pl.BlockSpec(memory_space=pltpu.VMEM)
LIMIT = 24 * 1024 * 1024
FAR_LIMIT = 63 * 1024 * 1024


def call(kernel, outs, flops, moved, scratch=(), scalar=False, far=False):
    def run(*args):
        specs = [pl.BlockSpec(memory_space=pltpu.HBM) if far else pl.BlockSpec() for _ in args]
        if scalar:
            specs[0] = pl.BlockSpec(memory_space=pltpu.SMEM)
        return pl.pallas_call(
            kernel,
            out_shape=outs,
            in_specs=specs,
            scratch_shapes=list(scratch),
            compiler_params=pltpu.CompilerParams(vmem_limit_bytes=FAR_LIMIT if far else LIMIT),
            cost_estimate=pl.CostEstimate(flops=flops, bytes_accessed=moved, transcendentals=0),
        )(*args)

    return run


def split2(value):
    high = value.astype(bf16)
    low = (value - high.astype(f32)).astype(bf16)
    return high, low


def split3(value):
    high = value.astype(bf16)
    rest = value - high.astype(f32)
    mid = rest.astype(bf16)
    low = (rest - mid.astype(f32)).astype(bf16)
    return high, mid, low


def dot(a, b, contract):
    return lax.dot_general(a, b, ((contract[0], contract[1]), ((), ())), preferred_element_type=f32)


def coefficients(table_ref):
    return [[table_ref[:, 6 * s + k : 6 * s + k + 1] for k in range(6)] for s in range(2)]


def side(v):
    n = v.shape[0]
    place = lax.broadcasted_iota(jnp.int32, v.shape, 0)
    left = jnp.where(place == 0, 0.0, pltpu.roll(v, 1, 0))
    right = jnp.where(place == n - 1, 0.0, pltpu.roll(v, n - 1, 0))
    return left + right


def forward_light(c, xa, pa, xb, hop_x, hop_p):
    d, w, g, l, m, j = c
    return (
        -0.5 * l * xa - d * pa - j * hop_p,
        d * xa - 0.5 * l * pa - 2.0 * g * xb + j * hop_x,
    )


def forward_heavy(c, xa, xb, pb):
    d, w, g, l, m, j = c
    return w * pb, -w * xb - 0.5 * m * pb - 2.0 * g * xa


def backward_light(c, xa, pa, pb, hop_x, hop_p):
    d, w, g, l, m, j = c
    return (
        -0.5 * l * xa + d * pa - 2.0 * g * pb + hop_p,
        -d * xa - 0.5 * l * pa - hop_x,
    )


def backward_heavy(c, pa, xb, pb):
    d, w, g, l, m, j = c
    return -2.0 * g * pa - w * pb, w * xb - 0.5 * m * pb


def forward_sources(core_ref, z_hbm, outer1_ref, sems):
    n = z_hbm.shape[2]
    copies = [
        pltpu.make_async_copy(z_hbm.at[k, core_ref[0]], outer1_ref.at[pl.ds(k * n, n)], sems.at[k]) for k in range(2)
    ]
    for copy in copies:
        copy.start()
    outer1_ref[2 * n :] = jnp.zeros((16, z_hbm.shape[3]), f32)
    for copy in copies:
        copy.wait()


def forward_rim(core_ref, coeff_ref, z_ref, outer2_ref, inner1_ref, inner2_ref, table_ref):
    n = z_ref.shape[2]
    core = core_ref[0]
    z = [[z_ref[k, row] for k in range(3)] for row in (core, 1 - core)]
    cols = jnp.transpose(jnp.concatenate([coeff_ref[k] for k in range(6)], axis=0))
    swapped = core == 1
    both = []
    for s in range(2):
        for k in range(6):
            column = jnp.where(swapped, cols[:, 2 * k + 1 - s : 2 * k + 2 - s], cols[:, 2 * k + s : 2 * k + s + 1])
            both.append(column * rate_scales[k])
    for place, column in enumerate(both):
        table_ref[:, place : place + 1] = column
    far = []
    for s in range(2):
        xa, pa, xb = z[s]
        hop_x = z[1 - s][0] + side(xa)
        hop_p = z[1 - s][1] + side(pa)
        far.append(forward_light(both[6 * s : 6 * s + 6], xa, pa, xb, hop_x, hop_p))
    inner1_ref[0:n] = z[1][0]
    inner1_ref[n : 2 * n] = z[1][1]
    for s, out in ((0, outer2_ref), (1, inner2_ref)):
        out[0:n], out[n : 2 * n] = far[s]
        hopping = jnp.where(swapped, coeff_ref[5, 1 - s : 2 - s, :], coeff_ref[5, s : s + 1, :]) * rate_scales[5]
        pieces = [hopping[:, k * 128 : (k + 1) * 128] for k in range(n // 128)]
        pieces.append(jnp.zeros((8 - n // 128, 128), f32))
        out[2 * n :] = jnp.concatenate(pieces, axis=0)


def far_hopping(recv_ref, n):
    size = recv_ref.shape[0]
    tail = jnp.transpose(recv_ref[size - 8 : size])
    return jnp.concatenate([tail[:, k : k + 1] for k in range(n // 128)], axis=0)


def cells(row, k, n):
    return pl.ds(pl.multiple_of((2 * k + row) * n, 128), n)


def packed(gram, cross):
    row = lax.broadcasted_iota(jnp.int32, gram.shape, 0)
    col = lax.broadcasted_iota(jnp.int32, gram.shape, 1)
    diagonal = jnp.sum(jnp.where(row == col, cross, 0.0), axis=0, keepdims=True)
    return jnp.where(row <= col, gram, cross), jnp.broadcast_to(diagonal, (8, gram.shape[1]))


def noise_products(noise_ref, q_ref, pack_ref, nh_ref, nl_ref, qh_ref, ql_ref, nht_ref, nlt_ref, qht_ref, qlt_ref):
    nh, nl = split2(noise_ref[...])
    qh, ql = split2(q_ref[...])
    nh_ref[...] = nh
    nl_ref[...] = nl
    qh_ref[...] = qh
    ql_ref[...] = ql
    for value, out in ((nh, nht_ref), (nl, nlt_ref), (qh, qht_ref), (ql, qlt_ref)):
        out[...] = jnp.transpose(value)
    plain = ((1,), (0,))
    high = dot(jnp.concatenate([nht_ref[...], qht_ref[128:]], axis=0), jnp.concatenate([nh, nl], axis=1), plain)
    low = dot(qlt_ref[128:], nh, plain)
    mixed = high[:128, 128:]
    gram = high[:128, :128] + mixed + jnp.transpose(mixed)
    cross = high[128:, :128] + high[128:, 128:] + low
    pack_ref[0:128], pack_ref[128:] = packed(gram, cross)


def row_products(xh, xl, nht, nlt, qht, qlt):
    plain = ((1,), (0,))
    left = jnp.concatenate([jnp.transpose(xh), nht, qht], axis=0)
    high = dot(left, jnp.concatenate([xh, xl], axis=1), plain)
    low = dot(jnp.concatenate([nlt, qlt], axis=0), xh, plain)
    mixed = high[:128, 128:]
    return (
        high[:128, :128] + mixed + jnp.transpose(mixed),
        high[128:, :128] + high[128:, 128:] + low,
    )


def expand_first(
    core_ref, table_ref, z_ref, outer1_ref, inner1_ref, inner2_ref, nht_ref, nlt_ref, qht_ref, qlt_ref,
    light_ref, hh_ref, hl_ref, ih_ref, il_ref, gram_ref, rest_ref, first_ref,
):
    c = coefficients(table_ref)
    n = z_ref.shape[2]
    core = core_ref[0]
    rows = (core, 1 - core)
    z = [[z_ref[k, row] for k in range(4)] for row in rows]
    for s, beyond in enumerate((outer1_ref, inner1_ref)):
        xa, pa, xb, pb = z[s]
        hop_x = z[1 - s][0] + beyond[0:n] + side(xa)
        hop_p = z[1 - s][1] + beyond[n : 2 * n] + side(pa)
        first_ref[0, s], first_ref[1, s] = forward_light(c[s], xa, pa, xb, hop_x, hop_p)
        first_ref[2, s], first_ref[3, s] = forward_heavy(c[s], xa, xb, pb)
    for s in range(2):
        xa, pa, xb, pb = (first_ref[k, s] for k in range(4))
        for k, (f, second) in enumerate(zip((xb, pb), forward_heavy(c[s], xa, xb, pb))):
            h, l = split2(z[s][2 + k] + f + 0.5 * second)
            hh_ref[cells(rows[s], k, n)] = h
            hl_ref[cells(rows[s], k, n)] = l
    jfar = far_hopping(inner2_ref, n)
    for s in range(2):
        xa, pa, xb, pb = (first_ref[k, s] for k in range(4))
        hop_x = first_ref[0, 1 - s] + side(xa)
        hop_p = first_ref[1, 1 - s] + side(pa)
        if s == 1:
            hop_x = hop_x + inner2_ref[0:n] - jfar * z[s][1]
            hop_p = hop_p + inner2_ref[n : 2 * n] + jfar * z[s][0]
        second = forward_light(c[s], xa, pa, xb, hop_x, hop_p)
        for k in range(2):
            value = z[s][k] + first_ref[k, s] + 0.5 * second[k]
            if s == 0:
                light_ref[k] = value
            else:
                ih_ref[k * n : (k + 1) * n], il_ref[k * n : (k + 1) * n] = split2(value)
    half = 4 * n
    parts = (nht_ref, nlt_ref, qht_ref, qlt_ref)
    gram, rest = row_products(hh_ref[...], hl_ref[...], *(ref[:, half:] for ref in parts))
    for k in range(2):
        there = cells(1 - core, k, n)
        here = slice(k * n, (k + 1) * n)
        more = row_products(ih_ref[here], il_ref[here], *(ref[:, there] for ref in parts))
        gram = gram + more[0]
        rest = rest + more[1]
    gram_ref[...] = gram
    rest_ref[...] = rest


def quarters(core):
    parts = []
    for owner in (core, 1 - core):
        first = pl.multiple_of(owner * 264, 8)
        parts += [pl.ds(first, 136), pl.ds(pl.multiple_of(first + 136, 8), 128)]
    return parts


def expand_last(
    core_ref, table_ref, z_ref, outer2_ref, light_ref, gram_ref, rest_ref, pack_ref,
    nht_ref, nlt_ref, qht_ref, qlt_ref, mine1_ref, mine2_ref, other1_ref, other2_ref, oh_ref, ol_ref, sums_ref,
):
    n = z_ref.shape[2]
    core = core_ref[0]
    jfar = far_hopping(outer2_ref, n)
    far_x = outer2_ref[0:n] - jfar * z_ref[1, core]
    far_p = outer2_ref[n : 2 * n] + jfar * z_ref[0, core]
    j = 0.5 * table_ref[:, 5:6]
    gram, rest = gram_ref[...], rest_ref[...]
    for k, value in enumerate((light_ref[0] - j * far_p, light_ref[1] + j * far_x)):
        h, l = split2(value)
        oh_ref[k * n : (k + 1) * n] = h
        ol_ref[k * n : (k + 1) * n] = l
        there = cells(core, k, n)
        more = row_products(h, l, *(ref[:, there] for ref in (nht_ref, nlt_ref, qht_ref, qlt_ref)))
        gram = gram + more[0]
        rest = rest + more[1]
    sums_ref[0:128], sums_ref[512:520] = packed(gram, rest[128:256])
    sums_ref[128:256] = jnp.transpose(rest[:128])
    sums_ref[256:384] = rest[256:]
    sums_ref[384:512] = pack_ref[0:128]
    sums_ref[520:528] = pack_ref[128:136]
    for part, out in zip(quarters(core), (mine1_ref, mine2_ref, other1_ref, other2_ref)):
        out[...] = sums_ref[part]


def inverse_factor(w_ref, out_ref):
    size = w_ref.shape[0]
    step = 8
    lane = lax.broadcasted_iota(jnp.int32, (step, size), 1)
    place = lax.broadcasted_iota(jnp.int32, (step, size), 0)

    def load(start):
        return [jnp.broadcast_to(w_ref[start + i : start + i + 1, :], (step, size)) for i in range(step)]

    rows = load(0)
    for start in range(0, size, step):
        last = start + step >= size
        reach = step if last else 2 * step
        s = {
            (i, m): jnp.broadcast_to(rows[i][:, start + m : start + m + 1], (step, size))
            for i in range(step)
            for m in range(i, reach)
        }
        inside = (lane >= start) & (lane < start + step)
        rows = [jnp.where(lane == start + i, 1.0, jnp.where(inside, 0.0, rows[i])) for i in range(step)]
        if not last:
            following = [jnp.where(inside, 0.0, row) for row in load(start + step)]
        done = []
        for i in range(step):
            inverse = pl.reciprocal(s[i, i])
            root = lax.rsqrt(s[i, i])
            for k in range(i + 1, step):
                ratio = s[i, k] * inverse
                for m in range(k, reach):
                    s[k, m] = s[k, m] - ratio * s[i, m]
                rows[k] = rows[k] - ratio * rows[i]
            if not last:
                scaled = rows[i] * inverse
                for k in range(step):
                    following[k] = following[k] - s[i, step + k] * scaled
            done.append(rows[i] * root)
        panel = done[0]
        for i in range(1, step):
            panel = jnp.where(place == i, done[i], panel)
        out_ref[start : start + step, :] = panel
        beyond = start + 2 * step
        if beyond < size:
            high, mid, low = (part.astype(f32) for part in split3(panel))
            left = jnp.concatenate([high, high, mid, mid, high, low], axis=0).astype(bf16)
            right = jnp.concatenate([high, mid, high, mid, low, high], axis=0).astype(bf16)
            change = dot(left, right, ((0,), (0,)))[beyond:]
            old = w_ref[beyond:, :]
            column = lax.broadcasted_iota(jnp.int32, old.shape, 1)
            old = jnp.where((column >= start) & (column < start + step), 0.0, old)
            w_ref[beyond:, :] = old - change
        if not last:
            rows = following
    value = out_ref[...]
    row = lax.broadcasted_iota(jnp.int32, value.shape, 0)
    column = lax.broadcasted_iota(jnp.int32, value.shape, 1)
    out_ref[...] = jnp.where(row >= column, value, 0.0)


def factor(
    core_ref, mine1_ref, mine2_ref, other1_ref, other2_ref, r_bar_ref, nh_ref, nl_ref, sh_ref, sl_ref, sums_ref, w_ref, inv1_ref, inv2_ref
):
    tile = 128
    core = core_ref[0]
    for part, value in zip(quarters(core), (mine1_ref, mine2_ref, other1_ref, other2_ref)):
        sums_ref[part] = value[...]

    def product(a, b, contract):
        return lax.dot_general(a, b, ((contract[0], contract[1]), ((), ())), precision=exact, preferred_element_type=f32)

    down, across, plain = ((0,), (0,)), ((1,), (1,)), ((1,), (0,))
    row = lax.broadcasted_iota(jnp.int32, (2 * tile, 2 * tile), 0)
    col = lax.broadcasted_iota(jnp.int32, (2 * tile, 2 * tile), 1)

    def corner(value, keep):
        return jnp.where(keep[:tile, :tile], value, 0.0)

    def whole(value):
        return corner(value, row <= col) + jnp.transpose(corner(value, row < col))

    pack1, g12, pack2 = sums_ref[0:tile], sums_ref[tile : 2 * tile], sums_ref[3 * tile : 4 * tile]
    w_ref[...] = corner(pack1, row <= col)
    inverse_factor(w_ref, inv1_ref)
    inv1 = inv1_ref[...]
    u12 = product(inv1, g12, plain)
    w_ref[...] = corner(pack2, row <= col) - product(u12, u12, down)
    inverse_factor(w_ref, inv2_ref)
    inv2 = inv2_ref[...]
    inv21 = -product(inv2, product(u12, inv1, down), plain)
    zero = jnp.zeros((tile, tile), f32)
    inv = jnp.concatenate(
        [jnp.concatenate([inv1, zero], axis=1), jnp.concatenate([inv21, inv2], axis=1)], axis=0
    )
    gram = jnp.concatenate(
        [
            jnp.concatenate([whole(pack1), g12], axis=1),
            jnp.concatenate([jnp.transpose(g12), whole(pack2)], axis=1),
        ],
        axis=0,
    )
    bar = jnp.where(row <= col, r_bar_ref[...], 0.0)
    top = jnp.concatenate([pack1, zero], axis=1)
    bottom = jnp.concatenate([sums_ref[2 * tile : 3 * tile], pack2], axis=1)
    cross = jnp.concatenate([top, bottom], axis=0)
    diagonal = jnp.concatenate([sums_ref[512:513], sums_ref[520:521]], axis=1)
    cross = jnp.where(row > col, cross, jnp.where(row == col, diagonal, 0.0))
    middle = product(inv, product(gram, bar, across), plain) - product(cross, inv, across)
    symmetric = jnp.where(row >= col, middle, 0.0) + jnp.transpose(jnp.where(row > col, middle, 0.0))
    spread = product(inv, product(symmetric, inv, plain), down)
    nh_ref[...], nl_ref[...] = split2(inv)
    sh_ref[...], sl_ref[...] = split2(spread)


def columns(qh, ql, nh, nl, xh, xl, ih, il, sh, sl):
    plain = ((1,), (0,))
    xh = jnp.concatenate([xh, nh], axis=1)
    xl = jnp.concatenate([xl, nl], axis=1)
    high = dot(qh, jnp.concatenate([ih, il], axis=1), plain) + dot(xh, jnp.concatenate([sh, sl], axis=1), plain)
    return high[:, :128] + high[:, 128:] + dot(ql, ih, plain) + dot(xl, sh, plain)


def gradient_outer(
    core_ref, table_ref, qh_ref, ql_ref, nh_ref, nl_ref, oh_ref, ol_ref, ih_ref, il_ref, sh_ref, sl_ref,
    w_ref, outer1_ref,
):
    n = w_ref.shape[1]
    j = table_ref[:, 5:6]
    weights = [ref[:, :128] for ref in (ih_ref, il_ref, sh_ref, sl_ref)]
    for k in range(2):
        there = cells(core_ref[0], k, n)
        here = slice(k * n, (k + 1) * n)
        parts = [ref[there] for ref in (qh_ref, ql_ref, nh_ref, nl_ref)] + [oh_ref[here], ol_ref[here]]
        w = columns(*parts, *weights)
        w_ref[k] = w
        outer1_ref[here] = j * w
    outer1_ref[2 * n :] = jnp.zeros((8, w_ref.shape[2]), f32)


def gradient_rest(
    core_ref, table_ref, outer_ref, outer1_ref, qh_ref, ql_ref, nh_ref, nl_ref, lh_ref, ll_ref, hh_ref, hl_ref,
    ih_ref, il_ref, sh_ref, sl_ref, light_ref, heavy_ref, outer2_ref, inner1_ref, inner2_ref,
):
    c = coefficients(table_ref)
    n = outer_ref.shape[1]
    core = core_ref[0]
    weights = [ref[:, :128] for ref in (ih_ref, il_ref, sh_ref, sl_ref)]
    left = (qh_ref, ql_ref, nh_ref, nl_ref)
    for k in range(2):
        there = cells(1 - core, k, n)
        here = slice(k * n, (k + 1) * n)
        w = columns(*[ref[there] for ref in left], lh_ref[here], ll_ref[here], *weights)
        light_ref[k] = w
        inner1_ref[here] = c[1][5] * w
    for k in (1, 0):
        for s, row in enumerate((core, 1 - core)):
            there = cells(row, 2 + k, n)
            here = cells(row, k, n)
            heavy_ref[k, s] = columns(*[ref[there] for ref in left], hh_ref[here], hl_ref[here], *weights)
    own = (outer1_ref, inner1_ref)
    for s, w, out in ((0, outer_ref, outer2_ref), (1, light_ref, inner2_ref)):
        hop_x = own[1 - s][0:n] + side(own[s][0:n])
        hop_p = own[1 - s][n : 2 * n] + side(own[s][n : 2 * n])
        bx, bp = backward_light(c[s], w[0], w[1], heavy_ref[1, s], hop_x, hop_p)
        out[0:n] = c[s][5] * bx
        out[n : 2 * n] = c[s][5] * bp


def gradient_noise(
    core_ref, qh_ref, ql_ref, nh_ref, nl_ref, oh_ref, ol_ref, lh_ref, ll_ref, hh_ref, hl_ref,
    ih_ref, il_ref, sh_ref, sl_ref, out_ref,
):
    n = out_ref.shape[2]
    core = core_ref[0]
    weights = [ref[:, 128:] for ref in (ih_ref, il_ref, sh_ref, sl_ref)]
    for k in range(4):
        for s, row in enumerate((core, 1 - core)):
            there = cells(row, k, n)
            if k < 2:
                here = slice(k * n, (k + 1) * n)
                x = (oh_ref[here], ol_ref[here]) if s == 0 else (lh_ref[here], ll_ref[here])
            else:
                here = cells(row, k - 2, n)
                x = (hh_ref[here], hl_ref[here])
            out_ref[k, row] = columns(*[ref[there] for ref in (qh_ref, ql_ref, nh_ref, nl_ref)], *x, *weights)


def contract_first(
    outer1_ref, table_ref, outer_ref, light_ref, heavy_ref, own1_ref, own2_ref, inner1_ref, inner2_ref,
    fouter2_ref, finner_ref,
    out_light_ref, out_heavy_ref, first_ref,
):
    c = coefficients(table_ref)
    n = outer_ref.shape[1]
    w = [
        (outer_ref[0], outer_ref[1], heavy_ref[0, 0], heavy_ref[1, 0]),
        (light_ref[0], light_ref[1], heavy_ref[0, 1], heavy_ref[1, 1]),
    ]
    own = [(ref[0:n], ref[n : 2 * n]) for ref in (own1_ref, own2_ref)]
    for s, far in enumerate((outer1_ref, inner1_ref)):
        xa, pa, xb, pb = w[s]
        hop_x = own[1 - s][0] + far[0:n] + side(own[s][0])
        hop_p = own[1 - s][1] + far[n : 2 * n] + side(own[s][1])
        first_ref[0, s], first_ref[1, s] = backward_light(c[s], xa, pa, pb, hop_x, hop_p)
        first_ref[2, s], first_ref[3, s] = backward_heavy(c[s], pa, xb, pb)
    for s, fref in enumerate((fouter2_ref, finner_ref)):
        xa, pa, xb, pb = (first_ref[k, s] for k in range(4))
        jfar = far_hopping(fref, n)
        j, jother = c[s][5], c[1 - s][5]
        hop_x = jother * first_ref[0, 1 - s] + jfar * own[s][1] + side(j * xa)
        hop_p = jother * first_ref[1, 1 - s] - jfar * own[s][0] + side(j * pa)
        if s == 1:
            hop_x = hop_x + inner2_ref[0:n]
            hop_p = hop_p + inner2_ref[n : 2 * n]
        light = backward_light(c[s], xa, pa, pb, hop_x, hop_p)
        heavy = backward_heavy(c[s], pa, xb, pb)
        for k in range(2):
            out_light_ref[k, s] = w[s][k] + first_ref[k, s] + 0.5 * light[k]
            out_heavy_ref[k, s] = w[s][2 + k] + first_ref[2 + k, s] + 0.5 * heavy[k]


def contract_last(core_ref, light_ref, heavy_ref, outer2_ref, out_ref):
    n = out_ref.shape[2]
    core = core_ref[0]
    out_ref[0, core] = light_ref[0, 0] + 0.5 * outer2_ref[n : 2 * n]
    out_ref[1, core] = light_ref[1, 0] - 0.5 * outer2_ref[0:n]
    for k in range(2):
        out_ref[k, 1 - core] = light_ref[k, 1]
        out_ref[2 + k, core] = heavy_ref[k, 0]
        out_ref[2 + k, 1 - core] = heavy_ref[k, 1]


def swap_inner(message):
    count = lax.axis_size("row")
    return lax.ppermute(message, "row", [(i, i ^ 1) for i in range(count)])


def swap_outer(message):
    count = lax.axis_size("row")
    pairs = [(i, i + 1) for i in range(1, count - 1, 2)]
    return lax.ppermute(message, "row", pairs + [(j, i) for i, j in pairs])


def sum_over_rows(mine, other):
    count = lax.axis_size("row")
    bits = count.bit_length() - 1
    mine = [m + swap_inner(o) for m, o in zip(mine, other)]
    for step in range(bits - 1):
        for stream in range(2):
            turn = [1 + (step + (core ^ stream)) % (bits - 1) for core in range(2)]
            pairs = [(i, i ^ (1 << turn[i & 1])) for i in range(count)]
            mine[stream] = mine[stream] + lax.ppermute(mine[stream], "row", pairs)
    return mine + [swap_inner(m) for m in mine]


def on_device(cell_coeffs, z_factor, noise_cols, q_bar, r_bar):
    quads, lattice, n, rank = z_factor.shape
    flat = quads * lattice * n
    coeffs = cell_coeffs
    core = (lax.axis_index("row") & 1).reshape(1)
    noise = noise_cols.reshape(flat, -1)
    bar = q_bar.reshape(flat, -1)
    shape = jax.ShapeDtypeStruct
    hops = shape((2 * n, rank), f32)
    rim = shape((2 * n + 8, rank), f32)
    table = shape((n, 16), f32)
    outer1 = call(
        forward_sources, shape((2 * n + 16, rank), f32), 0, 10**6, [pltpu.SemaphoreType.DMA((2,))], scalar=True, far=True
    )(core, z_factor)
    outer1, behind = lax.optimization_barrier((outer1, core))
    outer2, inner1, inner2, table = call(
        forward_rim, (rim, hops, rim, table), 10**6, 3 * 10**6, scalar=True
    )(behind, coeffs, z_factor)
    outer1, outer2 = swap_outer(outer1), swap_outer(outer2)
    inner1, inner2 = swap_inner(inner1), swap_inner(inner2)
    wide, tall = shape((flat, 256), bf16), shape((flat, 128), bf16)
    wide_t, tall_t = shape((256, flat), bf16), shape((128, flat), bf16)
    work = 2 * flat * 128 * 128
    pack, nh, nl, qh, ql, nht, nlt, qht, qlt = call(
        noise_products, (shape((136, 128), f32), tall, tall, wide, wide, tall_t, tall_t, wide_t, wide_t),
        work * 5, 9 * 10**6,
    )(noise, bar)
    transposed = (nht, nlt, qht, qlt)
    half, quarter = shape((flat // 2, 128), bf16), shape((flat // 4, 128), bf16)
    single, pair = shape((2, n, rank), f32), shape((2, lattice, n, rank), f32)
    light, hh, hl, lh, ll, gram, rest = call(
        expand_first,
        (single, half, half, quarter, quarter, shape((128, 128), f32), shape((384, 128), f32)),
        work * 8, 9 * 10**6, [pltpu.VMEM(z_factor.shape, f32)], scalar=True,
    )(core, table, z_factor, outer1, inner1, inner2, *transposed)
    part1, part2 = shape((136, 128), f32), shape((128, 128), f32)
    *parts, oh, ol = call(
        expand_last, (part1, part2, part1, part2, quarter, quarter), work * 3, 5 * 10**6, [pltpu.VMEM((528, 128), f32)], scalar=True
    )(core, table, z_factor, outer2, light, gram, rest, pack, *transposed)
    parts = sum_over_rows(parts[:2], parts[2:])
    square = shape((256, 256), bf16)
    weights = call(
        factor, (square,) * 4, 10**9, 10**6,
        [
            pltpu.VMEM((528, 128), f32),
            pltpu.VMEM((128, 128), f32),
            pltpu.VMEM((128, 128), f32),
            pltpu.VMEM((128, 128), f32),
        ],
        scalar=True,
    )(core, *parts, r_bar)
    left = (qh, ql, nh, nl)
    w_outer, own1 = call(gradient_outer, (single, rim), work * 3, 3 * 10**6, scalar=True)(
        core, table, *left, oh, ol, *weights
    )
    back1 = swap_outer(own1)
    w_inner, w_heavy, last, own2, own3 = call(
        gradient_rest, (single, pair, hops, hops, hops), 10**10, 6 * 10**6, scalar=True
    )(core, table, w_outer, own1, *left, lh, ll, hh, hl, *weights)
    back2, near1, near2 = swap_outer(last), swap_inner(own2), swap_inner(own3)
    noise_grad = call(gradient_noise, shape(noise_cols.shape, f32), 0, 0, scalar=True)(
        core, *left, oh, ol, lh, ll, hh, hl, *weights
    )
    out_light, out_heavy = call(contract_first, (pair, pair), 10**7, 6 * 10**6, [pltpu.VMEM(z_factor.shape, f32)])(
        back1, table, w_outer, w_inner, w_heavy, own1, own2, near1, near2, outer2, inner2
    )
    z_grad = call(contract_last, shape(z_factor.shape, f32), 10**6, 6 * 10**6, scalar=True)(
        core, out_light, out_heavy, back2
    )
    return z_grad, noise_grad


def solution(mesh):
    return jax.shard_map(
        on_device,
        mesh=mesh,
        in_specs=(
            P(None, "row", None),
            P(None, ("grp", "row"), None, None),
            P(None, ("grp", "row"), None, None),
            P(None, ("grp", "row"), None, None),
            P("grp", None),
        ),
        out_specs=(P(None, ("grp", "row"), None, None), P(None, ("grp", "row"), None, None)),
        check_vma=False,
    )
```

```python
import jax
import jax.numpy as jnp
from jax import lax
from jax.experimental import pallas as pl
from jax.experimental.pallas import tpu as pltpu
from jax.sharding import PartitionSpec as P

rate_scales = (0.4, 0.4, 0.1, 0.2, 0.1, 0.1)
exact = lax.Precision.HIGHEST
f32 = jnp.float32
bf16 = jnp.bfloat16
VMEM = pl.BlockSpec(memory_space=pltpu.VMEM)
LIMIT = 24 * 1024 * 1024
FAR_LIMIT = 63 * 1024 * 1024


def call(kernel, outs, flops, moved, scratch=(), scalar=False, far=False):
    def run(*args):
        specs = [pl.BlockSpec(memory_space=pltpu.HBM) if far else pl.BlockSpec() for _ in args]
        if scalar:
            specs[0] = pl.BlockSpec(memory_space=pltpu.SMEM)
        return pl.pallas_call(
            kernel,
            out_shape=outs,
            in_specs=specs,
            scratch_shapes=list(scratch),
            compiler_params=pltpu.CompilerParams(vmem_limit_bytes=FAR_LIMIT if far else LIMIT),
            cost_estimate=pl.CostEstimate(flops=flops, bytes_accessed=moved, transcendentals=0),
        )(*args)

    return run


def split2(value):
    high = value.astype(bf16)
    low = (value - high.astype(f32)).astype(bf16)
    return high, low


def split3(value):
    high = value.astype(bf16)
    rest = value - high.astype(f32)
    mid = rest.astype(bf16)
    low = (rest - mid.astype(f32)).astype(bf16)
    return high, mid, low


def dot(a, b, contract):
    return lax.dot_general(a, b, ((contract[0], contract[1]), ((), ())), preferred_element_type=f32)


def coefficients(table_ref):
    return [[table_ref[:, 6 * s + k : 6 * s + k + 1] for k in range(6)] for s in range(2)]


def side(v):
    n = v.shape[0]
    place = lax.broadcasted_iota(jnp.int32, v.shape, 0)
    left = jnp.where(place == 0, 0.0, pltpu.roll(v, 1, 0))
    right = jnp.where(place == n - 1, 0.0, pltpu.roll(v, n - 1, 0))
    return left + right


def forward_light(c, xa, pa, xb, hop_x, hop_p):
    d, w, g, l, m, j = c
    return (
        -0.5 * l * xa - d * pa - j * hop_p,
        d * xa - 0.5 * l * pa - 2.0 * g * xb + j * hop_x,
    )


def forward_heavy(c, xa, xb, pb):
    d, w, g, l, m, j = c
    return w * pb, -w * xb - 0.5 * m * pb - 2.0 * g * xa


def backward_light(c, xa, pa, pb, hop_x, hop_p):
    d, w, g, l, m, j = c
    return (
        -0.5 * l * xa + d * pa - 2.0 * g * pb + hop_p,
        -d * xa - 0.5 * l * pa - hop_x,
    )


def backward_heavy(c, pa, xb, pb):
    d, w, g, l, m, j = c
    return -2.0 * g * pa - w * pb, w * xb - 0.5 * m * pb


def forward_sources(core_ref, z_hbm, outer1_ref, sems):
    n = z_hbm.shape[2]
    copies = [
        pltpu.make_async_copy(z_hbm.at[k, core_ref[0]], outer1_ref.at[pl.ds(k * n, n)], sems.at[k]) for k in range(2)
    ]
    for copy in copies:
        copy.start()
    outer1_ref[2 * n :] = jnp.zeros((16, z_hbm.shape[3]), f32)
    for copy in copies:
        copy.wait()


def forward_rim(core_ref, coeff_ref, z_ref, outer2_ref, inner1_ref, inner2_ref, table_ref):
    n = z_ref.shape[2]
    core = core_ref[0]
    z = [[z_ref[k, row] for k in range(3)] for row in (core, 1 - core)]
    cols = jnp.transpose(jnp.concatenate([coeff_ref[k] for k in range(6)], axis=0))
    swapped = core == 1
    both = []
    for s in range(2):
        for k in range(6):
            column = jnp.where(swapped, cols[:, 2 * k + 1 - s : 2 * k + 2 - s], cols[:, 2 * k + s : 2 * k + s + 1])
            both.append(column * rate_scales[k])
    for place, column in enumerate(both):
        table_ref[:, place : place + 1] = column
    far = []
    for s in range(2):
        xa, pa, xb = z[s]
        hop_x = z[1 - s][0] + side(xa)
        hop_p = z[1 - s][1] + side(pa)
        far.append(forward_light(both[6 * s : 6 * s + 6], xa, pa, xb, hop_x, hop_p))
    inner1_ref[0:n] = z[1][0]
    inner1_ref[n : 2 * n] = z[1][1]
    for s, out in ((0, outer2_ref), (1, inner2_ref)):
        out[0:n], out[n : 2 * n] = far[s]
        hopping = jnp.where(swapped, coeff_ref[5, 1 - s : 2 - s, :], coeff_ref[5, s : s + 1, :]) * rate_scales[5]
        pieces = [hopping[:, k * 128 : (k + 1) * 128] for k in range(n // 128)]
        pieces.append(jnp.zeros((8 - n // 128, 128), f32))
        out[2 * n :] = jnp.concatenate(pieces, axis=0)


def far_hopping(recv_ref, n):
    size = recv_ref.shape[0]
    tail = jnp.transpose(recv_ref[size - 8 : size])
    return jnp.concatenate([tail[:, k : k + 1] for k in range(n // 128)], axis=0)


def cells(row, k, n):
    return pl.ds(pl.multiple_of((2 * k + row) * n, 128), n)


def packed(gram, cross):
    row = lax.broadcasted_iota(jnp.int32, gram.shape, 0)
    col = lax.broadcasted_iota(jnp.int32, gram.shape, 1)
    diagonal = jnp.sum(jnp.where(row == col, cross, 0.0), axis=0, keepdims=True)
    return jnp.where(row <= col, gram, cross), jnp.broadcast_to(diagonal, (8, gram.shape[1]))


def noise_products(noise_ref, q_ref, pack_ref, nh_ref, nl_ref, qh_ref, ql_ref, nht_ref, nlt_ref, qht_ref, qlt_ref):
    nh, nl = split2(noise_ref[...])
    qh, ql = split2(q_ref[...])
    nh_ref[...] = nh
    nl_ref[...] = nl
    qh_ref[...] = qh
    ql_ref[...] = ql
    for value, out in ((nh, nht_ref), (nl, nlt_ref), (qh, qht_ref), (ql, qlt_ref)):
        out[...] = jnp.transpose(value)
    plain = ((1,), (0,))
    high = dot(jnp.concatenate([nht_ref[...], qht_ref[128:]], axis=0), jnp.concatenate([nh, nl], axis=1), plain)
    low = dot(qlt_ref[128:], nh, plain)
    mixed = high[:128, 128:]
    gram = high[:128, :128] + mixed + jnp.transpose(mixed)
    cross = high[128:, :128] + high[128:, 128:] + low
    pack_ref[0:128], pack_ref[128:] = packed(gram, cross)


def row_products(xh, xl, nht, nlt, qht, qlt):
    plain = ((1,), (0,))
    left = jnp.concatenate([jnp.transpose(xh), nht, qht], axis=0)
    high = dot(left, jnp.concatenate([xh, xl], axis=1), plain)
    low = dot(jnp.concatenate([nlt, qlt], axis=0), xh, plain)
    mixed = high[:128, 128:]
    return (
        high[:128, :128] + mixed + jnp.transpose(mixed),
        high[128:, :128] + high[128:, 128:] + low,
    )


def expand_first(
    core_ref, table_ref, z_ref, outer1_ref, inner1_ref, inner2_ref, nht_ref, nlt_ref, qht_ref, qlt_ref,
    light_ref, hh_ref, hl_ref, ih_ref, il_ref, gram_ref, rest_ref, first_ref,
):
    c = coefficients(table_ref)
    n = z_ref.shape[2]
    core = core_ref[0]
    rows = (core, 1 - core)
    z = [[z_ref[k, row] for k in range(4)] for row in rows]
    for s, beyond in enumerate((outer1_ref, inner1_ref)):
        xa, pa, xb, pb = z[s]
        hop_x = z[1 - s][0] + beyond[0:n] + side(xa)
        hop_p = z[1 - s][1] + beyond[n : 2 * n] + side(pa)
        first_ref[0, s], first_ref[1, s] = forward_light(c[s], xa, pa, xb, hop_x, hop_p)
        first_ref[2, s], first_ref[3, s] = forward_heavy(c[s], xa, xb, pb)
    for s in range(2):
        xa, pa, xb, pb = (first_ref[k, s] for k in range(4))
        for k, (f, second) in enumerate(zip((xb, pb), forward_heavy(c[s], xa, xb, pb))):
            h, l = split2(z[s][2 + k] + f + 0.5 * second)
            hh_ref[cells(rows[s], k, n)] = h
            hl_ref[cells(rows[s], k, n)] = l
    jfar = far_hopping(inner2_ref, n)
    for s in range(2):
        xa, pa, xb, pb = (first_ref[k, s] for k in range(4))
        hop_x = first_ref[0, 1 - s] + side(xa)
        hop_p = first_ref[1, 1 - s] + side(pa)
        if s == 1:
            hop_x = hop_x + inner2_ref[0:n] - jfar * z[s][1]
            hop_p = hop_p + inner2_ref[n : 2 * n] + jfar * z[s][0]
        second = forward_light(c[s], xa, pa, xb, hop_x, hop_p)
        for k in range(2):
            value = z[s][k] + first_ref[k, s] + 0.5 * second[k]
            if s == 0:
                light_ref[k] = value
            else:
                ih_ref[k * n : (k + 1) * n], il_ref[k * n : (k + 1) * n] = split2(value)
    half = 4 * n
    parts = (nht_ref, nlt_ref, qht_ref, qlt_ref)
    gram, rest = row_products(hh_ref[...], hl_ref[...], *(ref[:, half:] for ref in parts))
    for k in range(2):
        there = cells(1 - core, k, n)
        here = slice(k * n, (k + 1) * n)
        more = row_products(ih_ref[here], il_ref[here], *(ref[:, there] for ref in parts))
        gram = gram + more[0]
        rest = rest + more[1]
    gram_ref[...] = gram
    rest_ref[...] = rest


def quarters(core):
    parts = []
    for owner in (core, 1 - core):
        first = pl.multiple_of(owner * 264, 8)
        parts += [pl.ds(first, 136), pl.ds(pl.multiple_of(first + 136, 8), 128)]
    return parts


def expand_last(
    core_ref, table_ref, z_ref, outer2_ref, light_ref, gram_ref, rest_ref, pack_ref,
    nht_ref, nlt_ref, qht_ref, qlt_ref, mine1_ref, mine2_ref, other1_ref, other2_ref, oh_ref, ol_ref, sums_ref,
):
    n = z_ref.shape[2]
    core = core_ref[0]
    jfar = far_hopping(outer2_ref, n)
    far_x = outer2_ref[0:n] - jfar * z_ref[1, core]
    far_p = outer2_ref[n : 2 * n] + jfar * z_ref[0, core]
    j = 0.5 * table_ref[:, 5:6]
    gram, rest = gram_ref[...], rest_ref[...]
    for k, value in enumerate((light_ref[0] - j * far_p, light_ref[1] + j * far_x)):
        h, l = split2(value)
        oh_ref[k * n : (k + 1) * n] = h
        ol_ref[k * n : (k + 1) * n] = l
        there = cells(core, k, n)
        more = row_products(h, l, *(ref[:, there] for ref in (nht_ref, nlt_ref, qht_ref, qlt_ref)))
        gram = gram + more[0]
        rest = rest + more[1]
    sums_ref[0:128], sums_ref[512:520] = packed(gram, rest[128:256])
    sums_ref[128:256] = jnp.transpose(rest[:128])
    sums_ref[256:384] = rest[256:]
    sums_ref[384:512] = pack_ref[0:128]
    sums_ref[520:528] = pack_ref[128:136]
    for part, out in zip(quarters(core), (mine1_ref, mine2_ref, other1_ref, other2_ref)):
        out[...] = sums_ref[part]


def inverse_factor(w_ref, out_ref):
    size = w_ref.shape[0]
    step = 8
    lane = lax.broadcasted_iota(jnp.int32, (step, size), 1)
    place = lax.broadcasted_iota(jnp.int32, (step, size), 0)

    def load(start):
        return [jnp.broadcast_to(w_ref[start + i : start + i + 1, :], (step, size)) for i in range(step)]

    rows = load(0)
    for start in range(0, size, step):
        last = start + step >= size
        reach = step if last else 2 * step
        s = {
            (i, m): jnp.broadcast_to(rows[i][:, start + m : start + m + 1], (step, size))
            for i in range(step)
            for m in range(i, reach)
        }
        inside = (lane >= start) & (lane < start + step)
        rows = [jnp.where(lane == start + i, 1.0, jnp.where(inside, 0.0, rows[i])) for i in range(step)]
        if not last:
            following = [jnp.where(inside, 0.0, row) for row in load(start + step)]
        done = []
        for i in range(step):
            inverse = pl.reciprocal(s[i, i])
            root = lax.rsqrt(s[i, i])
            for k in range(i + 1, step):
                ratio = s[i, k] * inverse
                for m in range(k, reach):
                    s[k, m] = s[k, m] - ratio * s[i, m]
                rows[k] = rows[k] - ratio * rows[i]
            if not last:
                scaled = rows[i] * inverse
                for k in range(step):
                    following[k] = following[k] - s[i, step + k] * scaled
            done.append(rows[i] * root)
        panel = done[0]
        for i in range(1, step):
            panel = jnp.where(place == i, done[i], panel)
        out_ref[start : start + step, :] = panel
        beyond = start + 2 * step
        if beyond < size:
            high, mid, low = (part.astype(f32) for part in split3(panel))
            left = jnp.concatenate([high, high, mid, mid, high, low], axis=0).astype(bf16)
            right = jnp.concatenate([high, mid, high, mid, low, high], axis=0).astype(bf16)
            change = dot(left, right, ((0,), (0,)))[beyond:]
            old = w_ref[beyond:, :]
            column = lax.broadcasted_iota(jnp.int32, old.shape, 1)
            old = jnp.where((column >= start) & (column < start + step), 0.0, old)
            w_ref[beyond:, :] = old - change
        if not last:
            rows = following
    value = out_ref[...]
    row = lax.broadcasted_iota(jnp.int32, value.shape, 0)
    column = lax.broadcasted_iota(jnp.int32, value.shape, 1)
    out_ref[...] = jnp.where(row >= column, value, 0.0)


def factor(
    core_ref, mine1_ref, mine2_ref, other1_ref, other2_ref, r_bar_ref, nh_ref, nl_ref, sh_ref, sl_ref, sums_ref, w_ref, inv1_ref, inv2_ref
):
    tile = 128
    core = core_ref[0]
    for part, value in zip(quarters(core), (mine1_ref, mine2_ref, other1_ref, other2_ref)):
        sums_ref[part] = value[...]

    def product(a, b, contract):
        return lax.dot_general(a, b, ((contract[0], contract[1]), ((), ())), precision=exact, preferred_element_type=f32)

    down, across, plain = ((0,), (0,)), ((1,), (1,)), ((1,), (0,))
    row = lax.broadcasted_iota(jnp.int32, (2 * tile, 2 * tile), 0)
    col = lax.broadcasted_iota(jnp.int32, (2 * tile, 2 * tile), 1)

    def corner(value, keep):
        return jnp.where(keep[:tile, :tile], value, 0.0)

    def whole(value):
        return corner(value, row <= col) + jnp.transpose(corner(value, row < col))

    pack1, g12, pack2 = sums_ref[0:tile], sums_ref[tile : 2 * tile], sums_ref[3 * tile : 4 * tile]
    w_ref[...] = corner(pack1, row <= col)
    inverse_factor(w_ref, inv1_ref)
    inv1 = inv1_ref[...]
    u12 = product(inv1, g12, plain)
    w_ref[...] = corner(pack2, row <= col) - product(u12, u12, down)
    inverse_factor(w_ref, inv2_ref)
    inv2 = inv2_ref[...]
    inv21 = -product(inv2, product(u12, inv1, down), plain)
    zero = jnp.zeros((tile, tile), f32)
    inv = jnp.concatenate(
        [jnp.concatenate([inv1, zero], axis=1), jnp.concatenate([inv21, inv2], axis=1)], axis=0
    )
    gram = jnp.concatenate(
        [
            jnp.concatenate([whole(pack1), g12], axis=1),
            jnp.concatenate([jnp.transpose(g12), whole(pack2)], axis=1),
        ],
        axis=0,
    )
    bar = jnp.where(row <= col, r_bar_ref[...], 0.0)
    top = jnp.concatenate([pack1, zero], axis=1)
    bottom = jnp.concatenate([sums_ref[2 * tile : 3 * tile], pack2], axis=1)
    cross = jnp.concatenate([top, bottom], axis=0)
    diagonal = jnp.concatenate([sums_ref[512:513], sums_ref[520:521]], axis=1)
    cross = jnp.where(row > col, cross, jnp.where(row == col, diagonal, 0.0))
    middle = product(inv, product(gram, bar, across), plain) - product(cross, inv, across)
    symmetric = jnp.where(row >= col, middle, 0.0) + jnp.transpose(jnp.where(row > col, middle, 0.0))
    spread = product(inv, product(symmetric, inv, plain), down)
    nh_ref[...], nl_ref[...] = split2(inv)
    sh_ref[...], sl_ref[...] = split2(spread)


def columns(qh, ql, nh, nl, xh, xl, ih, il, sh, sl):
    plain = ((1,), (0,))
    xh = jnp.concatenate([xh, nh], axis=1)
    xl = jnp.concatenate([xl, nl], axis=1)
    high = dot(qh, jnp.concatenate([ih, il], axis=1), plain) + dot(xh, jnp.concatenate([sh, sl], axis=1), plain)
    return high[:, :128] + high[:, 128:] + dot(ql, ih, plain) + dot(xl, sh, plain)


def gradient_outer(
    core_ref, table_ref, qh_ref, ql_ref, nh_ref, nl_ref, oh_ref, ol_ref, ih_ref, il_ref, sh_ref, sl_ref,
    w_ref, outer1_ref,
):
    n = w_ref.shape[1]
    j = table_ref[:, 5:6]
    weights = [ref[:, :128] for ref in (ih_ref, il_ref, sh_ref, sl_ref)]
    for k in range(2):
        there = cells(core_ref[0], k, n)
        here = slice(k * n, (k + 1) * n)
        parts = [ref[there] for ref in (qh_ref, ql_ref, nh_ref, nl_ref)] + [oh_ref[here], ol_ref[here]]
        w = columns(*parts, *weights)
        w_ref[k] = w
        outer1_ref[here] = j * w
    outer1_ref[2 * n :] = jnp.zeros((8, w_ref.shape[2]), f32)


def gradient_rest(
    core_ref, table_ref, outer_ref, outer1_ref, qh_ref, ql_ref, nh_ref, nl_ref, lh_ref, ll_ref, hh_ref, hl_ref,
    ih_ref, il_ref, sh_ref, sl_ref, light_ref, heavy_ref, outer2_ref, inner1_ref, inner2_ref,
):
    c = coefficients(table_ref)
    n = outer_ref.shape[1]
    core = core_ref[0]
    weights = [ref[:, :128] for ref in (ih_ref, il_ref, sh_ref, sl_ref)]
    left = (qh_ref, ql_ref, nh_ref, nl_ref)
    for k in range(2):
        there = cells(1 - core, k, n)
        here = slice(k * n, (k + 1) * n)
        w = columns(*[ref[there] for ref in left], lh_ref[here], ll_ref[here], *weights)
        light_ref[k] = w
        inner1_ref[here] = c[1][5] * w
    for k in (1, 0):
        for s, row in enumerate((core, 1 - core)):
            there = cells(row, 2 + k, n)
            here = cells(row, k, n)
            heavy_ref[k, s] = columns(*[ref[there] for ref in left], hh_ref[here], hl_ref[here], *weights)
    own = (outer1_ref, inner1_ref)
    for s, w, out in ((0, outer_ref, outer2_ref), (1, light_ref, inner2_ref)):
        hop_x = own[1 - s][0:n] + side(own[s][0:n])
        hop_p = own[1 - s][n : 2 * n] + side(own[s][n : 2 * n])
        bx, bp = backward_light(c[s], w[0], w[1], heavy_ref[1, s], hop_x, hop_p)
        out[0:n] = c[s][5] * bx
        out[n : 2 * n] = c[s][5] * bp


def gradient_noise(
    core_ref, qh_ref, ql_ref, nh_ref, nl_ref, oh_ref, ol_ref, lh_ref, ll_ref, hh_ref, hl_ref,
    ih_ref, il_ref, sh_ref, sl_ref, out_ref,
):
    n = out_ref.shape[2]
    core = core_ref[0]
    weights = [ref[:, 128:] for ref in (ih_ref, il_ref, sh_ref, sl_ref)]
    for k in range(4):
        for s, row in enumerate((core, 1 - core)):
            there = cells(row, k, n)
            if k < 2:
                here = slice(k * n, (k + 1) * n)
                x = (oh_ref[here], ol_ref[here]) if s == 0 else (lh_ref[here], ll_ref[here])
            else:
                here = cells(row, k - 2, n)
                x = (hh_ref[here], hl_ref[here])
            out_ref[k, row] = columns(*[ref[there] for ref in (qh_ref, ql_ref, nh_ref, nl_ref)], *x, *weights)


def contract_first(
    outer1_ref, table_ref, outer_ref, light_ref, heavy_ref, own1_ref, own2_ref, inner1_ref, inner2_ref,
    fouter2_ref, finner_ref,
    out_light_ref, out_heavy_ref, first_ref,
):
    c = coefficients(table_ref)
    n = outer_ref.shape[1]
    w = [
        (outer_ref[0], outer_ref[1], heavy_ref[0, 0], heavy_ref[1, 0]),
        (light_ref[0], light_ref[1], heavy_ref[0, 1], heavy_ref[1, 1]),
    ]
    own = [(ref[0:n], ref[n : 2 * n]) for ref in (own1_ref, own2_ref)]
    for s, far in enumerate((outer1_ref, inner1_ref)):
        xa, pa, xb, pb = w[s]
        hop_x = own[1 - s][0] + far[0:n] + side(own[s][0])
        hop_p = own[1 - s][1] + far[n : 2 * n] + side(own[s][1])
        first_ref[0, s], first_ref[1, s] = backward_light(c[s], xa, pa, pb, hop_x, hop_p)
        first_ref[2, s], first_ref[3, s] = backward_heavy(c[s], pa, xb, pb)
    for s, fref in enumerate((fouter2_ref, finner_ref)):
        xa, pa, xb, pb = (first_ref[k, s] for k in range(4))
        jfar = far_hopping(fref, n)
        j, jother = c[s][5], c[1 - s][5]
        hop_x = jother * first_ref[0, 1 - s] + jfar * own[s][1] + side(j * xa)
        hop_p = jother * first_ref[1, 1 - s] - jfar * own[s][0] + side(j * pa)
        if s == 1:
            hop_x = hop_x + inner2_ref[0:n]
            hop_p = hop_p + inner2_ref[n : 2 * n]
        light = backward_light(c[s], xa, pa, pb, hop_x, hop_p)
        heavy = backward_heavy(c[s], pa, xb, pb)
        for k in range(2):
            out_light_ref[k, s] = w[s][k] + first_ref[k, s] + 0.5 * light[k]
            out_heavy_ref[k, s] = w[s][2 + k] + first_ref[2 + k, s] + 0.5 * heavy[k]


def contract_last(core_ref, light_ref, heavy_ref, outer2_ref, out_ref):
    n = out_ref.shape[2]
    core = core_ref[0]
    out_ref[0, core] = light_ref[0, 0] + 0.5 * outer2_ref[n : 2 * n]
    out_ref[1, core] = light_ref[1, 0] - 0.5 * outer2_ref[0:n]
    for k in range(2):
        out_ref[k, 1 - core] = light_ref[k, 1]
        out_ref[2 + k, core] = heavy_ref[k, 0]
        out_ref[2 + k, 1 - core] = heavy_ref[k, 1]


def swap_inner(message):
    count = lax.axis_size("row")
    return lax.ppermute(message, "row", [(i, i ^ 1) for i in range(count)])


def swap_outer(message):
    count = lax.axis_size("row")
    pairs = [(i, i + 1) for i in range(1, count - 1, 2)]
    return lax.ppermute(message, "row", pairs + [(j, i) for i, j in pairs])


def sum_over_rows(mine, other):
    count = lax.axis_size("row")
    bits = count.bit_length() - 1
    mine = [m + swap_inner(o) for m, o in zip(mine, other)]
    for step in range(bits - 1):
        turn = [1 + (step + core) % (bits - 1) for core in range(2)]
        pairs = [(i, i ^ (1 << turn[i & 1])) for i in range(count)]
        for stream in range(2):
            mine[stream] = mine[stream] + lax.ppermute(mine[stream], "row", pairs)
    return mine + [swap_inner(m) for m in mine]


def on_device(cell_coeffs, z_factor, noise_cols, q_bar, r_bar):
    quads, lattice, n, rank = z_factor.shape
    flat = quads * lattice * n
    coeffs = cell_coeffs
    core = (lax.axis_index("row") & 1).reshape(1)
    noise = noise_cols.reshape(flat, -1)
    bar = q_bar.reshape(flat, -1)
    shape = jax.ShapeDtypeStruct
    hops = shape((2 * n, rank), f32)
    rim = shape((2 * n + 8, rank), f32)
    table = shape((n, 16), f32)
    outer1 = call(
        forward_sources, shape((2 * n + 16, rank), f32), 0, 10**6, [pltpu.SemaphoreType.DMA((2,))], scalar=True, far=True
    )(core, z_factor)
    outer1, behind = lax.optimization_barrier((outer1, core))
    outer2, inner1, inner2, table = call(
        forward_rim, (rim, hops, rim, table), 10**6, 3 * 10**6, scalar=True
    )(behind, coeffs, z_factor)
    outer1, outer2 = swap_outer(outer1), swap_outer(outer2)
    inner1, inner2 = swap_inner(inner1), swap_inner(inner2)
    wide, tall = shape((flat, 256), bf16), shape((flat, 128), bf16)
    wide_t, tall_t = shape((256, flat), bf16), shape((128, flat), bf16)
    work = 2 * flat * 128 * 128
    pack, nh, nl, qh, ql, nht, nlt, qht, qlt = call(
        noise_products, (shape((136, 128), f32), tall, tall, wide, wide, tall_t, tall_t, wide_t, wide_t),
        work * 5, 9 * 10**6,
    )(noise, bar)
    transposed = (nht, nlt, qht, qlt)
    half, quarter = shape((flat // 2, 128), bf16), shape((flat // 4, 128), bf16)
    single, pair = shape((2, n, rank), f32), shape((2, lattice, n, rank), f32)
    light, hh, hl, lh, ll, gram, rest = call(
        expand_first,
        (single, half, half, quarter, quarter, shape((128, 128), f32), shape((384, 128), f32)),
        work * 8, 9 * 10**6, [pltpu.VMEM(z_factor.shape, f32)], scalar=True,
    )(core, table, z_factor, outer1, inner1, inner2, *transposed)
    part1, part2 = shape((136, 128), f32), shape((128, 128), f32)
    *parts, oh, ol = call(
        expand_last, (part1, part2, part1, part2, quarter, quarter), work * 3, 5 * 10**6, [pltpu.VMEM((528, 128), f32)], scalar=True
    )(core, table, z_factor, outer2, light, gram, rest, pack, *transposed)
    parts = sum_over_rows(parts[:2], parts[2:])
    square = shape((256, 256), bf16)
    weights = call(
        factor, (square,) * 4, 10**9, 10**6,
        [
            pltpu.VMEM((528, 128), f32),
            pltpu.VMEM((128, 128), f32),
            pltpu.VMEM((128, 128), f32),
            pltpu.VMEM((128, 128), f32),
        ],
        scalar=True,
    )(core, *parts, r_bar)
    left = (qh, ql, nh, nl)
    w_outer, own1 = call(gradient_outer, (single, rim), work * 3, 3 * 10**6, scalar=True)(
        core, table, *left, oh, ol, *weights
    )
    back1 = swap_outer(own1)
    w_inner, w_heavy, last, own2, own3 = call(
        gradient_rest, (single, pair, hops, hops, hops), 10**10, 6 * 10**6, scalar=True
    )(core, table, w_outer, own1, *left, lh, ll, hh, hl, *weights)
    back2, near1, near2 = swap_outer(last), swap_inner(own2), swap_inner(own3)
    noise_grad = call(gradient_noise, shape(noise_cols.shape, f32), 0, 0, scalar=True)(
        core, *left, oh, ol, lh, ll, hh, hl, *weights
    )
    out_light, out_heavy = call(contract_first, (pair, pair), 10**7, 6 * 10**6, [pltpu.VMEM(z_factor.shape, f32)])(
        back1, table, w_outer, w_inner, w_heavy, own1, own2, near1, near2, outer2, inner2
    )
    z_grad = call(contract_last, shape(z_factor.shape, f32), 10**6, 6 * 10**6, scalar=True)(
        core, out_light, out_heavy, back2
    )
    return z_grad, noise_grad


def solution(mesh):
    return jax.shard_map(
        on_device,
        mesh=mesh,
        in_specs=(
            P(None, "row", None),
            P(None, ("grp", "row"), None, None),
            P(None, ("grp", "row"), None, None),
            P(None, ("grp", "row"), None, None),
            P("grp", None),
        ),
        out_specs=(P(None, ("grp", "row"), None, None), P(None, ("grp", "row"), None, None)),
        check_vma=False,
    )
```

```python
import jax
import jax.numpy as jnp
from jax import lax
from jax.experimental import pallas as pl
from jax.experimental.pallas import tpu as pltpu
from jax.sharding import PartitionSpec as P

rate_scales = (0.4, 0.4, 0.1, 0.2, 0.1, 0.1)
exact = lax.Precision.HIGHEST
f32 = jnp.float32
bf16 = jnp.bfloat16
VMEM = pl.BlockSpec(memory_space=pltpu.VMEM)
LIMIT = 24 * 1024 * 1024
FIRST_ROWS = 72
FAR_LIMIT = 63 * 1024 * 1024


def call(kernel, outs, flops, moved, scratch=(), scalar=False, far=False):
    def run(*args):
        specs = [pl.BlockSpec(memory_space=pltpu.HBM) if far else pl.BlockSpec() for _ in args]
        if scalar:
            specs[0] = pl.BlockSpec(memory_space=pltpu.SMEM)
        return pl.pallas_call(
            kernel,
            out_shape=outs,
            in_specs=specs,
            scratch_shapes=list(scratch),
            compiler_params=pltpu.CompilerParams(vmem_limit_bytes=FAR_LIMIT if far else LIMIT),
            cost_estimate=pl.CostEstimate(flops=flops, bytes_accessed=moved, transcendentals=0),
        )(*args)

    return run


def split2(value):
    high = value.astype(bf16)
    low = (value - high.astype(f32)).astype(bf16)
    return high, low


def split3(value):
    high = value.astype(bf16)
    rest = value - high.astype(f32)
    mid = rest.astype(bf16)
    low = (rest - mid.astype(f32)).astype(bf16)
    return high, mid, low


def dot(a, b, contract):
    return lax.dot_general(a, b, ((contract[0], contract[1]), ((), ())), preferred_element_type=f32)


def coefficients(table_ref):
    return [[table_ref[:, 6 * s + k : 6 * s + k + 1] for k in range(6)] for s in range(2)]


def side(v):
    n = v.shape[0]
    place = lax.broadcasted_iota(jnp.int32, v.shape, 0)
    left = jnp.where(place == 0, 0.0, pltpu.roll(v, 1, 0))
    right = jnp.where(place == n - 1, 0.0, pltpu.roll(v, n - 1, 0))
    return left + right


def forward_light(c, xa, pa, xb, hop_x, hop_p):
    d, w, g, l, m, j = c
    return (
        -0.5 * l * xa - d * pa - j * hop_p,
        d * xa - 0.5 * l * pa - 2.0 * g * xb + j * hop_x,
    )


def forward_heavy(c, xa, xb, pb):
    d, w, g, l, m, j = c
    return w * pb, -w * xb - 0.5 * m * pb - 2.0 * g * xa


def backward_light(c, xa, pa, pb, hop_x, hop_p):
    d, w, g, l, m, j = c
    return (
        -0.5 * l * xa + d * pa - 2.0 * g * pb + hop_p,
        -d * xa - 0.5 * l * pa - hop_x,
    )


def backward_heavy(c, pa, xb, pb):
    d, w, g, l, m, j = c
    return -2.0 * g * pa - w * pb, w * xb - 0.5 * m * pb


def forward_sources(core_ref, z_hbm, outer1_ref, sems):
    n = z_hbm.shape[2]
    copies = [
        pltpu.make_async_copy(z_hbm.at[k, core_ref[0]], outer1_ref.at[pl.ds(k * n, n)], sems.at[k]) for k in range(2)
    ]
    for copy in copies:
        copy.start()
    outer1_ref[2 * n :] = jnp.zeros((16, z_hbm.shape[3]), f32)
    for copy in copies:
        copy.wait()


def forward_rim(core_ref, coeff_ref, z_ref, outer2_ref, inner1_ref, inner2_ref, table_ref):
    n = z_ref.shape[2]
    core = core_ref[0]
    z = [[z_ref[k, row] for k in range(3)] for row in (core, 1 - core)]
    cols = jnp.transpose(jnp.concatenate([coeff_ref[k] for k in range(6)], axis=0))
    swapped = core == 1
    both = []
    for s in range(2):
        for k in range(6):
            column = jnp.where(swapped, cols[:, 2 * k + 1 - s : 2 * k + 2 - s], cols[:, 2 * k + s : 2 * k + s + 1])
            both.append(column * rate_scales[k])
    for place, column in enumerate(both):
        table_ref[:, place : place + 1] = column
    far = []
    for s in range(2):
        xa, pa, xb = z[s]
        hop_x = z[1 - s][0] + side(xa)
        hop_p = z[1 - s][1] + side(pa)
        far.append(forward_light(both[6 * s : 6 * s + 6], xa, pa, xb, hop_x, hop_p))
    inner1_ref[0:n] = z[1][0]
    inner1_ref[n : 2 * n] = z[1][1]
    for s, out in ((0, outer2_ref), (1, inner2_ref)):
        out[0:n], out[n : 2 * n] = far[s]
        hopping = jnp.where(swapped, coeff_ref[5, 1 - s : 2 - s, :], coeff_ref[5, s : s + 1, :]) * rate_scales[5]
        pieces = [hopping[:, k * 128 : (k + 1) * 128] for k in range(n // 128)]
        pieces.append(jnp.zeros((8 - n // 128, 128), f32))
        out[2 * n :] = jnp.concatenate(pieces, axis=0)


def far_hopping(recv_ref, n):
    size = recv_ref.shape[0]
    tail = jnp.transpose(recv_ref[size - 8 : size])
    return jnp.concatenate([tail[:, k : k + 1] for k in range(n // 128)], axis=0)


def cells(row, k, n):
    return pl.ds(pl.multiple_of((2 * k + row) * n, 128), n)


def packed(gram, cross):
    row = lax.broadcasted_iota(jnp.int32, gram.shape, 0)
    col = lax.broadcasted_iota(jnp.int32, gram.shape, 1)
    diagonal = jnp.sum(jnp.where(row == col, cross, 0.0), axis=0, keepdims=True)
    return jnp.where(row <= col, gram, cross), jnp.broadcast_to(diagonal, (8, gram.shape[1]))


def noise_products(noise_ref, q_ref, pack_ref, nh_ref, nl_ref, qh_ref, ql_ref, nht_ref, nlt_ref, qht_ref, qlt_ref):
    nh, nl = split2(noise_ref[...])
    qh, ql = split2(q_ref[...])
    nh_ref[...] = nh
    nl_ref[...] = nl
    qh_ref[...] = qh
    ql_ref[...] = ql
    for value, out in ((nh, nht_ref), (nl, nlt_ref), (qh, qht_ref), (ql, qlt_ref)):
        out[...] = jnp.transpose(value)
    plain = ((1,), (0,))
    high = dot(jnp.concatenate([nht_ref[...], qht_ref[128:]], axis=0), jnp.concatenate([nh, nl], axis=1), plain)
    low = dot(qlt_ref[128:], nh, plain)
    mixed = high[:128, 128:]
    gram = high[:128, :128] + mixed + jnp.transpose(mixed)
    cross = high[128:, :128] + high[128:, 128:] + low
    pack_ref[0:128], pack_ref[128:] = packed(gram, cross)


def row_products(xh, xl, nht, nlt, qht, qlt):
    plain = ((1,), (0,))
    left = jnp.concatenate([jnp.transpose(xh), nht, qht], axis=0)
    high = dot(left, jnp.concatenate([xh, xl], axis=1), plain)
    low = dot(jnp.concatenate([nlt, qlt], axis=0), xh, plain)
    mixed = high[:128, 128:]
    return (
        high[:128, :128] + mixed + jnp.transpose(mixed),
        high[128:, :128] + high[128:, 128:] + low,
    )


def expand_first(
    core_ref, table_ref, z_ref, outer1_ref, inner1_ref, inner2_ref, nht_ref, nlt_ref, qht_ref, qlt_ref,
    light_ref, hh_ref, hl_ref, ih_ref, il_ref, gram_ref, rest_ref, first_ref,
):
    c = coefficients(table_ref)
    n = z_ref.shape[2]
    core = core_ref[0]
    rows = (core, 1 - core)
    z = [[z_ref[k, row] for k in range(4)] for row in rows]
    for s, beyond in enumerate((outer1_ref, inner1_ref)):
        xa, pa, xb, pb = z[s]
        hop_x = z[1 - s][0] + beyond[0:n] + side(xa)
        hop_p = z[1 - s][1] + beyond[n : 2 * n] + side(pa)
        first_ref[0, s], first_ref[1, s] = forward_light(c[s], xa, pa, xb, hop_x, hop_p)
        first_ref[2, s], first_ref[3, s] = forward_heavy(c[s], xa, xb, pb)
    for s in range(2):
        xa, pa, xb, pb = (first_ref[k, s] for k in range(4))
        for k, (f, second) in enumerate(zip((xb, pb), forward_heavy(c[s], xa, xb, pb))):
            h, l = split2(z[s][2 + k] + f + 0.5 * second)
            hh_ref[cells(rows[s], k, n)] = h
            hl_ref[cells(rows[s], k, n)] = l
    jfar = far_hopping(inner2_ref, n)
    for s in range(2):
        xa, pa, xb, pb = (first_ref[k, s] for k in range(4))
        hop_x = first_ref[0, 1 - s] + side(xa)
        hop_p = first_ref[1, 1 - s] + side(pa)
        if s == 1:
            hop_x = hop_x + inner2_ref[0:n] - jfar * z[s][1]
            hop_p = hop_p + inner2_ref[n : 2 * n] + jfar * z[s][0]
        second = forward_light(c[s], xa, pa, xb, hop_x, hop_p)
        for k in range(2):
            value = z[s][k] + first_ref[k, s] + 0.5 * second[k]
            if s == 0:
                light_ref[k] = value
            else:
                ih_ref[k * n : (k + 1) * n], il_ref[k * n : (k + 1) * n] = split2(value)
    half = 4 * n
    parts = (nht_ref, nlt_ref, qht_ref, qlt_ref)
    gram, rest = row_products(hh_ref[...], hl_ref[...], *(ref[:, half:] for ref in parts))
    for k in range(2):
        there = cells(1 - core, k, n)
        here = slice(k * n, (k + 1) * n)
        more = row_products(ih_ref[here], il_ref[here], *(ref[:, there] for ref in parts))
        gram = gram + more[0]
        rest = rest + more[1]
    gram_ref[...] = gram
    rest_ref[...] = rest


def first_part(core):
    return pl.ds(pl.multiple_of(core * 64, 8), 64)


def second_part(core):
    return pl.ds(pl.multiple_of(128 + core * 200, 8), 200)


def expand_last(
    core_ref, table_ref, z_ref, outer2_ref, light_ref, gram_ref, rest_ref, pack_ref,
    nht_ref, nlt_ref, qht_ref, qlt_ref, mine1_ref, mine2_ref, other1_ref, other2_ref, oh_ref, ol_ref, sums_ref,
):
    n = z_ref.shape[2]
    core = core_ref[0]
    jfar = far_hopping(outer2_ref, n)
    far_x = outer2_ref[0:n] - jfar * z_ref[1, core]
    far_p = outer2_ref[n : 2 * n] + jfar * z_ref[0, core]
    j = 0.5 * table_ref[:, 5:6]
    gram, rest = gram_ref[...], rest_ref[...]
    for k, value in enumerate((light_ref[0] - j * far_p, light_ref[1] + j * far_x)):
        h, l = split2(value)
        oh_ref[k * n : (k + 1) * n] = h
        ol_ref[k * n : (k + 1) * n] = l
        there = cells(core, k, n)
        more = row_products(h, l, *(ref[:, there] for ref in (nht_ref, nlt_ref, qht_ref, qlt_ref)))
        gram = gram + more[0]
        rest = rest + more[1]
    sums_ref[0:128], sums_ref[512:520] = packed(gram, rest[128:256])
    sums_ref[128:256] = jnp.transpose(rest[:128])
    sums_ref[256:384] = rest[256:]
    sums_ref[384:512] = pack_ref[0:128]
    sums_ref[520:528] = pack_ref[128:136]
    mine1_ref[...] = sums_ref[first_part(core)]
    mine2_ref[...] = sums_ref[second_part(core)]
    other1_ref[...] = sums_ref[first_part(1 - core)]
    other2_ref[...] = sums_ref[second_part(1 - core)]


def inverse_factor(w_ref, out_ref, begin=0, end=None):
    size = w_ref.shape[0]
    end = size if end is None else end
    step = 8
    lane = lax.broadcasted_iota(jnp.int32, (step, size), 1)
    place = lax.broadcasted_iota(jnp.int32, (step, size), 0)

    def load(start):
        return [jnp.broadcast_to(w_ref[start + i : start + i + 1, :], (step, size)) for i in range(step)]

    rows = load(begin)
    for start in range(begin, end, step):
        last = start + step >= size
        reach = step if last else 2 * step
        s = {
            (i, m): jnp.broadcast_to(rows[i][:, start + m : start + m + 1], (step, size))
            for i in range(step)
            for m in range(i, reach)
        }
        inside = (lane >= start) & (lane < start + step)
        rows = [jnp.where(lane == start + i, 1.0, jnp.where(inside, 0.0, rows[i])) for i in range(step)]
        if not last:
            following = [jnp.where(inside, 0.0, row) for row in load(start + step)]
        done = []
        for i in range(step):
            inverse = pl.reciprocal(s[i, i])
            root = lax.rsqrt(s[i, i])
            for k in range(i + 1, step):
                ratio = s[i, k] * inverse
                for m in range(k, reach):
                    s[k, m] = s[k, m] - ratio * s[i, m]
                rows[k] = rows[k] - ratio * rows[i]
            if not last:
                scaled = rows[i] * inverse
                for k in range(step):
                    following[k] = following[k] - s[i, step + k] * scaled
            done.append(rows[i] * root)
        panel = done[0]
        for i in range(1, step):
            panel = jnp.where(place == i, done[i], panel)
        out_ref[start : start + step, :] = panel
        beyond = start + 2 * step
        if beyond < size:
            high, mid, low = (part.astype(f32) for part in split3(panel))
            left = jnp.concatenate([high, high, mid, mid, high, low], axis=0).astype(bf16)
            right = jnp.concatenate([high, mid, high, mid, low, high], axis=0).astype(bf16)
            change = dot(left, right, ((0,), (0,)))[beyond:]
            old = w_ref[beyond:, :]
            column = lax.broadcasted_iota(jnp.int32, old.shape, 1)
            old = jnp.where((column >= start) & (column < start + step), 0.0, old)
            w_ref[beyond:, :] = old - change
        if not last:
            rows = following
    if end < size:
        for i in range(step):
            w_ref[end + i : end + i + 1, :] = rows[i][0:1]
        return
    value = out_ref[...]
    row = lax.broadcasted_iota(jnp.int32, value.shape, 0)
    column = lax.broadcasted_iota(jnp.int32, value.shape, 1)
    out_ref[...] = jnp.where(row >= column, value, 0.0)


def factor_first(core_ref, mine_ref, other_ref, pack_ref, w_ref, inv_ref):
    core = core_ref[0]
    pack_ref[first_part(core)] = mine_ref[...]
    pack_ref[first_part(1 - core)] = other_ref[...]
    row = lax.broadcasted_iota(jnp.int32, w_ref.shape, 0)
    col = lax.broadcasted_iota(jnp.int32, w_ref.shape, 1)
    w_ref[...] = jnp.where(row <= col, pack_ref[...], 0.0)
    inv_ref[...] = jnp.zeros(inv_ref.shape, f32)
    inverse_factor(w_ref, inv_ref, end=FIRST_ROWS)


def factor_second(w0_ref, inv0_ref, inv_ref, w_ref):
    w_ref[...] = w0_ref[...]
    inv_ref[...] = inv0_ref[...]
    inverse_factor(w_ref, inv_ref, begin=FIRST_ROWS)


def factor_last(
    core_ref, mine_ref, other_ref, pack1_ref, inv1_ref, r_bar_ref, nh_ref, nl_ref, sh_ref, sl_ref,
    sums_ref, w_ref, inv2_ref,
):
    tile = 128
    core = core_ref[0]
    sums_ref[second_part(core)] = mine_ref[...]
    sums_ref[second_part(1 - core)] = other_ref[...]

    def product(a, b, contract):
        return lax.dot_general(a, b, ((contract[0], contract[1]), ((), ())), precision=exact, preferred_element_type=f32)

    down, across, plain = ((0,), (0,)), ((1,), (1,)), ((1,), (0,))
    row = lax.broadcasted_iota(jnp.int32, (2 * tile, 2 * tile), 0)
    col = lax.broadcasted_iota(jnp.int32, (2 * tile, 2 * tile), 1)

    def corner(value, keep):
        return jnp.where(keep[:tile, :tile], value, 0.0)

    def whole(value):
        return corner(value, row <= col) + jnp.transpose(corner(value, row < col))

    pack1, g12, pack2 = pack1_ref[...], sums_ref[tile : 2 * tile], sums_ref[3 * tile : 4 * tile]
    inv1 = inv1_ref[...]
    u12 = product(inv1, g12, plain)
    w_ref[...] = corner(pack2, row <= col) - product(u12, u12, down)
    inverse_factor(w_ref, inv2_ref)
    inv2 = inv2_ref[...]
    inv21 = -product(inv2, product(u12, inv1, down), plain)
    zero = jnp.zeros((tile, tile), f32)
    inv = jnp.concatenate(
        [jnp.concatenate([inv1, zero], axis=1), jnp.concatenate([inv21, inv2], axis=1)], axis=0
    )
    gram = jnp.concatenate(
        [
            jnp.concatenate([whole(pack1), g12], axis=1),
            jnp.concatenate([jnp.transpose(g12), whole(pack2)], axis=1),
        ],
        axis=0,
    )
    bar = jnp.where(row <= col, r_bar_ref[...], 0.0)
    top = jnp.concatenate([pack1, zero], axis=1)
    bottom = jnp.concatenate([sums_ref[2 * tile : 3 * tile], pack2], axis=1)
    cross = jnp.concatenate([top, bottom], axis=0)
    diagonal = jnp.concatenate([sums_ref[512:513], sums_ref[520:521]], axis=1)
    cross = jnp.where(row > col, cross, jnp.where(row == col, diagonal, 0.0))
    middle = product(inv, product(gram, bar, across), plain) - product(cross, inv, across)
    symmetric = jnp.where(row >= col, middle, 0.0) + jnp.transpose(jnp.where(row > col, middle, 0.0))
    spread = product(inv, product(symmetric, inv, plain), down)
    nh_ref[...], nl_ref[...] = split2(inv)
    sh_ref[...], sl_ref[...] = split2(spread)


def columns(qh, ql, nh, nl, xh, xl, ih, il, sh, sl):
    plain = ((1,), (0,))
    xh = jnp.concatenate([xh, nh], axis=1)
    xl = jnp.concatenate([xl, nl], axis=1)
    high = dot(qh, jnp.concatenate([ih, il], axis=1), plain) + dot(xh, jnp.concatenate([sh, sl], axis=1), plain)
    return high[:, :128] + high[:, 128:] + dot(ql, ih, plain) + dot(xl, sh, plain)


def gradient_outer(
    core_ref, table_ref, qh_ref, ql_ref, nh_ref, nl_ref, oh_ref, ol_ref, ih_ref, il_ref, sh_ref, sl_ref,
    w_ref, outer1_ref,
):
    n = w_ref.shape[1]
    j = table_ref[:, 5:6]
    weights = [ref[:, :128] for ref in (ih_ref, il_ref, sh_ref, sl_ref)]
    for k in range(2):
        there = cells(core_ref[0], k, n)
        here = slice(k * n, (k + 1) * n)
        parts = [ref[there] for ref in (qh_ref, ql_ref, nh_ref, nl_ref)] + [oh_ref[here], ol_ref[here]]
        w = columns(*parts, *weights)
        w_ref[k] = w
        outer1_ref[here] = j * w
    outer1_ref[2 * n :] = jnp.zeros((8, w_ref.shape[2]), f32)


def gradient_rest(
    core_ref, table_ref, outer_ref, outer1_ref, qh_ref, ql_ref, nh_ref, nl_ref, lh_ref, ll_ref, hh_ref, hl_ref,
    ih_ref, il_ref, sh_ref, sl_ref, light_ref, heavy_ref, outer2_ref, inner1_ref, inner2_ref,
):
    c = coefficients(table_ref)
    n = outer_ref.shape[1]
    core = core_ref[0]
    weights = [ref[:, :128] for ref in (ih_ref, il_ref, sh_ref, sl_ref)]
    left = (qh_ref, ql_ref, nh_ref, nl_ref)
    for k in range(2):
        there = cells(1 - core, k, n)
        here = slice(k * n, (k + 1) * n)
        w = columns(*[ref[there] for ref in left], lh_ref[here], ll_ref[here], *weights)
        light_ref[k] = w
        inner1_ref[here] = c[1][5] * w
    for k in (1, 0):
        for s, row in enumerate((core, 1 - core)):
            there = cells(row, 2 + k, n)
            here = cells(row, k, n)
            heavy_ref[k, s] = columns(*[ref[there] for ref in left], hh_ref[here], hl_ref[here], *weights)
    own = (outer1_ref, inner1_ref)
    for s, w, out in ((0, outer_ref, outer2_ref), (1, light_ref, inner2_ref)):
        hop_x = own[1 - s][0:n] + side(own[s][0:n])
        hop_p = own[1 - s][n : 2 * n] + side(own[s][n : 2 * n])
        bx, bp = backward_light(c[s], w[0], w[1], heavy_ref[1, s], hop_x, hop_p)
        out[0:n] = c[s][5] * bx
        out[n : 2 * n] = c[s][5] * bp


def gradient_noise(
    core_ref, qh_ref, ql_ref, nh_ref, nl_ref, oh_ref, ol_ref, lh_ref, ll_ref, hh_ref, hl_ref,
    ih_ref, il_ref, sh_ref, sl_ref, out_ref,
):
    n = out_ref.shape[2]
    core = core_ref[0]
    weights = [ref[:, 128:] for ref in (ih_ref, il_ref, sh_ref, sl_ref)]
    for k in range(4):
        for s, row in enumerate((core, 1 - core)):
            there = cells(row, k, n)
            if k < 2:
                here = slice(k * n, (k + 1) * n)
                x = (oh_ref[here], ol_ref[here]) if s == 0 else (lh_ref[here], ll_ref[here])
            else:
                here = cells(row, k - 2, n)
                x = (hh_ref[here], hl_ref[here])
            out_ref[k, row] = columns(*[ref[there] for ref in (qh_ref, ql_ref, nh_ref, nl_ref)], *x, *weights)


def contract_first(
    outer1_ref, table_ref, outer_ref, light_ref, heavy_ref, own1_ref, own2_ref, inner1_ref, inner2_ref,
    fouter2_ref, finner_ref,
    out_light_ref, out_heavy_ref, first_ref,
):
    c = coefficients(table_ref)
    n = outer_ref.shape[1]
    w = [
        (outer_ref[0], outer_ref[1], heavy_ref[0, 0], heavy_ref[1, 0]),
        (light_ref[0], light_ref[1], heavy_ref[0, 1], heavy_ref[1, 1]),
    ]
    own = [(ref[0:n], ref[n : 2 * n]) for ref in (own1_ref, own2_ref)]
    for s, far in enumerate((outer1_ref, inner1_ref)):
        xa, pa, xb, pb = w[s]
        hop_x = own[1 - s][0] + far[0:n] + side(own[s][0])
        hop_p = own[1 - s][1] + far[n : 2 * n] + side(own[s][1])
        first_ref[0, s], first_ref[1, s] = backward_light(c[s], xa, pa, pb, hop_x, hop_p)
        first_ref[2, s], first_ref[3, s] = backward_heavy(c[s], pa, xb, pb)
    for s, fref in enumerate((fouter2_ref, finner_ref)):
        xa, pa, xb, pb = (first_ref[k, s] for k in range(4))
        jfar = far_hopping(fref, n)
        j, jother = c[s][5], c[1 - s][5]
        hop_x = jother * first_ref[0, 1 - s] + jfar * own[s][1] + side(j * xa)
        hop_p = jother * first_ref[1, 1 - s] - jfar * own[s][0] + side(j * pa)
        if s == 1:
            hop_x = hop_x + inner2_ref[0:n]
            hop_p = hop_p + inner2_ref[n : 2 * n]
        light = backward_light(c[s], xa, pa, pb, hop_x, hop_p)
        heavy = backward_heavy(c[s], pa, xb, pb)
        for k in range(2):
            out_light_ref[k, s] = w[s][k] + first_ref[k, s] + 0.5 * light[k]
            out_heavy_ref[k, s] = w[s][2 + k] + first_ref[2 + k, s] + 0.5 * heavy[k]


def contract_last(core_ref, light_ref, heavy_ref, outer2_ref, out_ref):
    n = out_ref.shape[2]
    core = core_ref[0]
    out_ref[0, core] = light_ref[0, 0] + 0.5 * outer2_ref[n : 2 * n]
    out_ref[1, core] = light_ref[1, 0] - 0.5 * outer2_ref[0:n]
    for k in range(2):
        out_ref[k, 1 - core] = light_ref[k, 1]
        out_ref[2 + k, core] = heavy_ref[k, 0]
        out_ref[2 + k, 1 - core] = heavy_ref[k, 1]


def swap_inner(message):
    count = lax.axis_size("row")
    return lax.ppermute(message, "row", [(i, i ^ 1) for i in range(count)])


def swap_outer(message):
    count = lax.axis_size("row")
    pairs = [(i, i + 1) for i in range(1, count - 1, 2)]
    return lax.ppermute(message, "row", pairs + [(j, i) for i, j in pairs])


def tied(first, second):
    return first, lax.optimization_barrier((first, second))[1]


def chip_rounds():
    count = lax.axis_size("row")
    bits = count.bit_length() - 1
    rounds = []
    for step in range(bits - 1):
        turn = [1 + (step + core) % (bits - 1) for core in range(2)]
        rounds.append([(i, i ^ (1 << turn[i & 1])) for i in range(count)])
    return rounds


def on_device(cell_coeffs, z_factor, noise_cols, q_bar, r_bar):
    quads, lattice, n, rank = z_factor.shape
    flat = quads * lattice * n
    coeffs = cell_coeffs
    core = (lax.axis_index("row") & 1).reshape(1)
    noise = noise_cols.reshape(flat, -1)
    bar = q_bar.reshape(flat, -1)
    shape = jax.ShapeDtypeStruct
    hops = shape((2 * n, rank), f32)
    rim = shape((2 * n + 8, rank), f32)
    table = shape((n, 16), f32)
    outer1 = call(
        forward_sources, shape((2 * n + 16, rank), f32), 0, 10**6, [pltpu.SemaphoreType.DMA((2,))], scalar=True, far=True
    )(core, z_factor)
    outer1, behind = lax.optimization_barrier((outer1, core))
    outer2, inner1, inner2, table = call(
        forward_rim, (rim, hops, rim, table), 10**6, 3 * 10**6, scalar=True
    )(behind, coeffs, z_factor)
    outer1, outer2 = swap_outer(outer1), swap_outer(outer2)
    inner1, inner2 = swap_inner(inner1), swap_inner(inner2)
    wide, tall = shape((flat, 256), bf16), shape((flat, 128), bf16)
    wide_t, tall_t = shape((256, flat), bf16), shape((128, flat), bf16)
    work = 2 * flat * 128 * 128
    pack, nh, nl, qh, ql, nht, nlt, qht, qlt = call(
        noise_products, (shape((136, 128), f32), tall, tall, wide, wide, tall_t, tall_t, wide_t, wide_t),
        work * 5, 9 * 10**6,
    )(noise, bar)
    transposed = (nht, nlt, qht, qlt)
    half, quarter = shape((flat // 2, 128), bf16), shape((flat // 4, 128), bf16)
    single, pair = shape((2, n, rank), f32), shape((2, lattice, n, rank), f32)
    light, hh, hl, lh, ll, gram, rest = call(
        expand_first,
        (single, half, half, quarter, quarter, shape((128, 128), f32), shape((384, 128), f32)),
        work * 8, 9 * 10**6, [pltpu.VMEM(z_factor.shape, f32)], scalar=True,
    )(core, table, z_factor, outer1, inner1, inner2, *transposed)
    part1, part2 = shape((64, 128), f32), shape((200, 128), f32)
    mine1, mine2, other1, other2, oh, ol = call(
        expand_last, (part1, part2, part1, part2, quarter, quarter), work * 3, 5 * 10**6,
        [pltpu.VMEM((528, 128), f32)], scalar=True,
    )(core, table, z_factor, outer2, light, gram, rest, pack, *transposed)
    mine1, mine2 = mine1 + swap_inner(other1), mine2 + swap_inner(other2)
    rounds = chip_rounds()
    for pairs in rounds[:-1]:
        mine1, mine2 = tied(mine1, mine2)
        arriving = lax.ppermute(mine2, "row", pairs)
        mine1 = mine1 + lax.ppermute(mine1, "row", pairs)
        mine1, arriving = tied(mine1, arriving)
        mine2 = mine2 + arriving
    arriving = lax.ppermute(mine2, "row", rounds[-1])
    mine1 = mine1 + lax.ppermute(mine1, "row", rounds[-1])
    other1 = swap_inner(mine1)
    tile = shape((128, 128), f32)
    pack1, w1, inv1 = call(factor_first, (tile,) * 3, 10**8, 10**5, scalar=True)(core, mine1, other1)
    arriving, w1 = lax.optimization_barrier((arriving, w1))
    mine2 = mine2 + arriving
    other2 = swap_inner(mine2)
    inv1 = call(factor_second, tile, 10**8, 10**5, [pltpu.VMEM((128, 128), f32)])(w1, inv1)
    square = shape((256, 256), bf16)
    weights = call(
        factor_last, (square,) * 4, 10**9, 10**6,
        [pltpu.VMEM((528, 128), f32), pltpu.VMEM((128, 128), f32), pltpu.VMEM((128, 128), f32)],
        scalar=True,
    )(core, mine2, other2, pack1, inv1, r_bar)
    left = (qh, ql, nh, nl)
    w_outer, own1 = call(gradient_outer, (single, rim), work * 3, 3 * 10**6, scalar=True)(
        core, table, *left, oh, ol, *weights
    )
    back1 = swap_outer(own1)
    w_inner, w_heavy, last, own2, own3 = call(
        gradient_rest, (single, pair, hops, hops, hops), 10**10, 6 * 10**6, scalar=True
    )(core, table, w_outer, own1, *left, lh, ll, hh, hl, *weights)
    back2, near1, near2 = swap_outer(last), swap_inner(own2), swap_inner(own3)
    noise_grad = call(gradient_noise, shape(noise_cols.shape, f32), 0, 0, scalar=True)(
        core, *left, oh, ol, lh, ll, hh, hl, *weights
    )
    out_light, out_heavy = call(contract_first, (pair, pair), 10**7, 6 * 10**6, [pltpu.VMEM(z_factor.shape, f32)])(
        back1, table, w_outer, w_inner, w_heavy, own1, own2, near1, near2, outer2, inner2
    )
    z_grad = call(contract_last, shape(z_factor.shape, f32), 10**6, 6 * 10**6, scalar=True)(
        core, out_light, out_heavy, back2
    )
    return z_grad, noise_grad


def solution(mesh):
    return jax.shard_map(
        on_device,
        mesh=mesh,
        in_specs=(
            P(None, "row", None),
            P(None, ("grp", "row"), None, None),
            P(None, ("grp", "row"), None, None),
            P(None, ("grp", "row"), None, None),
            P("grp", None),
        ),
        out_specs=(P(None, ("grp", "row"), None, None), P(None, ("grp", "row"), None, None)),
        check_vma=False,
    )
```

```python
import jax
import jax.numpy as jnp
from jax import lax
from jax.experimental import pallas as pl
from jax.experimental.pallas import tpu as pltpu
from jax.sharding import PartitionSpec as P

rate_scales = (0.4, 0.4, 0.1, 0.2, 0.1, 0.1)
exact = lax.Precision.HIGHEST
f32 = jnp.float32
bf16 = jnp.bfloat16
VMEM = pl.BlockSpec(memory_space=pltpu.VMEM)
LIMIT = 24 * 1024 * 1024
FAR_LIMIT = 63 * 1024 * 1024


def call(kernel, outs, flops, moved, scratch=(), scalar=False, far=False):
    def run(*args):
        specs = [pl.BlockSpec(memory_space=pltpu.HBM) if far else pl.BlockSpec() for _ in args]
        if scalar:
            specs[0] = pl.BlockSpec(memory_space=pltpu.SMEM)
        return pl.pallas_call(
            kernel,
            out_shape=outs,
            in_specs=specs,
            scratch_shapes=list(scratch),
            compiler_params=pltpu.CompilerParams(vmem_limit_bytes=FAR_LIMIT if far else LIMIT),
            cost_estimate=pl.CostEstimate(flops=flops, bytes_accessed=moved, transcendentals=0),
        )(*args)

    return run


def split2(value):
    high = value.astype(bf16)
    low = (value - high.astype(f32)).astype(bf16)
    return high, low


def split3(value):
    high = value.astype(bf16)
    rest = value - high.astype(f32)
    mid = rest.astype(bf16)
    low = (rest - mid.astype(f32)).astype(bf16)
    return high, mid, low


def dot(a, b, contract):
    return lax.dot_general(a, b, ((contract[0], contract[1]), ((), ())), preferred_element_type=f32)


def coefficients(table_ref):
    return [[table_ref[:, 6 * s + k : 6 * s + k + 1] for k in range(6)] for s in range(2)]


def side(v):
    n = v.shape[0]
    place = lax.broadcasted_iota(jnp.int32, v.shape, 0)
    left = jnp.where(place == 0, 0.0, pltpu.roll(v, 1, 0))
    right = jnp.where(place == n - 1, 0.0, pltpu.roll(v, n - 1, 0))
    return left + right


def forward_light(c, xa, pa, xb, hop_x, hop_p):
    d, w, g, l, m, j = c
    return (
        -0.5 * l * xa - d * pa - j * hop_p,
        d * xa - 0.5 * l * pa - 2.0 * g * xb + j * hop_x,
    )


def forward_heavy(c, xa, xb, pb):
    d, w, g, l, m, j = c
    return w * pb, -w * xb - 0.5 * m * pb - 2.0 * g * xa


def backward_light(c, xa, pa, pb, hop_x, hop_p):
    d, w, g, l, m, j = c
    return (
        -0.5 * l * xa + d * pa - 2.0 * g * pb + hop_p,
        -d * xa - 0.5 * l * pa - hop_x,
    )


def backward_heavy(c, pa, xb, pb):
    d, w, g, l, m, j = c
    return -2.0 * g * pa - w * pb, w * xb - 0.5 * m * pb


def forward_sources(core_ref, z_hbm, outer1_ref, sems):
    n = z_hbm.shape[2]
    copies = [
        pltpu.make_async_copy(z_hbm.at[k, core_ref[0]], outer1_ref.at[pl.ds(k * n, n)], sems.at[k]) for k in range(2)
    ]
    for copy in copies:
        copy.start()
    outer1_ref[2 * n :] = jnp.zeros((16, z_hbm.shape[3]), f32)
    for copy in copies:
        copy.wait()


def forward_rim(core_ref, coeff_ref, z_ref, outer2_ref, inner1_ref, inner2_ref, table_ref):
    n = z_ref.shape[2]
    core = core_ref[0]
    z = [[z_ref[k, row] for k in range(3)] for row in (core, 1 - core)]
    cols = jnp.transpose(jnp.concatenate([coeff_ref[k] for k in range(6)], axis=0))
    swapped = core == 1
    both = []
    for s in range(2):
        for k in range(6):
            column = jnp.where(swapped, cols[:, 2 * k + 1 - s : 2 * k + 2 - s], cols[:, 2 * k + s : 2 * k + s + 1])
            both.append(column * rate_scales[k])
    for place, column in enumerate(both):
        table_ref[:, place : place + 1] = column
    far = []
    for s in range(2):
        xa, pa, xb = z[s]
        hop_x = z[1 - s][0] + side(xa)
        hop_p = z[1 - s][1] + side(pa)
        far.append(forward_light(both[6 * s : 6 * s + 6], xa, pa, xb, hop_x, hop_p))
    inner1_ref[0:n] = z[1][0]
    inner1_ref[n : 2 * n] = z[1][1]
    for s, out in ((0, outer2_ref), (1, inner2_ref)):
        out[0:n], out[n : 2 * n] = far[s]
        hopping = jnp.where(swapped, coeff_ref[5, 1 - s : 2 - s, :], coeff_ref[5, s : s + 1, :]) * rate_scales[5]
        pieces = [hopping[:, k * 128 : (k + 1) * 128] for k in range(n // 128)]
        pieces.append(jnp.zeros((8 - n // 128, 128), f32))
        out[2 * n :] = jnp.concatenate(pieces, axis=0)


def far_hopping(recv_ref, n):
    size = recv_ref.shape[0]
    tail = jnp.transpose(recv_ref[size - 8 : size])
    return jnp.concatenate([tail[:, k : k + 1] for k in range(n // 128)], axis=0)


def cells(row, k, n):
    return pl.ds(pl.multiple_of((2 * k + row) * n, 128), n)


def packed(gram, cross):
    row = lax.broadcasted_iota(jnp.int32, gram.shape, 0)
    col = lax.broadcasted_iota(jnp.int32, gram.shape, 1)
    diagonal = jnp.sum(jnp.where(row == col, cross, 0.0), axis=0, keepdims=True)
    return jnp.where(row <= col, gram, cross), jnp.broadcast_to(diagonal, (8, gram.shape[1]))


def noise_products(noise_ref, q_ref, pack_ref, nh_ref, nl_ref, qh_ref, ql_ref, nht_ref, nlt_ref, qht_ref, qlt_ref):
    nh, nl = split2(noise_ref[...])
    qh, ql = split2(q_ref[...])
    nh_ref[...] = nh
    nl_ref[...] = nl
    qh_ref[...] = qh
    ql_ref[...] = ql
    for value, out in ((nh, nht_ref), (nl, nlt_ref), (qh, qht_ref), (ql, qlt_ref)):
        out[...] = jnp.transpose(value)
    plain = ((1,), (0,))
    high = dot(jnp.concatenate([nht_ref[...], qht_ref[128:]], axis=0), jnp.concatenate([nh, nl], axis=1), plain)
    low = dot(qlt_ref[128:], nh, plain)
    mixed = high[:128, 128:]
    gram = high[:128, :128] + mixed + jnp.transpose(mixed)
    cross = high[128:, :128] + high[128:, 128:] + low
    pack_ref[0:128], pack_ref[128:] = packed(gram, cross)


def row_products(xh, xl, nht, nlt, qht, qlt):
    plain = ((1,), (0,))
    left = jnp.concatenate([jnp.transpose(xh), nht, qht], axis=0)
    high = dot(left, jnp.concatenate([xh, xl], axis=1), plain)
    low = dot(jnp.concatenate([nlt, qlt], axis=0), xh, plain)
    mixed = high[:128, 128:]
    return (
        high[:128, :128] + mixed + jnp.transpose(mixed),
        high[128:, :128] + high[128:, 128:] + low,
    )


def expand_first(
    core_ref, table_ref, z_ref, outer1_ref, inner1_ref, inner2_ref, nht_ref, nlt_ref, qht_ref, qlt_ref,
    light_ref, hh_ref, hl_ref, ih_ref, il_ref, gram_ref, rest_ref, first_ref,
):
    c = coefficients(table_ref)
    n = z_ref.shape[2]
    core = core_ref[0]
    rows = (core, 1 - core)
    z = [[z_ref[k, row] for k in range(4)] for row in rows]
    for s, beyond in enumerate((outer1_ref, inner1_ref)):
        xa, pa, xb, pb = z[s]
        hop_x = z[1 - s][0] + beyond[0:n] + side(xa)
        hop_p = z[1 - s][1] + beyond[n : 2 * n] + side(pa)
        first_ref[0, s], first_ref[1, s] = forward_light(c[s], xa, pa, xb, hop_x, hop_p)
        first_ref[2, s], first_ref[3, s] = forward_heavy(c[s], xa, xb, pb)
    for s in range(2):
        xa, pa, xb, pb = (first_ref[k, s] for k in range(4))
        for k, (f, second) in enumerate(zip((xb, pb), forward_heavy(c[s], xa, xb, pb))):
            h, l = split2(z[s][2 + k] + f + 0.5 * second)
            hh_ref[cells(rows[s], k, n)] = h
            hl_ref[cells(rows[s], k, n)] = l
    jfar = far_hopping(inner2_ref, n)
    for s in range(2):
        xa, pa, xb, pb = (first_ref[k, s] for k in range(4))
        hop_x = first_ref[0, 1 - s] + side(xa)
        hop_p = first_ref[1, 1 - s] + side(pa)
        if s == 1:
            hop_x = hop_x + inner2_ref[0:n] - jfar * z[s][1]
            hop_p = hop_p + inner2_ref[n : 2 * n] + jfar * z[s][0]
        second = forward_light(c[s], xa, pa, xb, hop_x, hop_p)
        for k in range(2):
            value = z[s][k] + first_ref[k, s] + 0.5 * second[k]
            if s == 0:
                light_ref[k] = value
            else:
                ih_ref[k * n : (k + 1) * n], il_ref[k * n : (k + 1) * n] = split2(value)
    half = 4 * n
    parts = (nht_ref, nlt_ref, qht_ref, qlt_ref)
    gram, rest = row_products(hh_ref[...], hl_ref[...], *(ref[:, half:] for ref in parts))
    for k in range(2):
        there = cells(1 - core, k, n)
        here = slice(k * n, (k + 1) * n)
        more = row_products(ih_ref[here], il_ref[here], *(ref[:, there] for ref in parts))
        gram = gram + more[0]
        rest = rest + more[1]
    gram_ref[...] = gram
    rest_ref[...] = rest


def quarters(core):
    parts = []
    for owner in (core, 1 - core):
        first = pl.multiple_of(owner * 264, 8)
        parts += [pl.ds(first, 136), pl.ds(pl.multiple_of(first + 136, 8), 128)]
    return parts


def expand_last(
    core_ref, table_ref, z_ref, outer2_ref, light_ref, gram_ref, rest_ref, pack_ref,
    nht_ref, nlt_ref, qht_ref, qlt_ref, mine1_ref, mine2_ref, other1_ref, other2_ref, oh_ref, ol_ref, sums_ref,
):
    n = z_ref.shape[2]
    core = core_ref[0]
    jfar = far_hopping(outer2_ref, n)
    far_x = outer2_ref[0:n] - jfar * z_ref[1, core]
    far_p = outer2_ref[n : 2 * n] + jfar * z_ref[0, core]
    j = 0.5 * table_ref[:, 5:6]
    gram, rest = gram_ref[...], rest_ref[...]
    for k, value in enumerate((light_ref[0] - j * far_p, light_ref[1] + j * far_x)):
        h, l = split2(value)
        oh_ref[k * n : (k + 1) * n] = h
        ol_ref[k * n : (k + 1) * n] = l
        there = cells(core, k, n)
        more = row_products(h, l, *(ref[:, there] for ref in (nht_ref, nlt_ref, qht_ref, qlt_ref)))
        gram = gram + more[0]
        rest = rest + more[1]
    sums_ref[0:128], sums_ref[512:520] = packed(gram, rest[128:256])
    sums_ref[128:256] = jnp.transpose(rest[:128])
    sums_ref[256:384] = rest[256:]
    sums_ref[384:512] = pack_ref[0:128]
    sums_ref[520:528] = pack_ref[128:136]
    for part, out in zip(quarters(core), (mine1_ref, mine2_ref, other1_ref, other2_ref)):
        out[...] = sums_ref[part]


def inverse_factor(w_ref, out_ref):
    size = w_ref.shape[0]
    step = 8
    lane = lax.broadcasted_iota(jnp.int32, (step, size), 1)
    place = lax.broadcasted_iota(jnp.int32, (step, size), 0)

    def load(start):
        return [jnp.broadcast_to(w_ref[start + i : start + i + 1, :], (step, size)) for i in range(step)]

    rows = load(0)
    for start in range(0, size, step):
        last = start + step >= size
        reach = step if last else 2 * step
        s = {
            (i, m): jnp.broadcast_to(rows[i][:, start + m : start + m + 1], (step, size))
            for i in range(step)
            for m in range(i, reach)
        }
        inside = (lane >= start) & (lane < start + step)
        rows = [jnp.where(lane == start + i, 1.0, jnp.where(inside, 0.0, rows[i])) for i in range(step)]
        done = []
        change = [None] * step
        for i in range(step):
            inverse = pl.reciprocal(s[i, i])
            root = lax.rsqrt(s[i, i])
            for k in range(i + 1, step):
                ratio = s[i, k] * inverse
                for m in range(k, reach):
                    s[k, m] = s[k, m] - ratio * s[i, m]
                rows[k] = rows[k] - ratio * rows[i]
            if not last:
                scaled = rows[i] * inverse
                for k in range(step):
                    term = s[i, step + k] * scaled
                    change[k] = term if i == 0 else change[k] + term
            done.append(rows[i] * root)
        panel = done[0]
        for i in range(1, step):
            panel = jnp.where(place == i, done[i], panel)
        out_ref[start : start + step, :] = panel
        if not last:
            rows = [jnp.where(inside, 0.0, row) - c for row, c in zip(load(start + step), change)]
        beyond = start + 2 * step
        if beyond < size:
            high, mid, low = (part.astype(f32) for part in split3(panel))
            left = jnp.concatenate([high, high, mid, mid, high, low], axis=0).astype(bf16)
            right = jnp.concatenate([high, mid, high, mid, low, high], axis=0).astype(bf16)
            update = dot(left, right, ((0,), (0,)))[beyond:]
            old = w_ref[beyond:, :]
            column = lax.broadcasted_iota(jnp.int32, old.shape, 1)
            old = jnp.where((column >= start) & (column < start + step), 0.0, old)
            w_ref[beyond:, :] = old - update
    value = out_ref[...]
    row = lax.broadcasted_iota(jnp.int32, value.shape, 0)
    column = lax.broadcasted_iota(jnp.int32, value.shape, 1)
    out_ref[...] = jnp.where(row >= column, value, 0.0)


def factor(
    core_ref, mine1_ref, mine2_ref, other1_ref, other2_ref, r_bar_ref, nh_ref, nl_ref, sh_ref, sl_ref, sums_ref, w_ref, inv1_ref, inv2_ref
):
    tile = 128
    core = core_ref[0]
    for part, value in zip(quarters(core), (mine1_ref, mine2_ref, other1_ref, other2_ref)):
        sums_ref[part] = value[...]

    def product(a, b, contract):
        return lax.dot_general(a, b, ((contract[0], contract[1]), ((), ())), precision=exact, preferred_element_type=f32)

    down, across, plain = ((0,), (0,)), ((1,), (1,)), ((1,), (0,))

    def stacked(a, b, contract):
        a, b = split3(a), split3(b)
        left = jnp.concatenate([a[k] for k in (0, 0, 1, 1, 0, 2)], axis=contract[0][0])
        right = jnp.concatenate([b[k] for k in (0, 1, 0, 1, 2, 0)], axis=contract[1][0])
        return dot(left, right, contract)

    def stacked2(a, b, contract):
        left = jnp.concatenate([a[0], a[0], a[1]], axis=contract[0][0])
        right = jnp.concatenate([b[0], b[1], b[0]], axis=contract[1][0])
        return dot(left, right, contract)

    row = lax.broadcasted_iota(jnp.int32, (2 * tile, 2 * tile), 0)
    col = lax.broadcasted_iota(jnp.int32, (2 * tile, 2 * tile), 1)

    def corner(value, keep):
        return jnp.where(keep[:tile, :tile], value, 0.0)

    def whole(value):
        return corner(value, row <= col) + jnp.transpose(corner(value, row < col))

    pack1, g12, pack2 = sums_ref[0:tile], sums_ref[tile : 2 * tile], sums_ref[3 * tile : 4 * tile]
    w_ref[...] = corner(pack1, row <= col)
    inverse_factor(w_ref, inv1_ref)
    inv1 = inv1_ref[...]
    u12 = stacked(inv1, g12, plain)
    w_ref[...] = corner(pack2, row <= col) - stacked(u12, u12, down)
    inverse_factor(w_ref, inv2_ref)
    inv2 = inv2_ref[...]
    inv21 = -stacked(inv2, stacked(u12, inv1, down), plain)
    zero = jnp.zeros((tile, tile), f32)
    inv = jnp.concatenate(
        [jnp.concatenate([inv1, zero], axis=1), jnp.concatenate([inv21, inv2], axis=1)], axis=0
    )
    gram = jnp.concatenate(
        [
            jnp.concatenate([whole(pack1), g12], axis=1),
            jnp.concatenate([jnp.transpose(g12), whole(pack2)], axis=1),
        ],
        axis=0,
    )
    bar = jnp.where(row <= col, r_bar_ref[...], 0.0)
    top = jnp.concatenate([pack1, zero], axis=1)
    bottom = jnp.concatenate([sums_ref[2 * tile : 3 * tile], pack2], axis=1)
    cross = jnp.concatenate([top, bottom], axis=0)
    diagonal = jnp.concatenate([sums_ref[512:513], sums_ref[520:521]], axis=1)
    cross = jnp.where(row > col, cross, jnp.where(row == col, diagonal, 0.0))
    middle = product(inv, product(gram, bar, across), plain) - product(cross, inv, across)
    symmetric = jnp.where(row >= col, middle, 0.0) + jnp.transpose(jnp.where(row > col, middle, 0.0))
    parts = split2(inv)
    spread = stacked2(parts, split2(stacked2(split2(symmetric), parts, plain)), down)
    nh_ref[...], nl_ref[...] = parts
    sh_ref[...], sl_ref[...] = split2(spread)


def columns(qh, ql, nh, nl, xh, xl, ih, il, sh, sl):
    plain = ((1,), (0,))
    xh = jnp.concatenate([xh, nh], axis=1)
    xl = jnp.concatenate([xl, nl], axis=1)
    high = dot(qh, jnp.concatenate([ih, il], axis=1), plain) + dot(xh, jnp.concatenate([sh, sl], axis=1), plain)
    return high[:, :128] + high[:, 128:] + dot(ql, ih, plain) + dot(xl, sh, plain)


def gradient_outer(
    core_ref, table_ref, qh_ref, ql_ref, nh_ref, nl_ref, oh_ref, ol_ref, ih_ref, il_ref, sh_ref, sl_ref,
    w_ref, outer1_ref,
):
    n = w_ref.shape[1]
    j = table_ref[:, 5:6]
    weights = [ref[:, :128] for ref in (ih_ref, il_ref, sh_ref, sl_ref)]
    for k in range(2):
        there = cells(core_ref[0], k, n)
        here = slice(k * n, (k + 1) * n)
        parts = [ref[there] for ref in (qh_ref, ql_ref, nh_ref, nl_ref)] + [oh_ref[here], ol_ref[here]]
        w = columns(*parts, *weights)
        w_ref[k] = w
        outer1_ref[here] = j * w
    outer1_ref[2 * n :] = jnp.zeros((8, w_ref.shape[2]), f32)


def gradient_rest(
    core_ref, table_ref, outer_ref, outer1_ref, qh_ref, ql_ref, nh_ref, nl_ref, lh_ref, ll_ref, hh_ref, hl_ref,
    ih_ref, il_ref, sh_ref, sl_ref, light_ref, heavy_ref, outer2_ref, inner1_ref, inner2_ref,
):
    c = coefficients(table_ref)
    n = outer_ref.shape[1]
    core = core_ref[0]
    weights = [ref[:, :128] for ref in (ih_ref, il_ref, sh_ref, sl_ref)]
    left = (qh_ref, ql_ref, nh_ref, nl_ref)
    for k in range(2):
        there = cells(1 - core, k, n)
        here = slice(k * n, (k + 1) * n)
        w = columns(*[ref[there] for ref in left], lh_ref[here], ll_ref[here], *weights)
        light_ref[k] = w
        inner1_ref[here] = c[1][5] * w
    for k in (1, 0):
        for s, row in enumerate((core, 1 - core)):
            there = cells(row, 2 + k, n)
            here = cells(row, k, n)
            heavy_ref[k, s] = columns(*[ref[there] for ref in left], hh_ref[here], hl_ref[here], *weights)
    own = (outer1_ref, inner1_ref)
    for s, w, out in ((0, outer_ref, outer2_ref), (1, light_ref, inner2_ref)):
        hop_x = own[1 - s][0:n] + side(own[s][0:n])
        hop_p = own[1 - s][n : 2 * n] + side(own[s][n : 2 * n])
        bx, bp = backward_light(c[s], w[0], w[1], heavy_ref[1, s], hop_x, hop_p)
        out[0:n] = c[s][5] * bx
        out[n : 2 * n] = c[s][5] * bp


def gradient_noise(
    core_ref, qh_ref, ql_ref, nh_ref, nl_ref, oh_ref, ol_ref, lh_ref, ll_ref, hh_ref, hl_ref,
    ih_ref, il_ref, sh_ref, sl_ref, out_ref,
):
    n = out_ref.shape[2]
    core = core_ref[0]
    weights = [ref[:, 128:] for ref in (ih_ref, il_ref, sh_ref, sl_ref)]
    for k in range(4):
        for s, row in enumerate((core, 1 - core)):
            there = cells(row, k, n)
            if k < 2:
                here = slice(k * n, (k + 1) * n)
                x = (oh_ref[here], ol_ref[here]) if s == 0 else (lh_ref[here], ll_ref[here])
            else:
                here = cells(row, k - 2, n)
                x = (hh_ref[here], hl_ref[here])
            out_ref[k, row] = columns(*[ref[there] for ref in (qh_ref, ql_ref, nh_ref, nl_ref)], *x, *weights)


def contract_first(
    outer1_ref, table_ref, outer_ref, light_ref, heavy_ref, own1_ref, own2_ref, inner1_ref, inner2_ref,
    fouter2_ref, finner_ref,
    out_light_ref, out_heavy_ref, first_ref,
):
    c = coefficients(table_ref)
    n = outer_ref.shape[1]
    w = [
        (outer_ref[0], outer_ref[1], heavy_ref[0, 0], heavy_ref[1, 0]),
        (light_ref[0], light_ref[1], heavy_ref[0, 1], heavy_ref[1, 1]),
    ]
    own = [(ref[0:n], ref[n : 2 * n]) for ref in (own1_ref, own2_ref)]
    for s, far in enumerate((outer1_ref, inner1_ref)):
        xa, pa, xb, pb = w[s]
        hop_x = own[1 - s][0] + far[0:n] + side(own[s][0])
        hop_p = own[1 - s][1] + far[n : 2 * n] + side(own[s][1])
        first_ref[0, s], first_ref[1, s] = backward_light(c[s], xa, pa, pb, hop_x, hop_p)
        first_ref[2, s], first_ref[3, s] = backward_heavy(c[s], pa, xb, pb)
    for s, fref in enumerate((fouter2_ref, finner_ref)):
        xa, pa, xb, pb = (first_ref[k, s] for k in range(4))
        jfar = far_hopping(fref, n)
        j, jother = c[s][5], c[1 - s][5]
        hop_x = jother * first_ref[0, 1 - s] + jfar * own[s][1] + side(j * xa)
        hop_p = jother * first_ref[1, 1 - s] - jfar * own[s][0] + side(j * pa)
        if s == 1:
            hop_x = hop_x + inner2_ref[0:n]
            hop_p = hop_p + inner2_ref[n : 2 * n]
        light = backward_light(c[s], xa, pa, pb, hop_x, hop_p)
        heavy = backward_heavy(c[s], pa, xb, pb)
        for k in range(2):
            out_light_ref[k, s] = w[s][k] + first_ref[k, s] + 0.5 * light[k]
            out_heavy_ref[k, s] = w[s][2 + k] + first_ref[2 + k, s] + 0.5 * heavy[k]


def contract_last(core_ref, light_ref, heavy_ref, outer2_ref, out_ref):
    n = out_ref.shape[2]
    core = core_ref[0]
    out_ref[0, core] = light_ref[0, 0] + 0.5 * outer2_ref[n : 2 * n]
    out_ref[1, core] = light_ref[1, 0] - 0.5 * outer2_ref[0:n]
    for k in range(2):
        out_ref[k, 1 - core] = light_ref[k, 1]
        out_ref[2 + k, core] = heavy_ref[k, 0]
        out_ref[2 + k, 1 - core] = heavy_ref[k, 1]


def swap_inner(message):
    count = lax.axis_size("row")
    return lax.ppermute(message, "row", [(i, i ^ 1) for i in range(count)])


def swap_outer(message):
    count = lax.axis_size("row")
    pairs = [(i, i + 1) for i in range(1, count - 1, 2)]
    return lax.ppermute(message, "row", pairs + [(j, i) for i, j in pairs])


def sum_over_rows(mine, other):
    count = lax.axis_size("row")
    bits = count.bit_length() - 1
    mine = [m + swap_inner(o) for m, o in zip(mine, other)]
    for step in range(bits - 1):
        for stream in range(2):
            turn = [1 + (step + (core ^ stream)) % (bits - 1) for core in range(2)]
            pairs = [(i, i ^ (1 << turn[i & 1])) for i in range(count)]
            mine[stream] = mine[stream] + lax.ppermute(mine[stream], "row", pairs)
    return mine + [swap_inner(m) for m in mine]


def on_device(cell_coeffs, z_factor, noise_cols, q_bar, r_bar):
    quads, lattice, n, rank = z_factor.shape
    flat = quads * lattice * n
    coeffs = cell_coeffs
    core = (lax.axis_index("row") & 1).reshape(1)
    noise = noise_cols.reshape(flat, -1)
    bar = q_bar.reshape(flat, -1)
    shape = jax.ShapeDtypeStruct
    hops = shape((2 * n, rank), f32)
    rim = shape((2 * n + 8, rank), f32)
    table = shape((n, 16), f32)
    outer1 = call(
        forward_sources, shape((2 * n + 16, rank), f32), 0, 10**6, [pltpu.SemaphoreType.DMA((2,))], scalar=True, far=True
    )(core, z_factor)
    outer1, behind = lax.optimization_barrier((outer1, core))
    outer2, inner1, inner2, table = call(
        forward_rim, (rim, hops, rim, table), 10**6, 3 * 10**6, scalar=True
    )(behind, coeffs, z_factor)
    outer1, outer2 = swap_outer(outer1), swap_outer(outer2)
    inner1, inner2 = swap_inner(inner1), swap_inner(inner2)
    wide, tall = shape((flat, 256), bf16), shape((flat, 128), bf16)
    wide_t, tall_t = shape((256, flat), bf16), shape((128, flat), bf16)
    work = 2 * flat * 128 * 128
    pack, nh, nl, qh, ql, nht, nlt, qht, qlt = call(
        noise_products, (shape((136, 128), f32), tall, tall, wide, wide, tall_t, tall_t, wide_t, wide_t),
        work * 5, 9 * 10**6,
    )(noise, bar)
    transposed = (nht, nlt, qht, qlt)
    half, quarter = shape((flat // 2, 128), bf16), shape((flat // 4, 128), bf16)
    single, pair = shape((2, n, rank), f32), shape((2, lattice, n, rank), f32)
    light, hh, hl, lh, ll, gram, rest = call(
        expand_first,
        (single, half, half, quarter, quarter, shape((128, 128), f32), shape((384, 128), f32)),
        work * 8, 9 * 10**6, [pltpu.VMEM(z_factor.shape, f32)], scalar=True,
    )(core, table, z_factor, outer1, inner1, inner2, *transposed)
    part1, part2 = shape((136, 128), f32), shape((128, 128), f32)
    *parts, oh, ol = call(
        expand_last, (part1, part2, part1, part2, quarter, quarter), work * 3, 5 * 10**6, [pltpu.VMEM((528, 128), f32)], scalar=True
    )(core, table, z_factor, outer2, light, gram, rest, pack, *transposed)
    parts = sum_over_rows(parts[:2], parts[2:])
    square = shape((256, 256), bf16)
    weights = call(
        factor, (square,) * 4, 10**9, 10**6,
        [
            pltpu.VMEM((528, 128), f32),
            pltpu.VMEM((128, 128), f32),
            pltpu.VMEM((128, 128), f32),
            pltpu.VMEM((128, 128), f32),
        ],
        scalar=True,
    )(core, *parts, r_bar)
    left = (qh, ql, nh, nl)
    w_outer, own1 = call(gradient_outer, (single, rim), work * 3, 3 * 10**6, scalar=True)(
        core, table, *left, oh, ol, *weights
    )
    back1 = swap_outer(own1)
    w_inner, w_heavy, last, own2, own3 = call(
        gradient_rest, (single, pair, hops, hops, hops), 10**10, 6 * 10**6, scalar=True
    )(core, table, w_outer, own1, *left, lh, ll, hh, hl, *weights)
    back2, near1, near2 = swap_outer(last), swap_inner(own2), swap_inner(own3)
    noise_grad = call(gradient_noise, shape(noise_cols.shape, f32), 0, 0, scalar=True)(
        core, *left, oh, ol, lh, ll, hh, hl, *weights
    )
    out_light, out_heavy = call(contract_first, (pair, pair), 10**7, 6 * 10**6, [pltpu.VMEM(z_factor.shape, f32)])(
        back1, table, w_outer, w_inner, w_heavy, own1, own2, near1, near2, outer2, inner2
    )
    z_grad = call(contract_last, shape(z_factor.shape, f32), 10**6, 6 * 10**6, scalar=True)(
        core, out_light, out_heavy, back2
    )
    return z_grad, noise_grad


def solution(mesh):
    return jax.shard_map(
        on_device,
        mesh=mesh,
        in_specs=(
            P(None, "row", None),
            P(None, ("grp", "row"), None, None),
            P(None, ("grp", "row"), None, None),
            P(None, ("grp", "row"), None, None),
            P("grp", None),
        ),
        out_specs=(P(None, ("grp", "row"), None, None), P(None, ("grp", "row"), None, None)),
        check_vma=False,
    )
```

```python
import jax
import jax.numpy as jnp
from jax import lax
from jax.experimental import pallas as pl
from jax.experimental.pallas import tpu as pltpu
from jax.sharding import PartitionSpec as P

rate_scales = (0.4, 0.4, 0.1, 0.2, 0.1, 0.1)
f32 = jnp.float32
bf16 = jnp.bfloat16
VMEM = pl.BlockSpec(memory_space=pltpu.VMEM)
LIMIT = 24 * 1024 * 1024
FAR_LIMIT = 63 * 1024 * 1024


def call(kernel, outs, flops, moved, scratch=(), scalar=False, far=False):
    def run(*args):
        specs = [pl.BlockSpec(memory_space=pltpu.HBM) if far else pl.BlockSpec() for _ in args]
        if scalar:
            specs[0] = pl.BlockSpec(memory_space=pltpu.SMEM)
        return pl.pallas_call(
            kernel,
            out_shape=outs,
            in_specs=specs,
            scratch_shapes=list(scratch),
            compiler_params=pltpu.CompilerParams(vmem_limit_bytes=FAR_LIMIT if far else LIMIT),
            cost_estimate=pl.CostEstimate(flops=flops, bytes_accessed=moved, transcendentals=0),
        )(*args)

    return run


def split2(value):
    high = value.astype(bf16)
    low = (value - high.astype(f32)).astype(bf16)
    return high, low


def split3(value):
    high = value.astype(bf16)
    rest = value - high.astype(f32)
    mid = rest.astype(bf16)
    low = (rest - mid.astype(f32)).astype(bf16)
    return high, mid, low


def dot(a, b, contract):
    return lax.dot_general(a, b, ((contract[0], contract[1]), ((), ())), preferred_element_type=f32)


def coefficients(table_ref):
    return [[table_ref[:, 6 * s + k : 6 * s + k + 1] for k in range(6)] for s in range(2)]


def side(v):
    n = v.shape[0]
    place = lax.broadcasted_iota(jnp.int32, v.shape, 0)
    left = jnp.where(place == 0, 0.0, pltpu.roll(v, 1, 0))
    right = jnp.where(place == n - 1, 0.0, pltpu.roll(v, n - 1, 0))
    return left + right


def forward_light(c, xa, pa, xb, hop_x, hop_p):
    d, w, g, l, m, j = c
    return (
        -0.5 * l * xa - d * pa - j * hop_p,
        d * xa - 0.5 * l * pa - 2.0 * g * xb + j * hop_x,
    )


def forward_heavy(c, xa, xb, pb):
    d, w, g, l, m, j = c
    return w * pb, -w * xb - 0.5 * m * pb - 2.0 * g * xa


def backward_light(c, xa, pa, pb, hop_x, hop_p):
    d, w, g, l, m, j = c
    return (
        -0.5 * l * xa + d * pa - 2.0 * g * pb + hop_p,
        -d * xa - 0.5 * l * pa - hop_x,
    )


def backward_heavy(c, pa, xb, pb):
    d, w, g, l, m, j = c
    return -2.0 * g * pa - w * pb, w * xb - 0.5 * m * pb


def forward_sources(core_ref, z_hbm, outer1_ref, sems):
    n = z_hbm.shape[2]
    copies = [
        pltpu.make_async_copy(z_hbm.at[k, core_ref[0]], outer1_ref.at[pl.ds(k * n, n)], sems.at[k]) for k in range(2)
    ]
    for copy in copies:
        copy.start()
    outer1_ref[2 * n :] = jnp.zeros((16, z_hbm.shape[3]), f32)
    for copy in copies:
        copy.wait()


def forward_rim(core_ref, coeff_ref, z_ref, outer2_ref, inner1_ref, inner2_ref, table_ref):
    n = z_ref.shape[2]
    core = core_ref[0]
    z = [[z_ref[k, row] for k in range(3)] for row in (core, 1 - core)]
    cols = jnp.transpose(jnp.concatenate([coeff_ref[k] for k in range(6)], axis=0))
    swapped = core == 1
    both = []
    for s in range(2):
        for k in range(6):
            column = jnp.where(swapped, cols[:, 2 * k + 1 - s : 2 * k + 2 - s], cols[:, 2 * k + s : 2 * k + s + 1])
            both.append(column * rate_scales[k])
    for place, column in enumerate(both):
        table_ref[:, place : place + 1] = column
    far = []
    for s in range(2):
        xa, pa, xb = z[s]
        hop_x = z[1 - s][0] + side(xa)
        hop_p = z[1 - s][1] + side(pa)
        far.append(forward_light(both[6 * s : 6 * s + 6], xa, pa, xb, hop_x, hop_p))
    inner1_ref[0:n] = z[1][0]
    inner1_ref[n : 2 * n] = z[1][1]
    for s, out in ((0, outer2_ref), (1, inner2_ref)):
        out[0:n], out[n : 2 * n] = far[s]
        hopping = jnp.where(swapped, coeff_ref[5, 1 - s : 2 - s, :], coeff_ref[5, s : s + 1, :]) * rate_scales[5]
        pieces = [hopping[:, k * 128 : (k + 1) * 128] for k in range(n // 128)]
        pieces.append(jnp.zeros((8 - n // 128, 128), f32))
        out[2 * n :] = jnp.concatenate(pieces, axis=0)


def far_hopping(recv_ref, n):
    size = recv_ref.shape[0]
    tail = jnp.transpose(recv_ref[size - 8 : size])
    return jnp.concatenate([tail[:, k : k + 1] for k in range(n // 128)], axis=0)


def cells(row, k, n):
    return pl.ds(pl.multiple_of((2 * k + row) * n, 128), n)


def packed(gram, cross):
    row = lax.broadcasted_iota(jnp.int32, gram.shape, 0)
    col = lax.broadcasted_iota(jnp.int32, gram.shape, 1)
    diagonal = jnp.sum(jnp.where(row == col, cross, 0.0), axis=0, keepdims=True)
    return jnp.where(row <= col, gram, cross), jnp.broadcast_to(diagonal, (8, gram.shape[1]))


def noise_products(noise_ref, q_ref, pack_ref, nh_ref, nl_ref, qh_ref, ql_ref, nht_ref, nlt_ref, qht_ref, qlt_ref):
    nh, nl = split2(noise_ref[...])
    qh, ql = split2(q_ref[...])
    nh_ref[...] = nh
    nl_ref[...] = nl
    qh_ref[...] = qh
    ql_ref[...] = ql
    for value, out in ((nh, nht_ref), (nl, nlt_ref), (qh, qht_ref), (ql, qlt_ref)):
        out[...] = jnp.transpose(value)
    plain = ((1,), (0,))
    high = dot(jnp.concatenate([nht_ref[...], qht_ref[128:]], axis=0), jnp.concatenate([nh, nl], axis=1), plain)
    low = dot(qlt_ref[128:], nh, plain)
    mixed = high[:128, 128:]
    gram = high[:128, :128] + mixed + jnp.transpose(mixed)
    cross = high[128:, :128] + high[128:, 128:] + low
    pack_ref[0:128], pack_ref[128:] = packed(gram, cross)


def row_products(xh, xl, nht, nlt, qht, qlt):
    plain = ((1,), (0,))
    left = jnp.concatenate([jnp.transpose(xh), nht, qht], axis=0)
    high = dot(left, jnp.concatenate([xh, xl], axis=1), plain)
    low = dot(jnp.concatenate([nlt, qlt], axis=0), xh, plain)
    mixed = high[:128, 128:]
    return (
        high[:128, :128] + mixed + jnp.transpose(mixed),
        high[128:, :128] + high[128:, 128:] + low,
    )


def expand_first(
    core_ref, table_ref, z_ref, outer1_ref, inner1_ref, inner2_ref, nht_ref, nlt_ref, qht_ref, qlt_ref,
    light_ref, hh_ref, hl_ref, ih_ref, il_ref, gram_ref, rest_ref, first_ref,
):
    c = coefficients(table_ref)
    n = z_ref.shape[2]
    core = core_ref[0]
    rows = (core, 1 - core)
    z = [[z_ref[k, row] for k in range(4)] for row in rows]
    for s, beyond in enumerate((outer1_ref, inner1_ref)):
        xa, pa, xb, pb = z[s]
        hop_x = z[1 - s][0] + beyond[0:n] + side(xa)
        hop_p = z[1 - s][1] + beyond[n : 2 * n] + side(pa)
        first_ref[0, s], first_ref[1, s] = forward_light(c[s], xa, pa, xb, hop_x, hop_p)
        first_ref[2, s], first_ref[3, s] = forward_heavy(c[s], xa, xb, pb)
    for s in range(2):
        xa, pa, xb, pb = (first_ref[k, s] for k in range(4))
        for k, (f, second) in enumerate(zip((xb, pb), forward_heavy(c[s], xa, xb, pb))):
            h, l = split2(z[s][2 + k] + f + 0.5 * second)
            hh_ref[cells(rows[s], k, n)] = h
            hl_ref[cells(rows[s], k, n)] = l
    jfar = far_hopping(inner2_ref, n)
    for s in range(2):
        xa, pa, xb, pb = (first_ref[k, s] for k in range(4))
        hop_x = first_ref[0, 1 - s] + side(xa)
        hop_p = first_ref[1, 1 - s] + side(pa)
        if s == 1:
            hop_x = hop_x + inner2_ref[0:n] - jfar * z[s][1]
            hop_p = hop_p + inner2_ref[n : 2 * n] + jfar * z[s][0]
        second = forward_light(c[s], xa, pa, xb, hop_x, hop_p)
        for k in range(2):
            value = z[s][k] + first_ref[k, s] + 0.5 * second[k]
            if s == 0:
                light_ref[k] = value
            else:
                ih_ref[k * n : (k + 1) * n], il_ref[k * n : (k + 1) * n] = split2(value)
    half = 4 * n
    parts = (nht_ref, nlt_ref, qht_ref, qlt_ref)
    gram, rest = row_products(hh_ref[...], hl_ref[...], *(ref[:, half:] for ref in parts))
    for k in range(2):
        there = cells(1 - core, k, n)
        here = slice(k * n, (k + 1) * n)
        more = row_products(ih_ref[here], il_ref[here], *(ref[:, there] for ref in parts))
        gram = gram + more[0]
        rest = rest + more[1]
    gram_ref[...] = gram
    rest_ref[...] = rest


def quarters(core):
    parts = []
    for owner in (core, 1 - core):
        first = pl.multiple_of(owner * 264, 8)
        parts += [pl.ds(first, 136), pl.ds(pl.multiple_of(first + 136, 8), 128)]
    return parts


def expand_last(
    core_ref, table_ref, z_ref, outer2_ref, light_ref, gram_ref, rest_ref, pack_ref,
    nht_ref, nlt_ref, qht_ref, qlt_ref, mine1_ref, mine2_ref, other1_ref, other2_ref, oh_ref, ol_ref, sums_ref,
):
    n = z_ref.shape[2]
    core = core_ref[0]
    jfar = far_hopping(outer2_ref, n)
    far_x = outer2_ref[0:n] - jfar * z_ref[1, core]
    far_p = outer2_ref[n : 2 * n] + jfar * z_ref[0, core]
    j = 0.5 * table_ref[:, 5:6]
    gram, rest = gram_ref[...], rest_ref[...]
    for k, value in enumerate((light_ref[0] - j * far_p, light_ref[1] + j * far_x)):
        h, l = split2(value)
        oh_ref[k * n : (k + 1) * n] = h
        ol_ref[k * n : (k + 1) * n] = l
        there = cells(core, k, n)
        more = row_products(h, l, *(ref[:, there] for ref in (nht_ref, nlt_ref, qht_ref, qlt_ref)))
        gram = gram + more[0]
        rest = rest + more[1]
    sums_ref[0:128], sums_ref[512:520] = packed(gram, rest[128:256])
    sums_ref[128:256] = jnp.transpose(rest[:128])
    sums_ref[256:384] = rest[256:]
    sums_ref[384:512] = pack_ref[0:128]
    sums_ref[520:528] = pack_ref[128:136]
    for part, out in zip(quarters(core), (mine1_ref, mine2_ref, other1_ref, other2_ref)):
        out[...] = sums_ref[part]


def inverse_factor(w_ref, out_ref):
    size = w_ref.shape[0]
    step = 8
    lane = lax.broadcasted_iota(jnp.int32, (step, size), 1)
    place = lax.broadcasted_iota(jnp.int32, (step, size), 0)

    def load(start):
        return [jnp.broadcast_to(w_ref[start + i : start + i + 1, :], (step, size)) for i in range(step)]

    rows = load(0)
    for start in range(0, size, step):
        last = start + step >= size
        reach = step if last else 2 * step
        s = {
            (i, m): jnp.broadcast_to(rows[i][:, start + m : start + m + 1], (step, size))
            for i in range(step)
            for m in range(i, reach)
        }
        inside = (lane >= start) & (lane < start + step)
        rows = [jnp.where(lane == start + i, 1.0, jnp.where(inside, 0.0, rows[i])) for i in range(step)]
        done = []
        change = [None] * step
        for i in range(step):
            inverse = pl.reciprocal(s[i, i])
            root = lax.rsqrt(s[i, i])
            for k in range(i + 1, step):
                ratio = s[i, k] * inverse
                for m in range(k, reach):
                    s[k, m] = s[k, m] - ratio * s[i, m]
                rows[k] = rows[k] - ratio * rows[i]
            if not last:
                scaled = rows[i] * inverse
                for k in range(step):
                    term = s[i, step + k] * scaled
                    change[k] = term if i == 0 else change[k] + term
            done.append(rows[i] * root)
        panel = done[0]
        for i in range(1, step):
            panel = jnp.where(place == i, done[i], panel)
        out_ref[start : start + step, :] = panel
        if not last:
            rows = [jnp.where(inside, 0.0, row) - c for row, c in zip(load(start + step), change)]
        beyond = start + 2 * step
        if beyond < size:
            high, mid, low = (part.astype(f32) for part in split3(panel))
            left = jnp.concatenate([high, high, mid, mid, high, low], axis=0).astype(bf16)
            right = jnp.concatenate([high, mid, high, mid, low, high], axis=0).astype(bf16)
            update = dot(left, right, ((0,), (0,)))[beyond:]
            old = w_ref[beyond:, :]
            column = lax.broadcasted_iota(jnp.int32, old.shape, 1)
            old = jnp.where((column >= start) & (column < start + step), 0.0, old)
            w_ref[beyond:, :] = old - update
    value = out_ref[...]
    row = lax.broadcasted_iota(jnp.int32, value.shape, 0)
    column = lax.broadcasted_iota(jnp.int32, value.shape, 1)
    out_ref[...] = jnp.where(row >= column, value, 0.0)


def factor(
    core_ref, mine1_ref, mine2_ref, other1_ref, other2_ref, r_bar_ref, nh_ref, nl_ref, sh_ref, sl_ref, sums_ref, w_ref, inv1_ref, inv2_ref
):
    tile = 128
    core = core_ref[0]
    for part, value in zip(quarters(core), (mine1_ref, mine2_ref, other1_ref, other2_ref)):
        sums_ref[part] = value[...]

    down, across, plain = ((0,), (0,)), ((1,), (1,)), ((1,), (0,))

    def stacked(a, b, contract):
        a, b = split3(a), split3(b)
        left = jnp.concatenate([a[k] for k in (0, 0, 1, 1, 0, 2)], axis=contract[0][0])
        right = jnp.concatenate([b[k] for k in (0, 1, 0, 1, 2, 0)], axis=contract[1][0])
        return dot(left, right, contract)

    def stacked2(a, b, contract):
        left = jnp.concatenate([a[0], a[0], a[1]], axis=contract[0][0])
        right = jnp.concatenate([b[0], b[1], b[0]], axis=contract[1][0])
        return dot(left, right, contract)

    row = lax.broadcasted_iota(jnp.int32, (2 * tile, 2 * tile), 0)
    col = lax.broadcasted_iota(jnp.int32, (2 * tile, 2 * tile), 1)

    def corner(value, keep):
        return jnp.where(keep[:tile, :tile], value, 0.0)

    def whole(value):
        return corner(value, row <= col) + jnp.transpose(corner(value, row < col))

    pack1, g12, pack2 = sums_ref[0:tile], sums_ref[tile : 2 * tile], sums_ref[3 * tile : 4 * tile]
    w_ref[...] = corner(pack1, row <= col)
    inverse_factor(w_ref, inv1_ref)
    inv1 = inv1_ref[...]
    u12 = stacked(inv1, g12, plain)
    w_ref[...] = corner(pack2, row <= col) - stacked(u12, u12, down)
    inverse_factor(w_ref, inv2_ref)
    inv2 = inv2_ref[...]
    inv21 = -stacked(inv2, stacked(u12, inv1, down), plain)
    zero = jnp.zeros((tile, tile), f32)
    inv = jnp.concatenate(
        [jnp.concatenate([inv1, zero], axis=1), jnp.concatenate([inv21, inv2], axis=1)], axis=0
    )
    gram = jnp.concatenate(
        [
            jnp.concatenate([whole(pack1), g12], axis=1),
            jnp.concatenate([jnp.transpose(g12), whole(pack2)], axis=1),
        ],
        axis=0,
    )
    bar = jnp.where(row <= col, r_bar_ref[...], 0.0)
    top = jnp.concatenate([pack1, zero], axis=1)
    bottom = jnp.concatenate([sums_ref[2 * tile : 3 * tile], pack2], axis=1)
    cross = jnp.concatenate([top, bottom], axis=0)
    diagonal = jnp.concatenate([sums_ref[512:513], sums_ref[520:521]], axis=1)
    cross = jnp.where(row > col, cross, jnp.where(row == col, diagonal, 0.0))
    middle = stacked(inv, stacked(gram, bar, across), plain) - stacked(cross, inv, across)
    symmetric = jnp.where(row >= col, middle, 0.0) + jnp.transpose(jnp.where(row > col, middle, 0.0))
    parts = split2(inv)
    spread = stacked2(parts, split2(stacked2(split2(symmetric), parts, plain)), down)
    nh_ref[...], nl_ref[...] = parts
    sh_ref[...], sl_ref[...] = split2(spread)


def columns(qh, ql, nh, nl, xh, xl, ih, il, sh, sl):
    plain = ((1,), (0,))
    xh = jnp.concatenate([xh, nh], axis=1)
    xl = jnp.concatenate([xl, nl], axis=1)
    high = dot(qh, jnp.concatenate([ih, il], axis=1), plain) + dot(xh, jnp.concatenate([sh, sl], axis=1), plain)
    return high[:, :128] + high[:, 128:] + dot(ql, ih, plain) + dot(xl, sh, plain)


def gradient_outer(
    core_ref, table_ref, qh_ref, ql_ref, nh_ref, nl_ref, oh_ref, ol_ref, ih_ref, il_ref, sh_ref, sl_ref,
    w_ref, outer1_ref,
):
    n = w_ref.shape[1]
    j = table_ref[:, 5:6]
    weights = [ref[:, :128] for ref in (ih_ref, il_ref, sh_ref, sl_ref)]
    for k in range(2):
        there = cells(core_ref[0], k, n)
        here = slice(k * n, (k + 1) * n)
        parts = [ref[there] for ref in (qh_ref, ql_ref, nh_ref, nl_ref)] + [oh_ref[here], ol_ref[here]]
        w = columns(*parts, *weights)
        w_ref[k] = w
        outer1_ref[here] = j * w
    outer1_ref[2 * n :] = jnp.zeros((8, w_ref.shape[2]), f32)


def gradient_rest(
    core_ref, table_ref, outer_ref, outer1_ref, qh_ref, ql_ref, nh_ref, nl_ref, lh_ref, ll_ref, hh_ref, hl_ref,
    ih_ref, il_ref, sh_ref, sl_ref, light_ref, heavy_ref, outer2_ref, inner1_ref, inner2_ref,
):
    c = coefficients(table_ref)
    n = outer_ref.shape[1]
    core = core_ref[0]
    weights = [ref[:, :128] for ref in (ih_ref, il_ref, sh_ref, sl_ref)]
    left = (qh_ref, ql_ref, nh_ref, nl_ref)
    for k in range(2):
        there = cells(1 - core, k, n)
        here = slice(k * n, (k + 1) * n)
        w = columns(*[ref[there] for ref in left], lh_ref[here], ll_ref[here], *weights)
        light_ref[k] = w
        inner1_ref[here] = c[1][5] * w
    for k in (1, 0):
        for s, row in enumerate((core, 1 - core)):
            there = cells(row, 2 + k, n)
            here = cells(row, k, n)
            heavy_ref[k, s] = columns(*[ref[there] for ref in left], hh_ref[here], hl_ref[here], *weights)
    own = (outer1_ref, inner1_ref)
    for s, w, out in ((0, outer_ref, outer2_ref), (1, light_ref, inner2_ref)):
        hop_x = own[1 - s][0:n] + side(own[s][0:n])
        hop_p = own[1 - s][n : 2 * n] + side(own[s][n : 2 * n])
        bx, bp = backward_light(c[s], w[0], w[1], heavy_ref[1, s], hop_x, hop_p)
        out[0:n] = c[s][5] * bx
        out[n : 2 * n] = c[s][5] * bp


def gradient_noise(
    core_ref, qh_ref, ql_ref, nh_ref, nl_ref, oh_ref, ol_ref, lh_ref, ll_ref, hh_ref, hl_ref,
    ih_ref, il_ref, sh_ref, sl_ref, out_ref,
):
    n = out_ref.shape[2]
    core = core_ref[0]
    weights = [ref[:, 128:] for ref in (ih_ref, il_ref, sh_ref, sl_ref)]
    for k in range(4):
        for s, row in enumerate((core, 1 - core)):
            there = cells(row, k, n)
            if k < 2:
                here = slice(k * n, (k + 1) * n)
                x = (oh_ref[here], ol_ref[here]) if s == 0 else (lh_ref[here], ll_ref[here])
            else:
                here = cells(row, k - 2, n)
                x = (hh_ref[here], hl_ref[here])
            out_ref[k, row] = columns(*[ref[there] for ref in (qh_ref, ql_ref, nh_ref, nl_ref)], *x, *weights)


def contract_first(
    core_ref, outer1_ref, table_ref, outer_ref, light_ref, heavy_ref, own1_ref, own2_ref, inner1_ref, inner2_ref,
    fouter2_ref, finner_ref, out_ref, light_out_ref, first_ref,
):
    c = coefficients(table_ref)
    n = outer_ref.shape[1]
    w = [
        (outer_ref[0], outer_ref[1], heavy_ref[0, 0], heavy_ref[1, 0]),
        (light_ref[0], light_ref[1], heavy_ref[0, 1], heavy_ref[1, 1]),
    ]
    own = [(ref[0:n], ref[n : 2 * n]) for ref in (own1_ref, own2_ref)]
    for s, far in enumerate((outer1_ref, inner1_ref)):
        xa, pa, xb, pb = w[s]
        hop_x = own[1 - s][0] + far[0:n] + side(own[s][0])
        hop_p = own[1 - s][1] + far[n : 2 * n] + side(own[s][1])
        first_ref[0, s], first_ref[1, s] = backward_light(c[s], xa, pa, pb, hop_x, hop_p)
        first_ref[2, s], first_ref[3, s] = backward_heavy(c[s], pa, xb, pb)
    for s, fref in enumerate((fouter2_ref, finner_ref)):
        xa, pa, xb, pb = (first_ref[k, s] for k in range(4))
        jfar = far_hopping(fref, n)
        j, jother = c[s][5], c[1 - s][5]
        hop_x = jother * first_ref[0, 1 - s] + jfar * own[s][1] + side(j * xa)
        hop_p = jother * first_ref[1, 1 - s] - jfar * own[s][0] + side(j * pa)
        if s == 1:
            hop_x = hop_x + inner2_ref[0:n]
            hop_p = hop_p + inner2_ref[n : 2 * n]
        light = backward_light(c[s], xa, pa, pb, hop_x, hop_p)
        heavy = backward_heavy(c[s], pa, xb, pb)
        row = core_ref[0] if s == 0 else 1 - core_ref[0]
        for k in range(2):
            value = w[s][k] + first_ref[k, s] + 0.5 * light[k]
            out_ref[k, row] = value
            if s == 0:
                light_out_ref[k] = value
            out_ref[2 + k, row] = w[s][2 + k] + first_ref[2 + k, s] + 0.5 * heavy[k]


def contract_last(core_ref, light_ref, outer2_ref, whole_hbm, out_hbm, value_ref, sems):
    n = light_ref.shape[1]
    core = core_ref[0]
    value_ref[0] = light_ref[0] + 0.5 * outer2_ref[n : 2 * n]
    first = pltpu.make_async_copy(value_ref.at[0], out_hbm.at[0, core], sems.at[0])
    first.start()
    value_ref[1] = light_ref[1] - 0.5 * outer2_ref[0:n]
    second = pltpu.make_async_copy(value_ref.at[1], out_hbm.at[1, core], sems.at[1])
    second.start()
    first.wait()
    second.wait()


def swap_inner(message):
    count = lax.axis_size("row")
    return lax.ppermute(message, "row", [(i, i ^ 1) for i in range(count)])


def swap_outer(message):
    count = lax.axis_size("row")
    pairs = [(i, i + 1) for i in range(1, count - 1, 2)]
    return lax.ppermute(message, "row", pairs + [(j, i) for i, j in pairs])


def sum_over_rows(mine, other):
    count = lax.axis_size("row")
    bits = count.bit_length() - 1
    mine = [m + swap_inner(o) for m, o in zip(mine, other)]
    for step in range(bits - 1):
        for stream in range(2):
            turn = [1 + (step + (core ^ stream)) % (bits - 1) for core in range(2)]
            pairs = [(i, i ^ (1 << turn[i & 1])) for i in range(count)]
            mine[stream] = mine[stream] + lax.ppermute(mine[stream], "row", pairs)
    return mine + [swap_inner(m) for m in mine]


def on_device(cell_coeffs, z_factor, noise_cols, q_bar, r_bar):
    quads, lattice, n, rank = z_factor.shape
    flat = quads * lattice * n
    coeffs = cell_coeffs
    core = (lax.axis_index("row") & 1).reshape(1)
    noise = noise_cols.reshape(flat, -1)
    bar = q_bar.reshape(flat, -1)
    shape = jax.ShapeDtypeStruct
    hops = shape((2 * n, rank), f32)
    rim = shape((2 * n + 8, rank), f32)
    table = shape((n, 16), f32)
    outer1 = call(
        forward_sources, shape((2 * n + 16, rank), f32), 0, 10**6, [pltpu.SemaphoreType.DMA((2,))], scalar=True, far=True
    )(core, z_factor)
    outer1, behind = lax.optimization_barrier((outer1, core))
    outer2, inner1, inner2, table = call(
        forward_rim, (rim, hops, rim, table), 10**6, 3 * 10**6, scalar=True
    )(behind, coeffs, z_factor)
    outer1, outer2 = swap_outer(outer1), swap_outer(outer2)
    inner1, inner2 = swap_inner(inner1), swap_inner(inner2)
    wide, tall = shape((flat, 256), bf16), shape((flat, 128), bf16)
    wide_t, tall_t = shape((256, flat), bf16), shape((128, flat), bf16)
    work = 2 * flat * 128 * 128
    pack, nh, nl, qh, ql, nht, nlt, qht, qlt = call(
        noise_products, (shape((136, 128), f32), tall, tall, wide, wide, tall_t, tall_t, wide_t, wide_t),
        work * 5, 9 * 10**6,
    )(noise, bar)
    transposed = (nht, nlt, qht, qlt)
    half, quarter = shape((flat // 2, 128), bf16), shape((flat // 4, 128), bf16)
    single, pair = shape((2, n, rank), f32), shape((2, lattice, n, rank), f32)
    light, hh, hl, lh, ll, gram, rest = call(
        expand_first,
        (single, half, half, quarter, quarter, shape((128, 128), f32), shape((384, 128), f32)),
        work * 8, 9 * 10**6, [pltpu.VMEM(z_factor.shape, f32)], scalar=True,
    )(core, table, z_factor, outer1, inner1, inner2, *transposed)
    part1, part2 = shape((136, 128), f32), shape((128, 128), f32)
    *parts, oh, ol = call(
        expand_last, (part1, part2, part1, part2, quarter, quarter), work * 3, 5 * 10**6, [pltpu.VMEM((528, 128), f32)], scalar=True
    )(core, table, z_factor, outer2, light, gram, rest, pack, *transposed)
    parts = sum_over_rows(parts[:2], parts[2:])
    square = shape((256, 256), bf16)
    weights = call(
        factor, (square,) * 4, 10**9, 10**6,
        [
            pltpu.VMEM((528, 128), f32),
            pltpu.VMEM((128, 128), f32),
            pltpu.VMEM((128, 128), f32),
            pltpu.VMEM((128, 128), f32),
        ],
        scalar=True,
    )(core, *parts, r_bar)
    left = (qh, ql, nh, nl)
    w_outer, own1 = call(gradient_outer, (single, rim), work * 3, 3 * 10**6, scalar=True)(
        core, table, *left, oh, ol, *weights
    )
    back1 = swap_outer(own1)
    w_inner, w_heavy, last, own2, own3 = call(
        gradient_rest, (single, pair, hops, hops, hops), 10**10, 6 * 10**6, scalar=True
    )(core, table, w_outer, own1, *left, lh, ll, hh, hl, *weights)
    back2, near1, near2 = swap_outer(last), swap_inner(own2), swap_inner(own3)
    noise_grad = call(gradient_noise, shape(noise_cols.shape, f32), 0, 0, scalar=True)(
        core, *left, oh, ol, lh, ll, hh, hl, *weights
    )
    whole, light = call(
        contract_first, (shape(z_factor.shape, f32), single), 10**7, 6 * 10**6,
        [pltpu.VMEM(z_factor.shape, f32)], scalar=True,
    )(core, back1, table, w_outer, w_inner, w_heavy, own1, own2, near1, near2, outer2, inner2)
    z_grad = pl.pallas_call(
        contract_last,
        out_shape=shape(z_factor.shape, f32),
        in_specs=[
            pl.BlockSpec(memory_space=pltpu.SMEM),
            pl.BlockSpec(),
            pl.BlockSpec(),
            pl.BlockSpec(memory_space=pltpu.HBM),
        ],
        out_specs=pl.BlockSpec(memory_space=pltpu.HBM),
        input_output_aliases={3: 0},
        scratch_shapes=[pltpu.VMEM((2, n, rank), f32), pltpu.SemaphoreType.DMA((2,))],
        compiler_params=pltpu.CompilerParams(vmem_limit_bytes=LIMIT),
        cost_estimate=pl.CostEstimate(flops=10**6, bytes_accessed=10**6, transcendentals=0),
    )(core, light, back2, whole)
    return z_grad, noise_grad


def solution(mesh):
    return jax.shard_map(
        on_device,
        mesh=mesh,
        in_specs=(
            P(None, "row", None),
            P(None, ("grp", "row"), None, None),
            P(None, ("grp", "row"), None, None),
            P(None, ("grp", "row"), None, None),
            P("grp", None),
        ),
        out_specs=(P(None, ("grp", "row"), None, None), P(None, ("grp", "row"), None, None)),
        check_vma=False,
    )
```

```python
import jax
import jax.numpy as jnp
from jax import lax
from jax.experimental import pallas as pl
from jax.experimental.pallas import tpu as pltpu
from jax.sharding import PartitionSpec as P

rate_scales = (0.4, 0.4, 0.1, 0.2, 0.1, 0.1)
f32 = jnp.float32
bf16 = jnp.bfloat16
VMEM = pl.BlockSpec(memory_space=pltpu.VMEM)
LIMIT = 24 * 1024 * 1024
FAR_LIMIT = 63 * 1024 * 1024


def call(kernel, outs, flops, moved, scratch=(), scalar=False, far=False):
    def run(*args):
        specs = [pl.BlockSpec(memory_space=pltpu.HBM) if far else pl.BlockSpec() for _ in args]
        if scalar:
            specs[0] = pl.BlockSpec(memory_space=pltpu.SMEM)
        return pl.pallas_call(
            kernel,
            out_shape=outs,
            in_specs=specs,
            scratch_shapes=list(scratch),
            compiler_params=pltpu.CompilerParams(vmem_limit_bytes=FAR_LIMIT if far else LIMIT),
            cost_estimate=pl.CostEstimate(flops=flops, bytes_accessed=moved, transcendentals=0),
        )(*args)

    return run


def split2(value):
    high = value.astype(bf16)
    low = (value - high.astype(f32)).astype(bf16)
    return high, low


def split3(value):
    high = value.astype(bf16)
    rest = value - high.astype(f32)
    mid = rest.astype(bf16)
    low = (rest - mid.astype(f32)).astype(bf16)
    return high, mid, low


def dot(a, b, contract):
    return lax.dot_general(a, b, ((contract[0], contract[1]), ((), ())), preferred_element_type=f32)


def coefficients(table_ref):
    return [[table_ref[:, 6 * s + k : 6 * s + k + 1] for k in range(6)] for s in range(2)]


def side(v):
    n = v.shape[0]
    place = lax.broadcasted_iota(jnp.int32, v.shape, 0)
    left = jnp.where(place == 0, 0.0, pltpu.roll(v, 1, 0))
    right = jnp.where(place == n - 1, 0.0, pltpu.roll(v, n - 1, 0))
    return left + right


def forward_light(c, xa, pa, xb, hop_x, hop_p):
    d, w, g, l, m, j = c
    return (
        -0.5 * l * xa - d * pa - j * hop_p,
        d * xa - 0.5 * l * pa - 2.0 * g * xb + j * hop_x,
    )


def forward_heavy(c, xa, xb, pb):
    d, w, g, l, m, j = c
    return w * pb, -w * xb - 0.5 * m * pb - 2.0 * g * xa


def backward_light(c, xa, pa, pb, hop_x, hop_p):
    d, w, g, l, m, j = c
    return (
        -0.5 * l * xa + d * pa - 2.0 * g * pb + hop_p,
        -d * xa - 0.5 * l * pa - hop_x,
    )


def backward_heavy(c, pa, xb, pb):
    d, w, g, l, m, j = c
    return -2.0 * g * pa - w * pb, w * xb - 0.5 * m * pb


def forward_rim(core_ref, coeff_ref, z_ref, outer2_ref, inner1_ref, inner2_ref, table_ref):
    n = z_ref.shape[2]
    core = core_ref[0]
    z = [[z_ref[k, row] for k in range(3)] for row in (core, 1 - core)]
    cols = jnp.transpose(jnp.concatenate([coeff_ref[k] for k in range(6)], axis=0))
    swapped = core == 1
    both = []
    for s in range(2):
        for k in range(6):
            column = jnp.where(swapped, cols[:, 2 * k + 1 - s : 2 * k + 2 - s], cols[:, 2 * k + s : 2 * k + s + 1])
            both.append(column * rate_scales[k])
    for place, column in enumerate(both):
        table_ref[:, place : place + 1] = column
    far = []
    for s in range(2):
        xa, pa, xb = z[s]
        hop_x = z[1 - s][0] + side(xa)
        hop_p = z[1 - s][1] + side(pa)
        far.append(forward_light(both[6 * s : 6 * s + 6], xa, pa, xb, hop_x, hop_p))
    inner1_ref[0:n] = z[1][0]
    inner1_ref[n : 2 * n] = z[1][1]
    for s, out in ((0, outer2_ref), (1, inner2_ref)):
        out[0:n], out[n : 2 * n] = far[s]
        hopping = jnp.where(swapped, coeff_ref[5, 1 - s : 2 - s, :], coeff_ref[5, s : s + 1, :]) * rate_scales[5]
        pieces = [hopping[:, k * 128 : (k + 1) * 128] for k in range(n // 128)]
        pieces.append(jnp.zeros((8 - n // 128, 128), f32))
        out[2 * n :] = jnp.concatenate(pieces, axis=0)


def far_hopping(recv_ref, n):
    size = recv_ref.shape[0]
    tail = jnp.transpose(recv_ref[size - 8 : size])
    return jnp.concatenate([tail[:, k : k + 1] for k in range(n // 128)], axis=0)


def cells(row, k, n):
    return pl.ds(pl.multiple_of((2 * k + row) * n, 128), n)


def packed(gram, cross):
    row = lax.broadcasted_iota(jnp.int32, gram.shape, 0)
    col = lax.broadcasted_iota(jnp.int32, gram.shape, 1)
    diagonal = jnp.sum(jnp.where(row == col, cross, 0.0), axis=0, keepdims=True)
    return jnp.where(row <= col, gram, cross), jnp.broadcast_to(diagonal, (8, gram.shape[1]))


def noise_products(noise_ref, q_ref, pack_ref, nh_ref, nl_ref, qh_ref, ql_ref, nht_ref, nlt_ref, qht_ref, qlt_ref):
    nh, nl = split2(noise_ref[...])
    qh, ql = split2(q_ref[...])
    nh_ref[...] = nh
    nl_ref[...] = nl
    qh_ref[...] = qh
    ql_ref[...] = ql
    for value, out in ((nh, nht_ref), (nl, nlt_ref), (qh, qht_ref), (ql, qlt_ref)):
        out[...] = jnp.transpose(value)
    plain = ((1,), (0,))
    high = dot(jnp.concatenate([nht_ref[...], qht_ref[128:]], axis=0), jnp.concatenate([nh, nl], axis=1), plain)
    low = dot(qlt_ref[128:], nh, plain)
    mixed = high[:128, 128:]
    gram = high[:128, :128] + mixed + jnp.transpose(mixed)
    cross = high[128:, :128] + high[128:, 128:] + low
    pack_ref[0:128], pack_ref[128:] = packed(gram, cross)


def row_products(xh, xl, nht, nlt, qht, qlt):
    plain = ((1,), (0,))
    left = jnp.concatenate([jnp.transpose(xh), nht, qht], axis=0)
    high = dot(left, jnp.concatenate([xh, xl], axis=1), plain)
    low = dot(jnp.concatenate([nlt, qlt], axis=0), xh, plain)
    mixed = high[:128, 128:]
    return (
        high[:128, :128] + mixed + jnp.transpose(mixed),
        high[128:, :128] + high[128:, 128:] + low,
    )


def expand_first(
    core_ref, table_ref, z_ref, outer1_ref, inner1_ref, inner2_ref, nht_ref, nlt_ref, qht_ref, qlt_ref,
    light_ref, hh_ref, hl_ref, ih_ref, il_ref, gram_ref, rest_ref, first_ref,
):
    c = coefficients(table_ref)
    n = z_ref.shape[2]
    core = core_ref[0]
    rows = (core, 1 - core)
    z = [[z_ref[k, row] for k in range(4)] for row in rows]
    for s, beyond in enumerate((outer1_ref, inner1_ref)):
        xa, pa, xb, pb = z[s]
        hop_x = z[1 - s][0] + beyond[0:n] + side(xa)
        hop_p = z[1 - s][1] + beyond[n : 2 * n] + side(pa)
        first_ref[0, s], first_ref[1, s] = forward_light(c[s], xa, pa, xb, hop_x, hop_p)
        first_ref[2, s], first_ref[3, s] = forward_heavy(c[s], xa, xb, pb)
    for s in range(2):
        xa, pa, xb, pb = (first_ref[k, s] for k in range(4))
        for k, (f, second) in enumerate(zip((xb, pb), forward_heavy(c[s], xa, xb, pb))):
            h, l = split2(z[s][2 + k] + f + 0.5 * second)
            hh_ref[cells(rows[s], k, n)] = h
            hl_ref[cells(rows[s], k, n)] = l
    jfar = far_hopping(inner2_ref, n)
    for s in range(2):
        xa, pa, xb, pb = (first_ref[k, s] for k in range(4))
        hop_x = first_ref[0, 1 - s] + side(xa)
        hop_p = first_ref[1, 1 - s] + side(pa)
        if s == 1:
            hop_x = hop_x + inner2_ref[0:n] - jfar * z[s][1]
            hop_p = hop_p + inner2_ref[n : 2 * n] + jfar * z[s][0]
        second = forward_light(c[s], xa, pa, xb, hop_x, hop_p)
        for k in range(2):
            value = z[s][k] + first_ref[k, s] + 0.5 * second[k]
            if s == 0:
                light_ref[k] = value
            else:
                ih_ref[k * n : (k + 1) * n], il_ref[k * n : (k + 1) * n] = split2(value)
    half = 4 * n
    parts = (nht_ref, nlt_ref, qht_ref, qlt_ref)
    gram, rest = row_products(hh_ref[...], hl_ref[...], *(ref[:, half:] for ref in parts))
    for k in range(2):
        there = cells(1 - core, k, n)
        here = slice(k * n, (k + 1) * n)
        more = row_products(ih_ref[here], il_ref[here], *(ref[:, there] for ref in parts))
        gram = gram + more[0]
        rest = rest + more[1]
    gram_ref[...] = gram
    rest_ref[...] = rest


def quarters(core):
    parts = []
    for owner in (core, 1 - core):
        first = pl.multiple_of(owner * 264, 8)
        parts += [pl.ds(first, 136), pl.ds(pl.multiple_of(first + 136, 8), 128)]
    return parts


def expand_last(
    core_ref, table_ref, z_ref, outer2_ref, light_ref, gram_ref, rest_ref, pack_ref,
    nht_ref, nlt_ref, qht_ref, qlt_ref, mine1_ref, mine2_ref, other1_ref, other2_ref, oh_ref, ol_ref, sums_ref,
):
    n = z_ref.shape[2]
    core = core_ref[0]
    jfar = far_hopping(outer2_ref, n)
    far_x = outer2_ref[0:n] - jfar * z_ref[1, core]
    far_p = outer2_ref[n : 2 * n] + jfar * z_ref[0, core]
    j = 0.5 * table_ref[:, 5:6]
    gram, rest = gram_ref[...], rest_ref[...]
    for k, value in enumerate((light_ref[0] - j * far_p, light_ref[1] + j * far_x)):
        h, l = split2(value)
        oh_ref[k * n : (k + 1) * n] = h
        ol_ref[k * n : (k + 1) * n] = l
        there = cells(core, k, n)
        more = row_products(h, l, *(ref[:, there] for ref in (nht_ref, nlt_ref, qht_ref, qlt_ref)))
        gram = gram + more[0]
        rest = rest + more[1]
    sums_ref[0:128], sums_ref[512:520] = packed(gram, rest[128:256])
    sums_ref[128:256] = jnp.transpose(rest[:128])
    sums_ref[256:384] = rest[256:]
    sums_ref[384:512] = pack_ref[0:128]
    sums_ref[520:528] = pack_ref[128:136]
    for part, out in zip(quarters(core), (mine1_ref, mine2_ref, other1_ref, other2_ref)):
        out[...] = sums_ref[part]


def inverse_factor(w_ref, out_ref):
    size = w_ref.shape[0]
    step = 8
    lane = lax.broadcasted_iota(jnp.int32, (step, size), 1)
    place = lax.broadcasted_iota(jnp.int32, (step, size), 0)

    def load(start):
        return [jnp.broadcast_to(w_ref[start + i : start + i + 1, :], (step, size)) for i in range(step)]

    rows = load(0)
    for start in range(0, size, step):
        last = start + step >= size
        reach = step if last else 2 * step
        s = {
            (i, m): jnp.broadcast_to(rows[i][:, start + m : start + m + 1], (step, size))
            for i in range(step)
            for m in range(i, reach)
        }
        inside = (lane >= start) & (lane < start + step)
        rows = [jnp.where(lane == start + i, 1.0, jnp.where(inside, 0.0, rows[i])) for i in range(step)]
        done = []
        change = [None] * step
        for i in range(step):
            inverse = pl.reciprocal(s[i, i])
            root = lax.rsqrt(s[i, i])
            for k in range(i + 1, step):
                ratio = s[i, k] * inverse
                for m in range(k, reach):
                    s[k, m] = s[k, m] - ratio * s[i, m]
                rows[k] = rows[k] - ratio * rows[i]
            if not last:
                scaled = rows[i] * inverse
                for k in range(step):
                    term = s[i, step + k] * scaled
                    change[k] = term if i == 0 else change[k] + term
            done.append(rows[i] * root)
        panel = done[0]
        for i in range(1, step):
            panel = jnp.where(place == i, done[i], panel)
        out_ref[start : start + step, :] = panel
        if not last:
            rows = [jnp.where(inside, 0.0, row) - c for row, c in zip(load(start + step), change)]
        beyond = start + 2 * step
        if beyond < size:
            high, mid, low = (part.astype(f32) for part in split3(panel))
            left = jnp.concatenate([high, high, mid, mid, high, low], axis=0).astype(bf16)
            right = jnp.concatenate([high, mid, high, mid, low, high], axis=0).astype(bf16)
            update = dot(left, right, ((0,), (0,)))[beyond:]
            old = w_ref[beyond:, :]
            column = lax.broadcasted_iota(jnp.int32, old.shape, 1)
            old = jnp.where((column >= start) & (column < start + step), 0.0, old)
            w_ref[beyond:, :] = old - update
    value = out_ref[...]
    row = lax.broadcasted_iota(jnp.int32, value.shape, 0)
    column = lax.broadcasted_iota(jnp.int32, value.shape, 1)
    out_ref[...] = jnp.where(row >= column, value, 0.0)


def factor(
    core_ref, mine1_ref, mine2_ref, other1_ref, other2_ref, r_bar_ref, *refs
):
    *gradient_refs, nh_ref, nl_ref, sh_ref, sl_ref, grad_ref, outer1_ref, sums_ref, w_ref, inv1_ref, inv2_ref = refs
    tile = 128
    core = core_ref[0]
    for part, value in zip(quarters(core), (mine1_ref, mine2_ref, other1_ref, other2_ref)):
        sums_ref[part] = value[...]

    down, across, plain = ((0,), (0,)), ((1,), (1,)), ((1,), (0,))

    def stacked(a, b, contract):
        a, b = split3(a), split3(b)
        left = jnp.concatenate([a[k] for k in (0, 0, 1, 1, 0, 2)], axis=contract[0][0])
        right = jnp.concatenate([b[k] for k in (0, 1, 0, 1, 2, 0)], axis=contract[1][0])
        return dot(left, right, contract)

    def stacked2(a, b, contract):
        left = jnp.concatenate([a[0], a[0], a[1]], axis=contract[0][0])
        right = jnp.concatenate([b[0], b[1], b[0]], axis=contract[1][0])
        return dot(left, right, contract)

    row = lax.broadcasted_iota(jnp.int32, (2 * tile, 2 * tile), 0)
    col = lax.broadcasted_iota(jnp.int32, (2 * tile, 2 * tile), 1)

    def corner(value, keep):
        return jnp.where(keep[:tile, :tile], value, 0.0)

    def whole(value):
        return corner(value, row <= col) + jnp.transpose(corner(value, row < col))

    pack1, g12, pack2 = sums_ref[0:tile], sums_ref[tile : 2 * tile], sums_ref[3 * tile : 4 * tile]
    w_ref[...] = corner(pack1, row <= col)
    inverse_factor(w_ref, inv1_ref)
    inv1 = inv1_ref[...]
    u12 = stacked(inv1, g12, plain)
    w_ref[...] = corner(pack2, row <= col) - stacked(u12, u12, down)
    inverse_factor(w_ref, inv2_ref)
    inv2 = inv2_ref[...]
    inv21 = -stacked(inv2, stacked(u12, inv1, down), plain)
    zero = jnp.zeros((tile, tile), f32)
    inv = jnp.concatenate(
        [jnp.concatenate([inv1, zero], axis=1), jnp.concatenate([inv21, inv2], axis=1)], axis=0
    )
    gram = jnp.concatenate(
        [
            jnp.concatenate([whole(pack1), g12], axis=1),
            jnp.concatenate([jnp.transpose(g12), whole(pack2)], axis=1),
        ],
        axis=0,
    )
    bar = jnp.where(row <= col, r_bar_ref[...], 0.0)
    top = jnp.concatenate([pack1, zero], axis=1)
    bottom = jnp.concatenate([sums_ref[2 * tile : 3 * tile], pack2], axis=1)
    cross = jnp.concatenate([top, bottom], axis=0)
    diagonal = jnp.concatenate([sums_ref[512:513], sums_ref[520:521]], axis=1)
    cross = jnp.where(row > col, cross, jnp.where(row == col, diagonal, 0.0))
    middle = stacked(inv, stacked(gram, bar, across), plain) - stacked(cross, inv, across)
    symmetric = jnp.where(row >= col, middle, 0.0) + jnp.transpose(jnp.where(row > col, middle, 0.0))
    parts = split2(inv)
    spread = stacked2(parts, split2(stacked2(split2(symmetric), parts, plain)), down)
    nh_ref[...], nl_ref[...] = parts
    sh_ref[...], sl_ref[...] = split2(spread)
    gradient_outer(core_ref, *gradient_refs, nh_ref, nl_ref, sh_ref, sl_ref, grad_ref, outer1_ref)


def columns(qh, ql, nh, nl, xh, xl, ih, il, sh, sl):
    plain = ((1,), (0,))
    xh = jnp.concatenate([xh, nh], axis=1)
    xl = jnp.concatenate([xl, nl], axis=1)
    high = dot(qh, jnp.concatenate([ih, il], axis=1), plain) + dot(xh, jnp.concatenate([sh, sl], axis=1), plain)
    return high[:, :128] + high[:, 128:] + dot(ql, ih, plain) + dot(xl, sh, plain)


def gradient_outer(
    core_ref, table_ref, qh_ref, ql_ref, nh_ref, nl_ref, oh_ref, ol_ref, ih_ref, il_ref, sh_ref, sl_ref,
    w_ref, outer1_ref,
):
    n = w_ref.shape[1]
    j = table_ref[:, 5:6]
    weights = [ref[:, :128] for ref in (ih_ref, il_ref, sh_ref, sl_ref)]
    for k in range(2):
        there = cells(core_ref[0], k, n)
        here = slice(k * n, (k + 1) * n)
        parts = [ref[there] for ref in (qh_ref, ql_ref, nh_ref, nl_ref)] + [oh_ref[here], ol_ref[here]]
        w = columns(*parts, *weights)
        w_ref[k] = w
        outer1_ref[here] = j * w
    outer1_ref[2 * n :] = jnp.zeros((8, w_ref.shape[2]), f32)


def gradient_rest(
    core_ref, table_ref, outer_ref, outer1_ref, qh_ref, ql_ref, nh_ref, nl_ref, lh_ref, ll_ref, hh_ref, hl_ref,
    ih_ref, il_ref, sh_ref, sl_ref, light_ref, heavy_ref, outer2_ref, inner1_ref, inner2_ref,
):
    c = coefficients(table_ref)
    n = outer_ref.shape[1]
    core = core_ref[0]
    weights = [ref[:, :128] for ref in (ih_ref, il_ref, sh_ref, sl_ref)]
    left = (qh_ref, ql_ref, nh_ref, nl_ref)
    for k in range(2):
        there = cells(1 - core, k, n)
        here = slice(k * n, (k + 1) * n)
        w = columns(*[ref[there] for ref in left], lh_ref[here], ll_ref[here], *weights)
        light_ref[k] = w
        inner1_ref[here] = c[1][5] * w
    for k in (1, 0):
        for s, row in enumerate((core, 1 - core)):
            there = cells(row, 2 + k, n)
            here = cells(row, k, n)
            heavy_ref[k, s] = columns(*[ref[there] for ref in left], hh_ref[here], hl_ref[here], *weights)
    own = (outer1_ref, inner1_ref)
    for s, w, out in ((0, outer_ref, outer2_ref), (1, light_ref, inner2_ref)):
        hop_x = own[1 - s][0:n] + side(own[s][0:n])
        hop_p = own[1 - s][n : 2 * n] + side(own[s][n : 2 * n])
        bx, bp = backward_light(c[s], w[0], w[1], heavy_ref[1, s], hop_x, hop_p)
        out[0:n] = c[s][5] * bx
        out[n : 2 * n] = c[s][5] * bp


def gradient_noise(
    core_ref, qh_ref, ql_ref, nh_ref, nl_ref, oh_ref, ol_ref, lh_ref, ll_ref, hh_ref, hl_ref,
    ih_ref, il_ref, sh_ref, sl_ref, out_ref,
):
    n = out_ref.shape[2]
    core = core_ref[0]
    weights = [ref[:, 128:] for ref in (ih_ref, il_ref, sh_ref, sl_ref)]
    for k in range(4):
        for s, row in enumerate((core, 1 - core)):
            there = cells(row, k, n)
            if k < 2:
                here = slice(k * n, (k + 1) * n)
                x = (oh_ref[here], ol_ref[here]) if s == 0 else (lh_ref[here], ll_ref[here])
            else:
                here = cells(row, k - 2, n)
                x = (hh_ref[here], hl_ref[here])
            out_ref[k, row] = columns(*[ref[there] for ref in (qh_ref, ql_ref, nh_ref, nl_ref)], *x, *weights)


def contract_first(
    core_ref, outer1_ref, table_ref, outer_ref, light_ref, heavy_ref, own1_ref, own2_ref, inner1_ref, inner2_ref,
    fouter2_ref, finner_ref, out_ref, light_out_ref, first_ref,
):
    c = coefficients(table_ref)
    n = outer_ref.shape[1]
    w = [
        (outer_ref[0], outer_ref[1], heavy_ref[0, 0], heavy_ref[1, 0]),
        (light_ref[0], light_ref[1], heavy_ref[0, 1], heavy_ref[1, 1]),
    ]
    own = [(ref[0:n], ref[n : 2 * n]) for ref in (own1_ref, own2_ref)]
    for s, far in enumerate((outer1_ref, inner1_ref)):
        xa, pa, xb, pb = w[s]
        hop_x = own[1 - s][0] + far[0:n] + side(own[s][0])
        hop_p = own[1 - s][1] + far[n : 2 * n] + side(own[s][1])
        first_ref[0, s], first_ref[1, s] = backward_light(c[s], xa, pa, pb, hop_x, hop_p)
        first_ref[2, s], first_ref[3, s] = backward_heavy(c[s], pa, xb, pb)
    for s, fref in enumerate((fouter2_ref, finner_ref)):
        xa, pa, xb, pb = (first_ref[k, s] for k in range(4))
        jfar = far_hopping(fref, n)
        j, jother = c[s][5], c[1 - s][5]
        hop_x = jother * first_ref[0, 1 - s] + jfar * own[s][1] + side(j * xa)
        hop_p = jother * first_ref[1, 1 - s] - jfar * own[s][0] + side(j * pa)
        if s == 1:
            hop_x = hop_x + inner2_ref[0:n]
            hop_p = hop_p + inner2_ref[n : 2 * n]
        light = backward_light(c[s], xa, pa, pb, hop_x, hop_p)
        heavy = backward_heavy(c[s], pa, xb, pb)
        row = core_ref[0] if s == 0 else 1 - core_ref[0]
        for k in range(2):
            value = w[s][k] + first_ref[k, s] + 0.5 * light[k]
            out_ref[k, row] = value
            if s == 0:
                light_out_ref[k] = value
            out_ref[2 + k, row] = w[s][2 + k] + first_ref[2 + k, s] + 0.5 * heavy[k]


def contract_last(core_ref, light_ref, outer2_ref, whole_hbm, out_hbm, value_ref, sems):
    n = light_ref.shape[1]
    core = core_ref[0]
    value_ref[0] = light_ref[0] + 0.5 * outer2_ref[n : 2 * n]
    first = pltpu.make_async_copy(value_ref.at[0], out_hbm.at[0, core], sems.at[0])
    first.start()
    value_ref[1] = light_ref[1] - 0.5 * outer2_ref[0:n]
    second = pltpu.make_async_copy(value_ref.at[1], out_hbm.at[1, core], sems.at[1])
    second.start()
    first.wait()
    second.wait()


def swap_inner(message):
    count = lax.axis_size("row")
    return lax.ppermute(message, "row", [(i, i ^ 1) for i in range(count)])


def swap_outer(message):
    count = lax.axis_size("row")
    pairs = [(i, i + 1) for i in range(1, count - 1, 2)]
    return lax.ppermute(message, "row", pairs + [(j, i) for i, j in pairs])


def sum_over_rows(mine, other):
    count = lax.axis_size("row")
    bits = count.bit_length() - 1
    mine = [m + swap_inner(o) for m, o in zip(mine, other)]
    for step in range(bits - 1):
        for stream in range(2):
            turn = [1 + (step + (core ^ stream)) % (bits - 1) for core in range(2)]
            pairs = [(i, i ^ (1 << turn[i & 1])) for i in range(count)]
            mine[stream] = mine[stream] + lax.ppermute(mine[stream], "row", pairs)
    return mine + [swap_inner(m) for m in mine]


def on_device(cell_coeffs, z_factor, noise_cols, q_bar, r_bar):
    quads, lattice, n, rank = z_factor.shape
    flat = quads * lattice * n
    coeffs = cell_coeffs
    core = (lax.axis_index("row") & 1).reshape(1)
    noise = noise_cols.reshape(flat, -1)
    bar = q_bar.reshape(flat, -1)
    shape = jax.ShapeDtypeStruct
    hops = shape((2 * n, rank), f32)
    rim = shape((2 * n + 8, rank), f32)
    table = shape((n, 16), f32)
    outer1 = lax.dynamic_index_in_dim(z_factor[0:2], core[0], axis=1, keepdims=False).reshape(2 * n, rank)
    outer1 = jnp.pad(outer1, ((0, 16), (0, 0)))
    outer1, behind = lax.optimization_barrier((outer1, core))
    outer2, inner1, inner2, table = call(
        forward_rim, (rim, hops, rim, table), 10**6, 3 * 10**6, scalar=True
    )(behind, coeffs, z_factor)
    outer1, outer2 = swap_outer(outer1), swap_outer(outer2)
    inner1, inner2 = swap_inner(inner1), swap_inner(inner2)
    wide, tall = shape((flat, 256), bf16), shape((flat, 128), bf16)
    wide_t, tall_t = shape((256, flat), bf16), shape((128, flat), bf16)
    work = 2 * flat * 128 * 128
    pack, nh, nl, qh, ql, nht, nlt, qht, qlt = call(
        noise_products, (shape((136, 128), f32), tall, tall, wide, wide, tall_t, tall_t, wide_t, wide_t),
        work * 5, 9 * 10**6,
    )(noise, bar)
    transposed = (nht, nlt, qht, qlt)
    half, quarter = shape((flat // 2, 128), bf16), shape((flat // 4, 128), bf16)
    single, pair = shape((2, n, rank), f32), shape((2, lattice, n, rank), f32)
    light, hh, hl, lh, ll, gram, rest = call(
        expand_first,
        (single, half, half, quarter, quarter, shape((128, 128), f32), shape((384, 128), f32)),
        work * 8, 9 * 10**6, [pltpu.VMEM(z_factor.shape, f32)], scalar=True,
    )(core, table, z_factor, outer1, inner1, inner2, *transposed)
    part1, part2 = shape((136, 128), f32), shape((128, 128), f32)
    *parts, oh, ol = call(
        expand_last, (part1, part2, part1, part2, quarter, quarter), work * 3, 5 * 10**6, [pltpu.VMEM((528, 128), f32)], scalar=True
    )(core, table, z_factor, outer2, light, gram, rest, pack, *transposed)
    parts = sum_over_rows(parts[:2], parts[2:])
    square = shape((256, 256), bf16)
    left = (qh, ql, nh, nl)
    *weights, w_outer, own1 = call(
        factor, (square,) * 4 + (single, rim), 10**9, 10**6,
        [
            pltpu.VMEM((528, 128), f32),
            pltpu.VMEM((128, 128), f32),
            pltpu.VMEM((128, 128), f32),
            pltpu.VMEM((128, 128), f32),
        ],
        scalar=True,
    )(core, *parts, r_bar, table, *left, oh, ol)
    back1 = swap_outer(own1)
    w_inner, w_heavy, last, own2, own3 = call(
        gradient_rest, (single, pair, hops, hops, hops), 10**10, 6 * 10**6, scalar=True
    )(core, table, w_outer, own1, *left, lh, ll, hh, hl, *weights)
    back2, near1, near2 = swap_outer(last), swap_inner(own2), swap_inner(own3)
    noise_grad = call(gradient_noise, shape(noise_cols.shape, f32), 0, 0, scalar=True)(
        core, *left, oh, ol, lh, ll, hh, hl, *weights
    )
    whole, light = call(
        contract_first, (shape(z_factor.shape, f32), single), 10**7, 6 * 10**6,
        [pltpu.VMEM(z_factor.shape, f32)], scalar=True,
    )(core, back1, table, w_outer, w_inner, w_heavy, own1, own2, near1, near2, outer2, inner2)
    z_grad = pl.pallas_call(
        contract_last,
        out_shape=shape(z_factor.shape, f32),
        in_specs=[
            pl.BlockSpec(memory_space=pltpu.SMEM),
            pl.BlockSpec(),
            pl.BlockSpec(),
            pl.BlockSpec(memory_space=pltpu.HBM),
        ],
        out_specs=pl.BlockSpec(memory_space=pltpu.HBM),
        input_output_aliases={3: 0},
        scratch_shapes=[pltpu.VMEM((2, n, rank), f32), pltpu.SemaphoreType.DMA((2,))],
        compiler_params=pltpu.CompilerParams(vmem_limit_bytes=LIMIT),
        cost_estimate=pl.CostEstimate(flops=10**6, bytes_accessed=10**6, transcendentals=0),
    )(core, light, back2, whole)
    return z_grad, noise_grad


def solution(mesh):
    return jax.shard_map(
        on_device,
        mesh=mesh,
        in_specs=(
            P(None, "row", None),
            P(None, ("grp", "row"), None, None),
            P(None, ("grp", "row"), None, None),
            P(None, ("grp", "row"), None, None),
            P("grp", None),
        ),
        out_specs=(P(None, ("grp", "row"), None, None), P(None, ("grp", "row"), None, None)),
        check_vma=False,
    )
```

```python
import jax
import jax.numpy as jnp
from jax import lax
from jax.experimental import pallas as pl
from jax.experimental.pallas import tpu as pltpu
from jax.sharding import PartitionSpec as P

rate_scales = (0.4, 0.4, 0.1, 0.2, 0.1, 0.1)
f32 = jnp.float32
bf16 = jnp.bfloat16
VMEM = pl.BlockSpec(memory_space=pltpu.VMEM)
LIMIT = 24 * 1024 * 1024
FAR_LIMIT = 63 * 1024 * 1024


def call(kernel, outs, flops, moved, scratch=(), scalar=False, far=False):
    def run(*args):
        specs = [pl.BlockSpec(memory_space=pltpu.HBM) if far else pl.BlockSpec() for _ in args]
        if scalar:
            specs[0] = pl.BlockSpec(memory_space=pltpu.SMEM)
        return pl.pallas_call(
            kernel,
            out_shape=outs,
            in_specs=specs,
            scratch_shapes=list(scratch),
            compiler_params=pltpu.CompilerParams(vmem_limit_bytes=FAR_LIMIT if far else LIMIT),
            cost_estimate=pl.CostEstimate(flops=flops, bytes_accessed=moved, transcendentals=0),
        )(*args)

    return run


def split2(value):
    high = value.astype(bf16)
    low = (value - high.astype(f32)).astype(bf16)
    return high, low


def split3(value):
    high = value.astype(bf16)
    rest = value - high.astype(f32)
    mid = rest.astype(bf16)
    low = (rest - mid.astype(f32)).astype(bf16)
    return high, mid, low


def dot(a, b, contract):
    return lax.dot_general(a, b, ((contract[0], contract[1]), ((), ())), preferred_element_type=f32)


def coefficients(table_ref):
    return [[table_ref[:, 6 * s + k : 6 * s + k + 1] for k in range(6)] for s in range(2)]


def side(v):
    n = v.shape[0]
    place = lax.broadcasted_iota(jnp.int32, v.shape, 0)
    left = jnp.where(place == 0, 0.0, pltpu.roll(v, 1, 0))
    right = jnp.where(place == n - 1, 0.0, pltpu.roll(v, n - 1, 0))
    return left + right


def forward_light(c, xa, pa, xb, hop_x, hop_p):
    d, w, g, l, m, j = c
    return (
        -0.5 * l * xa - d * pa - j * hop_p,
        d * xa - 0.5 * l * pa - 2.0 * g * xb + j * hop_x,
    )


def forward_heavy(c, xa, xb, pb):
    d, w, g, l, m, j = c
    return w * pb, -w * xb - 0.5 * m * pb - 2.0 * g * xa


def backward_light(c, xa, pa, pb, hop_x, hop_p):
    d, w, g, l, m, j = c
    return (
        -0.5 * l * xa + d * pa - 2.0 * g * pb + hop_p,
        -d * xa - 0.5 * l * pa - hop_x,
    )


def backward_heavy(c, pa, xb, pb):
    d, w, g, l, m, j = c
    return -2.0 * g * pa - w * pb, w * xb - 0.5 * m * pb


def forward_rim(core_ref, coeff_ref, z_ref, outer2_ref, inner1_ref, inner2_ref, table_ref):
    n = z_ref.shape[2]
    core = core_ref[0]
    z = [[z_ref[k, row] for k in range(3)] for row in (core, 1 - core)]
    cols = jnp.transpose(jnp.concatenate([coeff_ref[k] for k in range(6)], axis=0))
    swapped = core == 1
    both = []
    for s in range(2):
        for k in range(6):
            column = jnp.where(swapped, cols[:, 2 * k + 1 - s : 2 * k + 2 - s], cols[:, 2 * k + s : 2 * k + s + 1])
            both.append(column * rate_scales[k])
    for place, column in enumerate(both):
        table_ref[:, place : place + 1] = column
    far = []
    for s in range(2):
        xa, pa, xb = z[s]
        hop_x = z[1 - s][0] + side(xa)
        hop_p = z[1 - s][1] + side(pa)
        far.append(forward_light(both[6 * s : 6 * s + 6], xa, pa, xb, hop_x, hop_p))
    inner1_ref[0:n] = z[1][0]
    inner1_ref[n : 2 * n] = z[1][1]
    for s, out in ((0, outer2_ref), (1, inner2_ref)):
        out[0:n], out[n : 2 * n] = far[s]
        hopping = jnp.where(swapped, coeff_ref[5, 1 - s : 2 - s, :], coeff_ref[5, s : s + 1, :]) * rate_scales[5]
        pieces = [hopping[:, k * 128 : (k + 1) * 128] for k in range(n // 128)]
        pieces.append(jnp.zeros((8 - n // 128, 128), f32))
        out[2 * n :] = jnp.concatenate(pieces, axis=0)


def far_hopping(recv_ref, n):
    size = recv_ref.shape[0]
    tail = jnp.transpose(recv_ref[size - 8 : size])
    return jnp.concatenate([tail[:, k : k + 1] for k in range(n // 128)], axis=0)


def cells(row, k, n):
    return pl.ds(pl.multiple_of((2 * k + row) * n, 128), n)


def packed(gram, cross):
    row = lax.broadcasted_iota(jnp.int32, gram.shape, 0)
    col = lax.broadcasted_iota(jnp.int32, gram.shape, 1)
    diagonal = jnp.sum(jnp.where(row == col, cross, 0.0), axis=0, keepdims=True)
    return jnp.where(row <= col, gram, cross), jnp.broadcast_to(diagonal, (8, gram.shape[1]))


def noise_products(noise_ref, q_ref, pack_ref, nh_ref, nl_ref, qh_ref, ql_ref, nht_ref, nlt_ref, qht_ref, qlt_ref):
    nh, nl = split2(noise_ref[...])
    qh, ql = split2(q_ref[...])
    nh_ref[...] = nh
    nl_ref[...] = nl
    qh_ref[...] = qh
    ql_ref[...] = ql
    for value, out in ((nh, nht_ref), (nl, nlt_ref), (qh, qht_ref), (ql, qlt_ref)):
        out[...] = jnp.transpose(value)
    plain = ((1,), (0,))
    high = dot(jnp.concatenate([nht_ref[...], qht_ref[128:]], axis=0), jnp.concatenate([nh, nl], axis=1), plain)
    low = dot(qlt_ref[128:], nh, plain)
    mixed = high[:128, 128:]
    gram = high[:128, :128] + mixed + jnp.transpose(mixed)
    cross = high[128:, :128] + high[128:, 128:] + low
    pack_ref[0:128], pack_ref[128:] = packed(gram, cross)


def row_products(xh, xl, nht, nlt, qht, qlt):
    plain = ((1,), (0,))
    left = jnp.concatenate([jnp.transpose(xh), nht, qht], axis=0)
    high = dot(left, jnp.concatenate([xh, xl], axis=1), plain)
    low = dot(jnp.concatenate([nlt, qlt], axis=0), xh, plain)
    mixed = high[:128, 128:]
    return (
        high[:128, :128] + mixed + jnp.transpose(mixed),
        high[128:, :128] + high[128:, 128:] + low,
    )


def expand_first(
    core_ref, table_ref, z_ref, outer1_ref, inner1_ref, inner2_ref, nht_ref, nlt_ref, qht_ref, qlt_ref,
    light_ref, hh_ref, hl_ref, ih_ref, il_ref, gram_ref, rest_ref, first_ref,
):
    c = coefficients(table_ref)
    n = z_ref.shape[2]
    core = core_ref[0]
    rows = (core, 1 - core)
    z = [[z_ref[k, row] for k in range(4)] for row in rows]
    for s, beyond in enumerate((outer1_ref, inner1_ref)):
        xa, pa, xb, pb = z[s]
        hop_x = z[1 - s][0] + beyond[0:n] + side(xa)
        hop_p = z[1 - s][1] + beyond[n : 2 * n] + side(pa)
        first_ref[0, s], first_ref[1, s] = forward_light(c[s], xa, pa, xb, hop_x, hop_p)
        first_ref[2, s], first_ref[3, s] = forward_heavy(c[s], xa, xb, pb)
    for s in range(2):
        xa, pa, xb, pb = (first_ref[k, s] for k in range(4))
        for k, (f, second) in enumerate(zip((xb, pb), forward_heavy(c[s], xa, xb, pb))):
            h, l = split2(z[s][2 + k] + f + 0.5 * second)
            hh_ref[cells(rows[s], k, n)] = h
            hl_ref[cells(rows[s], k, n)] = l
    jfar = far_hopping(inner2_ref, n)
    for s in range(2):
        xa, pa, xb, pb = (first_ref[k, s] for k in range(4))
        hop_x = first_ref[0, 1 - s] + side(xa)
        hop_p = first_ref[1, 1 - s] + side(pa)
        if s == 1:
            hop_x = hop_x + inner2_ref[0:n] - jfar * z[s][1]
            hop_p = hop_p + inner2_ref[n : 2 * n] + jfar * z[s][0]
        second = forward_light(c[s], xa, pa, xb, hop_x, hop_p)
        for k in range(2):
            value = z[s][k] + first_ref[k, s] + 0.5 * second[k]
            if s == 0:
                light_ref[k] = value
            else:
                ih_ref[k * n : (k + 1) * n], il_ref[k * n : (k + 1) * n] = split2(value)
    half = 4 * n
    parts = (nht_ref, nlt_ref, qht_ref, qlt_ref)
    gram, rest = row_products(hh_ref[...], hl_ref[...], *(ref[:, half:] for ref in parts))
    for k in range(2):
        there = cells(1 - core, k, n)
        here = slice(k * n, (k + 1) * n)
        more = row_products(ih_ref[here], il_ref[here], *(ref[:, there] for ref in parts))
        gram = gram + more[0]
        rest = rest + more[1]
    gram_ref[...] = gram
    rest_ref[...] = rest


def quarters(core):
    parts = []
    for owner in (core, 1 - core):
        first = pl.multiple_of(owner * 264, 8)
        parts += [pl.ds(first, 136), pl.ds(pl.multiple_of(first + 136, 8), 128)]
    return parts


def expand_last(
    core_ref, table_ref, z_ref, outer2_ref, light_ref, gram_ref, rest_ref, pack_ref,
    nht_ref, nlt_ref, qht_ref, qlt_ref, mine1_ref, mine2_ref, other1_ref, other2_ref, oh_ref, ol_ref, sums_ref,
):
    n = z_ref.shape[2]
    core = core_ref[0]
    jfar = far_hopping(outer2_ref, n)
    far_x = outer2_ref[0:n] - jfar * z_ref[1, core]
    far_p = outer2_ref[n : 2 * n] + jfar * z_ref[0, core]
    j = 0.5 * table_ref[:, 5:6]
    gram, rest = gram_ref[...], rest_ref[...]
    for k, value in enumerate((light_ref[0] - j * far_p, light_ref[1] + j * far_x)):
        h, l = split2(value)
        oh_ref[k * n : (k + 1) * n] = h
        ol_ref[k * n : (k + 1) * n] = l
        there = cells(core, k, n)
        more = row_products(h, l, *(ref[:, there] for ref in (nht_ref, nlt_ref, qht_ref, qlt_ref)))
        gram = gram + more[0]
        rest = rest + more[1]
    sums_ref[0:128], sums_ref[512:520] = packed(gram, rest[128:256])
    sums_ref[128:256] = jnp.transpose(rest[:128])
    sums_ref[256:384] = rest[256:]
    sums_ref[384:512] = pack_ref[0:128]
    sums_ref[520:528] = pack_ref[128:136]
    for part, out in zip(quarters(core), (mine1_ref, mine2_ref, other1_ref, other2_ref)):
        out[...] = sums_ref[part]


def inverse_factor(w_ref, out_ref):
    size = w_ref.shape[0]
    step = 8
    lane = lax.broadcasted_iota(jnp.int32, (step, size), 1)
    place = lax.broadcasted_iota(jnp.int32, (step, size), 0)

    def load(start):
        return [jnp.broadcast_to(w_ref[start + i : start + i + 1, :], (step, size)) for i in range(step)]

    rows = load(0)
    for start in range(0, size, step):
        last = start + step >= size
        reach = step if last else 2 * step
        wanted = [(i, m) for i in range(step) for m in range(i, step)]
        wanted += [(i, m) for i in range(step) for m in range(step, reach)]
        s = {(i, m): jnp.broadcast_to(rows[i][:, start + m : start + m + 1], (step, size)) for i, m in wanted}
        inside = (lane >= start) & (lane < start + step)
        rows = [jnp.where(lane == start + i, 1.0, jnp.where(inside, 0.0, rows[i])) for i in range(step)]
        done = []
        change = [None] * step
        for i in range(step):
            inverse = pl.reciprocal(s[i, i])
            root = lax.rsqrt(s[i, i])
            ratio = {k: s[i, k] * inverse for k in range(i + 1, step)}
            for part in (range(step), range(step, reach)):
                for k in range(i + 1, step):
                    for m in part:
                        if m >= k:
                            s[k, m] = s[k, m] - ratio[k] * s[i, m]
            for k in range(i + 1, step):
                rows[k] = rows[k] - ratio[k] * rows[i]
            if not last:
                scaled = rows[i] * inverse
                for k in range(step):
                    term = s[i, step + k] * scaled
                    change[k] = term if i == 0 else change[k] + term
            done.append(rows[i] * root)
        panel = done[0]
        for i in range(1, step):
            panel = jnp.where(place == i, done[i], panel)
        out_ref[start : start + step, :] = panel
        if not last:
            rows = [jnp.where(inside, 0.0, row) - c for row, c in zip(load(start + step), change)]
        beyond = start + 2 * step
        if beyond < size:
            high, mid, low = (part.astype(f32) for part in split3(panel))
            left = jnp.concatenate([high, high, mid, mid, high, low], axis=0).astype(bf16)
            right = jnp.concatenate([high, mid, high, mid, low, high], axis=0).astype(bf16)
            update = dot(left, right, ((0,), (0,)))[beyond:]
            old = w_ref[beyond:, :]
            column = lax.broadcasted_iota(jnp.int32, old.shape, 1)
            old = jnp.where((column >= start) & (column < start + step), 0.0, old)
            w_ref[beyond:, :] = old - update
    value = out_ref[...]
    row = lax.broadcasted_iota(jnp.int32, value.shape, 0)
    column = lax.broadcasted_iota(jnp.int32, value.shape, 1)
    out_ref[...] = jnp.where(row >= column, value, 0.0)


def factor(
    core_ref, mine1_ref, mine2_ref, other1_ref, other2_ref, r_bar_ref, *refs
):
    *gradient_refs, nh_ref, nl_ref, sh_ref, sl_ref, grad_ref, outer1_ref, sums_ref, w_ref, inv1_ref, inv2_ref = refs
    tile = 128
    core = core_ref[0]
    for part, value in zip(quarters(core), (mine1_ref, mine2_ref, other1_ref, other2_ref)):
        sums_ref[part] = value[...]

    down, across, plain = ((0,), (0,)), ((1,), (1,)), ((1,), (0,))

    def stacked(a, b, contract):
        a, b = split3(a), split3(b)
        left = jnp.concatenate([a[k] for k in (0, 0, 1, 1, 0, 2)], axis=contract[0][0])
        right = jnp.concatenate([b[k] for k in (0, 1, 0, 1, 2, 0)], axis=contract[1][0])
        return dot(left, right, contract)

    def stacked2(a, b, contract):
        left = jnp.concatenate([a[0], a[0], a[1]], axis=contract[0][0])
        right = jnp.concatenate([b[0], b[1], b[0]], axis=contract[1][0])
        return dot(left, right, contract)

    row = lax.broadcasted_iota(jnp.int32, (2 * tile, 2 * tile), 0)
    col = lax.broadcasted_iota(jnp.int32, (2 * tile, 2 * tile), 1)

    def corner(value, keep):
        return jnp.where(keep[:tile, :tile], value, 0.0)

    def whole(value):
        return corner(value, row <= col) + jnp.transpose(corner(value, row < col))

    pack1, g12, pack2 = sums_ref[0:tile], sums_ref[tile : 2 * tile], sums_ref[3 * tile : 4 * tile]
    w_ref[...] = corner(pack1, row <= col)
    inverse_factor(w_ref, inv1_ref)
    inv1 = inv1_ref[...]
    u12 = stacked(inv1, g12, plain)
    w_ref[...] = corner(pack2, row <= col) - stacked(u12, u12, down)
    inverse_factor(w_ref, inv2_ref)
    inv2 = inv2_ref[...]
    inv21 = -stacked(inv2, stacked(u12, inv1, down), plain)
    zero = jnp.zeros((tile, tile), f32)
    inv = jnp.concatenate(
        [jnp.concatenate([inv1, zero], axis=1), jnp.concatenate([inv21, inv2], axis=1)], axis=0
    )
    gram = jnp.concatenate(
        [
            jnp.concatenate([whole(pack1), g12], axis=1),
            jnp.concatenate([jnp.transpose(g12), whole(pack2)], axis=1),
        ],
        axis=0,
    )
    bar = jnp.where(row <= col, r_bar_ref[...], 0.0)
    top = jnp.concatenate([pack1, zero], axis=1)
    bottom = jnp.concatenate([sums_ref[2 * tile : 3 * tile], pack2], axis=1)
    cross = jnp.concatenate([top, bottom], axis=0)
    diagonal = jnp.concatenate([sums_ref[512:513], sums_ref[520:521]], axis=1)
    cross = jnp.where(row > col, cross, jnp.where(row == col, diagonal, 0.0))
    middle = stacked(inv, stacked(gram, bar, across), plain) - stacked(cross, inv, across)
    symmetric = jnp.where(row >= col, middle, 0.0) + jnp.transpose(jnp.where(row > col, middle, 0.0))
    parts = split2(inv)
    spread = stacked2(parts, split2(stacked2(split2(symmetric), parts, plain)), down)
    nh_ref[...], nl_ref[...] = parts
    sh_ref[...], sl_ref[...] = split2(spread)
    gradient_outer(core_ref, *gradient_refs, nh_ref, nl_ref, sh_ref, sl_ref, grad_ref, outer1_ref)


def columns(qh, ql, nh, nl, xh, xl, ih, il, sh, sl):
    plain = ((1,), (0,))
    xh = jnp.concatenate([xh, nh], axis=1)
    xl = jnp.concatenate([xl, nl], axis=1)
    high = dot(qh, jnp.concatenate([ih, il], axis=1), plain) + dot(xh, jnp.concatenate([sh, sl], axis=1), plain)
    return high[:, :128] + high[:, 128:] + dot(ql, ih, plain) + dot(xl, sh, plain)


def gradient_outer(
    core_ref, table_ref, qh_ref, ql_ref, nh_ref, nl_ref, oh_ref, ol_ref, ih_ref, il_ref, sh_ref, sl_ref,
    w_ref, outer1_ref,
):
    n = w_ref.shape[1]
    j = table_ref[:, 5:6]
    weights = [ref[:, :128] for ref in (ih_ref, il_ref, sh_ref, sl_ref)]
    for k in range(2):
        there = cells(core_ref[0], k, n)
        here = slice(k * n, (k + 1) * n)
        parts = [ref[there] for ref in (qh_ref, ql_ref, nh_ref, nl_ref)] + [oh_ref[here], ol_ref[here]]
        w = columns(*parts, *weights)
        w_ref[k] = w
        outer1_ref[here] = j * w
    outer1_ref[2 * n :] = jnp.zeros((8, w_ref.shape[2]), f32)


def gradient_rest(
    core_ref, table_ref, outer_ref, outer1_ref, qh_ref, ql_ref, nh_ref, nl_ref, lh_ref, ll_ref, hh_ref, hl_ref,
    ih_ref, il_ref, sh_ref, sl_ref, light_ref, heavy_ref, outer2_ref, inner1_ref, inner2_ref,
):
    c = coefficients(table_ref)
    n = outer_ref.shape[1]
    core = core_ref[0]
    weights = [ref[:, :128] for ref in (ih_ref, il_ref, sh_ref, sl_ref)]
    left = (qh_ref, ql_ref, nh_ref, nl_ref)
    for k in range(2):
        there = cells(1 - core, k, n)
        here = slice(k * n, (k + 1) * n)
        w = columns(*[ref[there] for ref in left], lh_ref[here], ll_ref[here], *weights)
        light_ref[k] = w
        inner1_ref[here] = c[1][5] * w
    for k in (1, 0):
        for s, row in enumerate((core, 1 - core)):
            there = cells(row, 2 + k, n)
            here = cells(row, k, n)
            heavy_ref[k, s] = columns(*[ref[there] for ref in left], hh_ref[here], hl_ref[here], *weights)
    own = (outer1_ref, inner1_ref)
    for s, w, out in ((0, outer_ref, outer2_ref), (1, light_ref, inner2_ref)):
        hop_x = own[1 - s][0:n] + side(own[s][0:n])
        hop_p = own[1 - s][n : 2 * n] + side(own[s][n : 2 * n])
        bx, bp = backward_light(c[s], w[0], w[1], heavy_ref[1, s], hop_x, hop_p)
        out[0:n] = c[s][5] * bx
        out[n : 2 * n] = c[s][5] * bp


def gradient_noise(
    core_ref, qh_ref, ql_ref, nh_ref, nl_ref, oh_ref, ol_ref, lh_ref, ll_ref, hh_ref, hl_ref,
    ih_ref, il_ref, sh_ref, sl_ref, out_ref,
):
    n = out_ref.shape[2]
    core = core_ref[0]
    weights = [ref[:, 128:] for ref in (ih_ref, il_ref, sh_ref, sl_ref)]
    for k in range(4):
        for s, row in enumerate((core, 1 - core)):
            there = cells(row, k, n)
            if k < 2:
                here = slice(k * n, (k + 1) * n)
                x = (oh_ref[here], ol_ref[here]) if s == 0 else (lh_ref[here], ll_ref[here])
            else:
                here = cells(row, k - 2, n)
                x = (hh_ref[here], hl_ref[here])
            out_ref[k, row] = columns(*[ref[there] for ref in (qh_ref, ql_ref, nh_ref, nl_ref)], *x, *weights)


def contract_first(
    core_ref, outer1_ref, table_ref, outer_ref, light_ref, heavy_ref, own1_ref, own2_ref, inner1_ref, inner2_ref,
    fouter2_ref, finner_ref, out_ref, light_out_ref, first_ref,
):
    c = coefficients(table_ref)
    n = outer_ref.shape[1]
    w = [
        (outer_ref[0], outer_ref[1], heavy_ref[0, 0], heavy_ref[1, 0]),
        (light_ref[0], light_ref[1], heavy_ref[0, 1], heavy_ref[1, 1]),
    ]
    own = [(ref[0:n], ref[n : 2 * n]) for ref in (own1_ref, own2_ref)]
    for s, far in enumerate((outer1_ref, inner1_ref)):
        xa, pa, xb, pb = w[s]
        hop_x = own[1 - s][0] + far[0:n] + side(own[s][0])
        hop_p = own[1 - s][1] + far[n : 2 * n] + side(own[s][1])
        first_ref[0, s], first_ref[1, s] = backward_light(c[s], xa, pa, pb, hop_x, hop_p)
        first_ref[2, s], first_ref[3, s] = backward_heavy(c[s], pa, xb, pb)
    for s, fref in enumerate((fouter2_ref, finner_ref)):
        xa, pa, xb, pb = (first_ref[k, s] for k in range(4))
        jfar = far_hopping(fref, n)
        j, jother = c[s][5], c[1 - s][5]
        hop_x = jother * first_ref[0, 1 - s] + jfar * own[s][1] + side(j * xa)
        hop_p = jother * first_ref[1, 1 - s] - jfar * own[s][0] + side(j * pa)
        if s == 1:
            hop_x = hop_x + inner2_ref[0:n]
            hop_p = hop_p + inner2_ref[n : 2 * n]
        light = backward_light(c[s], xa, pa, pb, hop_x, hop_p)
        heavy = backward_heavy(c[s], pa, xb, pb)
        row = core_ref[0] if s == 0 else 1 - core_ref[0]
        for k in range(2):
            value = w[s][k] + first_ref[k, s] + 0.5 * light[k]
            out_ref[k, row] = value
            if s == 0:
                light_out_ref[k] = value
            out_ref[2 + k, row] = w[s][2 + k] + first_ref[2 + k, s] + 0.5 * heavy[k]


def contract_last(core_ref, light_ref, outer2_ref, whole_hbm, out_hbm, value_ref, sems):
    n = light_ref.shape[1]
    core = core_ref[0]
    value_ref[0] = light_ref[0] + 0.5 * outer2_ref[n : 2 * n]
    first = pltpu.make_async_copy(value_ref.at[0], out_hbm.at[0, core], sems.at[0])
    first.start()
    value_ref[1] = light_ref[1] - 0.5 * outer2_ref[0:n]
    second = pltpu.make_async_copy(value_ref.at[1], out_hbm.at[1, core], sems.at[1])
    second.start()
    first.wait()
    second.wait()


def swap_inner(message):
    count = lax.axis_size("row")
    return lax.ppermute(message, "row", [(i, i ^ 1) for i in range(count)])


def swap_outer(message):
    count = lax.axis_size("row")
    pairs = [(i, i + 1) for i in range(1, count - 1, 2)]
    return lax.ppermute(message, "row", pairs + [(j, i) for i, j in pairs])


def sum_over_rows(mine, other):
    count = lax.axis_size("row")
    bits = count.bit_length() - 1
    mine = [m + swap_inner(o) for m, o in zip(mine, other)]
    for step in range(bits - 1):
        for stream in range(2):
            turn = [1 + (step + (core ^ stream)) % (bits - 1) for core in range(2)]
            pairs = [(i, i ^ (1 << turn[i & 1])) for i in range(count)]
            mine[stream] = mine[stream] + lax.ppermute(mine[stream], "row", pairs)
    return mine + [swap_inner(m) for m in mine]


def on_device(cell_coeffs, z_factor, noise_cols, q_bar, r_bar):
    quads, lattice, n, rank = z_factor.shape
    flat = quads * lattice * n
    coeffs = cell_coeffs
    core = (lax.axis_index("row") & 1).reshape(1)
    noise = noise_cols.reshape(flat, -1)
    bar = q_bar.reshape(flat, -1)
    shape = jax.ShapeDtypeStruct
    hops = shape((2 * n, rank), f32)
    rim = shape((2 * n + 8, rank), f32)
    table = shape((n, 16), f32)
    outer1 = lax.dynamic_index_in_dim(z_factor[0:2], core[0], axis=1, keepdims=False).reshape(2 * n, rank)
    outer1 = jnp.pad(outer1, ((0, 16), (0, 0)))
    outer1, behind = lax.optimization_barrier((outer1, core))
    outer2, inner1, inner2, table = call(
        forward_rim, (rim, hops, rim, table), 10**6, 3 * 10**6, scalar=True
    )(behind, coeffs, z_factor)
    outer1, outer2 = swap_outer(outer1), swap_outer(outer2)
    inner1, inner2 = swap_inner(inner1), swap_inner(inner2)
    wide, tall = shape((flat, 256), bf16), shape((flat, 128), bf16)
    wide_t, tall_t = shape((256, flat), bf16), shape((128, flat), bf16)
    work = 2 * flat * 128 * 128
    pack, nh, nl, qh, ql, nht, nlt, qht, qlt = call(
        noise_products, (shape((136, 128), f32), tall, tall, wide, wide, tall_t, tall_t, wide_t, wide_t),
        work * 5, 9 * 10**6,
    )(noise, bar)
    transposed = (nht, nlt, qht, qlt)
    half, quarter = shape((flat // 2, 128), bf16), shape((flat // 4, 128), bf16)
    single, pair = shape((2, n, rank), f32), shape((2, lattice, n, rank), f32)
    light, hh, hl, lh, ll, gram, rest = call(
        expand_first,
        (single, half, half, quarter, quarter, shape((128, 128), f32), shape((384, 128), f32)),
        work * 8, 9 * 10**6, [pltpu.VMEM(z_factor.shape, f32)], scalar=True,
    )(core, table, z_factor, outer1, inner1, inner2, *transposed)
    part1, part2 = shape((136, 128), f32), shape((128, 128), f32)
    *parts, oh, ol = call(
        expand_last, (part1, part2, part1, part2, quarter, quarter), work * 3, 5 * 10**6, [pltpu.VMEM((528, 128), f32)], scalar=True
    )(core, table, z_factor, outer2, light, gram, rest, pack, *transposed)
    parts = sum_over_rows(parts[:2], parts[2:])
    square = shape((256, 256), bf16)
    left = (qh, ql, nh, nl)
    *weights, w_outer, own1 = call(
        factor, (square,) * 4 + (single, rim), 10**9, 10**6,
        [
            pltpu.VMEM((528, 128), f32),
            pltpu.VMEM((128, 128), f32),
            pltpu.VMEM((128, 128), f32),
            pltpu.VMEM((128, 128), f32),
        ],
        scalar=True,
    )(core, *parts, r_bar, table, *left, oh, ol)
    back1 = swap_outer(own1)
    w_inner, w_heavy, last, own2, own3 = call(
        gradient_rest, (single, pair, hops, hops, hops), 10**10, 6 * 10**6, scalar=True
    )(core, table, w_outer, own1, *left, lh, ll, hh, hl, *weights)
    back2, near1, near2 = swap_outer(last), swap_inner(own2), swap_inner(own3)
    noise_grad = call(gradient_noise, shape(noise_cols.shape, f32), 0, 0, scalar=True)(
        core, *left, oh, ol, lh, ll, hh, hl, *weights
    )
    whole, light = call(
        contract_first, (shape(z_factor.shape, f32), single), 10**7, 6 * 10**6,
        [pltpu.VMEM(z_factor.shape, f32)], scalar=True,
    )(core, back1, table, w_outer, w_inner, w_heavy, own1, own2, near1, near2, outer2, inner2)
    z_grad = pl.pallas_call(
        contract_last,
        out_shape=shape(z_factor.shape, f32),
        in_specs=[
            pl.BlockSpec(memory_space=pltpu.SMEM),
            pl.BlockSpec(),
            pl.BlockSpec(),
            pl.BlockSpec(memory_space=pltpu.HBM),
        ],
        out_specs=pl.BlockSpec(memory_space=pltpu.HBM),
        input_output_aliases={3: 0},
        scratch_shapes=[pltpu.VMEM((2, n, rank), f32), pltpu.SemaphoreType.DMA((2,))],
        compiler_params=pltpu.CompilerParams(vmem_limit_bytes=LIMIT),
        cost_estimate=pl.CostEstimate(flops=10**6, bytes_accessed=10**6, transcendentals=0),
    )(core, light, back2, whole)
    return z_grad, noise_grad


def solution(mesh):
    return jax.shard_map(
        on_device,
        mesh=mesh,
        in_specs=(
            P(None, "row", None),
            P(None, ("grp", "row"), None, None),
            P(None, ("grp", "row"), None, None),
            P(None, ("grp", "row"), None, None),
            P("grp", None),
        ),
        out_specs=(P(None, ("grp", "row"), None, None), P(None, ("grp", "row"), None, None)),
        check_vma=False,
    )
```

```python
import jax
import jax.numpy as jnp
from jax import lax
from jax.experimental import pallas as pl
from jax.experimental.pallas import tpu as pltpu
from jax.sharding import PartitionSpec as P

rate_scales = (0.4, 0.4, 0.1, 0.2, 0.1, 0.1)
f32 = jnp.float32
bf16 = jnp.bfloat16
VMEM = pl.BlockSpec(memory_space=pltpu.VMEM)
LIMIT = 24 * 1024 * 1024
FAR_LIMIT = 63 * 1024 * 1024


def call(kernel, outs, flops, moved, scratch=(), scalar=False, far=False):
    def run(*args):
        specs = [pl.BlockSpec(memory_space=pltpu.HBM) if far else pl.BlockSpec() for _ in args]
        if scalar:
            specs[0] = pl.BlockSpec(memory_space=pltpu.SMEM)
        return pl.pallas_call(
            kernel,
            out_shape=outs,
            in_specs=specs,
            scratch_shapes=list(scratch),
            compiler_params=pltpu.CompilerParams(vmem_limit_bytes=FAR_LIMIT if far else LIMIT),
            cost_estimate=pl.CostEstimate(flops=flops, bytes_accessed=moved, transcendentals=0),
        )(*args)

    return run


def split2(value):
    high = value.astype(bf16)
    low = (value - high.astype(f32)).astype(bf16)
    return high, low


def split3(value):
    high = value.astype(bf16)
    rest = value - high.astype(f32)
    mid = rest.astype(bf16)
    low = (rest - mid.astype(f32)).astype(bf16)
    return high, mid, low


def dot(a, b, contract):
    return lax.dot_general(a, b, ((contract[0], contract[1]), ((), ())), preferred_element_type=f32)


def coefficients(table_ref):
    return [[table_ref[:, 6 * s + k : 6 * s + k + 1] for k in range(6)] for s in range(2)]


def side(v):
    n = v.shape[0]
    place = lax.broadcasted_iota(jnp.int32, v.shape, 0)
    left = jnp.where(place == 0, 0.0, pltpu.roll(v, 1, 0))
    right = jnp.where(place == n - 1, 0.0, pltpu.roll(v, n - 1, 0))
    return left + right


def forward_light(c, xa, pa, xb, hop_x, hop_p):
    d, w, g, l, m, j = c
    return (
        -0.5 * l * xa - d * pa - j * hop_p,
        d * xa - 0.5 * l * pa - 2.0 * g * xb + j * hop_x,
    )


def forward_heavy(c, xa, xb, pb):
    d, w, g, l, m, j = c
    return w * pb, -w * xb - 0.5 * m * pb - 2.0 * g * xa


def backward_light(c, xa, pa, pb, hop_x, hop_p):
    d, w, g, l, m, j = c
    return (
        -0.5 * l * xa + d * pa - 2.0 * g * pb + hop_p,
        -d * xa - 0.5 * l * pa - hop_x,
    )


def backward_heavy(c, pa, xb, pb):
    d, w, g, l, m, j = c
    return -2.0 * g * pa - w * pb, w * xb - 0.5 * m * pb


def forward_rim(core_ref, coeff_ref, z_ref, outer2_ref, inner1_ref, inner2_ref, table_ref):
    n = z_ref.shape[2]
    core = core_ref[0]
    z = [[z_ref[k, row] for k in range(3)] for row in (core, 1 - core)]
    cols = jnp.transpose(jnp.concatenate([coeff_ref[k] for k in range(6)], axis=0))
    swapped = core == 1
    both = []
    for s in range(2):
        for k in range(6):
            column = jnp.where(swapped, cols[:, 2 * k + 1 - s : 2 * k + 2 - s], cols[:, 2 * k + s : 2 * k + s + 1])
            both.append(column * rate_scales[k])
    for place, column in enumerate(both):
        table_ref[:, place : place + 1] = column
    far = []
    for s in range(2):
        xa, pa, xb = z[s]
        hop_x = z[1 - s][0] + side(xa)
        hop_p = z[1 - s][1] + side(pa)
        far.append(forward_light(both[6 * s : 6 * s + 6], xa, pa, xb, hop_x, hop_p))
    inner1_ref[0:n] = z[1][0]
    inner1_ref[n : 2 * n] = z[1][1]
    for s, out in ((0, outer2_ref), (1, inner2_ref)):
        out[0:n], out[n : 2 * n] = far[s]
        hopping = jnp.where(swapped, coeff_ref[5, 1 - s : 2 - s, :], coeff_ref[5, s : s + 1, :]) * rate_scales[5]
        pieces = [hopping[:, k * 128 : (k + 1) * 128] for k in range(n // 128)]
        pieces.append(jnp.zeros((8 - n // 128, 128), f32))
        out[2 * n :] = jnp.concatenate(pieces, axis=0)


def far_hopping(recv_ref, n):
    size = recv_ref.shape[0]
    tail = jnp.transpose(recv_ref[size - 8 : size])
    return jnp.concatenate([tail[:, k : k + 1] for k in range(n // 128)], axis=0)


def cells(row, k, n):
    return pl.ds(pl.multiple_of((2 * k + row) * n, 128), n)


def packed(gram, cross):
    row = lax.broadcasted_iota(jnp.int32, gram.shape, 0)
    col = lax.broadcasted_iota(jnp.int32, gram.shape, 1)
    diagonal = jnp.sum(jnp.where(row == col, cross, 0.0), axis=0, keepdims=True)
    return jnp.where(row <= col, gram, cross), jnp.broadcast_to(diagonal, (8, gram.shape[1]))


def noise_products(noise_ref, q_ref, pack_ref, nh_ref, nl_ref, qh_ref, ql_ref, nht_ref, nlt_ref, qht_ref, qlt_ref):
    nh, nl = split2(noise_ref[...])
    qh, ql = split2(q_ref[...])
    nh_ref[...] = nh
    nl_ref[...] = nl
    qh_ref[...] = qh
    ql_ref[...] = ql
    for value, out in ((nh, nht_ref), (nl, nlt_ref), (qh, qht_ref), (ql, qlt_ref)):
        out[...] = jnp.transpose(value)
    plain = ((1,), (0,))
    high = dot(jnp.concatenate([nht_ref[...], qht_ref[128:]], axis=0), jnp.concatenate([nh, nl], axis=1), plain)
    low = dot(qlt_ref[128:], nh, plain)
    mixed = high[:128, 128:]
    gram = high[:128, :128] + mixed + jnp.transpose(mixed)
    cross = high[128:, :128] + high[128:, 128:] + low
    pack_ref[0:128], pack_ref[128:] = packed(gram, cross)


def row_products(xh, xl, nht, nlt, qht, qlt):
    plain = ((1,), (0,))
    left = jnp.concatenate([jnp.transpose(xh), nht, qht], axis=0)
    high = dot(left, jnp.concatenate([xh, xl], axis=1), plain)
    low = dot(jnp.concatenate([nlt, qlt], axis=0), xh, plain)
    mixed = high[:128, 128:]
    return (
        high[:128, :128] + mixed + jnp.transpose(mixed),
        high[128:, :128] + high[128:, 128:] + low,
    )


def expand_first(
    core_ref, table_ref, z_ref, outer1_ref, inner1_ref, inner2_ref, nht_ref, nlt_ref, qht_ref, qlt_ref,
    light_ref, hh_ref, hl_ref, ih_ref, il_ref, gram_ref, rest_ref, first_ref,
):
    c = coefficients(table_ref)
    n = z_ref.shape[2]
    core = core_ref[0]
    rows = (core, 1 - core)
    z = [[z_ref[k, row] for k in range(4)] for row in rows]
    for s, beyond in enumerate((outer1_ref, inner1_ref)):
        xa, pa, xb, pb = z[s]
        hop_x = z[1 - s][0] + beyond[0:n] + side(xa)
        hop_p = z[1 - s][1] + beyond[n : 2 * n] + side(pa)
        first_ref[0, s], first_ref[1, s] = forward_light(c[s], xa, pa, xb, hop_x, hop_p)
        first_ref[2, s], first_ref[3, s] = forward_heavy(c[s], xa, xb, pb)
    for s in range(2):
        xa, pa, xb, pb = (first_ref[k, s] for k in range(4))
        for k, (f, second) in enumerate(zip((xb, pb), forward_heavy(c[s], xa, xb, pb))):
            h, l = split2(z[s][2 + k] + f + 0.5 * second)
            hh_ref[cells(rows[s], k, n)] = h
            hl_ref[cells(rows[s], k, n)] = l
    jfar = far_hopping(inner2_ref, n)
    for s in range(2):
        xa, pa, xb, pb = (first_ref[k, s] for k in range(4))
        hop_x = first_ref[0, 1 - s] + side(xa)
        hop_p = first_ref[1, 1 - s] + side(pa)
        if s == 1:
            hop_x = hop_x + inner2_ref[0:n] - jfar * z[s][1]
            hop_p = hop_p + inner2_ref[n : 2 * n] + jfar * z[s][0]
        second = forward_light(c[s], xa, pa, xb, hop_x, hop_p)
        for k in range(2):
            value = z[s][k] + first_ref[k, s] + 0.5 * second[k]
            if s == 0:
                light_ref[k] = value
            else:
                ih_ref[k * n : (k + 1) * n], il_ref[k * n : (k + 1) * n] = split2(value)
    half = 4 * n
    parts = (nht_ref, nlt_ref, qht_ref, qlt_ref)
    gram, rest = row_products(hh_ref[...], hl_ref[...], *(ref[:, half:] for ref in parts))
    for k in range(2):
        there = cells(1 - core, k, n)
        here = slice(k * n, (k + 1) * n)
        more = row_products(ih_ref[here], il_ref[here], *(ref[:, there] for ref in parts))
        gram = gram + more[0]
        rest = rest + more[1]
    gram_ref[...] = gram
    rest_ref[...] = rest


def quarters(core):
    parts = []
    for owner in (core, 1 - core):
        first = pl.multiple_of(owner * 264, 8)
        parts += [pl.ds(first, 136), pl.ds(pl.multiple_of(first + 136, 8), 128)]
    return parts


def expand_last(
    core_ref, table_ref, z_ref, outer2_ref, light_ref, gram_ref, rest_ref, pack_ref,
    nht_ref, nlt_ref, qht_ref, qlt_ref, mine1_ref, mine2_ref, other1_ref, other2_ref, oh_ref, ol_ref, sums_ref,
):
    n = z_ref.shape[2]
    core = core_ref[0]
    jfar = far_hopping(outer2_ref, n)
    far_x = outer2_ref[0:n] - jfar * z_ref[1, core]
    far_p = outer2_ref[n : 2 * n] + jfar * z_ref[0, core]
    j = 0.5 * table_ref[:, 5:6]
    gram, rest = gram_ref[...], rest_ref[...]
    for k, value in enumerate((light_ref[0] - j * far_p, light_ref[1] + j * far_x)):
        h, l = split2(value)
        oh_ref[k * n : (k + 1) * n] = h
        ol_ref[k * n : (k + 1) * n] = l
        there = cells(core, k, n)
        more = row_products(h, l, *(ref[:, there] for ref in (nht_ref, nlt_ref, qht_ref, qlt_ref)))
        gram = gram + more[0]
        rest = rest + more[1]
    sums_ref[0:128], sums_ref[512:520] = packed(gram, rest[128:256])
    sums_ref[128:256] = jnp.transpose(rest[:128])
    sums_ref[256:384] = rest[256:]
    sums_ref[384:512] = pack_ref[0:128]
    sums_ref[520:528] = pack_ref[128:136]
    for part, out in zip(quarters(core), (mine1_ref, mine2_ref, other1_ref, other2_ref)):
        out[...] = sums_ref[part]


def inverse_factor(w_ref, out_ref):
    size = w_ref.shape[0]
    step = 8
    lane = lax.broadcasted_iota(jnp.int32, (step, size), 1)
    place = lax.broadcasted_iota(jnp.int32, (step, size), 0)

    def load(start):
        return [jnp.broadcast_to(w_ref[start + i : start + i + 1, :], (step, size)) for i in range(step)]

    rows = load(0)
    for start in range(0, size, step):
        last = start + step >= size
        reach = step if last else 2 * step
        wanted = [(i, m) for i in range(step) for m in range(i, step)]
        wanted += [(i, m) for i in range(step) for m in range(step, reach)]
        s = {(i, m): jnp.broadcast_to(rows[i][:, start + m : start + m + 1], (step, size)) for i, m in wanted}
        inside = (lane >= start) & (lane < start + step)
        rows = [jnp.where(lane == start + i, 1.0, jnp.where(inside, 0.0, rows[i])) for i in range(step)]
        done = []
        change = [None] * step
        for i in range(step):
            inverse = pl.reciprocal(s[i, i])
            root = lax.rsqrt(s[i, i])
            ratio = {k: s[i, k] * inverse for k in range(i + 1, step)}
            for part in (range(step), range(step, reach)):
                for k in range(i + 1, step):
                    for m in part:
                        if m >= k:
                            s[k, m] = s[k, m] - ratio[k] * s[i, m]
            for k in range(i + 1, step):
                rows[k] = rows[k] - ratio[k] * rows[i]
            if not last:
                scaled = rows[i] * inverse
                for k in range(step):
                    term = s[i, step + k] * scaled
                    change[k] = term if i == 0 else change[k] + term
            done.append(rows[i] * root)
        panel = done[0]
        for i in range(1, step):
            panel = jnp.where(place == i, done[i], panel)
        out_ref[start : start + step, :] = panel
        if not last:
            rows = [jnp.where(inside, 0.0, row) - c for row, c in zip(load(start + step), change)]
        beyond = start + 2 * step
        if beyond < size:
            high, mid, low = (part.astype(f32) for part in split3(panel))
            left = jnp.concatenate([high, high, mid, mid, high, low], axis=0).astype(bf16)
            right = jnp.concatenate([high, mid, high, mid, low, high], axis=0).astype(bf16)
            update = dot(left, right, ((0,), (0,)))[beyond:]
            old = w_ref[beyond:, :]
            column = lax.broadcasted_iota(jnp.int32, old.shape, 1)
            old = jnp.where((column >= start) & (column < start + step), 0.0, old)
            w_ref[beyond:, :] = old - update
    value = out_ref[...]
    row = lax.broadcasted_iota(jnp.int32, value.shape, 0)
    column = lax.broadcasted_iota(jnp.int32, value.shape, 1)
    out_ref[...] = jnp.where(row >= column, value, 0.0)


def stacked2(a, b, contract):
    left = jnp.concatenate([a[0], a[0], a[1]], axis=contract[0][0])
    right = jnp.concatenate([b[0], b[1], b[0]], axis=contract[1][0])
    return dot(left, right, contract)


def spread_columns(inv, symmetric, cols):
    inner = stacked2(symmetric, [part[:, cols] for part in inv], ((1,), (0,)))
    return split2(stacked2(inv, split2(inner), ((0,), (0,))))


def factor(
    core_ref, mine1_ref, mine2_ref, other1_ref, other2_ref, r_bar_ref, *refs
):
    *gradient_refs, nh_ref, nl_ref, sh_ref, sl_ref, yh_ref, yl_ref, grad_ref, outer1_ref, sums_ref, w_ref, inv1_ref, inv2_ref = refs
    tile = 128
    core = core_ref[0]
    for part, value in zip(quarters(core), (mine1_ref, mine2_ref, other1_ref, other2_ref)):
        sums_ref[part] = value[...]

    down, across, plain = ((0,), (0,)), ((1,), (1,)), ((1,), (0,))

    def stacked(a, b, contract):
        a, b = split3(a), split3(b)
        left = jnp.concatenate([a[k] for k in (0, 0, 1, 1, 0, 2)], axis=contract[0][0])
        right = jnp.concatenate([b[k] for k in (0, 1, 0, 1, 2, 0)], axis=contract[1][0])
        return dot(left, right, contract)

    row = lax.broadcasted_iota(jnp.int32, (2 * tile, 2 * tile), 0)
    col = lax.broadcasted_iota(jnp.int32, (2 * tile, 2 * tile), 1)

    def corner(value, keep):
        return jnp.where(keep[:tile, :tile], value, 0.0)

    def whole(value):
        return corner(value, row <= col) + jnp.transpose(corner(value, row < col))

    pack1, g12, pack2 = sums_ref[0:tile], sums_ref[tile : 2 * tile], sums_ref[3 * tile : 4 * tile]
    w_ref[...] = corner(pack1, row <= col)
    inverse_factor(w_ref, inv1_ref)
    inv1 = inv1_ref[...]
    u12 = stacked(inv1, g12, plain)
    w_ref[...] = corner(pack2, row <= col) - stacked(u12, u12, down)
    inverse_factor(w_ref, inv2_ref)
    inv2 = inv2_ref[...]
    inv21 = -stacked(inv2, stacked(u12, inv1, down), plain)
    zero = jnp.zeros((tile, tile), f32)
    inv = jnp.concatenate(
        [jnp.concatenate([inv1, zero], axis=1), jnp.concatenate([inv21, inv2], axis=1)], axis=0
    )
    gram = jnp.concatenate(
        [
            jnp.concatenate([whole(pack1), g12], axis=1),
            jnp.concatenate([jnp.transpose(g12), whole(pack2)], axis=1),
        ],
        axis=0,
    )
    bar = jnp.where(row <= col, r_bar_ref[...], 0.0)
    top = jnp.concatenate([pack1, zero], axis=1)
    bottom = jnp.concatenate([sums_ref[2 * tile : 3 * tile], pack2], axis=1)
    cross = jnp.concatenate([top, bottom], axis=0)
    diagonal = jnp.concatenate([sums_ref[512:513], sums_ref[520:521]], axis=1)
    cross = jnp.where(row > col, cross, jnp.where(row == col, diagonal, 0.0))
    middle = stacked(inv, stacked(gram, bar, across), plain) - stacked(cross, inv, across)
    symmetric = jnp.where(row >= col, middle, 0.0) + jnp.transpose(jnp.where(row > col, middle, 0.0))
    parts = split2(inv)
    symmetric = split2(symmetric)
    nh_ref[...], nl_ref[...] = parts
    yh_ref[...], yl_ref[...] = symmetric
    sh_ref[...], sl_ref[...] = spread_columns(parts, symmetric, slice(0, 128))
    gradient_outer(core_ref, *gradient_refs, nh_ref, nl_ref, sh_ref, sl_ref, grad_ref, outer1_ref)


def columns(qh, ql, nh, nl, xh, xl, ih, il, sh, sl):
    plain = ((1,), (0,))
    xh = jnp.concatenate([xh, nh], axis=1)
    xl = jnp.concatenate([xl, nl], axis=1)
    high = dot(qh, jnp.concatenate([ih, il], axis=1), plain) + dot(xh, jnp.concatenate([sh, sl], axis=1), plain)
    return high[:, :128] + high[:, 128:] + dot(ql, ih, plain) + dot(xl, sh, plain)


def gradient_outer(
    core_ref, table_ref, qh_ref, ql_ref, nh_ref, nl_ref, oh_ref, ol_ref, ih_ref, il_ref, sh_ref, sl_ref,
    w_ref, outer1_ref,
):
    n = w_ref.shape[1]
    j = table_ref[:, 5:6]
    weights = [ref[:, :128] for ref in (ih_ref, il_ref, sh_ref, sl_ref)]
    for k in range(2):
        there = cells(core_ref[0], k, n)
        here = slice(k * n, (k + 1) * n)
        parts = [ref[there] for ref in (qh_ref, ql_ref, nh_ref, nl_ref)] + [oh_ref[here], ol_ref[here]]
        w = columns(*parts, *weights)
        w_ref[k] = w
        outer1_ref[here] = j * w
    outer1_ref[2 * n :] = jnp.zeros((8, w_ref.shape[2]), f32)


def gradient_rest(
    core_ref, table_ref, outer_ref, outer1_ref, qh_ref, ql_ref, nh_ref, nl_ref, lh_ref, ll_ref, hh_ref, hl_ref,
    ih_ref, il_ref, sh_ref, sl_ref, light_ref, heavy_ref, outer2_ref, inner1_ref, inner2_ref,
):
    c = coefficients(table_ref)
    n = outer_ref.shape[1]
    core = core_ref[0]
    weights = [ref[:, :128] for ref in (ih_ref, il_ref, sh_ref, sl_ref)]
    left = (qh_ref, ql_ref, nh_ref, nl_ref)
    for k in range(2):
        there = cells(1 - core, k, n)
        here = slice(k * n, (k + 1) * n)
        w = columns(*[ref[there] for ref in left], lh_ref[here], ll_ref[here], *weights)
        light_ref[k] = w
        inner1_ref[here] = c[1][5] * w
    for k in (1, 0):
        for s, row in enumerate((core, 1 - core)):
            there = cells(row, 2 + k, n)
            here = cells(row, k, n)
            heavy_ref[k, s] = columns(*[ref[there] for ref in left], hh_ref[here], hl_ref[here], *weights)
    own = (outer1_ref, inner1_ref)
    for s, w, out in ((0, outer_ref, outer2_ref), (1, light_ref, inner2_ref)):
        hop_x = own[1 - s][0:n] + side(own[s][0:n])
        hop_p = own[1 - s][n : 2 * n] + side(own[s][n : 2 * n])
        bx, bp = backward_light(c[s], w[0], w[1], heavy_ref[1, s], hop_x, hop_p)
        out[0:n] = c[s][5] * bx
        out[n : 2 * n] = c[s][5] * bp


def gradient_noise(
    core_ref, qh_ref, ql_ref, nh_ref, nl_ref, oh_ref, ol_ref, lh_ref, ll_ref, hh_ref, hl_ref,
    ih_ref, il_ref, yh_ref, yl_ref, out_ref,
):
    n = out_ref.shape[2]
    core = core_ref[0]
    inv = (ih_ref[...], il_ref[...])
    cols = slice(128, 256)
    weights = [part[:, cols] for part in inv]
    weights += spread_columns(inv, (yh_ref[...], yl_ref[...]), cols)
    for k in range(4):
        for s, row in enumerate((core, 1 - core)):
            there = cells(row, k, n)
            if k < 2:
                here = slice(k * n, (k + 1) * n)
                x = (oh_ref[here], ol_ref[here]) if s == 0 else (lh_ref[here], ll_ref[here])
            else:
                here = cells(row, k - 2, n)
                x = (hh_ref[here], hl_ref[here])
            out_ref[k, row] = columns(*[ref[there] for ref in (qh_ref, ql_ref, nh_ref, nl_ref)], *x, *weights)


def contract_first(
    core_ref, outer1_ref, table_ref, outer_ref, light_ref, heavy_ref, own1_ref, own2_ref, inner1_ref, inner2_ref,
    fouter2_ref, finner_ref, out_ref, light_out_ref, first_ref,
):
    c = coefficients(table_ref)
    n = outer_ref.shape[1]
    w = [
        (outer_ref[0], outer_ref[1], heavy_ref[0, 0], heavy_ref[1, 0]),
        (light_ref[0], light_ref[1], heavy_ref[0, 1], heavy_ref[1, 1]),
    ]
    own = [(ref[0:n], ref[n : 2 * n]) for ref in (own1_ref, own2_ref)]
    for s, far in enumerate((outer1_ref, inner1_ref)):
        xa, pa, xb, pb = w[s]
        hop_x = own[1 - s][0] + far[0:n] + side(own[s][0])
        hop_p = own[1 - s][1] + far[n : 2 * n] + side(own[s][1])
        first_ref[0, s], first_ref[1, s] = backward_light(c[s], xa, pa, pb, hop_x, hop_p)
        first_ref[2, s], first_ref[3, s] = backward_heavy(c[s], pa, xb, pb)
    for s, fref in enumerate((fouter2_ref, finner_ref)):
        xa, pa, xb, pb = (first_ref[k, s] for k in range(4))
        jfar = far_hopping(fref, n)
        j, jother = c[s][5], c[1 - s][5]
        hop_x = jother * first_ref[0, 1 - s] + jfar * own[s][1] + side(j * xa)
        hop_p = jother * first_ref[1, 1 - s] - jfar * own[s][0] + side(j * pa)
        if s == 1:
            hop_x = hop_x + inner2_ref[0:n]
            hop_p = hop_p + inner2_ref[n : 2 * n]
        light = backward_light(c[s], xa, pa, pb, hop_x, hop_p)
        heavy = backward_heavy(c[s], pa, xb, pb)
        row = core_ref[0] if s == 0 else 1 - core_ref[0]
        for k in range(2):
            value = w[s][k] + first_ref[k, s] + 0.5 * light[k]
            out_ref[k, row] = value
            if s == 0:
                light_out_ref[k] = value
            out_ref[2 + k, row] = w[s][2 + k] + first_ref[2 + k, s] + 0.5 * heavy[k]


def contract_last(core_ref, light_ref, outer2_ref, whole_hbm, out_hbm, value_ref, sems):
    n = light_ref.shape[1]
    core = core_ref[0]
    value_ref[0] = light_ref[0] + 0.5 * outer2_ref[n : 2 * n]
    first = pltpu.make_async_copy(value_ref.at[0], out_hbm.at[0, core], sems.at[0])
    first.start()
    value_ref[1] = light_ref[1] - 0.5 * outer2_ref[0:n]
    second = pltpu.make_async_copy(value_ref.at[1], out_hbm.at[1, core], sems.at[1])
    second.start()
    first.wait()
    second.wait()


def swap_inner(message):
    count = lax.axis_size("row")
    return lax.ppermute(message, "row", [(i, i ^ 1) for i in range(count)])


def swap_outer(message):
    count = lax.axis_size("row")
    pairs = [(i, i + 1) for i in range(1, count - 1, 2)]
    return lax.ppermute(message, "row", pairs + [(j, i) for i, j in pairs])


def sum_over_rows(mine, other):
    count = lax.axis_size("row")
    bits = count.bit_length() - 1
    mine = [m + swap_inner(o) for m, o in zip(mine, other)]
    for step in range(bits - 1):
        for stream in range(2):
            turn = [1 + (step + (core ^ stream)) % (bits - 1) for core in range(2)]
            pairs = [(i, i ^ (1 << turn[i & 1])) for i in range(count)]
            mine[stream] = mine[stream] + lax.ppermute(mine[stream], "row", pairs)
    return mine + [swap_inner(m) for m in mine]


def on_device(cell_coeffs, z_factor, noise_cols, q_bar, r_bar):
    quads, lattice, n, rank = z_factor.shape
    flat = quads * lattice * n
    coeffs = cell_coeffs
    core = (lax.axis_index("row") & 1).reshape(1)
    noise = noise_cols.reshape(flat, -1)
    bar = q_bar.reshape(flat, -1)
    shape = jax.ShapeDtypeStruct
    hops = shape((2 * n, rank), f32)
    rim = shape((2 * n + 8, rank), f32)
    table = shape((n, 16), f32)
    outer1 = lax.dynamic_index_in_dim(z_factor[0:2], core[0], axis=1, keepdims=False).reshape(2 * n, rank)
    outer1 = jnp.pad(outer1, ((0, 16), (0, 0)))
    outer1, behind = lax.optimization_barrier((outer1, core))
    outer2, inner1, inner2, table = call(
        forward_rim, (rim, hops, rim, table), 10**6, 3 * 10**6, scalar=True
    )(behind, coeffs, z_factor)
    outer1, outer2 = swap_outer(outer1), swap_outer(outer2)
    inner1, inner2 = swap_inner(inner1), swap_inner(inner2)
    wide, tall = shape((flat, 256), bf16), shape((flat, 128), bf16)
    wide_t, tall_t = shape((256, flat), bf16), shape((128, flat), bf16)
    work = 2 * flat * 128 * 128
    pack, nh, nl, qh, ql, nht, nlt, qht, qlt = call(
        noise_products, (shape((136, 128), f32), tall, tall, wide, wide, tall_t, tall_t, wide_t, wide_t),
        work * 5, 9 * 10**6,
    )(noise, bar)
    transposed = (nht, nlt, qht, qlt)
    half, quarter = shape((flat // 2, 128), bf16), shape((flat // 4, 128), bf16)
    single, pair = shape((2, n, rank), f32), shape((2, lattice, n, rank), f32)
    light, hh, hl, lh, ll, gram, rest = call(
        expand_first,
        (single, half, half, quarter, quarter, shape((128, 128), f32), shape((384, 128), f32)),
        work * 8, 9 * 10**6, [pltpu.VMEM(z_factor.shape, f32)], scalar=True,
    )(core, table, z_factor, outer1, inner1, inner2, *transposed)
    part1, part2 = shape((136, 128), f32), shape((128, 128), f32)
    *parts, oh, ol = call(
        expand_last, (part1, part2, part1, part2, quarter, quarter), work * 3, 5 * 10**6, [pltpu.VMEM((528, 128), f32)], scalar=True
    )(core, table, z_factor, outer2, light, gram, rest, pack, *transposed)
    parts = sum_over_rows(parts[:2], parts[2:])
    square = shape((256, 256), bf16)
    left = (qh, ql, nh, nl)
    *weights, yh, yl, w_outer, own1 = call(
        factor, (square,) * 2 + (shape((256, 128), bf16),) * 2 + (square,) * 2 + (single, rim), 10**9, 10**6,
        [
            pltpu.VMEM((528, 128), f32),
            pltpu.VMEM((128, 128), f32),
            pltpu.VMEM((128, 128), f32),
            pltpu.VMEM((128, 128), f32),
        ],
        scalar=True,
    )(core, *parts, r_bar, table, *left, oh, ol)
    back1 = swap_outer(own1)
    w_inner, w_heavy, last, own2, own3 = call(
        gradient_rest, (single, pair, hops, hops, hops), 10**10, 6 * 10**6, scalar=True
    )(core, table, w_outer, own1, *left, lh, ll, hh, hl, *weights)
    back2, near1, near2 = swap_outer(last), swap_inner(own2), swap_inner(own3)
    noise_grad = call(gradient_noise, shape(noise_cols.shape, f32), 0, 0, scalar=True)(
        core, *left, oh, ol, lh, ll, hh, hl, *weights[:2], yh, yl
    )
    whole, light = call(
        contract_first, (shape(z_factor.shape, f32), single), 10**7, 6 * 10**6,
        [pltpu.VMEM(z_factor.shape, f32)], scalar=True,
    )(core, back1, table, w_outer, w_inner, w_heavy, own1, own2, near1, near2, outer2, inner2)
    z_grad = pl.pallas_call(
        contract_last,
        out_shape=shape(z_factor.shape, f32),
        in_specs=[
            pl.BlockSpec(memory_space=pltpu.SMEM),
            pl.BlockSpec(),
            pl.BlockSpec(),
            pl.BlockSpec(memory_space=pltpu.HBM),
        ],
        out_specs=pl.BlockSpec(memory_space=pltpu.HBM),
        input_output_aliases={3: 0},
        scratch_shapes=[pltpu.VMEM((2, n, rank), f32), pltpu.SemaphoreType.DMA((2,))],
        compiler_params=pltpu.CompilerParams(vmem_limit_bytes=LIMIT),
        cost_estimate=pl.CostEstimate(flops=10**6, bytes_accessed=10**6, transcendentals=0),
    )(core, light, back2, whole)
    return z_grad, noise_grad


def solution(mesh):
    return jax.shard_map(
        on_device,
        mesh=mesh,
        in_specs=(
            P(None, "row", None),
            P(None, ("grp", "row"), None, None),
            P(None, ("grp", "row"), None, None),
            P(None, ("grp", "row"), None, None),
            P("grp", None),
        ),
        out_specs=(P(None, ("grp", "row"), None, None), P(None, ("grp", "row"), None, None)),
        check_vma=False,
    )
```
